128 devices in a mesh: dp: 2 (over core), row: 8 (over y_hi, x), col: 8 (over z, y_lo).
Axes of the slice: x: 4, y: 4 (y_hi: 2, y_lo: 2; y = y_hi * 2 + y_lo), z: 4, core: 2. Of those that a mesh axis runs over, the one named last changes fastest.
Arguments:
- block_input: bfloat16 [8192, 2048], P(('dp', 'row'), 'col'), may hold values from -6 to 6
- cotangent: bfloat16 [8192, 2048], P(('dp', 'row'), 'col'), may hold values from -6 to 6
- doc_lengths: int32 [16, 6], P(('dp', 'col')), may hold values from 1 to 384, as said below
- heads_weight: float32 [2048, 6144], P('col', 'row'), may hold values from -0.13258252 to 0.13258252
- heads_first: float32 [2048, 6144], P('col', 'row'), may hold values from -1024 to 1024
- heads_second: float32 [2048, 6144], P('col', 'row'), may hold values from 32768 to 131072
- merge_weight: float32 [2048, 2048], P('row', 'col'), may hold values from -0.13258252 to 0.13258252
- merge_first: float32 [2048, 2048], P('row', 'col'), may hold values from -1024 to 1024
- merge_second: float32 [2048, 2048], P('row', 'col'), may hold values from 32768 to 131072
- expand_weight: float32 [2048, 16384], P('col', 'row'), may hold values from -0.125 to 0.125
- expand_first: float32 [2048, 16384], P('col', 'row'), may hold values from -256 to 256
- expand_second: float32 [2048, 16384], P('col', 'row'), may hold values from 2048 to 8192
- reduce_weight: float32 [8192, 2048], P('row', 'col'), may hold values from -0.06629126 to 0.06629126
- reduce_first: float32 [8192, 2048], P('row', 'col'), may hold values from -512 to 512
- reduce_second: float32 [8192, 2048], P('row', 'col'), may hold values from 8192 to 32768
- norm_gains: float32 [4, 2048], replicated, may hold values from 0.5 to 1.5
- gains_first: float32 [4, 2048], replicated, may hold values from -768 to 768
- gains_second: float32 [4, 2048], replicated, may hold values from 16384 to 65536
Outputs:
- block_output: bfloat16 [8192, 2048], P(('dp', 'row'), 'col')
- input_grad: float32 [8192, 2048], P(('dp', 'row'), 'col')
- heads_grad: float32 [2048, 6144], P('col', 'row')
- heads_mean: float32 [2048, 6144], P('col', 'row')
- heads_square: float32 [2048, 6144], P('col', 'row')
- heads_fresh: float32 [2048, 6144], P('col', 'row')
- heads_copy: bfloat16 [2048, 6144], P('col', 'row')
- merge_grad: float32 [2048, 2048], P('row', 'col')
- merge_mean: float32 [2048, 2048], P('row', 'col')
- merge_square: float32 [2048, 2048], P('row', 'col')
- merge_fresh: float32 [2048, 2048], P('row', 'col')
- merge_copy: bfloat16 [2048, 2048], P('row', 'col')
- expand_grad: float32 [2048, 16384], P('col', 'row')
- expand_mean: float32 [2048, 16384], P('col', 'row')
- expand_square: float32 [2048, 16384], P('col', 'row')
- expand_fresh: float32 [2048, 16384], P('col', 'row')
- expand_copy: bfloat16 [2048, 16384], P('col', 'row')
- reduce_grad: float32 [8192, 2048], P('row', 'col')
- reduce_mean: float32 [8192, 2048], P('row', 'col')
- reduce_square: float32 [8192, 2048], P('row', 'col')
- reduce_fresh: float32 [8192, 2048], P('row', 'col')
- reduce_copy: bfloat16 [8192, 2048], P('row', 'col')
- gains_grad: float32 [4, 2048], replicated
- gains_mean: float32 [4, 2048], replicated
- gains_square: float32 [4, 2048], replicated
- gains_fresh: float32 [4, 2048], replicated
The draws below stay inside these ranges and needn't reach their ends.
Inputs may be any that keep to these rules, and one draw needn't show every extreme that they name: `doc_lengths`: each row sums to 512; its last entry counts the padding tokens at the sequence's end; exactly one of the other entries is the largest, 384, and the rest together hold 128 tokens.
All inputs are finite; a program needn't handle non-finite values.
Results may differ from the reference program's by a relative error of at most 0.018.
Values may be sent and summed in bfloat16 or wider, within the bound.
A program may use at most 192 MiB of HBM per device.

```python
import math
import jax
import jax.numpy as jnp
from jax import lax

D = 2048
HD = 128
FF = 8192
SEQ = 512
WINDOW = 256
NDOC = 6
STEP = 5
NSEQ = 16
TOKENS = 8192
N_ROW = 8


def draw_doc_lengths(key, part):
    key = jax.random.fold_in(key, 41)
    longest = 3 * SEQ // 4
    remaining = SEQ - longest
    others = NDOC - 1
    slots = jnp.arange(NDOC, dtype=jnp.int32)

    def one_row(row_key):
        cut_key, place_key = jax.random.split(row_key)
        cuts = jnp.sort(jax.random.permutation(cut_key, remaining - 1)[:others - 1].astype(jnp.int32) + 1)
        bounds = jnp.concatenate([jnp.zeros((1,), jnp.int32), cuts, jnp.full((1,), remaining, jnp.int32)])
        pieces = (bounds[1:] - bounds[:-1]).astype(jnp.int32)
        spot = jax.random.randint(place_key, (), 0, NDOC - 1).astype(jnp.int32)
        before = pieces[jnp.minimum(slots, others - 1)]
        after = pieces[jnp.maximum(slots - 1, 0)]
        return jnp.where(slots < spot, before, jnp.where(slots == spot, jnp.int32(longest), after)).astype(jnp.int32)
    return jax.vmap(one_row)(jax.random.split(key, NSEQ)).astype(jnp.int32)


def draw_heads_weight(key, part):
    key = jax.random.fold_in(key, 11)
    group_width = D // N_ROW
    column_ids = jnp.arange(3 * D, dtype=jnp.int32)
    feature_ids = column_ids // (3 * group_width) * group_width + column_ids % group_width
    fraction = feature_ids.astype(jnp.float32) / D
    entries = jax.random.truncated_normal(key, -4.0, 4.0, (D, 3 * D), jnp.float32)
    return entries * (0.5 + fraction)[None, :] / math.sqrt(D)


def draw_merge_weight(key, part):
    key = jax.random.fold_in(key, 23)
    fraction = jnp.arange(D, dtype=jnp.int32).astype(jnp.float32) / D
    entries = jax.random.truncated_normal(key, -4.0, 4.0, (D, D), jnp.float32)
    return entries * (0.5 + fraction)[None, :] / math.sqrt(D)


def draw_reduce_weight(key, part):
    key = jax.random.fold_in(key, 37)
    fraction = jnp.arange(D, dtype=jnp.int32).astype(jnp.float32) / D
    entries = jax.random.truncated_normal(key, -4.0, 4.0, (FF, D), jnp.float32)
    return entries * (0.5 + fraction)[None, :] / math.sqrt(FF)


def levels(key, dims, cuts, low, largest):
    def one(axis_at, shards_of):
        heights = jax.random.uniform(jax.random.fold_in(jax.random.fold_in(key, 6), axis_at), (shards_of,), jnp.float32, low / len(cuts), largest / len(cuts))
        return jnp.repeat(jnp.exp(heights), dims[axis_at] // shards_of).reshape((-1,) + (1,) * (len(dims) - axis_at - 1))

    level = one(*cuts[0])
    for cut in cuts[1:]:
        level = level * one(*cut)
    return level


def centred(key, extent, scale, bound, cuts=(), kind=jnp.bfloat16):
    loudness = levels(key, extent, cuts, -0.22, 0.18) if cuts else 1.0
    values = jax.random.normal(key, extent, jnp.float32) * scale * loudness
    return jnp.minimum(jnp.maximum(values, -bound), bound).astype(kind)


def setup_inputs(seed: int = 0) -> dict:
    splits = jax.random.split(jax.random.key(seed), 19)
    return {
        "block_input": centred(splits[0], (TOKENS, D), 1.0, 6.0, ((0, 16), (1, 8))),
        "cotangent": centred(splits[1], (TOKENS, D), 1.0, 6.0, ((0, 16), (1, 8))),
        "doc_lengths": draw_doc_lengths(jax.random.fold_in(splits[18], 71), 0),
        "heads_weight": draw_heads_weight(jax.random.fold_in(splits[18], 71), 0),
        "heads_first": centred(splits[4], (D, 3 * D), (2.0 * TOKENS ** 0.5), 1024.0, ((0, 8), (1, 8)), jnp.float32),
        "heads_second": jnp.clip(jnp.exp(math.log(131072.0) - 1.3862944 * jax.random.uniform(splits[5], (D, 3 * D), jnp.float32) ** levels(splits[5], (D, 3 * D), ((0, 8), (1, 8)), -0.2, 0.2)), 32768.0, 131072.0),
        "merge_weight": draw_merge_weight(jax.random.fold_in(splits[18], 71), 0),
        "merge_first": centred(splits[7], (D, D), (2.0 * TOKENS ** 0.5), 1024.0, ((0, 8), (1, 8)), jnp.float32),
        "merge_second": jnp.clip(jnp.exp(math.log(131072.0) - 1.3862944 * jax.random.uniform(splits[8], (D, D), jnp.float32) ** levels(splits[8], (D, D), ((0, 8), (1, 8)), -0.2, 0.2)), 32768.0, 131072.0),
        "expand_weight": centred(splits[9], (D, 2 * FF), D ** -0.5, 0.125, ((0, 8), (1, 8)), jnp.float32),
        "expand_first": centred(splits[10], (D, 2 * FF), (0.5 * TOKENS ** 0.5), 256.0, ((0, 8), (1, 8)), jnp.float32),
        "expand_second": jnp.clip(jnp.exp(math.log(8192.0) - 1.3862944 * jax.random.uniform(splits[11], (D, 2 * FF), jnp.float32) ** levels(splits[11], (D, 2 * FF), ((0, 8), (1, 8)), -0.2, 0.2)), 2048.0, 8192.0),
        "reduce_weight": draw_reduce_weight(jax.random.fold_in(splits[18], 71), 0),
        "reduce_first": centred(splits[13], (FF, D), (TOKENS ** 0.5), 512.0, ((0, 8), (1, 8)), jnp.float32),
        "reduce_second": jnp.clip(jnp.exp(math.log(32768.0) - 1.3862944 * jax.random.uniform(splits[14], (FF, D), jnp.float32) ** levels(splits[14], (FF, D), ((0, 8), (1, 8)), -0.2, 0.2)), 8192.0, 32768.0),
        "norm_gains": jnp.clip(1.0 + 0.1 * jax.random.normal(splits[15], (4, D), jnp.float32), 0.5, 1.5),
        "gains_first": centred(splits[16], (4, D), (1.5 * TOKENS ** 0.5), 768.0, (), jnp.float32),
        "gains_second": jnp.clip(jnp.exp(jax.random.uniform(splits[17], (4, D), jnp.float32, math.log(16384.0), math.log(65536.0))), 16384.0, 65536.0),
    }


EPS = 1e-06
THETA = 500000.0
LR = 0.02
LR_GAIN = 0.2
BETA_ONE = 0.5
BETA_TWO = 0.5
DECAY = 0.1
ADAM_EPS = 1e-08
HIGHEST = lax.Precision.HIGHEST

@jax.custom_vjp
def low(v):
    return lax.optimization_barrier(v.astype(jnp.bfloat16)).astype(jnp.float32)

@jax.custom_vjp
def low_back(v):
    return v

def low_keep(v):
    return (low(v), None)

def low_pass(kept, grad):
    return (grad,)

def back_keep(v):
    return (v, None)

def back_low(kept, grad):
    return (low(grad),)
low.defvjp(low_keep, low_pass)
low_back.defvjp(back_keep, back_low)

def positions(lengths, row_count):
    lengths = lengths.astype(jnp.int32)
    doc_ends = jnp.cumsum(lengths).astype(jnp.int32)
    index_ids = jnp.arange(row_count, dtype=jnp.int32)
    passed = doc_ends[None, :] <= index_ids[:, None]
    doc_ids = lax.optimization_barrier(jnp.sum(passed.astype(jnp.int32), axis=1)).astype(jnp.int32)
    starts = lax.optimization_barrier(jnp.sum(jnp.where(passed, lengths[None, :], 0), axis=1)).astype(jnp.int32)
    live_rows = (doc_ids < lengths.shape[0] - 1).astype(jnp.float32)
    return (doc_ids, (index_ids - starts).astype(jnp.int32), live_rows)

def rotate(values, places, turn_sign):
    half_dim = values.shape[-1] // 2
    frequency = THETA ** (-2.0 * jnp.arange(half_dim, dtype=jnp.float32) / values.shape[-1])
    angles = places.astype(jnp.float32)[:, None] * frequency[None, :]
    cosine = jnp.cos(angles)[:, None, :]
    sine_part = turn_sign * jnp.sin(angles)[:, None, :]
    first_half = values[..., :half_dim]
    second_half = values[..., half_dim:]
    return jnp.concatenate([first_half * cosine - second_half * sine_part, second_half * cosine + first_half * sine_part], axis=-1)

def allowed_mask(doc_ids, row_count):
    index_ids = jnp.arange(row_count, dtype=jnp.int32)
    distance = index_ids[:, None] - index_ids[None, :]
    return (doc_ids[:, None] == doc_ids[None, :]) & (distance >= 0) & (distance < WINDOW)

def attend(queries, key_rows, value_rows, lengths):
    row_count = queries.shape[0]
    doc_ids, places, live_rows = positions(lengths, row_count)
    allowed = allowed_mask(doc_ids, row_count)
    scores = low_back(jnp.einsum('qhd,khd->hqk', queries, key_rows, precision=HIGHEST) * queries.shape[-1] ** (-0.5))
    scores = jnp.where(allowed[None], scores, -1e+30)
    highest = lax.optimization_barrier(jnp.max(scores, axis=-1, keepdims=True))
    weights = jnp.exp(scores - highest)
    shares = low(weights / lax.optimization_barrier(jnp.sum(weights, axis=-1, keepdims=True)))
    mixture = jnp.einsum('hqk,khd->qhd', shares, value_rows, precision=HIGHEST)
    return mixture * live_rows[:, None, None]

def norm_rows(values, gain_row):
    return values * lax.rsqrt(lax.optimization_barrier(jnp.mean(values * values, axis=-1, keepdims=True)) + EPS) * gain_row

def forward(block_input, heads_weight, merge_weight, expand_weight, reduce_weight, norm_gains, places, doc_lengths):
    total_rows = block_input.shape[0]
    model_width = block_input.shape[1]
    slice_width = model_width // N_ROW
    heads_total = model_width // HD
    joined_cols = low_back(jnp.dot(block_input, low(heads_weight), precision=HIGHEST)).reshape(total_rows, N_ROW, 3, slice_width)
    queries = norm_rows(joined_cols[:, :, 0].reshape(total_rows, model_width), norm_gains[0])
    key_rows = norm_rows(joined_cols[:, :, 1].reshape(total_rows, model_width), norm_gains[1])
    value_rows = joined_cols[:, :, 2].reshape(total_rows, model_width)
    queries = low(rotate(queries.reshape(total_rows, heads_total, HD), places, 1.0))
    key_rows = low(rotate(key_rows.reshape(total_rows, heads_total, HD), places, 1.0))
    value_rows = low(value_rows.reshape(total_rows, heads_total, HD))
    seq_count = doc_lengths.shape[0]

    def shaped(flat_rows):
        return flat_rows.reshape(seq_count, total_rows // seq_count, heads_total, HD)

    def per_sequence(packed):
        return jax.checkpoint(attend)(packed[0], packed[1], packed[2], packed[3])
    mixture = lax.map(per_sequence, (shaped(queries), shaped(key_rows), shaped(value_rows), doc_lengths))
    mixture = low(low_back(mixture.reshape(total_rows, model_width)))
    merged = low_back(jnp.dot(mixture, low(merge_weight), precision=HIGHEST))
    residual = block_input + norm_rows(merged, norm_gains[2])
    unit_width = expand_weight.shape[1] // (2 * N_ROW)
    gated_cols = low_back(jnp.dot(low(residual), low(expand_weight), precision=HIGHEST)).reshape(total_rows, N_ROW, 2, unit_width)
    gate_vals = gated_cols[:, :, 0].reshape(total_rows, N_ROW * unit_width)
    up_vals = gated_cols[:, :, 1].reshape(total_rows, N_ROW * unit_width)
    activity = low(jax.nn.silu(gate_vals) * up_vals)
    reduced = low_back(jnp.dot(activity, low(reduce_weight), precision=HIGHEST))
    return residual + norm_rows(reduced, norm_gains[3])

def adamw(weight, gradient, first_mom, second_mom, step_rate, decay_rate):
    mean_new = BETA_ONE * first_mom + (1.0 - BETA_ONE) * gradient
    square_new = BETA_TWO * second_mom + (1.0 - BETA_TWO) * gradient * gradient
    fix_one = 1.0 - BETA_ONE ** STEP
    fix_two = 1.0 - BETA_TWO ** STEP
    update = mean_new / fix_one / (jnp.sqrt(square_new / fix_two) + ADAM_EPS) + decay_rate * weight
    return (mean_new, square_new, weight - step_rate * update)

def reference(block_input, cotangent, doc_lengths, heads_weight, heads_first, heads_second, merge_weight, merge_first, merge_second, expand_weight, expand_first, expand_second, reduce_weight, reduce_first, reduce_second, norm_gains, gains_first, gains_second):
    seq_len = block_input.shape[0] // doc_lengths.shape[0]

    def place_row(row_lengths):
        return positions(row_lengths, seq_len)[1]
    places = jax.vmap(place_row)(doc_lengths).reshape(-1).astype(jnp.int32)

    def layer_fn(inputs_f, heads_mat, merge_mat, expand_mat, reduce_mat, gains_vec):
        return forward(inputs_f, heads_mat, merge_mat, expand_mat, reduce_mat, gains_vec, places, doc_lengths)
    output_f, pullback = jax.vjp(layer_fn, block_input.astype(jnp.float32), heads_weight, merge_weight, expand_weight, reduce_weight, norm_gains)
    gradients = pullback(cotangent.astype(jnp.float32))
    heads_mean, heads_square, heads_fresh = adamw(heads_weight, gradients[1], heads_first, heads_second, LR, DECAY)
    merge_mean, merge_square, merge_fresh = adamw(merge_weight, gradients[2], merge_first, merge_second, LR, DECAY)
    expand_mean, expand_square, expand_fresh = adamw(expand_weight, gradients[3], expand_first, expand_second, LR, DECAY)
    reduce_mean, reduce_square, reduce_fresh = adamw(reduce_weight, gradients[4], reduce_first, reduce_second, LR, DECAY)
    gains_mean, gains_square, gains_fresh = adamw(norm_gains, gradients[5], gains_first, gains_second, LR_GAIN, 0.0)
    return (output_f.astype(jnp.bfloat16), gradients[0], gradients[1], heads_mean, heads_square, heads_fresh, heads_fresh.astype(jnp.bfloat16), gradients[2], merge_mean, merge_square, merge_fresh, merge_fresh.astype(jnp.bfloat16), gradients[3], expand_mean, expand_square, expand_fresh, expand_fresh.astype(jnp.bfloat16), gradients[4], reduce_mean, reduce_square, reduce_fresh, reduce_fresh.astype(jnp.bfloat16), gradients[5], gains_mean, gains_square, gains_fresh)
```

```python
import functools

import jax
import jax.numpy as jnp
from jax import lax
from jax.experimental import pallas as pl
from jax.experimental.pallas import tpu as pltpu
from jax.sharding import PartitionSpec as P

HD = 128
WINDOW = 256
STEP = 5


EPS = 1e-06
THETA = 500000.0
LR = 0.02
LR_GAIN = 0.2
BETA_ONE = 0.5
BETA_TWO = 0.5
DECAY = 0.1
ADAM_EPS = 1e-08

BF16 = jnp.bfloat16
F32 = jnp.float32
MESH = pl.DeviceIdType.MESH
ANY = pl.BlockSpec(memory_space=pl.ANY)
VMEM = pl.BlockSpec(memory_space=pltpu.VMEM)
DMA = pltpu.SemaphoreType.DMA


def positions(lengths, row_count):
    doc_ends = jnp.cumsum(lengths)
    index_ids = jnp.arange(row_count, dtype=jnp.int32)
    passed = doc_ends[None, :] <= index_ids[:, None]
    doc_ids = jnp.sum(passed.astype(jnp.int32), axis=1)
    starts = jnp.sum(jnp.where(passed, lengths[None, :], 0), axis=1)
    live_rows = (doc_ids < lengths.shape[0] - 1).astype(jnp.float32)
    return (doc_ids, index_ids - starts, live_rows)


def rotate(values, places, turn_sign):
    half_dim = values.shape[-1] // 2
    frequency = THETA ** (-2.0 * jnp.arange(half_dim, dtype=jnp.float32) / values.shape[-1])
    angles = places.astype(jnp.float32)[:, None] * frequency[None, :]
    cosine = jnp.cos(angles)[:, None, :]
    sine_part = turn_sign * jnp.sin(angles)[:, None, :]
    first_half = values[..., :half_dim]
    second_half = values[..., half_dim:]
    return jnp.concatenate(
        [
            first_half * cosine - second_half * sine_part,
            second_half * cosine + first_half * sine_part,
        ],
        axis=-1,
    )


def allowed_mask(doc_ids, row_count):
    index_ids = jnp.arange(row_count, dtype=jnp.int32)
    distance = index_ids[:, None] - index_ids[None, :]
    return (doc_ids[:, None] == doc_ids[None, :]) & (distance >= 0) & (distance < WINDOW)


def product(left_side, right_side, flipped):
    if flipped:
        return lax.dot_general(
            left_side, right_side, (((1,), (1,)), ((), ())), preferred_element_type=jnp.float32
        )
    return jnp.dot(left_side, right_side, preferred_element_type=jnp.float32)


def column_total(left_side, right_side):
    return lax.dot_general(
        left_side, right_side, (((0,), (0,)), ((), ())), preferred_element_type=jnp.float32
    )


def norm_back(grad_hat, hat_vals, rates, dots, model_width):
    return rates * (grad_hat - hat_vals * (dots / model_width)[:, None])


def attend_forward(queries, key_rows, value_rows, allowed, live_rows):
    score_scale = queries.shape[-1] ** (-0.5)
    scores = (
        jnp.einsum("qhd,khd->hqk", queries, key_rows, preferred_element_type=jnp.float32)
        * score_scale
    )
    scores = jnp.where(allowed[None], scores, -1e30)
    highest = jnp.max(scores, axis=-1, keepdims=True)
    weights = jnp.exp(scores - highest)
    totals = jnp.sum(weights, axis=-1, keepdims=True)
    shares = (weights / totals).astype(jnp.bfloat16)
    mixture = jnp.einsum("hqk,khd->qhd", shares, value_rows, preferred_element_type=jnp.float32)
    return (mixture * live_rows[:, None, None], highest + jnp.log(totals))


def attend_backward(queries, key_rows, value_rows, allowed, log_totals, grad_mix):
    score_scale = queries.shape[-1] ** (-0.5)
    scores = (
        jnp.einsum("qhd,khd->hqk", queries, key_rows, preferred_element_type=jnp.float32)
        * score_scale
    )
    scores = jnp.where(allowed[None], scores, -1e30)
    shares = jnp.exp(scores - log_totals)
    grad_shares = jnp.einsum(
        "qhd,khd->hqk", grad_mix, value_rows, preferred_element_type=jnp.float32
    )
    grad_values = jnp.einsum(
        "hqk,qhd->khd", shares.astype(jnp.bfloat16), grad_mix, preferred_element_type=jnp.float32
    )
    center = jnp.sum(shares * grad_shares, axis=-1, keepdims=True)
    grad_scores = (shares * (grad_shares - center)).astype(jnp.bfloat16)
    grad_queries = (
        jnp.einsum("hqk,khd->qhd", grad_scores, key_rows, preferred_element_type=jnp.float32)
        * score_scale
    )
    grad_keys = (
        jnp.einsum("hqk,qhd->khd", grad_scores, queries, preferred_element_type=jnp.float32)
        * score_scale
    )
    return (grad_queries, grad_keys, grad_values)


def adamw(weight, gradient, first_mom, second_mom, step_rate, decay_rate):
    mean_new = BETA_ONE * first_mom + (1.0 - BETA_ONE) * gradient
    square_new = BETA_TWO * second_mom + (1.0 - BETA_TWO) * gradient * gradient
    fix_one = 1.0 - BETA_ONE**STEP
    fix_two = 1.0 - BETA_TWO**STEP
    update = mean_new / fix_one / (jnp.sqrt(square_new / fix_two) + ADAM_EPS) + decay_rate * weight
    return (mean_new, square_new, weight - step_rate * update)


def here():
    return lax.axis_index("dp"), lax.axis_index("row"), lax.axis_index("col")


def row_peer(row, d):
    return (row // 4 + d // 4) % 2 * 4 + (row % 4 + d % 4) % 4


def z_peer(col, d):
    return (col // 2 + d) % 4 * 2 + col % 2


def z_source(col, d):
    return (col // 2 + 4 - d) % 4 * 2 + col % 2


def y_peer(col):
    return col // 2 * 2 + 1 - col % 2


def remote(source, target, sent, arrived, **where):
    return pltpu.make_async_remote_copy(
        src_ref=source,
        dst_ref=target,
        send_sem=sent,
        recv_sem=arrived,
        device_id=where,
        device_id_type=MESH,
    )


def meet(rows=False, cols=False, weights=False, spread_in=False, spread_out=False):
    dp, row, col = here()
    barrier = pltpu.get_barrier_semaphore()
    count = 0

    def greet(**where):
        pl.semaphore_signal(barrier, inc=1, device_id=where, device_id_type=MESH)

    if rows:
        for d in range(1, 8):
            greet(row=row_peer(row, d))
        count = count + 7
    if cols:
        for d in range(1, 8):
            greet(col=(col + d) % 8)
        count = count + 7
    if weights:
        greet(col=y_peer(col))
        for d in range(1, 4):
            greet(col=z_peer(col, d))
        greet(dp=1 - dp)
        count = count + 5
    for wanted, inward in ((spread_in, True), (spread_out, False)):
        if wanted:
            for k in range(8):
                at_row, at_col = (col, k) if inward else (k, row)

                @pl.when(jnp.logical_not((at_row == row) & (at_col == col)))
                def _():
                    greet(row=at_row, col=at_col)

            count = count + 8 - (row == col).astype(jnp.int32)
    pl.semaphore_wait(barrier, count)


class Spread:
    def __init__(self, inward, source, target, sent, arrived):
        dp, row, col = here()
        self.row, self.col, self.inward = row, col, inward
        self.copies = []
        for k in range(8):
            to_row, to_col = (k, row) if inward else (col, k)
            mine = (row == to_row) & (col == to_col)
            copy = remote(
                source(k),
                target(col if inward else row),
                sent.at[k],
                arrived.at[col if inward else row],
                row=to_row,
                col=to_col,
            )
            waiter = remote(source(k), target(k), sent.at[k], arrived.at[k], row=to_row, col=to_col)
            local = pltpu.make_async_copy(
                source(k), target(col if inward else row), sent.at[k]
            )
            self.copies.append((mine, copy, waiter, local))

    def start(self):
        for mine, copy, _, local in self.copies:
            pl.when(jnp.logical_not(mine))(copy.start)
            pl.when(mine)(local.start)

    def wait(self):
        for k, (mine, copy, waiter, local) in enumerate(self.copies):
            from_row, from_col = (self.col, k) if self.inward else (k, self.row)
            me = (from_row == self.row) & (from_col == self.col)
            pl.when(jnp.logical_not(me))(waiter.wait_recv)
            pl.when(jnp.logical_not(mine))(copy.wait_send)
            pl.when(mine)(local.wait)


class RowScatter:
    def __init__(self, part, arrived_rows, sent, arrived):
        dp, self.row, col = here()
        self.part, self.arrived_rows = part, arrived_rows
        self.count = arrived_rows.shape[1]
        self.copies = [
            remote(
                part.at[self.block(row_peer(self.row, d))],
                arrived_rows.at[d - 1],
                sent.at[d - 1],
                arrived.at[d - 1],
                row=row_peer(self.row, d),
            )
            for d in range(1, 8)
        ]

    def block(self, k):
        return pl.ds(pl.multiple_of(k * self.count, self.count), self.count)

    def start(self):
        for copy in self.copies:
            copy.start()

    def total(self):
        for copy in self.copies:
            copy.wait_recv()
        total = self.part[self.block(self.row)].astype(F32)
        for d in range(7):
            total = total + self.arrived_rows[d].astype(F32)
        return total

    def finish(self):
        for copy in self.copies:
            copy.wait_send()


class RowGather:
    def __init__(self, rows, whole, sent, arrived):
        dp, row, col = here()
        count = rows.shape[0]
        block = pl.ds(pl.multiple_of(row * count, count), count)
        self.copies = [
            remote(rows, whole.at[block], sent.at[d - 1], arrived.at[d - 1], row=row_peer(row, d))
            for d in range(1, 8)
        ]
        self.local = pltpu.make_async_copy(rows, whole.at[block], sent.at[7])

    def start(self):
        for copy in self.copies:
            copy.start()
        self.local.start()

    def wait(self):
        for copy in self.copies:
            copy.wait()
        self.local.wait()


def half_of(kind, ref, c, h):
    if kind == "tall":
        count = ref.shape[0] // 16
        return ref.at[pl.ds(pl.multiple_of((2 * c + h) * count, count), count)]
    count, width = ref.shape[0] // 2, ref.shape[1] // 8
    return ref.at[
        pl.ds(pl.multiple_of(h * count, count), count), pl.ds(pl.multiple_of(c * width, width), width)
    ]


def half_shard(ref, h):
    count = ref.shape[0] // 2
    return ref.at[pl.ds(pl.multiple_of(h * count, count), count)]


class WeightGather:
    def __init__(self, kind, shard, whole, sent, arrived):
        dp, _, col = here()
        self.kind, self.whole, self.sent, self.arrived = kind, whole, sent, arrived
        self.dp, self.col = dp, col
        near = y_peer(col)
        mine = half_shard(shard, dp)
        self.local = [
            pltpu.make_async_copy(half_shard(shard, h), self.half(col, h), sent.at[14 + h])
            for h in range(2)
        ]
        self.first = [remote(mine, self.half(col, dp), sent.at[0], arrived.at[0], col=near)] + [
            remote(mine, self.half(col, dp), sent.at[d], arrived.at[d], col=z_peer(col, d))
            for d in range(1, 4)
        ]
        self.second = [
            remote(
                self.half(near, dp), self.half(near, dp), sent.at[3 + d], arrived.at[3 + d],
                col=z_peer(col, d),
            )
            for d in range(1, 4)
        ]
        blocks = (
            [near]
            + [z_source(col, d) for d in range(1, 4)]
            + [y_peer(z_source(col, d)) for d in range(1, 4)]
        )
        self.across = [
            remote(self.half(b, dp), self.half(b, dp), sent.at[7 + i], arrived.at[7 + i], dp=1 - dp)
            for i, b in enumerate(blocks)
        ]

    def half(self, c, h):
        return half_of(self.kind, self.whole, c, h)

    def start(self):
        for copy in self.first + self.local:
            copy.start()

    def relay(self):
        self.first[0].wait_recv()
        for copy in self.second:
            copy.start()
        self.across[0].start()

    def share(self):
        for i in range(1, 4):
            self.first[i].wait_recv()
            self.across[i].start()
        for i in range(3):
            self.second[i].wait_recv()
            self.across[4 + i].start()

    def wait(self):
        for copy in self.across:
            copy.wait()
        for copy in self.first + self.second:
            copy.wait_send()
        for copy in self.local:
            copy.wait()


def gather_sems(n):
    return [DMA((n, 16)), DMA((n, 14))]


class GradScatter:
    def __init__(self, kind, part, out, own, other, far, near, sent, arrived):
        dp, _, col = here()
        self.dp, self.col = dp, col
        self.own, self.other, self.far, self.near = own, other, far, near
        self.load = [
            pltpu.make_async_copy(half_of(kind, part, c, dp), own.at[c], sent.at[8 + c])
            for c in range(8)
        ]
        self.core = [
            remote(half_of(kind, part, c, 1 - dp), other.at[c], sent.at[c], arrived.at[c], dp=1 - dp)
            for c in range(8)
        ]
        self.zs = [
            remote(
                own.at[pl.ds(z_peer(col, d) // 2 * 2, 2)], far.at[d - 1], sent.at[15 + d],
                arrived.at[7 + d], col=z_peer(col, d),
            )
            for d in range(1, 4)
        ]
        self.ys = remote(near.at[0], near.at[1], sent.at[19], arrived.at[11], col=y_peer(col))
        self.last = remote(
            near.at[0], half_shard(out, dp), sent.at[20], arrived.at[12], dp=1 - dp
        )
        self.keep = pltpu.make_async_copy(near.at[0], half_shard(out, dp), sent.at[21])

    def start(self):
        for copy in self.load + self.core:
            copy.start()

    def each(self, rows, body):
        @pl.loop(0, rows // 16)
        def _(i):
            body(pl.ds(pl.multiple_of(i * 16, 16), 16))

    def over_z(self):
        for c in range(8):
            self.load[c].wait()
            self.core[c].wait_recv()
        rows = self.own.shape[1]

        @pl.loop(0, 8)
        def _(c):
            def add(at):
                self.own[c, at] = (self.own[c, at].astype(F32) + self.other[c, at].astype(F32)).astype(BF16)

            self.each(rows, add)

        for copy in self.zs:
            copy.start()

    def over_y(self):
        for copy in self.zs:
            copy.wait_recv()
        rows = self.own.shape[1]
        yl = self.col % 2

        def total(at, c, k):
            sums = self.own[c, at].astype(F32)
            for d in range(3):
                sums = sums + self.far[d, k, at].astype(F32)
            return sums.astype(BF16)

        def add(at):
            self.near[0, at] = total(at, y_peer(self.col), 1 - yl)

        self.each(rows, add)
        self.ys.start()
        for copy in self.zs:
            copy.wait_send()

        def keep(at):
            self.own[self.col, at] = total(at, self.col, yl)

        self.each(rows, keep)

    def over_core(self):
        self.ys.wait()
        rows = self.own.shape[1]

        def add(at):
            self.near[0, at] = (self.own[self.col, at].astype(F32) + self.near[1, at].astype(F32)).astype(BF16)

        self.each(rows, add)
        self.last.start()
        self.keep.start()

    def wait(self):
        for copy in self.core:
            copy.wait_send()
        self.last.wait()
        self.keep.wait()


def grad_scratch(rows, width):
    return [
        pltpu.VMEM((8, rows, width), BF16),
        pltpu.VMEM((8, rows, width), BF16),
        pltpu.VMEM((3, 2, rows, width), BF16),
        pltpu.VMEM((2, rows, width), BF16),
        DMA((22,)),
        DMA((13,)),
    ]


def mean_rate(values):
    return lax.rsqrt(jnp.mean(values * values, axis=-1, keepdims=True) + EPS)


def call(kernel, name, number, outs, ins, in_specs, out_specs, scratch):
    return pl.pallas_call(
        kernel,
        name=name,
        out_shape=outs,
        in_specs=in_specs,
        out_specs=out_specs,
        scratch_shapes=scratch,
        compiler_params=pltpu.CompilerParams(
            collective_id=number, has_side_effects=True, vmem_limit_bytes=56 * 2**20
        ),
    )(*ins)


def struct(shape, kind):
    return jax.ShapeDtypeStruct(shape, kind)


def cols(ref, k, width):
    return ref.at[:, pl.ds(pl.multiple_of(k * width, width), width)]


def rows_of(ref, k, count):
    return ref.at[pl.ds(pl.multiple_of(k * count, count), count)]


def bring_kernel(x, g, heads, merge, xs, gs, heads_all, merge_all, xsent, xcame, gsent, gcame, wsent, wcame):
    meet(weights=True, spread_in=True)
    spread_x = Spread(True, lambda k: x, lambda k: cols(xs, k, 256), xsent, xcame)
    spread_g = Spread(True, lambda k: rows_of(g, k, 64), lambda k: cols(gs, k, 256), gsent, gcame)
    gathers = [
        WeightGather("tall", heads, heads_all, wsent.at[0], wcame.at[0]),
        WeightGather("wide", merge, merge_all, wsent.at[1], wcame.at[1]),
    ]
    spread_x.start()
    for gather in gathers:
        gather.start()
    spread_g.start()
    for gather in gathers:
        gather.relay()
    for gather in gathers:
        gather.share()
    spread_x.wait()
    spread_g.wait()
    for gather in gathers:
        gather.wait()


def sums_kernel(part, out, came, sent, arrived):
    dp, row, col = here()
    meet(rows=True)
    copies = [
        remote(part, came.at[d - 1], sent.at[d - 1], arrived.at[d - 1], row=row_peer(row, d))
        for d in range(1, 8)
    ]
    for copy in copies:
        copy.start()
    total = part[...]
    for d, copy in enumerate(copies):
        copy.wait_recv()
        total = total + came[d]
    out[...] = total
    for copy in copies:
        copy.wait_send()


def merged_kernel(
    part, x, gain, expand, reduce, merged, residual, rows_all, expand_all, reduce_all,
    came, mine, ssent, scame, gsent, gcame, wsent, wcame,
):
    meet(rows=True, weights=True)
    scatter = RowScatter(part, came, ssent, scame)
    gather = RowGather(mine, rows_all, gsent, gcame)
    weights = [
        WeightGather("tall", expand, expand_all, wsent.at[0], wcame.at[0]),
        WeightGather("wide", reduce, reduce_all, wsent.at[1], wcame.at[1]),
    ]
    scatter.start()
    for weight in weights:
        weight.start()
    for weight in weights:
        weight.relay()
    total = scatter.total()
    merged[...] = total
    result = x[...].astype(F32) + total * mean_rate(total) * gain[...]
    residual[...] = result
    mine[...] = result.astype(BF16)
    gather.start()
    for weight in weights:
        weight.share()
    scatter.finish()
    gather.wait()
    for weight in weights:
        weight.wait()


def back_of(grad, values, gain):
    rate = mean_rate(values)
    hat = values * rate
    grad_hat = grad * gain
    dots = jnp.mean(grad_hat * hat, axis=-1, keepdims=True)
    return hat, rate * (grad_hat - hat * dots)


def reduced_kernel(
    part, residual, g, gain, out, rows_all, gain_part,
    came, mine, done, ssent, scame, gsent, gcame, osent, ocame,
):
    meet(rows=True, spread_out=True)
    scatter = RowScatter(part, came, ssent, scame)
    gather = RowGather(mine, rows_all, gsent, gcame)
    spread = Spread(False, lambda k: cols(done, k, 256), lambda k: rows_of(out, k, 64), osent, ocame)
    scatter.start()
    total = scatter.total()
    grad = g[...].astype(F32)
    hat, back = back_of(grad, total, gain[...])
    mine[...] = back.astype(BF16)
    gather.start()
    done[...] = (residual[...] + hat * gain[...]).astype(BF16)
    spread.start()
    gain_part[...] = jnp.sum(grad * hat, axis=0, keepdims=True)
    scatter.finish()
    gather.wait()
    spread.wait()


def branch_kernel(
    part, g, merged, gain, expand_part, grad_resid, rows_all, gain_part, expand_grad,
    came, mine, ssent, scame, gsent, gcame, *grad_refs,
):
    meet(rows=True, weights=True)
    scatter = RowScatter(part, came, ssent, scame)
    gather = RowGather(mine, rows_all, gsent, gcame)
    expand = GradScatter("tall", expand_part, expand_grad, *grad_refs)
    scatter.start()
    expand.start()
    expand.over_z()
    grad = g[...].astype(F32) + scatter.total()
    grad_resid[...] = grad
    hat, back = back_of(grad, merged[...], gain[...])
    mine[...] = back.astype(BF16)
    gather.start()
    gain_part[...] = jnp.sum(grad * hat, axis=0, keepdims=True)
    scatter.finish()
    expand.over_y()
    expand.over_core()
    gather.wait()
    expand.wait()


def last_kernel(
    part, grad_resid, gains, heads_part, merge_part, reduce_part,
    input_grad, gains_grad, heads_grad, merge_grad, reduce_grad,
    came, done, grow, gcol, gcore, gsum, ssent, scame, osent, ocame, gsent, gcame, *grad_refs,
):
    dp, row, col = here()
    meet(rows=True, cols=True, weights=True, spread_out=True)
    scatter = RowScatter(part, came, ssent, scame)
    spread = Spread(False, lambda k: cols(done, k, 256), lambda k: rows_of(input_grad, k, 64), osent, ocame)
    grads = [
        GradScatter("wide", reduce_part, reduce_grad, *grad_refs[:6]),
        GradScatter("tall", heads_part, heads_grad, *grad_refs[6:12]),
        GradScatter("wide", merge_part, merge_grad, *grad_refs[12:]),
    ]
    row_sums = [
        remote(gains, grow.at[row], gsent.at[d - 1], gcame.at[d - 1], row=row_peer(row, d))
        for d in range(1, 8)
    ]
    col_sums = [
        remote(gsum.at[0], gcol.at[col], gsent.at[6 + d], gcame.at[6 + d], col=(col + d) % 8)
        for d in range(1, 8)
    ]
    core_sum = remote(gsum.at[1], gcore, gsent.at[14], gcame.at[14], dp=1 - dp)
    for copy in row_sums:
        copy.start()
    scatter.start()
    for grad in grads:
        grad.start()
    grow[row] = gains[...]
    for grad in grads:
        grad.over_z()
    for copy in row_sums:
        copy.wait()
    total = grow[0]
    for k in range(1, 8):
        total = total + grow[k]
    gsum[0] = total
    for copy in col_sums:
        copy.start()
    gcol[col] = total
    done[...] = grad_resid[...] + scatter.total()
    spread.start()
    for copy in col_sums:
        copy.wait()
    total = gcol[0]
    for k in range(1, 8):
        total = total + gcol[k]
    gsum[1] = total
    core_sum.start()
    for grad in grads:
        grad.over_y()
    for grad in grads:
        grad.over_core()
    core_sum.wait()
    gains_grad[...] = total + gcore[...]
    scatter.finish()
    spread.wait()
    for grad in grads:
        grad.wait()


def on_device(
    block_input,
    cotangent,
    doc_lengths,
    heads_weight,
    heads_first,
    heads_second,
    merge_weight,
    merge_first,
    merge_second,
    expand_weight,
    expand_first,
    expand_second,
    reduce_weight,
    reduce_first,
    reduce_second,
    norm_gains,
    gains_first,
    gains_second,
):
    row_at = lax.axis_index("row")
    col_width = block_input.shape[1]
    model_width = col_width * lax.axis_size("col")
    head_width = merge_weight.shape[0]
    unit_width = reduce_weight.shape[0]
    seq_len = block_input.shape[0] * lax.axis_size("row") // lax.axis_size("col")
    share = seq_len // lax.axis_size("row")
    head_count = head_width // HD
    doc_ids, places, live_rows = positions(doc_lengths[0], seq_len)
    allowed = allowed_mask(doc_ids, seq_len)
    gain_query = lax.dynamic_slice_in_dim(norm_gains[0], row_at * head_width, head_width)
    gain_key = lax.dynamic_slice_in_dim(norm_gains[1], row_at * head_width, head_width)
    gain_merge, gain_reduce = norm_gains[2:3], norm_gains[3:4]
    rows_shape = struct((seq_len, model_width), BF16)
    mine_f32 = struct((share, model_width), F32)
    line = struct((1, model_width), F32)
    row_scratch = [
        pltpu.VMEM((7, share, model_width), BF16),
        pltpu.VMEM((share, model_width), BF16),
        DMA((7,)),
        DMA((7,)),
        DMA((8,)),
        DMA((7,)),
    ]

    input_rows, cot_share, heads_low, merge_low = call(
        bring_kernel, "bring", 1,
        [rows_shape, struct((share, model_width), BF16), struct((model_width, 3 * head_width), BF16),
         struct((head_width, model_width), BF16)],
        [block_input, cotangent, heads_weight.astype(BF16), merge_weight.astype(BF16)],
        [ANY] * 4, [ANY] * 4,
        [DMA((8,)), DMA((8,)), DMA((8,)), DMA((8,))] + gather_sems(2),
    )
    joined_cols = product(input_rows, heads_low, False)
    queries = joined_cols[:, :head_width]
    key_rows = joined_cols[:, head_width : 2 * head_width]
    value_rows = joined_cols[:, 2 * head_width :]

    def head_sums(one, two, number):
        part = jnp.concatenate([one, two]).reshape(8, 128)
        total = call(
            sums_kernel, "sums", number, struct((8, 128), F32), [part], [VMEM], VMEM,
            [pltpu.VMEM((7, 8, 128), F32), DMA((7,)), DMA((7,))],
        ).reshape(2, seq_len)
        return total[0], total[1]

    query_sq, key_sq = head_sums(
        jnp.sum(queries * queries, axis=1), jnp.sum(key_rows * key_rows, axis=1), 2
    )
    query_rate = lax.rsqrt(query_sq / model_width + EPS)[:, None]
    key_rate = lax.rsqrt(key_sq / model_width + EPS)[:, None]
    query_hat = queries * query_rate
    key_hat = key_rows * key_rate
    query_low = rotate(
        (query_hat * gain_query).reshape(seq_len, head_count, HD), places, 1.0
    ).astype(jnp.bfloat16)
    key_low = rotate((key_hat * gain_key).reshape(seq_len, head_count, HD), places, 1.0).astype(
        jnp.bfloat16
    )
    value_low = value_rows.reshape(seq_len, head_count, HD).astype(jnp.bfloat16)
    mixture, log_totals = attend_forward(query_low, key_low, value_low, allowed, live_rows)
    mixture_low = mixture.reshape(seq_len, head_width).astype(jnp.bfloat16)
    merged_part = product(mixture_low, merge_low, False).astype(BF16)

    input_share = lax.dynamic_slice_in_dim(input_rows, row_at * share, share)
    merged, residual, residual_rows, expand_low, reduce_low = call(
        merged_kernel, "merged", 3,
        [mine_f32, mine_f32, rows_shape, struct((model_width, 2 * unit_width), BF16),
         struct((unit_width, model_width), BF16)],
        [merged_part, input_share, gain_merge, expand_weight.astype(BF16), reduce_weight.astype(BF16)],
        [VMEM, VMEM, VMEM, ANY, ANY], [VMEM, VMEM, ANY, ANY, ANY],
        row_scratch + gather_sems(2),
    )
    gated_cols = product(residual_rows, expand_low, False)
    gate_vals = gated_cols[:, :unit_width]
    up_vals = gated_cols[:, unit_width:]
    activity = (jax.nn.silu(gate_vals) * up_vals).astype(jnp.bfloat16)
    reduced_part = product(activity, reduce_low, False).astype(BF16)

    block_output, reduced_grad_rows, reduce_gain_part = call(
        reduced_kernel, "reduced", 4,
        [struct(block_input.shape, BF16), rows_shape, line],
        [reduced_part, residual, cot_share, gain_reduce],
        [VMEM] * 4, [ANY, ANY, VMEM],
        row_scratch[:2] + [pltpu.VMEM((share, model_width), BF16)] + row_scratch[2:] + [DMA((8,)), DMA((8,))],
    )
    grad_activity = product(reduced_grad_rows, reduce_low, True)
    sigmoid_vals = jax.nn.sigmoid(gate_vals)
    grad_gate = grad_activity * up_vals * sigmoid_vals * (1.0 + gate_vals * (1.0 - sigmoid_vals))
    grad_up = grad_activity * jax.nn.silu(gate_vals)
    gated_grad = jnp.concatenate([grad_gate, grad_up], axis=1).astype(jnp.bfloat16)
    branch_part = product(gated_grad, expand_low, True).astype(BF16)
    expand_part = column_total(residual_rows, gated_grad).astype(BF16)
    reduce_part = column_total(activity, reduced_grad_rows).astype(BF16)

    grad_resid, merged_grad_rows, merge_gain_part, expand_grad = call(
        branch_kernel, "branch", 5,
        [mine_f32, rows_shape, line, struct(expand_weight.shape, BF16)],
        [branch_part, cot_share, merged, gain_merge, expand_part],
        [VMEM] * 4 + [ANY], [VMEM, ANY, VMEM, ANY],
        row_scratch + grad_scratch(expand_weight.shape[0] // 2, expand_weight.shape[1]),
    )
    grad_mixture = product(merged_grad_rows, merge_low, True)
    merge_part = column_total(mixture_low, merged_grad_rows).astype(BF16)
    grad_mix_low = (
        grad_mixture.astype(jnp.bfloat16).reshape(seq_len, head_count, HD)
        * live_rows.astype(jnp.bfloat16)[:, None, None]
    )
    grad_queries, grad_keys, grad_values = attend_backward(
        query_low, key_low, value_low, allowed, log_totals, grad_mix_low
    )
    query_norm_grad = rotate(grad_queries, places, -1.0).reshape(seq_len, head_width)
    key_norm_grad = rotate(grad_keys, places, -1.0).reshape(seq_len, head_width)
    query_gain_part = jnp.sum(query_norm_grad * query_hat, axis=0)
    key_gain_part = jnp.sum(key_norm_grad * key_hat, axis=0)
    query_hat_grad = query_norm_grad * gain_query
    key_hat_grad = key_norm_grad * gain_key
    query_dot, key_dot = head_sums(
        jnp.sum(query_hat_grad * query_hat, axis=1), jnp.sum(key_hat_grad * key_hat, axis=1), 6
    )
    grad_query_rows = norm_back(query_hat_grad, query_hat, query_rate, query_dot, model_width)
    grad_key_rows = norm_back(key_hat_grad, key_hat, key_rate, key_dot, model_width)
    joined_grad = jnp.concatenate(
        [grad_query_rows, grad_key_rows, grad_values.reshape(seq_len, head_width)], axis=1
    ).astype(jnp.bfloat16)
    input_part = product(joined_grad, heads_low, True).astype(BF16)
    heads_part = column_total(input_rows, joined_grad).astype(BF16)
    gain_parts = jnp.zeros((2, model_width), jnp.float32)
    gain_parts = lax.dynamic_update_slice(
        gain_parts, jnp.stack([query_gain_part, key_gain_part]), (jnp.int32(0), row_at * head_width)
    )
    gain_parts = jnp.concatenate([gain_parts, merge_gain_part, reduce_gain_part]).reshape(8, model_width // 2)
    gain_shape = (8, model_width // 2)

    input_grad, gains_grad, heads_grad, merge_grad, reduce_grad = call(
        last_kernel, "last", 7,
        [struct(block_input.shape, F32), struct(gain_shape, F32), struct(heads_weight.shape, BF16),
         struct(merge_weight.shape, BF16), struct(reduce_weight.shape, BF16)],
        [input_part, grad_resid, gain_parts, heads_part, merge_part, reduce_part],
        [VMEM] * 3 + [ANY] * 3, [ANY, VMEM] + [ANY] * 3,
        [row_scratch[0], pltpu.VMEM((share, model_width), F32), pltpu.VMEM((8, *gain_shape), F32),
         pltpu.VMEM((8, *gain_shape), F32), pltpu.VMEM(gain_shape, F32), pltpu.VMEM((2, *gain_shape), F32),
         DMA((7,)), DMA((7,)), DMA((8,)), DMA((8,)), DMA((15,)), DMA((15,))]
        + grad_scratch(reduce_weight.shape[0] // 2, reduce_weight.shape[1])
        + grad_scratch(heads_weight.shape[0] // 2, heads_weight.shape[1])
        + grad_scratch(merge_weight.shape[0] // 2, merge_weight.shape[1]),
    )
    gains_grad = gains_grad.reshape(4, model_width)
    heads_grad, merge_grad, expand_grad, reduce_grad = (
        heads_grad.astype(F32), merge_grad.astype(F32), expand_grad.astype(F32), reduce_grad.astype(F32)
    )
    heads_mean, heads_square, heads_fresh = adamw(
        heads_weight, heads_grad, heads_first, heads_second, LR, DECAY
    )
    merge_mean, merge_square, merge_fresh = adamw(
        merge_weight, merge_grad, merge_first, merge_second, LR, DECAY
    )
    expand_mean, expand_square, expand_fresh = adamw(
        expand_weight, expand_grad, expand_first, expand_second, LR, DECAY
    )
    reduce_mean, reduce_square, reduce_fresh = adamw(
        reduce_weight, reduce_grad, reduce_first, reduce_second, LR, DECAY
    )
    gains_mean, gains_square, gains_fresh = adamw(
        norm_gains, gains_grad, gains_first, gains_second, LR_GAIN, 0.0
    )
    return (
        block_output,
        input_grad,
        heads_grad,
        heads_mean,
        heads_square,
        heads_fresh,
        heads_fresh.astype(jnp.bfloat16),
        merge_grad,
        merge_mean,
        merge_square,
        merge_fresh,
        merge_fresh.astype(jnp.bfloat16),
        expand_grad,
        expand_mean,
        expand_square,
        expand_fresh,
        expand_fresh.astype(jnp.bfloat16),
        reduce_grad,
        reduce_mean,
        reduce_square,
        reduce_fresh,
        reduce_fresh.astype(jnp.bfloat16),
        gains_grad,
        gains_mean,
        gains_square,
        gains_fresh,
    )


def solution(mesh):
    return jax.shard_map(
        on_device,
        mesh=mesh,
        in_specs=(
            P(("dp", "row"), "col"),
            P(("dp", "row"), "col"),
            P(("dp", "col"), None),
            P("col", "row"),
            P("col", "row"),
            P("col", "row"),
            P("row", "col"),
            P("row", "col"),
            P("row", "col"),
            P("col", "row"),
            P("col", "row"),
            P("col", "row"),
            P("row", "col"),
            P("row", "col"),
            P("row", "col"),
            P(),
            P(),
            P(),
        ),
        out_specs=(
            P(("dp", "row"), "col"),
            P(("dp", "row"), "col"),
            P("col", "row"),
            P("col", "row"),
            P("col", "row"),
            P("col", "row"),
            P("col", "row"),
            P("row", "col"),
            P("row", "col"),
            P("row", "col"),
            P("row", "col"),
            P("row", "col"),
            P("col", "row"),
            P("col", "row"),
            P("col", "row"),
            P("col", "row"),
            P("col", "row"),
            P("row", "col"),
            P("row", "col"),
            P("row", "col"),
            P("row", "col"),
            P("row", "col"),
            P(),
            P(),
            P(),
            P(),
        ),
        check_vma=False,
    )
```

```python
import functools

import jax
import jax.numpy as jnp
from jax import lax
from jax.experimental import pallas as pl
from jax.experimental.pallas import tpu as pltpu
from jax.sharding import PartitionSpec as P

HD = 128
WINDOW = 256
STEP = 5


EPS = 1e-06
THETA = 500000.0
LR = 0.02
LR_GAIN = 0.2
BETA_ONE = 0.5
BETA_TWO = 0.5
DECAY = 0.1
ADAM_EPS = 1e-08

BF16 = jnp.bfloat16
F32 = jnp.float32
MESH = pl.DeviceIdType.MESH
ANY = pl.BlockSpec(memory_space=pl.ANY)
VMEM = pl.BlockSpec(memory_space=pltpu.VMEM)
DMA = pltpu.SemaphoreType.DMA


def positions(lengths, row_count):
    doc_ends = jnp.cumsum(lengths)
    index_ids = jnp.arange(row_count, dtype=jnp.int32)
    passed = doc_ends[None, :] <= index_ids[:, None]
    doc_ids = jnp.sum(passed.astype(jnp.int32), axis=1)
    starts = jnp.sum(jnp.where(passed, lengths[None, :], 0), axis=1)
    live_rows = (doc_ids < lengths.shape[0] - 1).astype(jnp.float32)
    return (doc_ids, index_ids - starts, live_rows)


def rotate(values, places, turn_sign):
    half_dim = values.shape[-1] // 2
    frequency = THETA ** (-2.0 * jnp.arange(half_dim, dtype=jnp.float32) / values.shape[-1])
    angles = places.astype(jnp.float32)[:, None] * frequency[None, :]
    cosine = jnp.cos(angles)[:, None, :]
    sine_part = turn_sign * jnp.sin(angles)[:, None, :]
    first_half = values[..., :half_dim]
    second_half = values[..., half_dim:]
    return jnp.concatenate(
        [
            first_half * cosine - second_half * sine_part,
            second_half * cosine + first_half * sine_part,
        ],
        axis=-1,
    )


def allowed_mask(doc_ids, row_count):
    index_ids = jnp.arange(row_count, dtype=jnp.int32)
    distance = index_ids[:, None] - index_ids[None, :]
    return (doc_ids[:, None] == doc_ids[None, :]) & (distance >= 0) & (distance < WINDOW)


def product(left_side, right_side, flipped):
    if flipped:
        return lax.dot_general(
            left_side, right_side, (((1,), (1,)), ((), ())), preferred_element_type=jnp.float32
        )
    return jnp.dot(left_side, right_side, preferred_element_type=jnp.float32)


def column_total(left_side, right_side):
    return lax.dot_general(
        left_side, right_side, (((0,), (0,)), ((), ())), preferred_element_type=jnp.float32
    )


def norm_back(grad_hat, hat_vals, rates, dots, model_width):
    return rates * (grad_hat - hat_vals * (dots / model_width)[:, None])


def attend_forward(queries, key_rows, value_rows, allowed, live_rows):
    score_scale = queries.shape[-1] ** (-0.5)
    scores = (
        jnp.einsum("qhd,khd->hqk", queries, key_rows, preferred_element_type=jnp.float32)
        * score_scale
    )
    scores = jnp.where(allowed[None], scores, -1e30)
    highest = jnp.max(scores, axis=-1, keepdims=True)
    weights = jnp.exp(scores - highest)
    totals = jnp.sum(weights, axis=-1, keepdims=True)
    shares = (weights / totals).astype(jnp.bfloat16)
    mixture = jnp.einsum("hqk,khd->qhd", shares, value_rows, preferred_element_type=jnp.float32)
    return (mixture * live_rows[:, None, None], highest + jnp.log(totals))


def attend_backward(queries, key_rows, value_rows, allowed, log_totals, grad_mix):
    score_scale = queries.shape[-1] ** (-0.5)
    scores = (
        jnp.einsum("qhd,khd->hqk", queries, key_rows, preferred_element_type=jnp.float32)
        * score_scale
    )
    scores = jnp.where(allowed[None], scores, -1e30)
    shares = jnp.exp(scores - log_totals)
    grad_shares = jnp.einsum(
        "qhd,khd->hqk", grad_mix, value_rows, preferred_element_type=jnp.float32
    )
    grad_values = jnp.einsum(
        "hqk,qhd->khd", shares.astype(jnp.bfloat16), grad_mix, preferred_element_type=jnp.float32
    )
    center = jnp.sum(shares * grad_shares, axis=-1, keepdims=True)
    grad_scores = (shares * (grad_shares - center)).astype(jnp.bfloat16)
    grad_queries = (
        jnp.einsum("hqk,khd->qhd", grad_scores, key_rows, preferred_element_type=jnp.float32)
        * score_scale
    )
    grad_keys = (
        jnp.einsum("hqk,qhd->khd", grad_scores, queries, preferred_element_type=jnp.float32)
        * score_scale
    )
    return (grad_queries, grad_keys, grad_values)


def adamw(weight, gradient, first_mom, second_mom, step_rate, decay_rate):
    mean_new = BETA_ONE * first_mom + (1.0 - BETA_ONE) * gradient
    square_new = BETA_TWO * second_mom + (1.0 - BETA_TWO) * gradient * gradient
    fix_one = 1.0 - BETA_ONE**STEP
    fix_two = 1.0 - BETA_TWO**STEP
    update = mean_new / fix_one / (jnp.sqrt(square_new / fix_two) + ADAM_EPS) + decay_rate * weight
    return (mean_new, square_new, weight - step_rate * update)


def here():
    return lax.axis_index("dp"), lax.axis_index("row"), lax.axis_index("col")


def row_peer(row, d):
    return (row // 4 + d // 4) % 2 * 4 + (row % 4 + d % 4) % 4


def z_peer(col, d):
    return (col // 2 + d) % 4 * 2 + col % 2


def z_source(col, d):
    return (col // 2 + 4 - d) % 4 * 2 + col % 2


def y_peer(col):
    return col // 2 * 2 + 1 - col % 2


def remote(source, target, sent, arrived, **where):
    return pltpu.make_async_remote_copy(
        src_ref=source,
        dst_ref=target,
        send_sem=sent,
        recv_sem=arrived,
        device_id=where,
        device_id_type=MESH,
    )


def meet(rows=False, cols=False, weights=False, spread_in=False, spread_out=False):
    dp, row, col = here()
    barrier = pltpu.get_barrier_semaphore()
    count = 0

    def greet(**where):
        pl.semaphore_signal(barrier, inc=1, device_id=where, device_id_type=MESH)

    if rows:
        for d in range(1, 8):
            greet(row=row_peer(row, d))
        count = count + 7
    if cols:
        for d in range(1, 8):
            greet(col=(col + d) % 8)
        count = count + 7
    if weights:
        greet(col=y_peer(col))
        for d in range(1, 4):
            greet(col=z_peer(col, d))
        greet(dp=1 - dp)
        count = count + 5
    for wanted, inward in ((spread_in, True), (spread_out, False)):
        if wanted:
            for k in range(8):
                at_row, at_col = (col, k) if inward else (k, row)

                @pl.when(jnp.logical_not((at_row == row) & (at_col == col)))
                def _():
                    greet(row=at_row, col=at_col)

            count = count + 8 - (row == col).astype(jnp.int32)
    pl.semaphore_wait(barrier, count)


class Spread:
    def __init__(self, inward, source, target, sent, arrived):
        dp, row, col = here()
        self.row, self.col, self.inward = row, col, inward
        self.copies = []
        for k in range(8):
            to_row, to_col = (k, row) if inward else (col, k)
            mine = (row == to_row) & (col == to_col)
            copy = remote(
                source(k),
                target(col if inward else row),
                sent.at[k],
                arrived.at[col if inward else row],
                row=to_row,
                col=to_col,
            )
            waiter = remote(source(k), target(k), sent.at[k], arrived.at[k], row=to_row, col=to_col)
            local = pltpu.make_async_copy(
                source(k), target(col if inward else row), sent.at[k]
            )
            self.copies.append((mine, copy, waiter, local))

    def start(self):
        for mine, copy, _, local in self.copies:
            pl.when(jnp.logical_not(mine))(copy.start)
            pl.when(mine)(local.start)

    def wait(self):
        for k, (mine, copy, waiter, local) in enumerate(self.copies):
            from_row, from_col = (self.col, k) if self.inward else (k, self.row)
            me = (from_row == self.row) & (from_col == self.col)
            pl.when(jnp.logical_not(me))(waiter.wait_recv)
            pl.when(jnp.logical_not(mine))(copy.wait_send)
            pl.when(mine)(local.wait)


class RowScatter:
    def __init__(self, part, arrived_rows, sent, arrived):
        dp, self.row, col = here()
        self.part, self.arrived_rows = part, arrived_rows
        self.count = arrived_rows.shape[1]
        self.copies = [
            remote(
                part.at[self.block(row_peer(self.row, d))],
                arrived_rows.at[d - 1],
                sent.at[d - 1],
                arrived.at[d - 1],
                row=row_peer(self.row, d),
            )
            for d in range(1, 8)
        ]

    def block(self, k):
        return pl.ds(pl.multiple_of(k * self.count, self.count), self.count)

    def start(self):
        for copy in self.copies:
            copy.start()

    def total(self):
        for copy in self.copies:
            copy.wait_recv()
        total = self.part[self.block(self.row)].astype(F32)
        for d in range(7):
            total = total + self.arrived_rows[d].astype(F32)
        return total

    def finish(self):
        for copy in self.copies:
            copy.wait_send()


class RowGather:
    def __init__(self, rows, whole, sent, arrived):
        dp, row, col = here()
        count = rows.shape[0]
        block = pl.ds(pl.multiple_of(row * count, count), count)
        self.copies = [
            remote(rows, whole.at[block], sent.at[d - 1], arrived.at[d - 1], row=row_peer(row, d))
            for d in range(1, 8)
        ]
        self.local = pltpu.make_async_copy(rows, whole.at[block], sent.at[7])

    def start(self):
        for copy in self.copies:
            copy.start()
        self.local.start()

    def wait(self):
        for copy in self.copies:
            copy.wait()
        self.local.wait()


def half_of(kind, ref, c, h):
    if kind == "tall":
        count = ref.shape[0] // 16
        return ref.at[pl.ds(pl.multiple_of((2 * c + h) * count, count), count)]
    count, width = ref.shape[0] // 2, ref.shape[1] // 8
    return ref.at[
        pl.ds(pl.multiple_of(h * count, count), count), pl.ds(pl.multiple_of(c * width, width), width)
    ]


def half_shard(ref, h):
    count = ref.shape[0] // 2
    return ref.at[pl.ds(pl.multiple_of(h * count, count), count)]


class WeightGather:
    def __init__(self, kind, shard, whole, sent, arrived):
        dp, _, col = here()
        self.kind, self.whole, self.sent, self.arrived = kind, whole, sent, arrived
        self.dp, self.col = dp, col
        near = y_peer(col)
        mine = half_shard(shard, dp)
        self.local = [
            pltpu.make_async_copy(half_shard(shard, h), self.half(col, h), sent.at[14 + h])
            for h in range(2)
        ]
        self.first = [remote(mine, self.half(col, dp), sent.at[0], arrived.at[0], col=near)] + [
            remote(mine, self.half(col, dp), sent.at[d], arrived.at[d], col=z_peer(col, d))
            for d in range(1, 4)
        ]
        self.second = [
            remote(
                self.half(near, dp), self.half(near, dp), sent.at[3 + d], arrived.at[3 + d],
                col=z_peer(col, d),
            )
            for d in range(1, 4)
        ]
        blocks = (
            [near]
            + [z_source(col, d) for d in range(1, 4)]
            + [y_peer(z_source(col, d)) for d in range(1, 4)]
        )
        self.across = [
            remote(self.half(b, dp), self.half(b, dp), sent.at[7 + i], arrived.at[7 + i], dp=1 - dp)
            for i, b in enumerate(blocks)
        ]

    def half(self, c, h):
        return half_of(self.kind, self.whole, c, h)

    def start(self):
        for copy in self.first + self.local:
            copy.start()

    def relay(self):
        self.first[0].wait_recv()
        for copy in self.second:
            copy.start()
        self.across[0].start()

    def share(self):
        for i in range(1, 4):
            self.first[i].wait_recv()
            self.across[i].start()
        for i in range(3):
            self.second[i].wait_recv()
            self.across[4 + i].start()

    def wait(self):
        for copy in self.across:
            copy.wait()
        for copy in self.first + self.second:
            copy.wait_send()
        for copy in self.local:
            copy.wait()


def gather_sems(n):
    return [DMA((n, 16)), DMA((n, 14))]


class GradScatter:
    def __init__(self, kind, part, out, own, other, far, near, sent, arrived):
        dp, _, col = here()
        self.dp, self.col = dp, col
        self.own, self.other, self.far, self.near = own, other, far, near
        self.load = [
            pltpu.make_async_copy(half_of(kind, part, c, dp), own.at[c], sent.at[8 + c])
            for c in range(8)
        ]
        self.core = [
            remote(half_of(kind, part, c, 1 - dp), other.at[c], sent.at[c], arrived.at[c], dp=1 - dp)
            for c in range(8)
        ]
        self.zs = [
            remote(
                own.at[pl.ds(z_peer(col, d) // 2 * 2, 2)], far.at[d - 1], sent.at[15 + d],
                arrived.at[7 + d], col=z_peer(col, d),
            )
            for d in range(1, 4)
        ]
        self.ys = remote(near.at[0], near.at[1], sent.at[19], arrived.at[11], col=y_peer(col))
        self.last = remote(
            near.at[0], half_shard(out, dp), sent.at[20], arrived.at[12], dp=1 - dp
        )
        self.keep = pltpu.make_async_copy(near.at[0], half_shard(out, dp), sent.at[21])

    def start(self):
        for copy in self.load + self.core:
            copy.start()

    def each(self, rows, body):
        @pl.loop(0, rows // 16)
        def _(i):
            body(pl.ds(pl.multiple_of(i * 16, 16), 16))

    def over_z(self):
        for c in range(8):
            self.load[c].wait()
            self.core[c].wait_recv()
        rows = self.own.shape[1]

        @pl.loop(0, 8)
        def _(c):
            def add(at):
                self.own[c, at] = (self.own[c, at].astype(F32) + self.other[c, at].astype(F32)).astype(BF16)

            self.each(rows, add)

        for copy in self.zs:
            copy.start()

    def over_y(self):
        for copy in self.zs:
            copy.wait_recv()
        rows = self.own.shape[1]
        yl = self.col % 2

        def total(at, c, k):
            sums = self.own[c, at].astype(F32)
            for d in range(3):
                sums = sums + self.far[d, k, at].astype(F32)
            return sums.astype(BF16)

        def add(at):
            self.near[0, at] = total(at, y_peer(self.col), 1 - yl)

        self.each(rows, add)
        self.ys.start()
        for copy in self.zs:
            copy.wait_send()

        def keep(at):
            self.own[self.col, at] = total(at, self.col, yl)

        self.each(rows, keep)

    def over_core(self):
        self.ys.wait()
        rows = self.own.shape[1]

        def add(at):
            self.near[0, at] = (self.own[self.col, at].astype(F32) + self.near[1, at].astype(F32)).astype(BF16)

        self.each(rows, add)
        self.last.start()
        self.keep.start()

    def wait(self):
        for copy in self.core:
            copy.wait_send()
        self.last.wait()
        self.keep.wait()


def grad_scratch(rows, width):
    return [
        pltpu.VMEM((8, rows, width), BF16),
        pltpu.VMEM((8, rows, width), BF16),
        pltpu.VMEM((3, 2, rows, width), BF16),
        pltpu.VMEM((2, rows, width), BF16),
        DMA((22,)),
        DMA((13,)),
    ]


def mean_rate(values):
    return lax.rsqrt(jnp.mean(values * values, axis=-1, keepdims=True) + EPS)


def call(kernel, name, number, outs, ins, in_specs, out_specs, scratch):
    return pl.pallas_call(
        kernel,
        name=name,
        out_shape=outs,
        in_specs=in_specs,
        out_specs=out_specs,
        scratch_shapes=scratch,
        compiler_params=pltpu.CompilerParams(
            collective_id=number, has_side_effects=True, vmem_limit_bytes=56 * 2**20
        ),
    )(*ins)


def struct(shape, kind):
    return jax.ShapeDtypeStruct(shape, kind)


def cols(ref, k, width):
    return ref.at[:, pl.ds(pl.multiple_of(k * width, width), width)]


def rows_of(ref, k, count):
    return ref.at[pl.ds(pl.multiple_of(k * count, count), count)]


def bring_kernel(x, g, heads, merge, xs, gs, heads_all, merge_all, xsent, xcame, gsent, gcame, wsent, wcame):
    meet(weights=True, spread_in=True)
    spread_x = Spread(True, lambda k: x, lambda k: cols(xs, k, 256), xsent, xcame)
    spread_g = Spread(True, lambda k: rows_of(g, k, 64), lambda k: cols(gs, k, 256), gsent, gcame)
    gathers = [
        WeightGather("tall", heads, heads_all, wsent.at[0], wcame.at[0]),
        WeightGather("wide", merge, merge_all, wsent.at[1], wcame.at[1]),
    ]
    spread_x.start()
    for gather in gathers:
        gather.start()
    spread_g.start()
    for gather in gathers:
        gather.relay()
    for gather in gathers:
        gather.share()
    spread_x.wait()
    spread_g.wait()
    for gather in gathers:
        gather.wait()


def sums_kernel(part, out, came, sent, arrived):
    dp, row, col = here()
    meet(rows=True)
    copies = [
        remote(part, came.at[d - 1], sent.at[d - 1], arrived.at[d - 1], row=row_peer(row, d))
        for d in range(1, 8)
    ]
    for copy in copies:
        copy.start()
    total = part[...]
    for d, copy in enumerate(copies):
        copy.wait_recv()
        total = total + came[d]
    out[...] = total
    for copy in copies:
        copy.wait_send()


def merged_kernel(
    part, x, gain, expand, reduce, merged, residual, rows_all, expand_all, reduce_all,
    came, mine, ssent, scame, gsent, gcame, wsent, wcame,
):
    meet(rows=True, weights=True)
    scatter = RowScatter(part, came, ssent, scame)
    gather = RowGather(mine, rows_all, gsent, gcame)
    weights = [
        WeightGather("tall", expand, expand_all, wsent.at[0], wcame.at[0]),
        WeightGather("wide", reduce, reduce_all, wsent.at[1], wcame.at[1]),
    ]
    scatter.start()
    for weight in weights:
        weight.start()
    for weight in weights:
        weight.relay()
    total = scatter.total()
    merged[...] = total
    result = x[...].astype(F32) + total * mean_rate(total) * gain[...]
    residual[...] = result
    mine[...] = result.astype(BF16)
    gather.start()
    for weight in weights:
        weight.share()
    scatter.finish()
    gather.wait()
    for weight in weights:
        weight.wait()


def back_of(grad, values, gain):
    rate = mean_rate(values)
    hat = values * rate
    grad_hat = grad * gain
    dots = jnp.mean(grad_hat * hat, axis=-1, keepdims=True)
    return hat, rate * (grad_hat - hat * dots)


def dot(left, right):
    return jnp.dot(left, right, preferred_element_type=F32)


def dot_flipped(left, right):
    return lax.dot_general(left, right, (((1,), (1,)), ((), ())), preferred_element_type=F32)


def span(k, count):
    return pl.ds(pl.multiple_of(k * count, count), count)


def near_row(row, dx, dy):
    return (row // 4 + dy) % 2 * 4 + (row % 4 + dx) % 4


def meet_near(weights=False, spread_in=False, spread_out=False, cols=False):
    dp, row, col = here()
    barrier = pltpu.get_barrier_semaphore()
    count = 4

    def greet(**where):
        pl.semaphore_signal(barrier, inc=1, device_id=where, device_id_type=MESH)

    for dx, dy in ((1, 0), (2, 0), (3, 0), (0, 1)):
        greet(row=near_row(row, dx, dy))
    if weights:
        greet(col=y_peer(col))
        for d in range(1, 4):
            greet(col=z_peer(col, d))
        greet(dp=1 - dp)
        count = count + 5
    if cols:
        for d in range(1, 8):
            greet(col=(col + d) % 8)
        count = count + 7
    for wanted, inward in ((spread_in, True), (spread_out, False)):
        if wanted:
            for k in range(8):
                at_row, at_col = (col, k) if inward else (k, row)

                @pl.when(jnp.logical_not((at_row == row) & (at_col == col)))
                def _():
                    greet(row=at_row, col=at_col)

            count = count + 8 - (row == col).astype(jnp.int32)
    pl.semaphore_wait(barrier, count)


class Scatter:
    def __init__(self, part, total, from_y, from_x, last_y, last_x, stage, sent, arrived):
        dp, row, col = here()
        self.row, self.part, self.total = row, part, total
        self.from_y, self.from_x, self.last_y, self.last_x, self.stage = from_y, from_x, last_y, last_x, stage
        self.count, self.half = total.shape[0], total.shape[1] // 2
        number = iter(range(14))

        def copy(source, target, dx, dy):
            i = next(number)
            return remote(source, target, sent.at[i], arrived.at[i], row=near_row(row, dx, dy))

        self.y_first = {dx: copy(self.block(dx, 1, 1), from_y.at[dx], 0, 1) for dx in (1, 3, 2, 0)}
        self.x_first = {
            (dx, dy): copy(self.block(dx, dy, 0), from_x.at[dy, dx - 1], dx, 0)
            for dy in (1, 0)
            for dx in (1, 3, 2)
        }
        self.x_last = {dx: copy(stage.at[dx], last_x.at[dx - 1], dx, 0) for dx in (1, 3, 2)}
        self.y_last = copy(stage.at[0], last_y, 0, 1)

    def block(self, dx, dy, side):
        return self.part.at[
            span(near_row(self.row, dx, dy), self.count), pl.ds(side * self.half, self.half)
        ]

    def start_right(self):
        for copy in self.y_first.values():
            copy.start()

    def start_left(self):
        for copy in self.x_first.values():
            copy.start()

    def chunks(self, body):
        @pl.loop(0, self.count // 16)
        def _(i):
            body(span(i, 16))

    def middle(self):
        for dx in (1, 3, 2):
            self.y_first[dx].wait_recv()
            own = self.block(dx, 0, 1)

            def add(at):
                self.stage[dx, at] = (own[at].astype(F32) + self.from_y[dx, at].astype(F32)).astype(BF16)

            self.chunks(add)
            self.x_last[dx].start()
        for dx in (1, 3, 2):
            self.x_first[dx, 1].wait_recv()
        other = self.block(0, 1, 0)

        def add(at):
            total = other[at].astype(F32)
            for k in range(3):
                total = total + self.from_x[1, k, at].astype(F32)
            self.stage[0, at] = total.astype(BF16)

        self.chunks(add)
        self.y_last.start()

    def end(self):
        self.y_first[0].wait_recv()
        for dx in (1, 3, 2):
            self.x_first[dx, 0].wait_recv()
            self.x_last[dx].wait_recv()
        self.y_last.wait_recv()
        left, right = self.block(0, 0, 0), self.block(0, 0, 1)

        def add(at):
            total = left[at].astype(F32) + self.last_y[at].astype(F32)
            for k in range(3):
                total = total + self.from_x[0, k, at].astype(F32)
            self.total[at, : self.half] = total
            total = right[at].astype(F32) + self.from_y[0, at].astype(F32)
            for k in range(3):
                total = total + self.last_x[k, at].astype(F32)
            self.total[at, self.half :] = total

        self.chunks(add)

    def finish(self):
        for copies in (self.y_first, self.x_first, self.x_last):
            for copy in copies.values():
                copy.wait_send()
        self.y_last.wait_send()


def scatter_scratch(share, width):
    half = width // 2
    return [
        pltpu.VMEM((share, width), F32),
        pltpu.VMEM((4, share, half), BF16),
        pltpu.VMEM((2, 3, share, half), BF16),
        pltpu.VMEM((share, half), BF16),
        pltpu.VMEM((3, share, half), BF16),
        pltpu.VMEM((4, share, half), BF16),
        DMA((14,)),
        DMA((14,)),
    ]


class Gather:
    def __init__(self, whole, share, sent, arrived):
        dp, row, col = here()
        self.row = row
        half = whole.shape[1] // 2
        number = iter(range(19))

        def copy(fx, fy, side, dx, dy, start=0, count=share):
            i = next(number)
            k = near_row(row, fx, fy)
            ref = whole.at[
                pl.ds(pl.multiple_of(k * share + start, count), count), pl.ds(side * half, half)
            ]
            return remote(ref, ref, sent.at[i], arrived.at[i], row=near_row(row, dx, dy))

        part = share // 2
        self.y_own = [copy(0, 0, 0, 0, 1), copy(0, 0, 1, 0, 1)]
        self.x_own = [[copy(0, 0, side, dx, 0) for dx in (1, 3)] for side in range(2)]
        self.x_other = [copy(0, 1, 0, dx, 0) for dx in (1, 3)]
        self.on = [
            [copy(4 - dx, 0, side, dx, 0, i * part, part) for i, dx in enumerate((1, 3))]
            for side in range(2)
        ]
        self.on_other = [copy(4 - dx, 1, 0, dx, 0, i * part, part) for i, dx in enumerate((1, 3))]
        self.y_near = [copy(4 - dx, 0, 1, 0, 1) for dx in (1, 3)]
        self.y_far = [copy(2, 0, 1, 0, 1, i * part, part) for i in range(2)]

    def start(self):
        for copy in (self.y_own[0], *self.x_own[1], self.y_own[1], *self.x_own[0]):
            copy.start()

    def relay(self):
        self.y_own[0].wait_recv()
        for copy in self.x_other:
            copy.start()
        for i in range(2):
            self.x_own[1][i].wait_recv()
            self.on[1][i].start()
            self.y_near[i].start()

    def relay_again(self):
        for i in range(2):
            self.x_own[0][i].wait_recv()
            self.on[0][i].start()
        for i in range(2):
            self.on[1][i].wait_recv()
            self.y_far[i].start()
        for i in range(2):
            self.x_other[i].wait_recv()
            self.on_other[i].start()

    def wait(self):
        self.y_own[1].wait_recv()
        for copy in (*self.on[0], *self.on_other, *self.y_near, *self.y_far):
            copy.wait_recv()
        for copy in (*self.y_own, *self.x_own[0], *self.x_own[1], *self.x_other, *self.on[0], *self.on[1],
                     *self.on_other, *self.y_near, *self.y_far):
            copy.wait_send()


def gather_scratch():
    return [DMA((19,)), DMA((19,))]


class GradSum:
    def __init__(self, kind, part, out, other, far, near, sent, arrived):
        dp, _, col = here()
        self.kind, self.part, self.dp, self.col = kind, part, dp, col
        self.other, self.far, self.near = other, far, near
        self.rows = near.shape[1]
        self.core = [
            remote(self.half(c, 1 - dp), other.at[c], sent.at[c], arrived.at[c], dp=1 - dp)
            for c in range(8)
        ]
        self.zs = [
            [
                remote(
                    self.half(z_peer(col, d) // 2 * 2 + k, dp), far.at[d - 1, k], sent.at[6 + 2 * d + k],
                    arrived.at[6 + 2 * d + k], col=z_peer(col, d),
                )
                for k in range(2)
            ]
            for d in (1, 3, 2)
        ]
        self.ys = remote(near.at[0], near.at[1], sent.at[14], arrived.at[14], col=y_peer(col))
        self.last = remote(near.at[0], half_shard(out, dp), sent.at[15], arrived.at[15], dp=1 - dp)
        self.keep = pltpu.make_async_copy(near.at[0], half_shard(out, dp), sent.at[16])

    def half(self, c, h):
        return half_of(self.kind, self.part, c, h)

    def start(self):
        for copy in self.core:
            copy.start()

    def each(self, body):
        @pl.loop(0, self.rows // 16)
        def _(i):
            body(span(i, 16))

    def over_z(self):
        for copy in self.core:
            copy.wait()

        @pl.loop(0, 8)
        def _(c):
            own = self.half(c, self.dp)

            def add(at):
                own[at] = (own[at].astype(F32) + self.other[c, at].astype(F32)).astype(BF16)

            self.each(add)

        for pair in self.zs:
            for copy in pair:
                copy.start()

    def over_y(self):
        for pair in self.zs:
            for copy in pair:
                copy.wait_recv()
        yl = self.col % 2
        keep, give = self.half(self.col, self.dp), self.half(y_peer(self.col), self.dp)

        def add(at):
            total = give[at].astype(F32)
            for d in range(3):
                total = total + self.far[d, 1 - yl, at].astype(F32)
            self.near[0, at] = total.astype(BF16)

        self.each(add)
        self.ys.start()

        def add(at):
            total = keep[at].astype(F32)
            for d in range(3):
                total = total + self.far[d, yl, at].astype(F32)
            keep[at] = total.astype(BF16)

        self.each(add)
        for pair in self.zs:
            for copy in pair:
                copy.wait_send()

    def over_core(self):
        self.ys.wait()
        keep = self.half(self.col, self.dp)

        def add(at):
            self.near[0, at] = (keep[at].astype(F32) + self.near[1, at].astype(F32)).astype(BF16)

        self.each(add)
        self.last.start()
        self.keep.start()

    def wait(self):
        self.last.wait()
        self.keep.wait()


def grad_sum_scratch(rows, width):
    return [
        pltpu.VMEM((8, rows, width), BF16),
        pltpu.VMEM((3, 2, rows, width), BF16),
        pltpu.VMEM((2, rows, width), BF16),
        DMA((17,)),
        DMA((16,)),
    ]


def feed_kernel(
    rows_in, expand_in, reduce_in, residual, g, merged, gain_merge, gain_reduce,
    out, grad_resid, rows_out, merge_gain, reduce_gain, expand_grad, reduce_grad,
    rows, turned, expand, reduce, gate, up, act, act_turned, part, back, hidden, new_rows, done, sums, grad_gate,
    load, osent, ocame, g1sent, g1came, g2sent, g2came, *refs,
):
    dp, row, col = here()
    share, width = residual.shape
    units = act.shape[1]
    tiles = units // 256
    own = span(row, share)
    first = Scatter(part, *refs[:8])
    second = Scatter(part, *refs[8:16])
    reduce_sum = GradSum("wide", reduce, reduce_grad, *refs[16:21])
    expand_sum = GradSum("tall", expand, expand_grad, *refs[21:26])
    gather = Gather(back, share, g1sent, g1came)
    last_gather = Gather(new_rows, share, g2sent, g2came)
    spread = Spread(False, lambda k: cols(done, k, 256), lambda k: rows_of(out, k, 64), osent, ocame)

    get_rows = pltpu.make_async_copy(rows_in, rows, load.at[0])
    get_reduce = pltpu.make_async_copy(reduce_in, reduce, load.at[1])

    def get_expand(j):
        at = span(j, 256)
        return pltpu.make_async_copy(expand_in.at[:, at], expand.at[:, at], load.at[2 + j])

    get_rows.start()
    for j in range(tiles):
        get_expand(j).start()
        get_expand(tiles + j).start()
    get_reduce.start()
    meet_near(weights=True, spread_out=True)
    get_rows.wait()

    @pl.loop(0, tiles)
    def _(j):
        get_expand(j).wait()
        get_expand(tiles + j).wait()
        at = span(j, 256)
        gate[:, at] = dot(rows[...], expand[:, at])
        up[:, at] = dot(rows[...], expand[:, span(tiles + j, 256)])

        @pl.loop(0, rows.shape[0] // 64)
        def _(i):
            some = span(i, 64)
            x = gate[some, at]
            act[some, at] = (x * jax.nn.sigmoid(x) * up[some, at]).astype(BF16)

    get_reduce.wait()

    def reduced(j):
        at = span(j, 256)
        part[:, at] = dot(act[...], reduce[:, at]).astype(BF16)

    n = width // 512
    pl.loop(n, 2 * n)(reduced)
    first.start_right()
    pl.loop(0, n)(reduced)
    first.start_left()

    @pl.loop(0, tiles)
    def _(j):
        at = span(j, 256)
        act_turned[at, :] = act[:, at].T

    first.middle()
    first.end()
    sums[...] = jnp.zeros_like(sums)

    @pl.loop(0, share // 16)
    def _(i):
        at = span(i, 16)
        grad = g[at].astype(F32)
        hat, change = back_of(grad, first.total[at], gain_reduce[...])
        back[pl.ds(pl.multiple_of(row * share + i * 16, 16), 16), :] = change.astype(BF16)
        done[at] = (residual[at] + hat * gain_reduce[...]).astype(BF16)
        product = grad * hat
        sums[...] += product[:8] + product[8:]

    gather.start()
    spread.start()
    reduce_gain[...] = jnp.sum(sums[...], axis=0, keepdims=True)
    first.finish()
    gather.relay()

    @pl.loop(0, 2 * tiles)
    def _(j):
        at = span(j, 256)
        turned[at, :] = rows[:, at].T

    gather.relay_again()
    gather.wait()

    @pl.loop(0, tiles)
    def _(j):
        at, up_at = span(j, 256), span(tiles + j, 256)
        grad_gate[...] = dot_flipped(back[...], reduce[at, :])

        @pl.loop(0, rows.shape[0] // 64)
        def _(i):
            some = span(i, 64)
            x, change = gate[some, at], grad_gate[some]
            s = jax.nn.sigmoid(x)
            hidden[some, at] = (change * up[some, at] * s * (1.0 + x * (1.0 - s))).astype(BF16)
            hidden[some, up_at] = (change * (x * s)).astype(BF16)

    def branch(j):
        at = span(j, 256)
        part[:, at] = dot_flipped(hidden[...], expand[at, :]).astype(BF16)

    pl.loop(n, 2 * n)(branch)
    second.start_right()
    pl.loop(0, n)(branch)
    second.start_left()

    @pl.loop(0, tiles)
    def _(j):
        at = span(j, 256)
        for side in range(2):
            wide = pl.ds(side * (width // 2), width // 2)
            reduce[at, wide] = dot(act_turned[at, :], back[:, wide]).astype(BF16)

    reduce_sum.start()
    second.middle()

    def expand_part(j):
        at = span(j, 256)
        for side in range(2):
            wide = pl.ds(side * (width // 2), width // 2)
            expand[at, wide] = dot(turned[at, :], hidden[:, wide]).astype(BF16)

    pl.loop(0, tiles)(expand_part)
    second.end()
    sums[...] = jnp.zeros_like(sums)

    @pl.loop(0, share // 16)
    def _(i):
        at = span(i, 16)
        grad = g[at].astype(F32) + second.total[at]
        grad_resid[at] = grad
        hat, change = back_of(grad, merged[at], gain_merge[...])
        new_rows[pl.ds(pl.multiple_of(row * share + i * 16, 16), 16), :] = change.astype(BF16)
        product = grad * hat
        sums[...] += product[:8] + product[8:]

    last_gather.start()
    merge_gain[...] = jnp.sum(sums[...], axis=0, keepdims=True)
    pl.loop(tiles, 2 * tiles)(expand_part)
    expand_sum.start()
    last_gather.relay()
    reduce_sum.over_z()
    last_gather.relay_again()
    expand_sum.over_z()
    second.finish()
    last_gather.wait()
    put_rows = pltpu.make_async_copy(new_rows, rows_out, load.at[0])
    put_rows.start()
    reduce_sum.over_y()
    expand_sum.over_y()
    reduce_sum.over_core()
    expand_sum.over_core()
    spread.wait()
    put_rows.wait()
    reduce_sum.wait()
    expand_sum.wait()


def last_kernel(
    part, grad_resid, gains, heads_part, merge_part,
    input_grad, gains_grad, heads_grad, merge_grad,
    came, done, grow, gcol, gcore, gsum, ssent, scame, osent, ocame, gsent, gcame, *grad_refs,
):
    dp, row, col = here()
    meet(rows=True, cols=True, weights=True, spread_out=True)
    scatter = RowScatter(part, came, ssent, scame)
    spread = Spread(False, lambda k: cols(done, k, 256), lambda k: rows_of(input_grad, k, 64), osent, ocame)
    grads = [
        GradScatter("tall", heads_part, heads_grad, *grad_refs[:6]),
        GradScatter("wide", merge_part, merge_grad, *grad_refs[6:]),
    ]
    row_sums = [
        remote(gains, grow.at[row], gsent.at[d - 1], gcame.at[d - 1], row=row_peer(row, d))
        for d in range(1, 8)
    ]
    col_sums = [
        remote(gsum.at[0], gcol.at[col], gsent.at[6 + d], gcame.at[6 + d], col=(col + d) % 8)
        for d in range(1, 8)
    ]
    core_sum = remote(gsum.at[1], gcore, gsent.at[14], gcame.at[14], dp=1 - dp)
    for copy in row_sums:
        copy.start()
    scatter.start()
    for grad in grads:
        grad.start()
    grow[row] = gains[...]
    for grad in grads:
        grad.over_z()
    for copy in row_sums:
        copy.wait()
    total = grow[0]
    for k in range(1, 8):
        total = total + grow[k]
    gsum[0] = total
    for copy in col_sums:
        copy.start()
    gcol[col] = total
    done[...] = grad_resid[...] + scatter.total()
    spread.start()
    for copy in col_sums:
        copy.wait()
    total = gcol[0]
    for k in range(1, 8):
        total = total + gcol[k]
    gsum[1] = total
    core_sum.start()
    for grad in grads:
        grad.over_y()
    for grad in grads:
        grad.over_core()
    core_sum.wait()
    gains_grad[...] = total + gcore[...]
    scatter.finish()
    spread.wait()
    for grad in grads:
        grad.wait()


def on_device(
    block_input,
    cotangent,
    doc_lengths,
    heads_weight,
    heads_first,
    heads_second,
    merge_weight,
    merge_first,
    merge_second,
    expand_weight,
    expand_first,
    expand_second,
    reduce_weight,
    reduce_first,
    reduce_second,
    norm_gains,
    gains_first,
    gains_second,
):
    row_at = lax.axis_index("row")
    col_width = block_input.shape[1]
    model_width = col_width * lax.axis_size("col")
    head_width = merge_weight.shape[0]
    unit_width = reduce_weight.shape[0]
    seq_len = block_input.shape[0] * lax.axis_size("row") // lax.axis_size("col")
    share = seq_len // lax.axis_size("row")
    head_count = head_width // HD
    doc_ids, places, live_rows = positions(doc_lengths[0], seq_len)
    allowed = allowed_mask(doc_ids, seq_len)
    gain_query = lax.dynamic_slice_in_dim(norm_gains[0], row_at * head_width, head_width)
    gain_key = lax.dynamic_slice_in_dim(norm_gains[1], row_at * head_width, head_width)
    gain_merge, gain_reduce = norm_gains[2:3], norm_gains[3:4]
    rows_shape = struct((seq_len, model_width), BF16)
    mine_f32 = struct((share, model_width), F32)
    line = struct((1, model_width), F32)
    row_scratch = [
        pltpu.VMEM((7, share, model_width), BF16),
        pltpu.VMEM((share, model_width), BF16),
        DMA((7,)),
        DMA((7,)),
        DMA((8,)),
        DMA((7,)),
    ]

    input_rows, cot_share, heads_low, merge_low = call(
        bring_kernel, "bring", 1,
        [rows_shape, struct((share, model_width), BF16), struct((model_width, 3 * head_width), BF16),
         struct((head_width, model_width), BF16)],
        [block_input, cotangent, heads_weight.astype(BF16), merge_weight.astype(BF16)],
        [ANY] * 4, [ANY] * 4,
        [DMA((8,)), DMA((8,)), DMA((8,)), DMA((8,))] + gather_sems(2),
    )
    joined_cols = product(input_rows, heads_low, False)
    queries = joined_cols[:, :head_width]
    key_rows = joined_cols[:, head_width : 2 * head_width]
    value_rows = joined_cols[:, 2 * head_width :]

    def head_sums(one, two, number):
        part = jnp.concatenate([one, two]).reshape(8, 128)
        total = call(
            sums_kernel, "sums", number, struct((8, 128), F32), [part], [VMEM], VMEM,
            [pltpu.VMEM((7, 8, 128), F32), DMA((7,)), DMA((7,))],
        ).reshape(2, seq_len)
        return total[0], total[1]

    query_sq, key_sq = head_sums(
        jnp.sum(queries * queries, axis=1), jnp.sum(key_rows * key_rows, axis=1), 2
    )
    query_rate = lax.rsqrt(query_sq / model_width + EPS)[:, None]
    key_rate = lax.rsqrt(key_sq / model_width + EPS)[:, None]
    query_hat = queries * query_rate
    key_hat = key_rows * key_rate
    query_low = rotate(
        (query_hat * gain_query).reshape(seq_len, head_count, HD), places, 1.0
    ).astype(jnp.bfloat16)
    key_low = rotate((key_hat * gain_key).reshape(seq_len, head_count, HD), places, 1.0).astype(
        jnp.bfloat16
    )
    value_low = value_rows.reshape(seq_len, head_count, HD).astype(jnp.bfloat16)
    mixture, log_totals = attend_forward(query_low, key_low, value_low, allowed, live_rows)
    mixture_low = mixture.reshape(seq_len, head_width).astype(jnp.bfloat16)
    merged_part = product(mixture_low, merge_low, False).astype(BF16)

    input_share = lax.dynamic_slice_in_dim(input_rows, row_at * share, share)
    merged, residual, residual_rows, expand_low, reduce_low = call(
        merged_kernel, "merged", 3,
        [mine_f32, mine_f32, rows_shape, struct((model_width, 2 * unit_width), BF16),
         struct((unit_width, model_width), BF16)],
        [merged_part, input_share, gain_merge, expand_weight.astype(BF16), reduce_weight.astype(BF16)],
        [VMEM, VMEM, VMEM, ANY, ANY], [VMEM, VMEM, ANY, ANY, ANY],
        row_scratch + gather_sems(2),
    )
    block_output, grad_resid, merged_grad_rows, merge_gain_part, reduce_gain_part, expand_grad, reduce_grad = call(
        feed_kernel, "feed", 4,
        [struct(block_input.shape, BF16), mine_f32, rows_shape, line, line, struct(expand_weight.shape, BF16),
         struct(reduce_weight.shape, BF16)],
        [residual_rows, expand_low, reduce_low, residual, cot_share, merged, gain_merge, gain_reduce],
        [ANY] * 3 + [VMEM] * 5, [ANY, VMEM, ANY, VMEM, VMEM, ANY, ANY],
        [
            pltpu.VMEM((seq_len, model_width), BF16),
            pltpu.VMEM((model_width, seq_len), BF16),
            pltpu.VMEM((model_width, 2 * unit_width), BF16),
            pltpu.VMEM((unit_width, model_width), BF16),
            pltpu.VMEM((seq_len, unit_width), F32),
            pltpu.VMEM((seq_len, unit_width), F32),
            pltpu.VMEM((seq_len, unit_width), BF16),
            pltpu.VMEM((unit_width, seq_len), BF16),
            pltpu.VMEM((seq_len, model_width), BF16),
            pltpu.VMEM((seq_len, model_width), BF16),
            pltpu.VMEM((seq_len, 2 * unit_width), BF16),
            pltpu.VMEM((seq_len, model_width), BF16),
            pltpu.VMEM((share, model_width), BF16),
            pltpu.VMEM((8, model_width), F32),
            pltpu.VMEM((seq_len, 256), F32),
            DMA((10,)), DMA((8,)), DMA((8,)),
        ]
        + gather_scratch() + gather_scratch()
        + scatter_scratch(share, model_width) + scatter_scratch(share, model_width)
        + grad_sum_scratch(reduce_weight.shape[0] // 2, reduce_weight.shape[1])
        + grad_sum_scratch(expand_weight.shape[0] // 2, expand_weight.shape[1]),
    )
    grad_mixture = product(merged_grad_rows, merge_low, True)
    merge_part = column_total(mixture_low, merged_grad_rows).astype(BF16)
    grad_mix_low = (
        grad_mixture.astype(jnp.bfloat16).reshape(seq_len, head_count, HD)
        * live_rows.astype(jnp.bfloat16)[:, None, None]
    )
    grad_queries, grad_keys, grad_values = attend_backward(
        query_low, key_low, value_low, allowed, log_totals, grad_mix_low
    )
    query_norm_grad = rotate(grad_queries, places, -1.0).reshape(seq_len, head_width)
    key_norm_grad = rotate(grad_keys, places, -1.0).reshape(seq_len, head_width)
    query_gain_part = jnp.sum(query_norm_grad * query_hat, axis=0)
    key_gain_part = jnp.sum(key_norm_grad * key_hat, axis=0)
    query_hat_grad = query_norm_grad * gain_query
    key_hat_grad = key_norm_grad * gain_key
    query_dot, key_dot = head_sums(
        jnp.sum(query_hat_grad * query_hat, axis=1), jnp.sum(key_hat_grad * key_hat, axis=1), 6
    )
    grad_query_rows = norm_back(query_hat_grad, query_hat, query_rate, query_dot, model_width)
    grad_key_rows = norm_back(key_hat_grad, key_hat, key_rate, key_dot, model_width)
    joined_grad = jnp.concatenate(
        [grad_query_rows, grad_key_rows, grad_values.reshape(seq_len, head_width)], axis=1
    ).astype(jnp.bfloat16)
    input_part = product(joined_grad, heads_low, True).astype(BF16)
    heads_part = column_total(input_rows, joined_grad).astype(BF16)
    gain_parts = jnp.zeros((2, model_width), jnp.float32)
    gain_parts = lax.dynamic_update_slice(
        gain_parts, jnp.stack([query_gain_part, key_gain_part]), (jnp.int32(0), row_at * head_width)
    )
    gain_parts = jnp.concatenate([gain_parts, merge_gain_part, reduce_gain_part]).reshape(8, model_width // 2)
    gain_shape = (8, model_width // 2)

    input_grad, gains_grad, heads_grad, merge_grad = call(
        last_kernel, "last", 7,
        [struct(block_input.shape, F32), struct(gain_shape, F32), struct(heads_weight.shape, BF16),
         struct(merge_weight.shape, BF16)],
        [input_part, grad_resid, gain_parts, heads_part, merge_part],
        [VMEM] * 3 + [ANY] * 2, [ANY, VMEM] + [ANY] * 2,
        [row_scratch[0], pltpu.VMEM((share, model_width), F32), pltpu.VMEM((8, *gain_shape), F32),
         pltpu.VMEM((8, *gain_shape), F32), pltpu.VMEM(gain_shape, F32), pltpu.VMEM((2, *gain_shape), F32),
         DMA((7,)), DMA((7,)), DMA((8,)), DMA((8,)), DMA((15,)), DMA((15,))]
        + grad_scratch(heads_weight.shape[0] // 2, heads_weight.shape[1])
        + grad_scratch(merge_weight.shape[0] // 2, merge_weight.shape[1]),
    )
    gains_grad = gains_grad.reshape(4, model_width)
    heads_grad, merge_grad, expand_grad, reduce_grad = (
        heads_grad.astype(F32), merge_grad.astype(F32), expand_grad.astype(F32), reduce_grad.astype(F32)
    )
    heads_mean, heads_square, heads_fresh = adamw(
        heads_weight, heads_grad, heads_first, heads_second, LR, DECAY
    )
    merge_mean, merge_square, merge_fresh = adamw(
        merge_weight, merge_grad, merge_first, merge_second, LR, DECAY
    )
    expand_mean, expand_square, expand_fresh = adamw(
        expand_weight, expand_grad, expand_first, expand_second, LR, DECAY
    )
    reduce_mean, reduce_square, reduce_fresh = adamw(
        reduce_weight, reduce_grad, reduce_first, reduce_second, LR, DECAY
    )
    gains_mean, gains_square, gains_fresh = adamw(
        norm_gains, gains_grad, gains_first, gains_second, LR_GAIN, 0.0
    )
    return (
        block_output,
        input_grad,
        heads_grad,
        heads_mean,
        heads_square,
        heads_fresh,
        heads_fresh.astype(jnp.bfloat16),
        merge_grad,
        merge_mean,
        merge_square,
        merge_fresh,
        merge_fresh.astype(jnp.bfloat16),
        expand_grad,
        expand_mean,
        expand_square,
        expand_fresh,
        expand_fresh.astype(jnp.bfloat16),
        reduce_grad,
        reduce_mean,
        reduce_square,
        reduce_fresh,
        reduce_fresh.astype(jnp.bfloat16),
        gains_grad,
        gains_mean,
        gains_square,
        gains_fresh,
    )


def solution(mesh):
    return jax.shard_map(
        on_device,
        mesh=mesh,
        in_specs=(
            P(("dp", "row"), "col"),
            P(("dp", "row"), "col"),
            P(("dp", "col"), None),
            P("col", "row"),
            P("col", "row"),
            P("col", "row"),
            P("row", "col"),
            P("row", "col"),
            P("row", "col"),
            P("col", "row"),
            P("col", "row"),
            P("col", "row"),
            P("row", "col"),
            P("row", "col"),
            P("row", "col"),
            P(),
            P(),
            P(),
        ),
        out_specs=(
            P(("dp", "row"), "col"),
            P(("dp", "row"), "col"),
            P("col", "row"),
            P("col", "row"),
            P("col", "row"),
            P("col", "row"),
            P("col", "row"),
            P("row", "col"),
            P("row", "col"),
            P("row", "col"),
            P("row", "col"),
            P("row", "col"),
            P("col", "row"),
            P("col", "row"),
            P("col", "row"),
            P("col", "row"),
            P("col", "row"),
            P("row", "col"),
            P("row", "col"),
            P("row", "col"),
            P("row", "col"),
            P("row", "col"),
            P(),
            P(),
            P(),
            P(),
        ),
        check_vma=False,
    )
```

```python
import functools

import jax
import jax.numpy as jnp
from jax import lax
from jax.experimental import pallas as pl
from jax.experimental.pallas import tpu as pltpu
from jax.sharding import PartitionSpec as P

HD = 128
WINDOW = 256
STEP = 5


EPS = 1e-06
THETA = 500000.0
LR = 0.02
LR_GAIN = 0.2
BETA_ONE = 0.5
BETA_TWO = 0.5
DECAY = 0.1
ADAM_EPS = 1e-08

BF16 = jnp.bfloat16
F32 = jnp.float32
MESH = pl.DeviceIdType.MESH
ANY = pl.BlockSpec(memory_space=pl.ANY)
VMEM = pl.BlockSpec(memory_space=pltpu.VMEM)
DMA = pltpu.SemaphoreType.DMA


def positions(lengths, row_count):
    doc_ends = jnp.cumsum(lengths)
    index_ids = jnp.arange(row_count, dtype=jnp.int32)
    passed = doc_ends[None, :] <= index_ids[:, None]
    doc_ids = jnp.sum(passed.astype(jnp.int32), axis=1)
    starts = jnp.sum(jnp.where(passed, lengths[None, :], 0), axis=1)
    live_rows = (doc_ids < lengths.shape[0] - 1).astype(jnp.float32)
    return (doc_ids, index_ids - starts, live_rows)


def rotate(values, places, turn_sign):
    half_dim = values.shape[-1] // 2
    frequency = THETA ** (-2.0 * jnp.arange(half_dim, dtype=jnp.float32) / values.shape[-1])
    angles = places.astype(jnp.float32)[:, None] * frequency[None, :]
    cosine = jnp.cos(angles)[:, None, :]
    sine_part = turn_sign * jnp.sin(angles)[:, None, :]
    first_half = values[..., :half_dim]
    second_half = values[..., half_dim:]
    return jnp.concatenate(
        [
            first_half * cosine - second_half * sine_part,
            second_half * cosine + first_half * sine_part,
        ],
        axis=-1,
    )


def product(left_side, right_side, flipped):
    if flipped:
        return lax.dot_general(
            left_side, right_side, (((1,), (1,)), ((), ())), preferred_element_type=jnp.float32
        )
    return jnp.dot(left_side, right_side, preferred_element_type=jnp.float32)


def column_total(left_side, right_side):
    return lax.dot_general(
        left_side, right_side, (((0,), (0,)), ((), ())), preferred_element_type=jnp.float32
    )


def norm_back(grad_hat, hat_vals, rates, dots, model_width):
    return rates * (grad_hat - hat_vals * (dots / model_width)[:, None])


def attend_backward(queries, key_rows, value_rows, shares, grad_mix):
    score_scale = queries.shape[-1] ** (-0.5)
    grad_shares = jnp.einsum(
        "qhd,khd->hqk", grad_mix, value_rows, preferred_element_type=jnp.float32
    )
    grad_values = jnp.einsum("hqk,qhd->khd", shares, grad_mix, preferred_element_type=jnp.float32)
    shares = shares.astype(F32)
    center = jnp.sum(shares * grad_shares, axis=-1, keepdims=True)
    grad_scores = (shares * (grad_shares - center)).astype(jnp.bfloat16)
    grad_queries = (
        jnp.einsum("hqk,khd->qhd", grad_scores, key_rows, preferred_element_type=jnp.float32)
        * score_scale
    )
    grad_keys = (
        jnp.einsum("hqk,qhd->khd", grad_scores, queries, preferred_element_type=jnp.float32)
        * score_scale
    )
    return (grad_queries, grad_keys, grad_values)


def adamw(weight, gradient, first_mom, second_mom, step_rate, decay_rate):
    mean_new = BETA_ONE * first_mom + (1.0 - BETA_ONE) * gradient
    square_new = BETA_TWO * second_mom + (1.0 - BETA_TWO) * gradient * gradient
    fix_one = 1.0 - BETA_ONE**STEP
    fix_two = 1.0 - BETA_TWO**STEP
    update = mean_new / fix_one / (jnp.sqrt(square_new / fix_two) + ADAM_EPS) + decay_rate * weight
    return (mean_new, square_new, weight - step_rate * update)


def here():
    return lax.axis_index("dp"), lax.axis_index("row"), lax.axis_index("col")


def row_peer(row, d):
    return (row // 4 + d // 4) % 2 * 4 + (row % 4 + d % 4) % 4


def z_peer(col, d):
    return (col // 2 + d) % 4 * 2 + col % 2


def z_source(col, d):
    return (col // 2 + 4 - d) % 4 * 2 + col % 2


def y_peer(col):
    return col // 2 * 2 + 1 - col % 2


def remote(source, target, sent, arrived, **where):
    return pltpu.make_async_remote_copy(
        src_ref=source,
        dst_ref=target,
        send_sem=sent,
        recv_sem=arrived,
        device_id=where,
        device_id_type=MESH,
    )


def meet(rows=False, cols=False, weights=False, spread_in=False, spread_out=False):
    dp, row, col = here()
    barrier = pltpu.get_barrier_semaphore()
    count = 0

    def greet(**where):
        pl.semaphore_signal(barrier, inc=1, device_id=where, device_id_type=MESH)

    if rows:
        for d in range(1, 8):
            greet(row=row_peer(row, d))
        count = count + 7
    if cols:
        for d in range(1, 8):
            greet(col=(col + d) % 8)
        count = count + 7
    if weights:
        greet(col=y_peer(col))
        for d in range(1, 4):
            greet(col=z_peer(col, d))
        greet(dp=1 - dp)
        count = count + 5
    for wanted, inward in ((spread_in, True), (spread_out, False)):
        if wanted:
            for k in range(8):
                at_row, at_col = (col, k) if inward else (k, row)

                @pl.when(jnp.logical_not((at_row == row) & (at_col == col)))
                def _():
                    greet(row=at_row, col=at_col)

            count = count + 8 - (row == col).astype(jnp.int32)
    pl.semaphore_wait(barrier, count)


class Spread:
    def __init__(self, inward, source, target, sent, arrived):
        dp, row, col = here()
        self.row, self.col, self.inward = row, col, inward
        self.copies = []
        for k in range(8):
            to_row, to_col = (k, row) if inward else (col, k)
            mine = (row == to_row) & (col == to_col)
            copy = remote(
                source(k),
                target(col if inward else row),
                sent.at[k],
                arrived.at[col if inward else row],
                row=to_row,
                col=to_col,
            )
            waiter = remote(source(k), target(k), sent.at[k], arrived.at[k], row=to_row, col=to_col)
            local = pltpu.make_async_copy(
                source(k), target(col if inward else row), sent.at[k]
            )
            self.copies.append((mine, copy, waiter, local))

    def start(self):
        for mine, copy, _, local in self.copies:
            pl.when(jnp.logical_not(mine))(copy.start)
            pl.when(mine)(local.start)

    def wait(self):
        for k, (mine, copy, waiter, local) in enumerate(self.copies):
            from_row, from_col = (self.col, k) if self.inward else (k, self.row)
            me = (from_row == self.row) & (from_col == self.col)
            pl.when(jnp.logical_not(me))(waiter.wait_recv)
            pl.when(jnp.logical_not(mine))(copy.wait_send)
            pl.when(mine)(local.wait)


class RowScatter:
    def __init__(self, part, arrived_rows, sent, arrived):
        dp, self.row, col = here()
        self.part, self.arrived_rows = part, arrived_rows
        self.count = arrived_rows.shape[1]
        self.copies = [
            remote(
                part.at[self.block(row_peer(self.row, d))],
                arrived_rows.at[d - 1],
                sent.at[d - 1],
                arrived.at[d - 1],
                row=row_peer(self.row, d),
            )
            for d in range(1, 8)
        ]

    def block(self, k):
        return pl.ds(pl.multiple_of(k * self.count, self.count), self.count)

    def start(self):
        for copy in self.copies:
            copy.start()

    def total(self):
        for copy in self.copies:
            copy.wait_recv()
        total = self.part[self.block(self.row)].astype(F32)
        for d in range(7):
            total = total + self.arrived_rows[d].astype(F32)
        return total

    def finish(self):
        for copy in self.copies:
            copy.wait_send()


class RowGather:
    def __init__(self, rows, whole, sent, arrived):
        dp, row, col = here()
        count = rows.shape[0]
        block = pl.ds(pl.multiple_of(row * count, count), count)
        self.copies = [
            remote(rows, whole.at[block], sent.at[d - 1], arrived.at[d - 1], row=row_peer(row, d))
            for d in range(1, 8)
        ]
        self.local = pltpu.make_async_copy(rows, whole.at[block], sent.at[7])

    def start(self):
        for copy in self.copies:
            copy.start()
        self.local.start()

    def wait(self):
        for copy in self.copies:
            copy.wait()
        self.local.wait()


def half_of(kind, ref, c, h):
    if kind == "tall":
        count = ref.shape[0] // 16
        return ref.at[pl.ds(pl.multiple_of((2 * c + h) * count, count), count)]
    count, width = ref.shape[0] // 2, ref.shape[1] // 8
    return ref.at[
        pl.ds(pl.multiple_of(h * count, count), count), pl.ds(pl.multiple_of(c * width, width), width)
    ]


def half_shard(ref, h):
    count = ref.shape[0] // 2
    return ref.at[pl.ds(pl.multiple_of(h * count, count), count)]


class WeightGather:
    def __init__(self, kind, shard, whole, sent, arrived):
        dp, _, col = here()
        self.kind, self.whole, self.sent, self.arrived = kind, whole, sent, arrived
        self.dp, self.col = dp, col
        near = y_peer(col)
        mine = half_shard(shard, dp)
        self.local = [
            pltpu.make_async_copy(half_shard(shard, h), self.half(col, h), sent.at[14 + h])
            for h in range(2)
        ]
        self.first = [remote(mine, self.half(col, dp), sent.at[0], arrived.at[0], col=near)] + [
            remote(mine, self.half(col, dp), sent.at[d], arrived.at[d], col=z_peer(col, d))
            for d in range(1, 4)
        ]
        self.second = [
            remote(
                self.half(near, dp), self.half(near, dp), sent.at[3 + d], arrived.at[3 + d],
                col=z_peer(col, d),
            )
            for d in range(1, 4)
        ]
        blocks = (
            [near]
            + [z_source(col, d) for d in range(1, 4)]
            + [y_peer(z_source(col, d)) for d in range(1, 4)]
        )
        self.across = [
            remote(self.half(b, dp), self.half(b, dp), sent.at[7 + i], arrived.at[7 + i], dp=1 - dp)
            for i, b in enumerate(blocks)
        ]

    def half(self, c, h):
        return half_of(self.kind, self.whole, c, h)

    def start(self):
        for copy in self.first + self.local:
            copy.start()

    def relay(self):
        self.first[0].wait_recv()
        for copy in self.second:
            copy.start()
        self.across[0].start()

    def share(self):
        for i in range(1, 4):
            self.first[i].wait_recv()
            self.across[i].start()
        for i in range(3):
            self.second[i].wait_recv()
            self.across[4 + i].start()

    def wait(self):
        for copy in self.across:
            copy.wait()
        for copy in self.first + self.second:
            copy.wait_send()
        for copy in self.local:
            copy.wait()


def gather_sems(n):
    return [DMA((n, 16)), DMA((n, 14))]


class GradScatter:
    def __init__(self, kind, part, out, own, other, far, near, sent, arrived):
        dp, _, col = here()
        self.dp, self.col = dp, col
        self.own, self.other, self.far, self.near = own, other, far, near
        self.load = [
            pltpu.make_async_copy(half_of(kind, part, c, dp), own.at[c], sent.at[8 + c])
            for c in range(8)
        ]
        self.core = [
            remote(half_of(kind, part, c, 1 - dp), other.at[c], sent.at[c], arrived.at[c], dp=1 - dp)
            for c in range(8)
        ]
        self.zs = [
            remote(
                own.at[pl.ds(z_peer(col, d) // 2 * 2, 2)], far.at[d - 1], sent.at[15 + d],
                arrived.at[7 + d], col=z_peer(col, d),
            )
            for d in range(1, 4)
        ]
        self.ys = remote(near.at[0], near.at[1], sent.at[19], arrived.at[11], col=y_peer(col))
        self.last = remote(
            near.at[0], half_shard(out, dp), sent.at[20], arrived.at[12], dp=1 - dp
        )
        self.keep = pltpu.make_async_copy(near.at[0], half_shard(out, dp), sent.at[21])

    def start(self):
        for copy in self.load + self.core:
            copy.start()

    def each(self, rows, body):
        @pl.loop(0, rows // 16)
        def _(i):
            body(pl.ds(pl.multiple_of(i * 16, 16), 16))

    def over_z(self):
        for c in range(8):
            self.load[c].wait()
            self.core[c].wait_recv()
        rows = self.own.shape[1]

        @pl.loop(0, 8)
        def _(c):
            def add(at):
                self.own[c, at] = (self.own[c, at].astype(F32) + self.other[c, at].astype(F32)).astype(BF16)

            self.each(rows, add)

        for copy in self.zs:
            copy.start()

    def over_y(self):
        for copy in self.zs:
            copy.wait_recv()
        rows = self.own.shape[1]
        yl = self.col % 2

        def total(at, c, k):
            sums = self.own[c, at].astype(F32)
            for d in range(3):
                sums = sums + self.far[d, k, at].astype(F32)
            return sums.astype(BF16)

        def add(at):
            self.near[0, at] = total(at, y_peer(self.col), 1 - yl)

        self.each(rows, add)
        self.ys.start()
        for copy in self.zs:
            copy.wait_send()

        def keep(at):
            self.own[self.col, at] = total(at, self.col, yl)

        self.each(rows, keep)

    def over_core(self):
        self.ys.wait()
        rows = self.own.shape[1]

        def add(at):
            self.near[0, at] = (self.own[self.col, at].astype(F32) + self.near[1, at].astype(F32)).astype(BF16)

        self.each(rows, add)
        self.last.start()
        self.keep.start()

    def wait(self):
        for copy in self.core:
            copy.wait_send()
        self.last.wait()
        self.keep.wait()


def grad_scratch(rows, width):
    return [
        pltpu.VMEM((8, rows, width), BF16),
        pltpu.VMEM((8, rows, width), BF16),
        pltpu.VMEM((3, 2, rows, width), BF16),
        pltpu.VMEM((2, rows, width), BF16),
        DMA((22,)),
        DMA((13,)),
    ]


def mean_rate(values):
    return lax.rsqrt(jnp.mean(values * values, axis=-1, keepdims=True) + EPS)


def call(kernel, name, number, outs, ins, in_specs, out_specs, scratch):
    return pl.pallas_call(
        kernel,
        name=name,
        out_shape=outs,
        in_specs=in_specs,
        out_specs=out_specs,
        scratch_shapes=scratch,
        compiler_params=pltpu.CompilerParams(
            collective_id=number, has_side_effects=True, vmem_limit_bytes=56 * 2**20
        ),
    )(*ins)


def struct(shape, kind):
    return jax.ShapeDtypeStruct(shape, kind)


def cols(ref, k, width):
    return ref.at[:, pl.ds(pl.multiple_of(k * width, width), width)]


def rows_of(ref, k, count):
    return ref.at[pl.ds(pl.multiple_of(k * count, count), count)]


def sums_kernel(part, out, came, sent, arrived):
    dp, row, col = here()
    meet(rows=True)
    copies = [
        remote(part, came.at[d - 1], sent.at[d - 1], arrived.at[d - 1], row=row_peer(row, d))
        for d in range(1, 8)
    ]
    for copy in copies:
        copy.start()
    total = part[...]
    for d, copy in enumerate(copies):
        copy.wait_recv()
        total = total + came[d]
    out[...] = total
    for copy in copies:
        copy.wait_send()


def back_of(grad, values, gain):
    rate = mean_rate(values)
    hat = values * rate
    grad_hat = grad * gain
    dots = jnp.mean(grad_hat * hat, axis=-1, keepdims=True)
    return hat, rate * (grad_hat - hat * dots)


def dot(left, right):
    return jnp.dot(left, right, preferred_element_type=F32)


def dot_flipped(left, right):
    return lax.dot_general(left, right, (((1,), (1,)), ((), ())), preferred_element_type=F32)


def span(k, count):
    return pl.ds(pl.multiple_of(k * count, count), count)


def near_row(row, dx, dy):
    return (row // 4 + dy) % 2 * 4 + (row % 4 + dx) % 4


def meet_near(weights=False, spread_in=False, spread_out=False, cols=False):
    dp, row, col = here()
    barrier = pltpu.get_barrier_semaphore()
    count = 4

    def greet(**where):
        pl.semaphore_signal(barrier, inc=1, device_id=where, device_id_type=MESH)

    for dx, dy in ((1, 0), (2, 0), (3, 0), (0, 1)):
        greet(row=near_row(row, dx, dy))
    if weights:
        greet(col=y_peer(col))
        for d in range(1, 4):
            greet(col=z_peer(col, d))
        greet(dp=1 - dp)
        count = count + 5
    if cols:
        for d in range(1, 8):
            greet(col=(col + d) % 8)
        count = count + 7
    for wanted, inward in ((spread_in, True), (spread_out, False)):
        if wanted:
            for k in range(8):
                at_row, at_col = (col, k) if inward else (k, row)

                @pl.when(jnp.logical_not((at_row == row) & (at_col == col)))
                def _():
                    greet(row=at_row, col=at_col)

            count = count + 8 - (row == col).astype(jnp.int32)
    pl.semaphore_wait(barrier, count)


class Scatter:
    def __init__(self, part, total, from_y, from_x, last_y, last_x, stage, sent, arrived):
        dp, row, col = here()
        self.row, self.part, self.total = row, part, total
        self.from_y, self.from_x, self.last_y, self.last_x, self.stage = from_y, from_x, last_y, last_x, stage
        self.count, self.half = total.shape[0], total.shape[1] // 2
        number = iter(range(14))

        def copy(source, target, dx, dy):
            i = next(number)
            return remote(source, target, sent.at[i], arrived.at[i], row=near_row(row, dx, dy))

        self.y_first = {dx: copy(self.block(dx, 1, 1), from_y.at[dx], 0, 1) for dx in (1, 3, 2, 0)}
        self.x_first = {
            (dx, dy): copy(self.block(dx, dy, 0), from_x.at[dy, dx - 1], dx, 0)
            for dy in (1, 0)
            for dx in (1, 3, 2)
        }
        self.x_last = {dx: copy(stage.at[dx], last_x.at[dx - 1], dx, 0) for dx in (1, 3, 2)}
        self.y_last = copy(stage.at[0], last_y, 0, 1)

    def block(self, dx, dy, side):
        return self.part.at[
            span(near_row(self.row, dx, dy), self.count), pl.ds(side * self.half, self.half)
        ]

    def start_right(self):
        for copy in self.y_first.values():
            copy.start()

    def start_left(self):
        for copy in self.x_first.values():
            copy.start()

    def chunks(self, body):
        @pl.loop(0, self.count // 16)
        def _(i):
            body(span(i, 16))

    def middle(self):
        for dx in (1, 3, 2):
            self.y_first[dx].wait_recv()
            own = self.block(dx, 0, 1)

            def add(at):
                self.stage[dx, at] = (own[at].astype(F32) + self.from_y[dx, at].astype(F32)).astype(BF16)

            self.chunks(add)
            self.x_last[dx].start()
        for dx in (1, 3, 2):
            self.x_first[dx, 1].wait_recv()
        other = self.block(0, 1, 0)

        def add(at):
            total = other[at].astype(F32)
            for k in range(3):
                total = total + self.from_x[1, k, at].astype(F32)
            self.stage[0, at] = total.astype(BF16)

        self.chunks(add)
        self.y_last.start()

    def end(self):
        self.y_first[0].wait_recv()
        for dx in (1, 3, 2):
            self.x_first[dx, 0].wait_recv()
            self.x_last[dx].wait_recv()
        self.y_last.wait_recv()
        left, right = self.block(0, 0, 0), self.block(0, 0, 1)

        def add(at):
            total = left[at].astype(F32) + self.last_y[at].astype(F32)
            for k in range(3):
                total = total + self.from_x[0, k, at].astype(F32)
            self.total[at, : self.half] = total
            total = right[at].astype(F32) + self.from_y[0, at].astype(F32)
            for k in range(3):
                total = total + self.last_x[k, at].astype(F32)
            self.total[at, self.half :] = total

        self.chunks(add)

    def finish(self):
        for copies in (self.y_first, self.x_first, self.x_last):
            for copy in copies.values():
                copy.wait_send()
        self.y_last.wait_send()


def scatter_scratch(share, width):
    half = width // 2
    return [
        pltpu.VMEM((share, width), F32),
        pltpu.VMEM((4, share, half), BF16),
        pltpu.VMEM((2, 3, share, half), BF16),
        pltpu.VMEM((share, half), BF16),
        pltpu.VMEM((3, share, half), BF16),
        pltpu.VMEM((4, share, half), BF16),
        DMA((14,)),
        DMA((14,)),
    ]


class Gather:
    def __init__(self, whole, share, sent, arrived):
        dp, row, col = here()
        self.row = row
        half = whole.shape[1] // 2
        number = iter(range(19))

        def copy(fx, fy, side, dx, dy, start=0, count=share):
            i = next(number)
            k = near_row(row, fx, fy)
            ref = whole.at[
                pl.ds(pl.multiple_of(k * share + start, count), count), pl.ds(side * half, half)
            ]
            return remote(ref, ref, sent.at[i], arrived.at[i], row=near_row(row, dx, dy))

        part = share // 2
        self.y_own = [copy(0, 0, 0, 0, 1), copy(0, 0, 1, 0, 1)]
        self.x_own = [[copy(0, 0, side, dx, 0) for dx in (1, 3)] for side in range(2)]
        self.x_other = [copy(0, 1, 0, dx, 0) for dx in (1, 3)]
        self.on = [
            [copy(4 - dx, 0, side, dx, 0, i * part, part) for i, dx in enumerate((1, 3))]
            for side in range(2)
        ]
        self.on_other = [copy(4 - dx, 1, 0, dx, 0, i * part, part) for i, dx in enumerate((1, 3))]
        self.y_near = [copy(4 - dx, 0, 1, 0, 1) for dx in (1, 3)]
        self.y_far = [copy(2, 0, 1, 0, 1, i * part, part) for i in range(2)]

    def start(self):
        for copy in (self.y_own[0], *self.x_own[1], self.y_own[1], *self.x_own[0]):
            copy.start()

    def relay(self):
        self.y_own[0].wait_recv()
        for copy in self.x_other:
            copy.start()
        for i in range(2):
            self.x_own[1][i].wait_recv()
            self.on[1][i].start()
            self.y_near[i].start()

    def relay_again(self):
        for i in range(2):
            self.x_own[0][i].wait_recv()
            self.on[0][i].start()
        for i in range(2):
            self.on[1][i].wait_recv()
            self.y_far[i].start()
        for i in range(2):
            self.x_other[i].wait_recv()
            self.on_other[i].start()

    def wait(self):
        self.y_own[1].wait_recv()
        for copy in (*self.on[0], *self.on_other, *self.y_near, *self.y_far):
            copy.wait_recv()
        for copy in (*self.y_own, *self.x_own[0], *self.x_own[1], *self.x_other, *self.on[0], *self.on[1],
                     *self.on_other, *self.y_near, *self.y_far):
            copy.wait_send()


def gather_scratch():
    return [DMA((19,)), DMA((19,))]


class GradSum:
    def __init__(self, kind, part, out, other, far, near, sent, arrived):
        dp, _, col = here()
        self.kind, self.part, self.dp, self.col = kind, part, dp, col
        self.other, self.far, self.near = other, far, near
        self.rows = near.shape[1]
        self.core = [
            remote(self.half(c, 1 - dp), other.at[c], sent.at[c], arrived.at[c], dp=1 - dp)
            for c in range(8)
        ]
        self.zs = [
            [
                remote(
                    self.half(z_peer(col, d) // 2 * 2 + k, dp), far.at[d - 1, k], sent.at[6 + 2 * d + k],
                    arrived.at[6 + 2 * d + k], col=z_peer(col, d),
                )
                for k in range(2)
            ]
            for d in (1, 3, 2)
        ]
        self.ys = remote(near.at[0], near.at[1], sent.at[14], arrived.at[14], col=y_peer(col))
        self.last = remote(near.at[0], half_shard(out, dp), sent.at[15], arrived.at[15], dp=1 - dp)
        self.keep = pltpu.make_async_copy(near.at[0], half_shard(out, dp), sent.at[16])

    def half(self, c, h):
        return half_of(self.kind, self.part, c, h)

    def start(self):
        for copy in self.core:
            copy.start()

    def each(self, body):
        @pl.loop(0, self.rows // 16)
        def _(i):
            body(span(i, 16))

    def over_z(self):
        for copy in self.core:
            copy.wait()

        @pl.loop(0, 8)
        def _(c):
            own = self.half(c, self.dp)

            def add(at):
                own[at] = (own[at].astype(F32) + self.other[c, at].astype(F32)).astype(BF16)

            self.each(add)

        for pair in self.zs:
            for copy in pair:
                copy.start()

    def over_y(self):
        for pair in self.zs:
            for copy in pair:
                copy.wait_recv()
        yl = self.col % 2
        keep, give = self.half(self.col, self.dp), self.half(y_peer(self.col), self.dp)

        def add(at):
            total = give[at].astype(F32)
            for d in range(3):
                total = total + self.far[d, 1 - yl, at].astype(F32)
            self.near[0, at] = total.astype(BF16)

        self.each(add)
        self.ys.start()

        def add(at):
            total = keep[at].astype(F32)
            for d in range(3):
                total = total + self.far[d, yl, at].astype(F32)
            keep[at] = total.astype(BF16)

        self.each(add)
        for pair in self.zs:
            for copy in pair:
                copy.wait_send()

    def over_core(self):
        self.ys.wait()
        keep = self.half(self.col, self.dp)

        def add(at):
            self.near[0, at] = (keep[at].astype(F32) + self.near[1, at].astype(F32)).astype(BF16)

        self.each(add)
        self.last.start()
        self.keep.start()

    def wait(self):
        self.last.wait()
        self.keep.wait()


def grad_sum_scratch(rows, width):
    return [
        pltpu.VMEM((8, rows, width), BF16),
        pltpu.VMEM((3, 2, rows, width), BF16),
        pltpu.VMEM((2, rows, width), BF16),
        DMA((17,)),
        DMA((16,)),
    ]


def feed_kernel(
    rows_in, expand_in, reduce_in, residual, g, merged, gain_merge, gain_reduce,
    out, grad_resid, rows_out, merge_gain, reduce_gain, expand_grad, reduce_grad,
    rows, turned, expand, reduce, gate, up, act, act_turned, part, back, hidden, new_rows, done, sums, grad_gate,
    load, osent, ocame, g1sent, g1came, g2sent, g2came, *refs,
):
    dp, row, col = here()
    share, width = residual.shape
    units = act.shape[1]
    tiles = units // 256
    own = span(row, share)
    first = Scatter(part, *refs[:8])
    second = Scatter(part, *refs[8:16])
    reduce_sum = GradSum("wide", reduce, reduce_grad, *refs[16:21])
    expand_sum = GradSum("tall", expand, expand_grad, *refs[21:26])
    gather = Gather(back, share, g1sent, g1came)
    last_gather = Gather(new_rows, share, g2sent, g2came)
    spread = Spread(False, lambda k: cols(done, k, 256), lambda k: rows_of(out, k, 64), osent, ocame)

    get_rows = pltpu.make_async_copy(rows_in, rows, load.at[0])
    get_reduce = pltpu.make_async_copy(reduce_in, reduce, load.at[1])

    def get_expand(j):
        at = span(j, 256)
        return pltpu.make_async_copy(expand_in.at[:, at], expand.at[:, at], load.at[2 + j])

    get_rows.start()
    for j in range(tiles):
        get_expand(j).start()
        get_expand(tiles + j).start()
    get_reduce.start()
    meet_near(weights=True, spread_out=True)
    get_rows.wait()

    @pl.loop(0, tiles)
    def _(j):
        get_expand(j).wait()
        get_expand(tiles + j).wait()
        at = span(j, 256)
        gate[:, at] = dot(rows[...], expand[:, at])
        up[:, at] = dot(rows[...], expand[:, span(tiles + j, 256)])

        @pl.loop(0, rows.shape[0] // 64)
        def _(i):
            some = span(i, 64)
            x = gate[some, at]
            act[some, at] = (x * jax.nn.sigmoid(x) * up[some, at]).astype(BF16)

    get_reduce.wait()

    def reduced(j):
        at = span(j, 256)
        part[:, at] = dot(act[...], reduce[:, at]).astype(BF16)

    n = width // 512
    pl.loop(n, 2 * n)(reduced)
    first.start_right()
    pl.loop(0, n)(reduced)
    first.start_left()

    @pl.loop(0, tiles)
    def _(j):
        at = span(j, 256)
        act_turned[at, :] = act[:, at].T

    first.middle()
    first.end()
    sums[...] = jnp.zeros_like(sums)

    @pl.loop(0, share // 16)
    def _(i):
        at = span(i, 16)
        grad = g[at].astype(F32)
        hat, change = back_of(grad, first.total[at], gain_reduce[...])
        back[pl.ds(pl.multiple_of(row * share + i * 16, 16), 16), :] = change.astype(BF16)
        done[at] = (residual[at] + hat * gain_reduce[...]).astype(BF16)
        product = grad * hat
        sums[...] += product[:8] + product[8:]

    gather.start()
    spread.start()
    reduce_gain[...] = jnp.sum(sums[...], axis=0, keepdims=True)
    first.finish()
    gather.relay()

    @pl.loop(0, 2 * tiles)
    def _(j):
        at = span(j, 256)
        turned[at, :] = rows[:, at].T

    gather.relay_again()
    gather.wait()

    @pl.loop(0, tiles)
    def _(j):
        at, up_at = span(j, 256), span(tiles + j, 256)
        grad_gate[...] = dot_flipped(back[...], reduce[at, :])

        @pl.loop(0, rows.shape[0] // 64)
        def _(i):
            some = span(i, 64)
            x, change = gate[some, at], grad_gate[some]
            s = jax.nn.sigmoid(x)
            hidden[some, at] = (change * up[some, at] * s * (1.0 + x * (1.0 - s))).astype(BF16)
            hidden[some, up_at] = (change * (x * s)).astype(BF16)

    def branch(j):
        at = span(j, 256)
        part[:, at] = dot_flipped(hidden[...], expand[at, :]).astype(BF16)

    pl.loop(n, 2 * n)(branch)
    second.start_right()
    pl.loop(0, n)(branch)
    second.start_left()

    @pl.loop(0, tiles)
    def _(j):
        at = span(j, 256)
        for side in range(2):
            wide = pl.ds(side * (width // 2), width // 2)
            reduce[at, wide] = dot(act_turned[at, :], back[:, wide]).astype(BF16)

    reduce_sum.start()
    second.middle()

    def expand_part(j):
        at = span(j, 256)
        for side in range(2):
            wide = pl.ds(side * (width // 2), width // 2)
            expand[at, wide] = dot(turned[at, :], hidden[:, wide]).astype(BF16)

    pl.loop(0, tiles)(expand_part)
    second.end()
    sums[...] = jnp.zeros_like(sums)

    @pl.loop(0, share // 16)
    def _(i):
        at = span(i, 16)
        grad = g[at].astype(F32) + second.total[at]
        grad_resid[at] = grad
        hat, change = back_of(grad, merged[at], gain_merge[...])
        new_rows[pl.ds(pl.multiple_of(row * share + i * 16, 16), 16), :] = change.astype(BF16)
        product = grad * hat
        sums[...] += product[:8] + product[8:]

    last_gather.start()
    merge_gain[...] = jnp.sum(sums[...], axis=0, keepdims=True)
    pl.loop(tiles, 2 * tiles)(expand_part)
    expand_sum.start()
    last_gather.relay()
    reduce_sum.over_z()
    last_gather.relay_again()
    expand_sum.over_z()
    second.finish()
    last_gather.wait()
    put_rows = pltpu.make_async_copy(new_rows, rows_out, load.at[0])
    put_rows.start()
    reduce_sum.over_y()
    expand_sum.over_y()
    reduce_sum.over_core()
    expand_sum.over_core()
    spread.wait()
    put_rows.wait()
    reduce_sum.wait()
    expand_sum.wait()


class Bring:
    def __init__(self, kind, shard, whole, sent, arrived):
        dp, _, col = here()
        rows, width = shard.shape
        count = rows // 4
        near = y_peer(col)
        number = iter(range(28))

        def block(c, s):
            if kind == "tall":
                return whole.at[span(4 * c + 2 * dp + s, count)]
            return whole.at[span(2 * dp + s, count), span(c, width)]

        def copy(source, target, **where):
            i = next(number)
            return remote(source, target, sent.at[i], arrived.at[i], **where)

        mine = [shard.at[span(2 * dp + s, count)] for s in range(2)]
        place = whole.at[span(col, rows)] if kind == "tall" else whole.at[:, span(col, width)]
        self.local = pltpu.make_async_copy(shard, place, sent.at[28])
        steps = (1, 3, 2)
        self.y_own = [copy(mine[s], block(col, s), col=near) for s in range(2)]
        self.z_own = [[copy(mine[s], block(col, s), col=z_peer(col, d)) for d in steps] for s in range(2)]
        self.z_near = [copy(block(near, 0), block(near, 0), col=z_peer(col, d)) for d in steps]
        far = [z_source(col, d) for d in steps]
        self.y_far = [copy(block(c, 1), block(c, 1), col=near) for c in far]

        def across(c, s):
            return copy(block(c, s), block(c, s), dp=1 - dp)

        self.a_near = [across(near, s) for s in range(2)]
        self.a_far = [[across(c, s) for c in far] for s in range(2)]
        self.a_last = [[across(y_peer(c), s) for c in far] for s in range(2)]

    def start(self):
        for copy in (self.y_own[0], *self.z_own[1], *self.z_own[0], self.y_own[1], self.local):
            copy.start()

    def relay(self):
        self.y_own[0].wait_recv()
        for copy in (*self.z_near, self.a_near[0]):
            copy.start()

    def relay_again(self):
        for i in range(3):
            self.z_own[1][i].wait_recv()
            self.y_far[i].start()
            self.a_far[1][i].start()
        self.y_own[1].wait_recv()
        self.a_near[1].start()
        for i in range(3):
            self.z_own[0][i].wait_recv()
            self.a_far[0][i].start()

    def hand_over(self):
        for i in range(3):
            self.z_near[i].wait_recv()
            self.a_last[0][i].start()
            self.y_far[i].wait_recv()
            self.a_last[1][i].start()

    def wait(self):
        for copy in (*self.a_near, *self.a_far[0], *self.a_far[1], *self.a_last[0], *self.a_last[1]):
            copy.wait()
        for copy in (*self.y_own, *self.z_own[0], *self.z_own[1], *self.z_near, *self.y_far):
            copy.wait_send()
        self.local.wait()


def bring_scratch():
    return [DMA((29,)), DMA((28,))]


class SpreadIn:
    def __init__(self, source, target, sent, arrived):
        dp, row, col = here()
        self.row, self.col = row, col
        self.copies, self.waits = [], []
        for k in range(8):
            out = remote(source(k), target(k, col), sent.at[k], arrived.at[col], row=k, col=row)
            came = remote(source(k), target(row, k), sent.at[k], arrived.at[k], row=k, col=row)
            local = pltpu.make_async_copy(source(k), target(k, col), sent.at[k])
            self.copies.append(((row == k) & (row == col), out, local))
            self.waits.append(((row == col) & (col == k), came))

    def start(self):
        for mine, out, local in self.copies:
            pl.when(jnp.logical_not(mine))(out.start)
            pl.when(mine)(local.start)

    def wait(self):
        for mine, came in self.waits:
            pl.when(jnp.logical_not(mine))(came.wait_recv)
        for mine, out, local in self.copies:
            pl.when(jnp.logical_not(mine))(out.wait_send)
            pl.when(mine)(local.wait)


class TokenSums:
    def __init__(self, stats, mine, came, sent, arrived):
        dp, row, col = here()
        self.stats, self.mine, self.came = stats, mine, came
        self.copies = [
            remote(mine, came.at[d - 1], sent.at[d - 1], arrived.at[d - 1], row=row_peer(row, d))
            for d in range(1, 8)
        ]

    def put(self, at, one, two):
        lane = lax.broadcasted_iota(jnp.int32, (one.shape[0], 128), 1)
        self.stats[at] = jnp.where(lane == 0, one, jnp.where(lane == 1, two, 0.0))

    def start(self):
        self.mine[...] = self.stats[...].T[:8]
        for copy in self.copies:
            copy.start()

    def end(self):
        total = self.mine[...]
        for d, copy in enumerate(self.copies):
            copy.wait_recv()
            total = total + self.came[d]
        self.stats[...] = jnp.concatenate([total] * 16, axis=0).T
        for copy in self.copies:
            copy.wait_send()


def sums_scratch(tokens):
    return [pltpu.VMEM((8, tokens), F32), pltpu.VMEM((7, 8, tokens), F32), DMA((7,)), DMA((7,))]


def turn(values, cosine, sine):
    heads = [values[:, i : i + HD] for i in range(0, values.shape[1], HD)]
    return jnp.concatenate([h * cosine + pltpu.roll(h, HD // 2, 1) * sine for h in heads], axis=1)


QUERY_BLOCK = 128


def key_span(b):
    start = max(0, b * QUERY_BLOCK - WINDOW)
    return start, (b + 1) * QUERY_BLOCK - start


def attend_kernel(
    x, g, heads_in, merge_in, expand_in, reduce_in, cosine, sine, docs, doc_row, gain_query, gain_key, gain_merge,
    xs_out, share_out, heads_out, merge_out, expand_out, reduce_out, raw_out, qkv_out, probs_out, mix_out, rates_out,
    merged, residual, rows_out,
    xs, heads32, merge32, expand32, reduce32, heads16, merge16, expand16, reduce16, heads, merge, raw, qkv, probs, mix,
    rates, part, rows, load, put, xsent, xcame, gsent, gcame, asent, acame, bsent, bcame, *refs,
):
    dp, row, col = here()
    share, width = merged.shape
    tokens = xs.shape[0]
    head_width = mix.shape[1]
    own = span(row, share)
    loads = [
        pltpu.make_async_copy(source, target, load.at[i])
        for i, (source, target) in enumerate(
            ((heads_in, heads32), (merge_in, merge32), (reduce_in, reduce32), (expand_in, expand32))
        )
    ]
    for copy in loads:
        copy.start()
    spread_x = SpreadIn(
        lambda k: rows_of(x, k, share), lambda k, c: xs.at[span(k, share), span(c, 256)], xsent, xcame
    )
    spread_g = SpreadIn(
        lambda k: rows_of(g, k, share), lambda k, c: share_out.at[:, span(c, 256)], gsent, gcame
    )
    gather_x = Gather(xs, share, asent, acame)
    gather = Gather(rows, share, bsent, bcame)
    scatter = Scatter(part, *refs[:8])
    sums = TokenSums(rates, *refs[8:12])
    bring_heads = Bring("tall", heads16, heads, *refs[12:14])
    bring_merge = Bring("wide", merge16, merge, *refs[14:16])
    bring_reduce = Bring("wide", reduce16, reduce_out, *refs[16:18])
    bring_expand = Bring("tall", expand16, expand_out, *refs[18:20])
    puts = [
        pltpu.make_async_copy(source, target, put.at[i])
        for i, (source, target) in enumerate(
            ((xs, xs_out), (heads, heads_out), (merge, merge_out), (raw, raw_out), (qkv, qkv_out),
             (probs, probs_out), (mix, mix_out), (rates, rates_out), (rows, rows_out))
        )
    ]

    def narrow(source, target):
        @pl.loop(0, source.shape[0] // 16)
        def _(i):
            at = span(i, 16)
            target[at] = source[at].astype(BF16)

    meet(rows=True, weights=True, spread_in=True)
    spread_x.start()
    loads[0].wait()
    narrow(heads32, heads16)
    bring_heads.start()
    loads[1].wait()
    narrow(merge32, merge16)
    bring_merge.start()
    loads[2].wait()
    narrow(reduce32, reduce16)
    loads[3].wait()
    narrow(expand32, expand16)
    spread_x.wait()
    gather_x.start()
    bring_heads.relay()
    gather_x.relay()
    bring_merge.relay()
    bring_heads.relay_again()
    gather_x.relay_again()
    bring_heads.hand_over()
    bring_reduce.start()
    bring_expand.start()
    spread_g.start()
    gather_x.wait()
    bring_heads.wait()
    puts[0].start()
    puts[1].start()

    for i in range(2):
        raw[:, i * head_width : (i + 1) * head_width] = dot(
            xs[...], heads[:, i * head_width : (i + 1) * head_width]
        )

    @pl.loop(0, tokens // 64)
    def _(i):
        at = span(i, 64)
        squares = raw[at] * raw[at]
        sums.put(
            at,
            jnp.sum(squares[:, :head_width], axis=1, keepdims=True),
            jnp.sum(squares[:, head_width:], axis=1, keepdims=True),
        )

    sums.start()
    qkv[:, 2 * head_width :] = dot(xs[...], heads[:, 2 * head_width :]).astype(BF16)
    bring_merge.relay_again()
    bring_expand.relay()
    bring_reduce.relay()
    bring_merge.hand_over()
    sums.end()

    @pl.loop(0, tokens // 64)
    def _(i):
        at = span(i, 64)
        rate = lax.rsqrt(rates[at] * (1.0 / width) + EPS)
        rates[at] = rate
        for j, gain in enumerate((gain_query, gain_key)):
            some = slice(j * head_width, (j + 1) * head_width)
            hat = raw[at, some] * rate[:, j : j + 1]
            qkv[at, some] = turn(hat * gain[...], cosine[at], sine[at]).astype(BF16)

    puts[3].start()
    puts[4].start()
    puts[7].start()
    for b in range(tokens // QUERY_BLOCK):
        start, count = key_span(b)
        query_at = pl.ds(b * QUERY_BLOCK, QUERY_BLOCK)
        key_at = pl.ds(start, count)
        there = lax.broadcasted_iota(jnp.int32, (QUERY_BLOCK, count), 0) + (b * QUERY_BLOCK - start)
        distance = there - lax.broadcasted_iota(jnp.int32, (QUERY_BLOCK, count), 1)
        doc = docs[query_at, 0:1]
        allowed = (doc == doc_row[0:1, start : start + count]) & (distance >= 0) & (distance < WINDOW)
        live = (doc < 5.0).astype(F32)
        for h in range(head_width // HD):
            query, key, value = (
                slice(i * head_width + h * HD, i * head_width + (h + 1) * HD) for i in range(3)
            )
            scores = dot_flipped(qkv[query_at, query], qkv[key_at, key]) * HD**-0.5
            scores = jnp.where(allowed, scores, -1e30)
            weights = jnp.exp(scores - jnp.max(scores, axis=1, keepdims=True))
            shares = (weights / jnp.sum(weights, axis=1, keepdims=True)).astype(BF16)
            probs[h, b, :, :count] = shares
            if count < probs.shape[3]:
                probs[h, b, :, count:] = jnp.zeros((QUERY_BLOCK, probs.shape[3] - count), BF16)
            mix[query_at, h * HD : (h + 1) * HD] = (dot(shares, qkv[key_at, value]) * live).astype(BF16)

    puts[5].start()
    puts[6].start()
    bring_merge.wait()
    puts[2].start()

    def merge_part(j):
        at = span(j, 256)
        part[:, at] = dot(mix[...], merge[:, at]).astype(BF16)

    n = width // 512
    pl.loop(n, 2 * n)(merge_part)
    scatter.start_right()
    pl.loop(0, n)(merge_part)
    scatter.start_left()
    bring_expand.relay_again()
    scatter.middle()
    bring_reduce.relay_again()
    scatter.end()

    @pl.loop(0, share // 16)
    def _(i):
        at = span(i, 16)
        total = scatter.total[at]
        merged[at] = total
        mine = pl.ds(pl.multiple_of(row * share + i * 16, 16), 16)
        result = xs[mine, :].astype(F32) + total * mean_rate(total) * gain_merge[...]
        residual[at] = result
        rows[mine, :] = result.astype(BF16)

    gather.start()
    gather.relay()
    bring_expand.hand_over()
    gather.relay_again()
    bring_reduce.hand_over()
    gather.wait()
    puts[8].start()
    scatter.finish()
    spread_g.wait()
    bring_expand.wait()
    bring_reduce.wait()
    for copy in puts:
        copy.wait()


def last_kernel(
    part, grad_resid, gains, heads_part, merge_part,
    input_grad, gains_grad, heads_grad, merge_grad,
    came, done, grow, gcol, gcore, gsum, ssent, scame, osent, ocame, gsent, gcame, *grad_refs,
):
    dp, row, col = here()
    meet(rows=True, cols=True, weights=True, spread_out=True)
    scatter = RowScatter(part, came, ssent, scame)
    spread = Spread(False, lambda k: cols(done, k, 256), lambda k: rows_of(input_grad, k, 64), osent, ocame)
    grads = [
        GradScatter("tall", heads_part, heads_grad, *grad_refs[:6]),
        GradScatter("wide", merge_part, merge_grad, *grad_refs[6:]),
    ]
    row_sums = [
        remote(gains, grow.at[row], gsent.at[d - 1], gcame.at[d - 1], row=row_peer(row, d))
        for d in range(1, 8)
    ]
    col_sums = [
        remote(gsum.at[0], gcol.at[col], gsent.at[6 + d], gcame.at[6 + d], col=(col + d) % 8)
        for d in range(1, 8)
    ]
    core_sum = remote(gsum.at[1], gcore, gsent.at[14], gcame.at[14], dp=1 - dp)
    for copy in row_sums:
        copy.start()
    scatter.start()
    for grad in grads:
        grad.start()
    grow[row] = gains[...]
    for grad in grads:
        grad.over_z()
    for copy in row_sums:
        copy.wait()
    total = grow[0]
    for k in range(1, 8):
        total = total + grow[k]
    gsum[0] = total
    for copy in col_sums:
        copy.start()
    gcol[col] = total
    done[...] = grad_resid[...] + scatter.total()
    spread.start()
    for copy in col_sums:
        copy.wait()
    total = gcol[0]
    for k in range(1, 8):
        total = total + gcol[k]
    gsum[1] = total
    core_sum.start()
    for grad in grads:
        grad.over_y()
    for grad in grads:
        grad.over_core()
    core_sum.wait()
    gains_grad[...] = total + gcore[...]
    scatter.finish()
    spread.wait()
    for grad in grads:
        grad.wait()


def on_device(
    block_input,
    cotangent,
    doc_lengths,
    heads_weight,
    heads_first,
    heads_second,
    merge_weight,
    merge_first,
    merge_second,
    expand_weight,
    expand_first,
    expand_second,
    reduce_weight,
    reduce_first,
    reduce_second,
    norm_gains,
    gains_first,
    gains_second,
):
    row_at = lax.axis_index("row")
    col_width = block_input.shape[1]
    model_width = col_width * lax.axis_size("col")
    head_width = merge_weight.shape[0]
    unit_width = reduce_weight.shape[0]
    seq_len = block_input.shape[0] * lax.axis_size("row") // lax.axis_size("col")
    share = seq_len // lax.axis_size("row")
    head_count = head_width // HD
    doc_ids, places, live_rows = positions(doc_lengths[0], seq_len)
    gain_query = lax.dynamic_slice_in_dim(norm_gains[0], row_at * head_width, head_width)
    gain_key = lax.dynamic_slice_in_dim(norm_gains[1], row_at * head_width, head_width)
    gain_merge, gain_reduce = norm_gains[2:3], norm_gains[3:4]
    rows_shape = struct((seq_len, model_width), BF16)
    mine_f32 = struct((share, model_width), F32)
    line = struct((1, model_width), F32)
    row_scratch = [
        pltpu.VMEM((7, share, model_width), BF16),
        pltpu.VMEM((share, model_width), BF16),
        DMA((7,)),
        DMA((7,)),
        DMA((8,)),
        DMA((7,)),
    ]

    half_dim = HD // 2
    frequency = THETA ** (-2.0 * jnp.arange(half_dim, dtype=F32) / HD)
    angles = places.astype(F32)[:, None] * frequency[None, :]
    cosine, sine = jnp.cos(angles), jnp.sin(angles)
    cosine = jnp.concatenate([cosine, cosine], axis=1)
    sine = jnp.concatenate([-sine, sine], axis=1)
    docs = jnp.broadcast_to(doc_ids.astype(F32)[:, None], (seq_len, 128))
    doc_row = jnp.broadcast_to(doc_ids.astype(F32)[None, :], (8, seq_len))
    blocks = seq_len // QUERY_BLOCK

    (
        input_rows, cot_share, heads_low, merge_low, expand_low, reduce_low, raw, qkv, probs, mixture_low, rates,
        merged, residual, residual_rows,
    ) = call(
        attend_kernel, "attend", 1,
        [
            rows_shape,
            struct((share, model_width), BF16),
            struct((model_width, 3 * head_width), BF16),
            struct((head_width, model_width), BF16),
            struct((model_width, 2 * unit_width), BF16),
            struct((unit_width, model_width), BF16),
            struct((seq_len, 2 * head_width), F32),
            struct((seq_len, 3 * head_width), BF16),
            struct((head_count, blocks, QUERY_BLOCK, WINDOW + QUERY_BLOCK), BF16),
            struct((seq_len, head_width), BF16),
            struct((seq_len, 128), F32),
            mine_f32,
            mine_f32,
            rows_shape,
        ],
        [
            block_input, cotangent, heads_weight, merge_weight, expand_weight, reduce_weight, cosine, sine, docs,
            doc_row, gain_query[None], gain_key[None], gain_merge,
        ],
        [ANY] * 6 + [VMEM] * 7,
        [ANY] * 11 + [VMEM] * 2 + [ANY],
        [
            pltpu.VMEM((seq_len, model_width), BF16),
            pltpu.VMEM(heads_weight.shape, F32),
            pltpu.VMEM(merge_weight.shape, F32),
            pltpu.VMEM(expand_weight.shape, F32),
            pltpu.VMEM(reduce_weight.shape, F32),
            pltpu.VMEM(heads_weight.shape, BF16),
            pltpu.VMEM(merge_weight.shape, BF16),
            pltpu.VMEM(expand_weight.shape, BF16),
            pltpu.VMEM(reduce_weight.shape, BF16),
            pltpu.VMEM((model_width, 3 * head_width), BF16),
            pltpu.VMEM((head_width, model_width), BF16),
            pltpu.VMEM((seq_len, 2 * head_width), F32),
            pltpu.VMEM((seq_len, 3 * head_width), BF16),
            pltpu.VMEM((head_count, blocks, QUERY_BLOCK, WINDOW + QUERY_BLOCK), BF16),
            pltpu.VMEM((seq_len, head_width), BF16),
            pltpu.VMEM((seq_len, 128), F32),
            pltpu.VMEM((seq_len, model_width), BF16),
            pltpu.VMEM((seq_len, model_width), BF16),
            DMA((4,)), DMA((9,)), DMA((8,)), DMA((8,)), DMA((8,)), DMA((8,)),
        ]
        + gather_scratch() + gather_scratch()
        + scatter_scratch(share, model_width) + sums_scratch(seq_len)
        + bring_scratch() + bring_scratch() + bring_scratch() + bring_scratch(),
    )
    query_rate, key_rate = rates[:, 0:1], rates[:, 1:2]
    query_hat = raw[:, :head_width] * query_rate
    key_hat = raw[:, head_width:] * key_rate
    query_low, key_low, value_low = (
        qkv[:, i * head_width : (i + 1) * head_width].reshape(seq_len, head_count, HD) for i in range(3)
    )

    def head_sums(one, two, number):
        part = jnp.concatenate([one, two]).reshape(8, 128)
        total = call(
            sums_kernel, "sums", number, struct((8, 128), F32), [part], [VMEM], VMEM,
            [pltpu.VMEM((7, 8, 128), F32), DMA((7,)), DMA((7,))],
        ).reshape(2, seq_len)
        return total[0], total[1]

    block_output, grad_resid, merged_grad_rows, merge_gain_part, reduce_gain_part, expand_grad, reduce_grad = call(
        feed_kernel, "feed", 4,
        [struct(block_input.shape, BF16), mine_f32, rows_shape, line, line, struct(expand_weight.shape, BF16),
         struct(reduce_weight.shape, BF16)],
        [residual_rows, expand_low, reduce_low, residual, cot_share, merged, gain_merge, gain_reduce],
        [ANY] * 3 + [VMEM] * 5, [ANY, VMEM, ANY, VMEM, VMEM, ANY, ANY],
        [
            pltpu.VMEM((seq_len, model_width), BF16),
            pltpu.VMEM((model_width, seq_len), BF16),
            pltpu.VMEM((model_width, 2 * unit_width), BF16),
            pltpu.VMEM((unit_width, model_width), BF16),
            pltpu.VMEM((seq_len, unit_width), F32),
            pltpu.VMEM((seq_len, unit_width), F32),
            pltpu.VMEM((seq_len, unit_width), BF16),
            pltpu.VMEM((unit_width, seq_len), BF16),
            pltpu.VMEM((seq_len, model_width), BF16),
            pltpu.VMEM((seq_len, model_width), BF16),
            pltpu.VMEM((seq_len, 2 * unit_width), BF16),
            pltpu.VMEM((seq_len, model_width), BF16),
            pltpu.VMEM((share, model_width), BF16),
            pltpu.VMEM((8, model_width), F32),
            pltpu.VMEM((seq_len, 256), F32),
            DMA((10,)), DMA((8,)), DMA((8,)),
        ]
        + gather_scratch() + gather_scratch()
        + scatter_scratch(share, model_width) + scatter_scratch(share, model_width)
        + grad_sum_scratch(reduce_weight.shape[0] // 2, reduce_weight.shape[1])
        + grad_sum_scratch(expand_weight.shape[0] // 2, expand_weight.shape[1]),
    )
    grad_mixture = product(merged_grad_rows, merge_low, True)
    merge_part = column_total(mixture_low, merged_grad_rows).astype(BF16)
    grad_mix_low = (
        grad_mixture.astype(jnp.bfloat16).reshape(seq_len, head_count, HD)
        * live_rows.astype(jnp.bfloat16)[:, None, None]
    )
    shares = jnp.zeros((head_count, seq_len, seq_len), BF16)
    for b in range(blocks):
        start, count = key_span(b)
        shares = lax.dynamic_update_slice(shares, probs[:, b, :, :count], (0, b * QUERY_BLOCK, start))
    grad_queries, grad_keys, grad_values = attend_backward(query_low, key_low, value_low, shares, grad_mix_low)
    query_norm_grad = rotate(grad_queries, places, -1.0).reshape(seq_len, head_width)
    key_norm_grad = rotate(grad_keys, places, -1.0).reshape(seq_len, head_width)
    query_gain_part = jnp.sum(query_norm_grad * query_hat, axis=0)
    key_gain_part = jnp.sum(key_norm_grad * key_hat, axis=0)
    query_hat_grad = query_norm_grad * gain_query
    key_hat_grad = key_norm_grad * gain_key
    query_dot, key_dot = head_sums(
        jnp.sum(query_hat_grad * query_hat, axis=1), jnp.sum(key_hat_grad * key_hat, axis=1), 6
    )
    grad_query_rows = norm_back(query_hat_grad, query_hat, query_rate, query_dot, model_width)
    grad_key_rows = norm_back(key_hat_grad, key_hat, key_rate, key_dot, model_width)
    joined_grad = jnp.concatenate(
        [grad_query_rows, grad_key_rows, grad_values.reshape(seq_len, head_width)], axis=1
    ).astype(jnp.bfloat16)
    input_part = product(joined_grad, heads_low, True).astype(BF16)
    heads_part = column_total(input_rows, joined_grad).astype(BF16)
    gain_parts = jnp.zeros((2, model_width), jnp.float32)
    gain_parts = lax.dynamic_update_slice(
        gain_parts, jnp.stack([query_gain_part, key_gain_part]), (jnp.int32(0), row_at * head_width)
    )
    gain_parts = jnp.concatenate([gain_parts, merge_gain_part, reduce_gain_part]).reshape(8, model_width // 2)
    gain_shape = (8, model_width // 2)

    input_grad, gains_grad, heads_grad, merge_grad = call(
        last_kernel, "last", 7,
        [struct(block_input.shape, F32), struct(gain_shape, F32), struct(heads_weight.shape, BF16),
         struct(merge_weight.shape, BF16)],
        [input_part, grad_resid, gain_parts, heads_part, merge_part],
        [VMEM] * 3 + [ANY] * 2, [ANY, VMEM] + [ANY] * 2,
        [row_scratch[0], pltpu.VMEM((share, model_width), F32), pltpu.VMEM((8, *gain_shape), F32),
         pltpu.VMEM((8, *gain_shape), F32), pltpu.VMEM(gain_shape, F32), pltpu.VMEM((2, *gain_shape), F32),
         DMA((7,)), DMA((7,)), DMA((8,)), DMA((8,)), DMA((15,)), DMA((15,))]
        + grad_scratch(heads_weight.shape[0] // 2, heads_weight.shape[1])
        + grad_scratch(merge_weight.shape[0] // 2, merge_weight.shape[1]),
    )
    gains_grad = gains_grad.reshape(4, model_width)
    heads_grad, merge_grad, expand_grad, reduce_grad = (
        heads_grad.astype(F32), merge_grad.astype(F32), expand_grad.astype(F32), reduce_grad.astype(F32)
    )
    heads_mean, heads_square, heads_fresh = adamw(
        heads_weight, heads_grad, heads_first, heads_second, LR, DECAY
    )
    merge_mean, merge_square, merge_fresh = adamw(
        merge_weight, merge_grad, merge_first, merge_second, LR, DECAY
    )
    expand_mean, expand_square, expand_fresh = adamw(
        expand_weight, expand_grad, expand_first, expand_second, LR, DECAY
    )
    reduce_mean, reduce_square, reduce_fresh = adamw(
        reduce_weight, reduce_grad, reduce_first, reduce_second, LR, DECAY
    )
    gains_mean, gains_square, gains_fresh = adamw(
        norm_gains, gains_grad, gains_first, gains_second, LR_GAIN, 0.0
    )
    return (
        block_output,
        input_grad,
        heads_grad,
        heads_mean,
        heads_square,
        heads_fresh,
        heads_fresh.astype(jnp.bfloat16),
        merge_grad,
        merge_mean,
        merge_square,
        merge_fresh,
        merge_fresh.astype(jnp.bfloat16),
        expand_grad,
        expand_mean,
        expand_square,
        expand_fresh,
        expand_fresh.astype(jnp.bfloat16),
        reduce_grad,
        reduce_mean,
        reduce_square,
        reduce_fresh,
        reduce_fresh.astype(jnp.bfloat16),
        gains_grad,
        gains_mean,
        gains_square,
        gains_fresh,
    )


def solution(mesh):
    return jax.shard_map(
        on_device,
        mesh=mesh,
        in_specs=(
            P(("dp", "row"), "col"),
            P(("dp", "row"), "col"),
            P(("dp", "col"), None),
            P("col", "row"),
            P("col", "row"),
            P("col", "row"),
            P("row", "col"),
            P("row", "col"),
            P("row", "col"),
            P("col", "row"),
            P("col", "row"),
            P("col", "row"),
            P("row", "col"),
            P("row", "col"),
            P("row", "col"),
            P(),
            P(),
            P(),
        ),
        out_specs=(
            P(("dp", "row"), "col"),
            P(("dp", "row"), "col"),
            P("col", "row"),
            P("col", "row"),
            P("col", "row"),
            P("col", "row"),
            P("col", "row"),
            P("row", "col"),
            P("row", "col"),
            P("row", "col"),
            P("row", "col"),
            P("row", "col"),
            P("col", "row"),
            P("col", "row"),
            P("col", "row"),
            P("col", "row"),
            P("col", "row"),
            P("row", "col"),
            P("row", "col"),
            P("row", "col"),
            P("row", "col"),
            P("row", "col"),
            P(),
            P(),
            P(),
            P(),
        ),
        check_vma=False,
    )
```

```python
import functools

import jax
import jax.numpy as jnp
from jax import lax
from jax.experimental import pallas as pl
from jax.experimental.pallas import tpu as pltpu
from jax.sharding import PartitionSpec as P

HD = 128
WINDOW = 256
STEP = 5


EPS = 1e-06
THETA = 500000.0
LR = 0.02
LR_GAIN = 0.2
BETA_ONE = 0.5
BETA_TWO = 0.5
DECAY = 0.1
ADAM_EPS = 1e-08

BF16 = jnp.bfloat16
F32 = jnp.float32
MESH = pl.DeviceIdType.MESH
ANY = pl.BlockSpec(memory_space=pl.ANY)
VMEM = pl.BlockSpec(memory_space=pltpu.VMEM)
DMA = pltpu.SemaphoreType.DMA


def positions(lengths, row_count):
    doc_ends = jnp.cumsum(lengths)
    index_ids = jnp.arange(row_count, dtype=jnp.int32)
    passed = doc_ends[None, :] <= index_ids[:, None]
    doc_ids = jnp.sum(passed.astype(jnp.int32), axis=1)
    starts = jnp.sum(jnp.where(passed, lengths[None, :], 0), axis=1)
    live_rows = (doc_ids < lengths.shape[0] - 1).astype(jnp.float32)
    return (doc_ids, index_ids - starts, live_rows)


def adamw(weight, gradient, first_mom, second_mom, step_rate, decay_rate):
    mean_new = BETA_ONE * first_mom + (1.0 - BETA_ONE) * gradient
    square_new = BETA_TWO * second_mom + (1.0 - BETA_TWO) * gradient * gradient
    fix_one = 1.0 - BETA_ONE**STEP
    fix_two = 1.0 - BETA_TWO**STEP
    update = mean_new / fix_one / (jnp.sqrt(square_new / fix_two) + ADAM_EPS) + decay_rate * weight
    return (mean_new, square_new, weight - step_rate * update)


def here():
    return lax.axis_index("dp"), lax.axis_index("row"), lax.axis_index("col")


def row_peer(row, d):
    return (row // 4 + d // 4) % 2 * 4 + (row % 4 + d % 4) % 4


def z_peer(col, d):
    return (col // 2 + d) % 4 * 2 + col % 2


def z_source(col, d):
    return (col // 2 + 4 - d) % 4 * 2 + col % 2


def y_peer(col):
    return col // 2 * 2 + 1 - col % 2


def remote(source, target, sent, arrived, **where):
    return pltpu.make_async_remote_copy(
        src_ref=source,
        dst_ref=target,
        send_sem=sent,
        recv_sem=arrived,
        device_id=where,
        device_id_type=MESH,
    )


def meet(rows=False, cols=False, weights=False, core=False, spread_in=False, spread_out=False):
    dp, row, col = here()
    barrier = pltpu.get_barrier_semaphore()
    count = 0

    def greet(**where):
        pl.semaphore_signal(barrier, inc=1, device_id=where, device_id_type=MESH)

    if rows:
        for d in range(1, 8):
            greet(row=row_peer(row, d))
        count = count + 7
    if cols:
        for d in range(1, 8):
            greet(col=(col + d) % 8)
        count = count + 7
    if weights:
        greet(col=y_peer(col))
        for d in (1, 3):
            greet(col=z_peer(col, d))
        count = count + 3
    if core:
        greet(dp=1 - dp)
        count = count + 1
    for wanted, inward in ((spread_in, True), (spread_out, False)):
        if wanted:
            for k in range(8):
                at_row, at_col = (col, k) if inward else (k, row)

                @pl.when(jnp.logical_not((at_row == row) & (at_col == col)))
                def _():
                    greet(row=at_row, col=at_col)

            count = count + 8 - (row == col).astype(jnp.int32)
    pl.semaphore_wait(barrier, count)


class Spread:
    def __init__(self, inward, source, target, sent, arrived):
        dp, row, col = here()
        self.row, self.col, self.inward = row, col, inward
        self.copies = []
        for k in range(8):
            to_row, to_col = (k, row) if inward else (col, k)
            mine = (row == to_row) & (col == to_col)
            copy = remote(
                source(k),
                target(col if inward else row),
                sent.at[k],
                arrived.at[col if inward else row],
                row=to_row,
                col=to_col,
            )
            waiter = remote(source(k), target(k), sent.at[k], arrived.at[k], row=to_row, col=to_col)
            local = pltpu.make_async_copy(
                source(k), target(col if inward else row), sent.at[k]
            )
            self.copies.append((mine, copy, waiter, local))

    def start(self):
        for mine, copy, _, local in self.copies:
            pl.when(jnp.logical_not(mine))(copy.start)
            pl.when(mine)(local.start)

    def wait(self):
        for k, (mine, copy, waiter, local) in enumerate(self.copies):
            from_row, from_col = (self.col, k) if self.inward else (k, self.row)
            me = (from_row == self.row) & (from_col == self.col)
            pl.when(jnp.logical_not(me))(waiter.wait_recv)
            pl.when(jnp.logical_not(mine))(copy.wait_send)
            pl.when(mine)(local.wait)


def half_of(kind, ref, c, h):
    if kind == "tall":
        count = ref.shape[0] // 16
        return ref.at[pl.ds(pl.multiple_of((2 * c + h) * count, count), count)]
    count, width = ref.shape[0] // 2, ref.shape[1] // 8
    return ref.at[
        pl.ds(pl.multiple_of(h * count, count), count), pl.ds(pl.multiple_of(c * width, width), width)
    ]


def half_shard(ref, h):
    count = ref.shape[0] // 2
    return ref.at[pl.ds(pl.multiple_of(h * count, count), count)]


def mean_rate(values):
    return lax.rsqrt(jnp.mean(values * values, axis=-1, keepdims=True) + EPS)


def call(kernel, name, number, outs, ins, in_specs, out_specs, scratch):
    return pl.pallas_call(
        kernel,
        name=name,
        out_shape=outs,
        in_specs=in_specs,
        out_specs=out_specs,
        scratch_shapes=scratch,
        compiler_params=pltpu.CompilerParams(
            collective_id=number, has_side_effects=True, vmem_limit_bytes=62 * 2**20
        ),
    )(*ins)


def struct(shape, kind):
    return jax.ShapeDtypeStruct(shape, kind)


def dot(left, right):
    return jnp.dot(left, right, preferred_element_type=F32)


def dot_flipped(left, right):
    return lax.dot_general(left, right, (((1,), (1,)), ((), ())), preferred_element_type=F32)


def span(k, count):
    return pl.ds(pl.multiple_of(k * count, count), count)


def near_row(row, dx, dy):
    return (row // 4 + dy) % 2 * 4 + (row % 4 + dx) % 4


class Scatter:
    def __init__(self, part, total, from_y, from_x, last_y, last_x, stage, sent, arrived):
        dp, row, col = here()
        self.row, self.part, self.total = row, part, total
        self.from_y, self.from_x, self.last_y, self.last_x, self.stage = from_y, from_x, last_y, last_x, stage
        self.count, self.half = total.shape[0], total.shape[1] // 2
        number = iter(range(14))

        def copy(source, target, dx, dy):
            i = next(number)
            return remote(source, target, sent.at[i], arrived.at[i], row=near_row(row, dx, dy))

        self.y_first = {dx: copy(self.block(dx, 1, 1), from_y.at[dx], 0, 1) for dx in (1, 3, 2, 0)}
        self.x_first = {
            (dx, dy): copy(self.block(dx, dy, 0), from_x.at[dy, dx - 1], dx, 0)
            for dy in (1, 0)
            for dx in (1, 3, 2)
        }
        self.x_last = {dx: copy(stage.at[dx], last_x.at[dx - 1], dx, 0) for dx in (1, 3, 2)}
        self.y_last = copy(stage.at[0], last_y, 0, 1)

    def block(self, dx, dy, side):
        return self.part.at[
            span(near_row(self.row, dx, dy), self.count), pl.ds(side * self.half, self.half)
        ]

    def start_right(self):
        for copy in self.y_first.values():
            copy.start()

    def start_left(self):
        for copy in self.x_first.values():
            copy.start()

    def chunks(self, body):
        @pl.loop(0, self.count // 16)
        def _(i):
            body(span(i, 16))

    def middle(self):
        for dx in (1, 3, 2):
            self.y_first[dx].wait_recv()
            own = self.block(dx, 0, 1)

            def add(at):
                self.stage[dx, at] = (own[at].astype(F32) + self.from_y[dx, at].astype(F32)).astype(BF16)

            self.chunks(add)
            self.x_last[dx].start()
        for dx in (1, 3, 2):
            self.x_first[dx, 1].wait_recv()
        other = self.block(0, 1, 0)

        def add(at):
            total = other[at].astype(F32)
            for k in range(3):
                total = total + self.from_x[1, k, at].astype(F32)
            self.stage[0, at] = total.astype(BF16)

        self.chunks(add)
        self.y_last.start()

    def end(self):
        self.y_first[0].wait_recv()
        for dx in (1, 3, 2):
            self.x_first[dx, 0].wait_recv()
            self.x_last[dx].wait_recv()
        self.y_last.wait_recv()
        left, right = self.block(0, 0, 0), self.block(0, 0, 1)

        def add(at):
            total = left[at].astype(F32) + self.last_y[at].astype(F32)
            for k in range(3):
                total = total + self.from_x[0, k, at].astype(F32)
            self.total[at, : self.half] = total
            total = right[at].astype(F32) + self.from_y[0, at].astype(F32)
            for k in range(3):
                total = total + self.last_x[k, at].astype(F32)
            self.total[at, self.half :] = total

        self.chunks(add)

    def finish(self):
        for copies in (self.y_first, self.x_first, self.x_last):
            for copy in copies.values():
                copy.wait_send()
        self.y_last.wait_send()


def scatter_scratch(share, width):
    half = width // 2
    return [
        pltpu.VMEM((share, width), F32),
        pltpu.VMEM((4, share, half), BF16),
        pltpu.VMEM((2, 3, share, half), BF16),
        pltpu.VMEM((share, half), BF16),
        pltpu.VMEM((3, share, half), BF16),
        pltpu.VMEM((4, share, half), BF16),
        DMA((14,)),
        DMA((14,)),
    ]


class Gather:
    def __init__(self, whole, share, sent, arrived):
        dp, row, col = here()
        self.row = row
        half = whole.shape[1] // 2
        number = iter(range(19))

        def copy(fx, fy, side, dx, dy, start=0, count=share):
            i = next(number)
            k = near_row(row, fx, fy)
            ref = whole.at[
                pl.ds(pl.multiple_of(k * share + start, count), count), pl.ds(side * half, half)
            ]
            return remote(ref, ref, sent.at[i], arrived.at[i], row=near_row(row, dx, dy))

        part = share // 2
        self.y_own = [copy(0, 0, 0, 0, 1), copy(0, 0, 1, 0, 1)]
        self.x_own = [[copy(0, 0, side, dx, 0) for dx in (1, 3)] for side in range(2)]
        self.x_other = [copy(0, 1, 0, dx, 0) for dx in (1, 3)]
        self.on = [
            [copy(4 - dx, 0, side, dx, 0, i * part, part) for i, dx in enumerate((1, 3))]
            for side in range(2)
        ]
        self.on_other = [copy(4 - dx, 1, 0, dx, 0, i * part, part) for i, dx in enumerate((1, 3))]
        self.y_near = [copy(4 - dx, 0, 1, 0, 1) for dx in (1, 3)]
        self.y_far = [copy(2, 0, 1, 0, 1, i * part, part) for i in range(2)]

    def start(self):
        for copy in (self.y_own[0], *self.x_own[1], self.y_own[1], *self.x_own[0]):
            copy.start()

    def relay(self):
        self.y_own[0].wait_recv()
        for copy in self.x_other:
            copy.start()
        for i in range(2):
            self.x_own[1][i].wait_recv()
            self.on[1][i].start()
            self.y_near[i].start()

    def relay_again(self):
        for i in range(2):
            self.x_own[0][i].wait_recv()
            self.on[0][i].start()
        for i in range(2):
            self.on[1][i].wait_recv()
            self.y_far[i].start()
        for i in range(2):
            self.x_other[i].wait_recv()
            self.on_other[i].start()

    def wait(self):
        self.y_own[1].wait_recv()
        for copy in (*self.on[0], *self.on_other, *self.y_near, *self.y_far):
            copy.wait_recv()
        for copy in (*self.y_own, *self.x_own[0], *self.x_own[1], *self.x_other, *self.on[0], *self.on[1],
                     *self.on_other, *self.y_near, *self.y_far):
            copy.wait_send()


def gather_scratch():
    return [DMA((19,)), DMA((19,))]


def cols(ref, k, width):
    return ref.at[:, pl.ds(pl.multiple_of(k * width, width), width)]


def rows_of(ref, k, count):
    return ref.at[pl.ds(pl.multiple_of(k * count, count), count)]


def back_of(grad, values, gain):
    rate = mean_rate(values)
    hat = values * rate
    grad_hat = grad * gain
    dots = jnp.mean(grad_hat * hat, axis=-1, keepdims=True)
    return hat, rate * (grad_hat - hat * dots)


class GradSum:
    def __init__(self, kind, part, out, other, between, far, near, sent, arrived):
        dp, _, col = here()
        self.kind, self.part, self.dp, self.col = kind, part, dp, col
        self.other, self.between, self.far, self.near = other, between, far, near
        self.rows = near.shape[1]
        number = iter(range(18))

        def copy(source, target, **where):
            i = next(number)
            return remote(source, target, sent.at[i], arrived.at[i], **where)

        self.core = [copy(self.half(c, 1 - dp), other.at[c], dp=1 - dp) for c in range(8)]
        self.steps = (1, 3)
        self.on = [
            [
                copy(self.piece(self.z_block(2, k), i), between.at[i, k], col=z_peer(col, d))
                for k in range(2)
            ]
            for i, d in enumerate(self.steps)
        ]
        self.zs = [
            [copy(self.half(self.z_block(d, k), dp), far.at[i, k], col=z_peer(col, d)) for k in range(2)]
            for i, d in enumerate(self.steps)
        ]
        self.ys = copy(near.at[0], near.at[1], col=y_peer(col))
        self.last = copy(near.at[0], half_shard(out, dp), dp=1 - dp)
        self.keep = pltpu.make_async_copy(near.at[0], half_shard(out, dp), sent.at[18])

    def z_block(self, d, k):
        return z_peer(self.col, d) // 2 * 2 + k

    def half(self, c, h):
        return half_of(self.kind, self.part, c, h)

    def piece(self, c, i):
        return self.half(c, self.dp).at[pl.ds(i * (self.rows // 2), self.rows // 2)]

    def start(self):
        for copy in self.core:
            copy.start()

    def each(self, rows, body):
        @pl.loop(0, rows // 16)
        def _(i):
            body(span(i, 16))

    def over_core(self):
        for copy in self.core:
            copy.wait()

        @pl.loop(0, 8)
        def _(c):
            own = self.half(c, self.dp)

            def add(at):
                own[at] = (own[at].astype(F32) + self.other[c, at].astype(F32)).astype(BF16)

            self.each(self.rows, add)

        for pair in self.on:
            for copy in pair:
                copy.start()

    def over_z(self):
        for i, d in enumerate(self.steps):
            for k in range(2):
                self.on[i][k].wait_recv()
                own = self.piece(self.z_block(d, k), i)

                def add(at):
                    own[at] = (own[at].astype(F32) + self.between[i, k, at].astype(F32)).astype(BF16)

                self.each(self.rows // 2, add)
            for k in range(2):
                self.zs[i][k].start()

    def over_y(self):
        for pair in self.zs:
            for copy in pair:
                copy.wait_recv()
        yl = self.col % 2
        keep, give = self.half(self.col, self.dp), self.half(y_peer(self.col), self.dp)

        def total(at, ref, k):
            return (
                ref[at].astype(F32) + self.far[0, k, at].astype(F32) + self.far[1, k, at].astype(F32)
            ).astype(BF16)

        def add(at):
            self.near[0, at] = total(at, give, 1 - yl)

        self.each(self.rows, add)
        self.ys.start()

        def add(at):
            keep[at] = total(at, keep, yl)

        self.each(self.rows, add)
        for pair in (*self.zs, *self.on):
            for copy in pair:
                copy.wait_send()

    def end(self):
        self.ys.wait()
        keep = self.half(self.col, self.dp)

        def add(at):
            self.near[0, at] = (keep[at].astype(F32) + self.near[1, at].astype(F32)).astype(BF16)

        self.each(self.rows, add)
        self.last.start()
        self.keep.start()

    def wait(self):
        self.last.wait()
        self.keep.wait()


def grad_sum_scratch(shape):
    rows, width = shape[0] // 2, shape[1]
    return [
        pltpu.VMEM((8, rows, width), BF16),
        pltpu.VMEM((2, 2, rows // 2, width), BF16),
        pltpu.VMEM((2, 2, rows, width), BF16),
        pltpu.VMEM((2, rows, width), BF16),
        DMA((19,)),
        DMA((18,)),
    ]


class Bring:
    def __init__(self, kind, shard, whole, sent, arrived):
        dp, _, col = here()
        rows, width = shard.shape
        near = y_peer(col)
        number = iter(range(20))

        def block(c, s=None):
            count, at = (rows // 2, dp) if s is None else (rows // 4, 2 * dp + s)
            if kind == "tall":
                return whole.at[span((2 if s is None else 4) * c + at, count)]
            return whole.at[span(at, count), span(c, width)]

        def copy(source, target, **where):
            i = next(number)
            return remote(source, target, sent.at[i], arrived.at[i], **where)

        mine = half_shard(shard, dp)
        place = whole.at[span(col, rows)] if kind == "tall" else whole.at[:, span(col, width)]
        self.local = pltpu.make_async_copy(shard, place, sent.at[20])
        self.y_own = copy(mine, block(col), col=near)
        self.z_own = [copy(mine, block(col), col=z_peer(col, d)) for d in (1, 3)]
        self.z_near = [copy(block(near), block(near), col=z_peer(col, d)) for d in (1, 3)]
        self.on, self.on_near, self.a_own, self.a_near = [], [], [], []
        self.a_far, self.a_far_near = [], []
        for i, d in enumerate((1, 3)):
            came, two = z_source(col, d), z_peer(col, 2)
            self.on.append(copy(block(came, i), block(came, i), col=z_peer(col, d)))
            self.on_near.append(copy(block(y_peer(came), i), block(y_peer(came), i), col=z_peer(col, d)))
            self.a_own.append(copy(block(came), block(came), dp=1 - dp))
            self.a_near.append(copy(block(y_peer(came)), block(y_peer(came)), dp=1 - dp))
            self.a_far.append(copy(block(two, i), block(two, i), dp=1 - dp))
            self.a_far_near.append(copy(block(y_peer(two), i), block(y_peer(two), i), dp=1 - dp))
        self.a_y = copy(block(near), block(near), dp=1 - dp)

    def start(self):
        for copy in (self.y_own, *self.z_own, self.local):
            copy.start()

    def relay(self):
        self.y_own.wait_recv()
        for copy in (*self.z_near, self.a_y):
            copy.start()

    def relay_own(self):
        for i in range(2):
            self.z_own[i].wait_recv()
            self.on[i].start()
            self.a_own[i].start()

    def relay_near(self):
        for i in range(2):
            self.z_near[i].wait_recv()
            self.on_near[i].start()
            self.a_near[i].start()

    def hand_over(self):
        for i in range(2):
            self.on[i].wait_recv()
            self.a_far[i].start()
        for i in range(2):
            self.on_near[i].wait_recv()
            self.a_far_near[i].start()

    def wait(self):
        for copy in (self.a_y, *self.a_own, *self.a_near, *self.a_far, *self.a_far_near):
            copy.wait()
        for copy in (self.y_own, *self.z_own, *self.z_near, *self.on, *self.on_near):
            copy.wait_send()
        self.local.wait()


def bring_scratch():
    return [DMA((21,)), DMA((20,))]


class SpreadIn:
    def __init__(self, source, target, sent, arrived):
        dp, row, col = here()
        self.row, self.col = row, col
        self.copies, self.waits = [], []
        for k in range(8):
            out = remote(source(k), target(k, col), sent.at[k], arrived.at[col], row=k, col=row)
            came = remote(source(k), target(row, k), sent.at[k], arrived.at[k], row=k, col=row)
            local = pltpu.make_async_copy(source(k), target(k, col), sent.at[k])
            self.copies.append(((row == k) & (row == col), out, local))
            self.waits.append(((row == col) & (col == k), came))

    def start(self):
        for mine, out, local in self.copies:
            pl.when(jnp.logical_not(mine))(out.start)
            pl.when(mine)(local.start)

    def wait(self):
        for mine, came in self.waits:
            pl.when(jnp.logical_not(mine))(came.wait_recv)
        for mine, out, local in self.copies:
            pl.when(jnp.logical_not(mine))(out.wait_send)
            pl.when(mine)(local.wait)


class TokenSums:
    def __init__(self, stats, mine, came, sent, arrived):
        dp, row, col = here()
        self.stats, self.mine, self.came = stats, mine, came
        self.copies = [
            remote(mine, came.at[d - 1], sent.at[d - 1], arrived.at[d - 1], row=row_peer(row, d))
            for d in range(1, 8)
        ]

    def put(self, at, one, two):
        lane = lax.broadcasted_iota(jnp.int32, (one.shape[0], 128), 1)
        self.stats[at] = jnp.where(lane == 0, one, jnp.where(lane == 1, two, 0.0))

    def start(self):
        self.mine[...] = self.stats[...].T[:8]
        for copy in self.copies:
            copy.start()

    def end(self):
        total = self.mine[...]
        for d, copy in enumerate(self.copies):
            copy.wait_recv()
            total = total + self.came[d]
        self.stats[...] = jnp.concatenate([total] * 16, axis=0).T
        for copy in self.copies:
            copy.wait_send()


def sums_scratch(tokens):
    return [pltpu.VMEM((8, tokens), F32), pltpu.VMEM((7, 8, tokens), F32), DMA((7,)), DMA((7,))]


def turn(values, cosine, sine):
    heads = [values[:, i : i + HD] for i in range(0, values.shape[1], HD)]
    return jnp.concatenate([h * cosine + pltpu.roll(h, HD // 2, 1) * sine for h in heads], axis=1)


QUERY_BLOCK = 128


def key_span(b):
    start = max(0, b * QUERY_BLOCK - WINDOW)
    return start, (b + 1) * QUERY_BLOCK - start


def attend_kernel(
    x, g, heads_in, merge_in, expand_in, reduce_in, cosine, sine, docs, doc_row, gain_query, gain_key, gain_merge,
    xs_out, share_out, heads_out, merge_out, expand_out, reduce_out, raw_out, qkv_out, probs_out, mix_out, rates_out,
    merged, residual, rows_out,
    xs, heads32, merge32, expand32, reduce32, heads16, merge16, expand16, reduce16, heads, merge, raw, qkv, probs, mix,
    rates, part, rows, load, put, xsent, xcame, gsent, gcame, asent, acame, bsent, bcame, *refs,
):
    dp, row, col = here()
    share, width = merged.shape
    tokens = xs.shape[0]
    head_width = mix.shape[1]
    own = span(row, share)
    loads = [
        pltpu.make_async_copy(source, target, load.at[i])
        for i, (source, target) in enumerate(
            ((heads_in, heads32), (merge_in, merge32), (reduce_in, reduce32), (expand_in, expand32))
        )
    ]
    for copy in loads:
        copy.start()
    spread_x = SpreadIn(
        lambda k: rows_of(x, k, share), lambda k, c: xs.at[span(k, share), span(c, 256)], xsent, xcame
    )
    spread_g = SpreadIn(
        lambda k: rows_of(g, k, share), lambda k, c: share_out.at[:, span(c, 256)], gsent, gcame
    )
    gather_x = Gather(xs, share, asent, acame)
    gather = Gather(rows, share, bsent, bcame)
    scatter = Scatter(part, *refs[:8])
    sums = TokenSums(rates, *refs[8:12])
    bring_heads = Bring("tall", heads16, heads, *refs[12:14])
    bring_merge = Bring("wide", merge16, merge, *refs[14:16])
    bring_reduce = Bring("wide", reduce16, reduce_out, *refs[16:18])
    bring_expand = Bring("tall", expand16, expand_out, *refs[18:20])
    puts = [
        pltpu.make_async_copy(source, target, put.at[i])
        for i, (source, target) in enumerate(
            ((xs, xs_out), (heads, heads_out), (merge, merge_out), (raw, raw_out), (qkv, qkv_out),
             (probs, probs_out), (mix, mix_out), (rates, rates_out), (rows, rows_out))
        )
    ]

    def narrow(source, target):
        @pl.loop(0, source.shape[0] // 16)
        def _(i):
            at = span(i, 16)
            target[at] = source[at].astype(BF16)

    meet(rows=True, weights=True, core=True, spread_in=True)
    spread_x.start()
    loads[0].wait()
    narrow(heads32, heads16)
    bring_heads.start()
    loads[1].wait()
    narrow(merge32, merge16)
    bring_merge.start()
    loads[2].wait()
    narrow(reduce32, reduce16)
    loads[3].wait()
    narrow(expand32, expand16)
    spread_x.wait()
    gather_x.start()
    bring_heads.relay()
    bring_heads.relay_own()
    gather_x.relay()
    bring_heads.relay_near()
    bring_merge.relay()
    gather_x.relay_again()
    bring_heads.hand_over()
    bring_expand.start()
    bring_reduce.start()
    gather_x.wait()
    bring_heads.wait()
    puts[0].start()
    puts[1].start()

    for i in range(2):
        raw[:, i * head_width : (i + 1) * head_width] = dot(
            xs[...], heads[:, i * head_width : (i + 1) * head_width]
        )

    @pl.loop(0, tokens // 64)
    def _(i):
        at = span(i, 64)
        squares = raw[at] * raw[at]
        sums.put(
            at,
            jnp.sum(squares[:, :head_width], axis=1, keepdims=True),
            jnp.sum(squares[:, head_width:], axis=1, keepdims=True),
        )

    sums.start()
    qkv[:, 2 * head_width :] = dot(xs[...], heads[:, 2 * head_width :]).astype(BF16)
    bring_merge.relay_own()
    bring_merge.relay_near()
    sums.end()
    spread_g.start()

    @pl.loop(0, tokens // 64)
    def _(i):
        at = span(i, 64)
        rate = lax.rsqrt(rates[at] * (1.0 / width) + EPS)
        rates[at] = rate
        for j, gain in enumerate((gain_query, gain_key)):
            some = slice(j * head_width, (j + 1) * head_width)
            hat = raw[at, some] * rate[:, j : j + 1]
            qkv[at, some] = turn(hat * gain[...], cosine[at], sine[at]).astype(BF16)

    puts[3].start()
    puts[4].start()
    puts[7].start()
    for b in range(tokens // QUERY_BLOCK):
        start, count = key_span(b)
        query_at = pl.ds(b * QUERY_BLOCK, QUERY_BLOCK)
        key_at = pl.ds(start, count)
        there = lax.broadcasted_iota(jnp.int32, (QUERY_BLOCK, count), 0) + (b * QUERY_BLOCK - start)
        distance = there - lax.broadcasted_iota(jnp.int32, (QUERY_BLOCK, count), 1)
        doc = docs[query_at, 0:1]
        allowed = (doc == doc_row[0:1, start : start + count]) & (distance >= 0) & (distance < WINDOW)
        live = (doc < 5.0).astype(F32)
        for h in range(head_width // HD):
            query, key, value = (
                slice(i * head_width + h * HD, i * head_width + (h + 1) * HD) for i in range(3)
            )
            scores = dot_flipped(qkv[query_at, query], qkv[key_at, key]) * HD**-0.5
            scores = jnp.where(allowed, scores, -1e30)
            weights = jnp.exp(scores - jnp.max(scores, axis=1, keepdims=True))
            shares = (weights / jnp.sum(weights, axis=1, keepdims=True)).astype(BF16)
            probs[h, b, :, :count] = shares
            if count < probs.shape[3]:
                probs[h, b, :, count:] = jnp.zeros((QUERY_BLOCK, probs.shape[3] - count), BF16)
            mix[query_at, h * HD : (h + 1) * HD] = (dot(shares, qkv[key_at, value]) * live).astype(BF16)

    puts[5].start()
    puts[6].start()
    bring_expand.relay()
    bring_reduce.relay()
    bring_merge.hand_over()
    bring_merge.wait()
    puts[2].start()

    def merge_part(j):
        at = span(j, 256)
        part[:, at] = dot(mix[...], merge[:, at]).astype(BF16)

    n = width // 512
    pl.loop(n, 2 * n)(merge_part)
    scatter.start_right()
    pl.loop(0, n)(merge_part)
    scatter.start_left()
    bring_expand.relay_own()
    bring_reduce.relay_own()
    scatter.middle()
    bring_expand.relay_near()
    bring_reduce.relay_near()
    scatter.end()

    @pl.loop(0, share // 16)
    def _(i):
        at = span(i, 16)
        total = scatter.total[at]
        merged[at] = total
        mine = pl.ds(pl.multiple_of(row * share + i * 16, 16), 16)
        result = xs[mine, :].astype(F32) + total * mean_rate(total) * gain_merge[...]
        residual[at] = result
        rows[mine, :] = result.astype(BF16)

    gather.start()
    gather.relay()
    bring_expand.hand_over()
    gather.relay_again()
    bring_reduce.hand_over()
    gather.wait()
    puts[8].start()
    scatter.finish()
    spread_g.wait()
    bring_expand.wait()
    bring_reduce.wait()
    for copy in puts:
        copy.wait()


def rest_kernel(
    rows_in, expand_in, reduce_in, heads_in, merge_in, xs_in, raw_in, qkv_in, probs_in, mix_in, rates_in,
    residual, g, merged, cosine, sine, docs, gain_query, gain_key, gain_merge, gain_reduce,
    out, input_grad, gains_grad, heads_grad, merge_grad, expand_grad, reduce_grad,
    rows, turned, expand, reduce, heads, merge, gate, up, act, act_turned, part, back, hidden, probs, mix, mix_turned,
    rates, stats, grad_mix, done, final, grad_resid, sums, grad_gate,
    gains, gain_row, gain_col, gain_core, gain_sum, load, late, osent, ocame, isent, icame, nsent, ncame,
    g1sent, g1came, g2sent, g2came, *refs,
):
    dp, row, col = here()
    share, width = residual.shape
    tokens, units = act.shape
    head_width = mix.shape[1]
    tiles = units // 256
    n = width // 512
    scatter = [Scatter(part, *refs[:6], *refs[6 + 2 * i : 8 + 2 * i]) for i in range(3)]
    token_sums = TokenSums(stats, *refs[12:16])
    reduce_sum = GradSum("wide", reduce, reduce_grad, *refs[16:22])
    expand_sum = GradSum("tall", expand, expand_grad, *refs[22:28])
    merge_sum = GradSum("wide", merge, merge_grad, *refs[28:34])
    heads_sum = GradSum("tall", heads, heads_grad, *refs[34:40])
    gather = Gather(back, share, g1sent, g1came)
    last_gather = Gather(back, share, g2sent, g2came)
    spread = Spread(False, lambda k: cols(done, k, 256), lambda k: rows_of(out, k, 64), osent, ocame)
    spread_grad = Spread(False, lambda k: cols(final, k, 256), lambda k: rows_of(input_grad, k, 64), isent, icame)
    row_gains = [
        remote(gains, gain_row.at[row], nsent.at[d - 1], ncame.at[d - 1], row=row_peer(row, d))
        for d in range(1, 8)
    ]
    col_gains = [
        remote(gain_sum.at[0], gain_col.at[col], nsent.at[6 + d], ncame.at[6 + d], col=(col + d) % 8)
        for d in range(1, 8)
    ]
    core_gains = remote(gain_sum.at[1], gain_core, nsent.at[14], ncame.at[14], dp=1 - dp)

    raw, qkv, new_rows = up.at[:, : 2 * head_width], act.at[:, : 3 * head_width], back
    heads_change = gate.at[:, : 3 * head_width]
    joined = hidden.at[:, : 3 * head_width]
    get_rows = pltpu.make_async_copy(rows_in, rows, load.at[0])
    get_reduce = pltpu.make_async_copy(reduce_in, reduce, load.at[1])

    def get_expand(j):
        at = span(j, 256)
        return pltpu.make_async_copy(expand_in.at[:, at], expand.at[:, at], load.at[2 + j])

    early = [
        pltpu.make_async_copy(source, target, late.at[i])
        for i, (source, target) in enumerate(
            ((heads_in, heads), (merge_in, merge), (probs_in, probs), (mix_in, mix), (rates_in, rates))
        )
    ]
    get_raw = pltpu.make_async_copy(raw_in, raw, late.at[5])
    get_qkv = pltpu.make_async_copy(qkv_in, qkv, late.at[6])
    get_xs = pltpu.make_async_copy(xs_in, rows, late.at[7])

    get_rows.start()
    for j in range(tiles):
        get_expand(j).start()
        get_expand(tiles + j).start()
    get_reduce.start()
    meet(rows=True, cols=True, core=True, spread_out=True)
    get_rows.wait()

    @pl.loop(0, tiles)
    def _(j):
        get_expand(j).wait()
        get_expand(tiles + j).wait()
        at = span(j, 256)
        gate[:, at] = dot(rows[...], expand[:, at])
        up[:, at] = dot(rows[...], expand[:, span(tiles + j, 256)])

        @pl.loop(0, tokens // 64)
        def _(i):
            some = span(i, 64)
            x = gate[some, at]
            act[some, at] = (x * jax.nn.sigmoid(x) * up[some, at]).astype(BF16)

    get_reduce.wait()

    def reduced(j):
        at = span(j, 256)
        part[:, at] = dot(act[...], reduce[:, at]).astype(BF16)

    pl.loop(n, 2 * n)(reduced)
    scatter[0].start_right()
    pl.loop(0, n)(reduced)
    scatter[0].start_left()

    @pl.loop(0, tiles)
    def _(j):
        at = span(j, 256)
        act_turned[at, :] = act[:, at].T

    for copy in early:
        copy.start()
    get_qkv.start()

    scatter[0].middle()
    scatter[0].end()
    sums[...] = jnp.zeros_like(sums)

    @pl.loop(0, share // 16)
    def _(i):
        at = span(i, 16)
        grad = g[at].astype(F32)
        hat, change = back_of(grad, scatter[0].total[at], gain_reduce[...])
        back[pl.ds(pl.multiple_of(row * share + i * 16, 16), 16), :] = change.astype(BF16)
        done[at] = (residual[at] + hat * gain_reduce[...]).astype(BF16)
        product = grad * hat
        sums[...] += product[:8] + product[8:]

    gather.start()
    gains[...] = jnp.zeros_like(gains)
    gains[3:4] = jnp.sum(sums[...], axis=0, keepdims=True)
    scatter[0].finish()
    gather.relay()

    @pl.loop(0, 2 * tiles)
    def _(j):
        at = span(j, 256)
        turned[at, :] = rows[:, at].T

    get_xs.start()
    gather.relay_again()
    gather.wait()
    spread.start()

    @pl.loop(0, tiles)
    def _(j):
        at, up_at = span(j, 256), span(tiles + j, 256)
        grad_gate[...] = dot_flipped(back[...], reduce[at, :])

        @pl.loop(0, tokens // 64)
        def _(i):
            some = span(i, 64)
            x, change = gate[some, at], grad_gate[some]
            s = jax.nn.sigmoid(x)
            hidden[some, at] = (change * up[some, at] * s * (1.0 + x * (1.0 - s))).astype(BF16)
            hidden[some, up_at] = (change * (x * s)).astype(BF16)

    get_raw.start()

    def branch(j):
        at = span(j, 256)
        part[:, at] = dot_flipped(hidden[...], expand[at, :]).astype(BF16)

    pl.loop(n, 2 * n)(branch)
    scatter[1].start_right()
    pl.loop(0, n)(branch)
    scatter[1].start_left()

    @pl.loop(0, tiles)
    def _(j):
        at = span(j, 256)
        for side in range(2):
            wide = pl.ds(side * (width // 2), width // 2)
            reduce[at, wide] = dot(act_turned[at, :], back[:, wide]).astype(BF16)

    reduce_sum.start()
    scatter[1].middle()

    def expand_part(j):
        at = span(j, 256)
        for side in range(2):
            wide = pl.ds(side * (width // 2), width // 2)
            expand[at, wide] = dot(turned[at, :], hidden[:, wide]).astype(BF16)

    pl.loop(0, tiles)(expand_part)
    scatter[1].end()
    sums[...] = jnp.zeros_like(sums)

    @pl.loop(0, share // 16)
    def _(i):
        at = span(i, 16)
        grad = g[at].astype(F32) + scatter[1].total[at]
        grad_resid[at] = grad
        hat, change = back_of(grad, merged[at], gain_merge[...])
        new_rows[pl.ds(pl.multiple_of(row * share + i * 16, 16), 16), :] = change.astype(BF16)
        product = grad * hat
        sums[...] += product[:8] + product[8:]

    last_gather.start()
    gains[2:3] = jnp.sum(sums[...], axis=0, keepdims=True)
    pl.loop(tiles, 2 * tiles)(expand_part)
    expand_sum.start()
    last_gather.relay()
    reduce_sum.over_core()
    last_gather.relay_again()
    get_xs.wait()

    @pl.loop(0, 2 * tiles)
    def _(j):
        at = span(j, 256)
        turned[at, :] = rows[:, at].T

    for copy in early:
        copy.wait()
    get_raw.wait()
    get_qkv.wait()
    mix_turned[...] = mix[...].T
    expand_sum.over_core()
    reduce_sum.over_z()
    scatter[1].finish()
    last_gather.wait()

    live = (docs[:, 0:1] < 5.0).astype(F32)
    grad_mix[...] = (dot_flipped(new_rows[...], merge[...]) * live).astype(BF16)
    heads_change[:, head_width:] = jnp.zeros((tokens, 2 * head_width), F32)
    for b in range(tokens // QUERY_BLOCK):
        start, count = key_span(b)
        query_at = pl.ds(b * QUERY_BLOCK, QUERY_BLOCK)
        key_at = pl.ds(start, count)
        for h in range(head_width // HD):
            query, key, value = (
                slice(i * head_width + h * HD, i * head_width + (h + 1) * HD) for i in range(3)
            )
            shares = probs[h, b, :, :count]
            change = grad_mix[query_at, h * HD : (h + 1) * HD]
            grad_shares = dot_flipped(change, qkv[key_at, value])
            weighted = shares.astype(F32) * grad_shares
            center = jnp.sum(weighted, axis=1, keepdims=True)
            grad_scores = (weighted - shares.astype(F32) * center).astype(BF16)
            heads_change[query_at, query] = dot(grad_scores, qkv[key_at, key]) * HD**-0.5
            heads_change[key_at, key] += dot(grad_scores.T, qkv[query_at, query]) * HD**-0.5
            heads_change[key_at, value] += dot(shares.T, change)

    sums[...] = jnp.zeros_like(sums)

    @pl.loop(0, tokens // 64)
    def _(i):
        at = span(i, 64)
        dots = []
        for j, gain in enumerate((gain_query, gain_key)):
            some = slice(j * head_width, (j + 1) * head_width)
            change = turn(heads_change[at, some], cosine[at], -sine[at])
            hat = raw[at, some] * rates[at, j : j + 1]
            product = change * hat
            sums[:, some] += jnp.sum(product.reshape(8, 8, head_width), axis=0)
            heads_change[at, some] = change * gain[...]
            dots.append(jnp.sum(product * gain[...], axis=1, keepdims=True))
        token_sums.put(at, *dots)

    token_sums.start()
    gains[0:1, span(row, head_width)] = jnp.sum(sums[:, :head_width], axis=0, keepdims=True)
    gains[1:2, span(row, head_width)] = jnp.sum(sums[:, head_width : 2 * head_width], axis=0, keepdims=True)
    for copy in row_gains:
        copy.start()
    for side in range(4):
        wide = pl.ds(side * (width // 4), width // 4)
        merge[:, wide] = dot(mix_turned[...], new_rows[:, wide]).astype(BF16)
    merge_sum.start()
    joined[:, 2 * head_width :] = heads_change[:, 2 * head_width :].astype(BF16)
    token_sums.end()

    @pl.loop(0, tokens // 64)
    def _(i):
        at = span(i, 64)
        dots = stats[at] * (1.0 / width)
        for j in range(2):
            some = slice(j * head_width, (j + 1) * head_width)
            rate = rates[at, j : j + 1]
            hat = raw[at, some] * rate
            joined[at, some] = (rate * (heads_change[at, some] - hat * dots[:, j : j + 1])).astype(BF16)

    def input_part(j):
        at = span(j, 256)
        part[:, at] = dot_flipped(joined[...], heads[at, :]).astype(BF16)

    pl.loop(n, 2 * n)(input_part)
    scatter[2].start_right()
    pl.loop(0, n)(input_part)
    scatter[2].start_left()

    @pl.loop(0, 2 * tiles)
    def _(j):
        at = span(j, 256)
        heads[at, :] = dot(turned[at, :], joined[...]).astype(BF16)

    heads_sum.start()
    merge_sum.over_core()
    scatter[2].middle()
    expand_sum.over_z()
    heads_sum.over_core()
    scatter[2].end()
    final[...] = grad_resid[...] + scatter[2].total[...]
    spread_grad.start()
    for copy in row_gains:
        copy.wait()
    gain_row[row] = gains[...]
    total = gain_row[0]
    for k in range(1, 8):
        total = total + gain_row[k]
    gain_sum[0] = total
    gain_col[col] = total
    for copy in col_gains:
        copy.start()
    merge_sum.over_z()
    heads_sum.over_z()
    for copy in col_gains:
        copy.wait()
    total = gain_col[0]
    for k in range(1, 8):
        total = total + gain_col[k]
    gain_sum[1] = total
    core_gains.start()
    reduce_sum.over_y()
    expand_sum.over_y()
    reduce_sum.end()
    merge_sum.over_y()
    heads_sum.over_y()
    expand_sum.end()
    merge_sum.end()
    heads_sum.end()
    core_gains.wait()
    gains_grad[...] = gain_sum[1] + gain_core[...]
    scatter[2].finish()
    spread.wait()
    spread_grad.wait()
    for grad in (reduce_sum, expand_sum, merge_sum, heads_sum):
        grad.wait()


def on_device(
    block_input,
    cotangent,
    doc_lengths,
    heads_weight,
    heads_first,
    heads_second,
    merge_weight,
    merge_first,
    merge_second,
    expand_weight,
    expand_first,
    expand_second,
    reduce_weight,
    reduce_first,
    reduce_second,
    norm_gains,
    gains_first,
    gains_second,
):
    row_at = lax.axis_index("row")
    col_width = block_input.shape[1]
    model_width = col_width * lax.axis_size("col")
    head_width = merge_weight.shape[0]
    unit_width = reduce_weight.shape[0]
    seq_len = block_input.shape[0] * lax.axis_size("row") // lax.axis_size("col")
    share = seq_len // lax.axis_size("row")
    head_count = head_width // HD
    doc_ids, places, live_rows = positions(doc_lengths[0], seq_len)
    gain_query = lax.dynamic_slice_in_dim(norm_gains[0], row_at * head_width, head_width)
    gain_key = lax.dynamic_slice_in_dim(norm_gains[1], row_at * head_width, head_width)
    gain_merge, gain_reduce = norm_gains[2:3], norm_gains[3:4]
    rows_shape = struct((seq_len, model_width), BF16)
    mine_f32 = struct((share, model_width), F32)
    half_dim = HD // 2
    frequency = THETA ** (-2.0 * jnp.arange(half_dim, dtype=F32) / HD)
    angles = places.astype(F32)[:, None] * frequency[None, :]
    cosine, sine = jnp.cos(angles), jnp.sin(angles)
    cosine = jnp.concatenate([cosine, cosine], axis=1)
    sine = jnp.concatenate([-sine, sine], axis=1)
    docs = jnp.broadcast_to(doc_ids.astype(F32)[:, None], (seq_len, 128))
    doc_row = jnp.broadcast_to(doc_ids.astype(F32)[None, :], (8, seq_len))
    blocks = seq_len // QUERY_BLOCK

    (
        input_rows, cot_share, heads_low, merge_low, expand_low, reduce_low, raw, qkv, probs, mixture_low, rates,
        merged, residual, residual_rows,
    ) = call(
        attend_kernel, "attend", 1,
        [
            rows_shape,
            struct((share, model_width), BF16),
            struct((model_width, 3 * head_width), BF16),
            struct((head_width, model_width), BF16),
            struct((model_width, 2 * unit_width), BF16),
            struct((unit_width, model_width), BF16),
            struct((seq_len, 2 * head_width), F32),
            struct((seq_len, 3 * head_width), BF16),
            struct((head_count, blocks, QUERY_BLOCK, WINDOW + QUERY_BLOCK), BF16),
            struct((seq_len, head_width), BF16),
            struct((seq_len, 128), F32),
            mine_f32,
            mine_f32,
            rows_shape,
        ],
        [
            block_input, cotangent, heads_weight, merge_weight, expand_weight, reduce_weight, cosine, sine, docs,
            doc_row, gain_query[None], gain_key[None], gain_merge,
        ],
        [ANY] * 6 + [VMEM] * 7,
        [ANY] * 11 + [VMEM] * 2 + [ANY],
        [
            pltpu.VMEM((seq_len, model_width), BF16),
            pltpu.VMEM(heads_weight.shape, F32),
            pltpu.VMEM(merge_weight.shape, F32),
            pltpu.VMEM(expand_weight.shape, F32),
            pltpu.VMEM(reduce_weight.shape, F32),
            pltpu.VMEM(heads_weight.shape, BF16),
            pltpu.VMEM(merge_weight.shape, BF16),
            pltpu.VMEM(expand_weight.shape, BF16),
            pltpu.VMEM(reduce_weight.shape, BF16),
            pltpu.VMEM((model_width, 3 * head_width), BF16),
            pltpu.VMEM((head_width, model_width), BF16),
            pltpu.VMEM((seq_len, 2 * head_width), F32),
            pltpu.VMEM((seq_len, 3 * head_width), BF16),
            pltpu.VMEM((head_count, blocks, QUERY_BLOCK, WINDOW + QUERY_BLOCK), BF16),
            pltpu.VMEM((seq_len, head_width), BF16),
            pltpu.VMEM((seq_len, 128), F32),
            pltpu.VMEM((seq_len, model_width), BF16),
            pltpu.VMEM((seq_len, model_width), BF16),
            DMA((4,)), DMA((9,)), DMA((8,)), DMA((8,)), DMA((8,)), DMA((8,)),
        ]
        + gather_scratch() + gather_scratch()
        + scatter_scratch(share, model_width) + sums_scratch(seq_len)
        + bring_scratch() + bring_scratch() + bring_scratch() + bring_scratch(),
    )
    gain_shape = (4, model_width)
    block_output, input_grad, gains_grad, heads_grad, merge_grad, expand_grad, reduce_grad = call(
        rest_kernel, "rest", 2,
        [
            struct(block_input.shape, BF16),
            struct(block_input.shape, F32),
            struct(gain_shape, F32),
            struct(heads_weight.shape, BF16),
            struct(merge_weight.shape, BF16),
            struct(expand_weight.shape, BF16),
            struct(reduce_weight.shape, BF16),
        ],
        [
            residual_rows, expand_low, reduce_low, heads_low, merge_low, input_rows, raw, qkv, probs, mixture_low, rates,
            residual, cot_share, merged, cosine, sine, docs, gain_query[None], gain_key[None], gain_merge, gain_reduce,
        ],
        [ANY] * 11 + [VMEM] * 10,
        [ANY] * 2 + [VMEM] + [ANY] * 4,
        [
            pltpu.VMEM((seq_len, model_width), BF16),
            pltpu.VMEM((model_width, seq_len), BF16),
            pltpu.VMEM((model_width, 2 * unit_width), BF16),
            pltpu.VMEM((unit_width, model_width), BF16),
            pltpu.VMEM((model_width, 3 * head_width), BF16),
            pltpu.VMEM((head_width, model_width), BF16),
            pltpu.VMEM((seq_len, unit_width), F32),
            pltpu.VMEM((seq_len, unit_width), F32),
            pltpu.VMEM((seq_len, unit_width), BF16),
            pltpu.VMEM((unit_width, seq_len), BF16),
            pltpu.VMEM((seq_len, model_width), BF16),
            pltpu.VMEM((seq_len, model_width), BF16),
            pltpu.VMEM((seq_len, 2 * unit_width), BF16),
            pltpu.VMEM((head_count, blocks, QUERY_BLOCK, WINDOW + QUERY_BLOCK), BF16),
            pltpu.VMEM((seq_len, head_width), BF16),
            pltpu.VMEM((head_width, seq_len), BF16),
            pltpu.VMEM((seq_len, 128), F32),
            pltpu.VMEM((seq_len, 128), F32),
            pltpu.VMEM((seq_len, head_width), BF16),
            pltpu.VMEM((share, model_width), BF16),
            pltpu.VMEM((share, model_width), F32),
            pltpu.VMEM((share, model_width), F32),
            pltpu.VMEM((8, model_width), F32),
            pltpu.VMEM((seq_len, 256), F32),
            pltpu.VMEM(gain_shape, F32),
            pltpu.VMEM((8, *gain_shape), F32),
            pltpu.VMEM((8, *gain_shape), F32),
            pltpu.VMEM(gain_shape, F32),
            pltpu.VMEM((2, *gain_shape), F32),
            DMA((10,)), DMA((8,)), DMA((8,)), DMA((8,)), DMA((8,)), DMA((8,)), DMA((15,)), DMA((15,)),
        ]
        + gather_scratch() + gather_scratch()
        + scatter_scratch(share, model_width) + [DMA((14,))] * 4
        + sums_scratch(seq_len)
        + grad_sum_scratch(reduce_weight.shape) + grad_sum_scratch(expand_weight.shape)
        + grad_sum_scratch(merge_weight.shape) + grad_sum_scratch(heads_weight.shape),
    )
    heads_grad, merge_grad, expand_grad, reduce_grad = (
        heads_grad.astype(F32), merge_grad.astype(F32), expand_grad.astype(F32), reduce_grad.astype(F32)
    )
    heads_mean, heads_square, heads_fresh = adamw(
        heads_weight, heads_grad, heads_first, heads_second, LR, DECAY
    )
    merge_mean, merge_square, merge_fresh = adamw(
        merge_weight, merge_grad, merge_first, merge_second, LR, DECAY
    )
    expand_mean, expand_square, expand_fresh = adamw(
        expand_weight, expand_grad, expand_first, expand_second, LR, DECAY
    )
    reduce_mean, reduce_square, reduce_fresh = adamw(
        reduce_weight, reduce_grad, reduce_first, reduce_second, LR, DECAY
    )
    gains_mean, gains_square, gains_fresh = adamw(
        norm_gains, gains_grad, gains_first, gains_second, LR_GAIN, 0.0
    )
    return (
        block_output,
        input_grad,
        heads_grad,
        heads_mean,
        heads_square,
        heads_fresh,
        heads_fresh.astype(jnp.bfloat16),
        merge_grad,
        merge_mean,
        merge_square,
        merge_fresh,
        merge_fresh.astype(jnp.bfloat16),
        expand_grad,
        expand_mean,
        expand_square,
        expand_fresh,
        expand_fresh.astype(jnp.bfloat16),
        reduce_grad,
        reduce_mean,
        reduce_square,
        reduce_fresh,
        reduce_fresh.astype(jnp.bfloat16),
        gains_grad,
        gains_mean,
        gains_square,
        gains_fresh,
    )


def solution(mesh):
    return jax.shard_map(
        on_device,
        mesh=mesh,
        in_specs=(
            P(("dp", "row"), "col"),
            P(("dp", "row"), "col"),
            P(("dp", "col"), None),
            P("col", "row"),
            P("col", "row"),
            P("col", "row"),
            P("row", "col"),
            P("row", "col"),
            P("row", "col"),
            P("col", "row"),
            P("col", "row"),
            P("col", "row"),
            P("row", "col"),
            P("row", "col"),
            P("row", "col"),
            P(),
            P(),
            P(),
        ),
        out_specs=(
            P(("dp", "row"), "col"),
            P(("dp", "row"), "col"),
            P("col", "row"),
            P("col", "row"),
            P("col", "row"),
            P("col", "row"),
            P("col", "row"),
            P("row", "col"),
            P("row", "col"),
            P("row", "col"),
            P("row", "col"),
            P("row", "col"),
            P("col", "row"),
            P("col", "row"),
            P("col", "row"),
            P("col", "row"),
            P("col", "row"),
            P("row", "col"),
            P("row", "col"),
            P("row", "col"),
            P("row", "col"),
            P("row", "col"),
            P(),
            P(),
            P(),
            P(),
        ),
        check_vma=False,
    )
```

```python
import functools

import jax
import jax.numpy as jnp
from jax import lax
from jax.experimental import pallas as pl
from jax.experimental.pallas import tpu as pltpu
from jax.sharding import PartitionSpec as P

HD = 128
WINDOW = 256
STEP = 5


EPS = 1e-06
THETA = 500000.0
LR = 0.02
LR_GAIN = 0.2
BETA_ONE = 0.5
BETA_TWO = 0.5
DECAY = 0.1
ADAM_EPS = 1e-08

BF16 = jnp.bfloat16
F32 = jnp.float32
MESH = pl.DeviceIdType.MESH
ANY = pl.BlockSpec(memory_space=pl.ANY)
VMEM = pl.BlockSpec(memory_space=pltpu.VMEM)
DMA = pltpu.SemaphoreType.DMA


def positions(lengths, row_count):
    doc_ends = jnp.cumsum(lengths)
    index_ids = jnp.arange(row_count, dtype=jnp.int32)
    passed = doc_ends[None, :] <= index_ids[:, None]
    doc_ids = jnp.sum(passed.astype(jnp.int32), axis=1)
    starts = jnp.sum(jnp.where(passed, lengths[None, :], 0), axis=1)
    live_rows = (doc_ids < lengths.shape[0] - 1).astype(jnp.float32)
    return (doc_ids, index_ids - starts, live_rows)


def adamw(weight, gradient, first_mom, second_mom, step_rate, decay_rate):
    mean_new = BETA_ONE * first_mom + (1.0 - BETA_ONE) * gradient
    square_new = BETA_TWO * second_mom + (1.0 - BETA_TWO) * gradient * gradient
    fix_one = 1.0 - BETA_ONE**STEP
    fix_two = 1.0 - BETA_TWO**STEP
    update = mean_new / fix_one / (jnp.sqrt(square_new / fix_two) + ADAM_EPS) + decay_rate * weight
    return (mean_new, square_new, weight - step_rate * update)


def here():
    return lax.axis_index("dp"), lax.axis_index("row"), lax.axis_index("col")


def row_peer(row, d):
    return (row // 4 + d // 4) % 2 * 4 + (row % 4 + d % 4) % 4


def z_peer(col, d):
    return (col // 2 + d) % 4 * 2 + col % 2


def z_source(col, d):
    return (col // 2 + 4 - d) % 4 * 2 + col % 2


def y_peer(col):
    return col // 2 * 2 + 1 - col % 2


def remote(source, target, sent, arrived, **where):
    return pltpu.make_async_remote_copy(
        src_ref=source,
        dst_ref=target,
        send_sem=sent,
        recv_sem=arrived,
        device_id=where,
        device_id_type=MESH,
    )


def meet(rows=False, cols=False, weights=False, core=False, spread_in=False, spread_out=False):
    dp, row, col = here()
    barrier = pltpu.get_barrier_semaphore()
    count = 0

    def greet(**where):
        pl.semaphore_signal(barrier, inc=1, device_id=where, device_id_type=MESH)

    if rows:
        for d in range(1, 8):
            greet(row=row_peer(row, d))
        count = count + 7
    if cols:
        for d in range(1, 8):
            greet(col=(col + d) % 8)
        count = count + 7
    if weights:
        greet(col=y_peer(col))
        for d in (1, 3):
            greet(col=z_peer(col, d))
        count = count + 3
    if core:
        greet(dp=1 - dp)
        count = count + 1
    for wanted, inward in ((spread_in, True), (spread_out, False)):
        if wanted:
            for k in range(8):
                at_row, at_col = (col, k) if inward else (k, row)

                @pl.when(jnp.logical_not((at_row == row) & (at_col == col)))
                def _():
                    greet(row=at_row, col=at_col)

            count = count + 8 - (row == col).astype(jnp.int32)
    pl.semaphore_wait(barrier, count)


class Spread:
    def __init__(self, inward, source, target, sent, arrived):
        dp, row, col = here()
        self.row, self.col, self.inward = row, col, inward
        self.copies = []
        for k in range(8):
            to_row, to_col = (k, row) if inward else (col, k)
            mine = (row == to_row) & (col == to_col)
            copy = remote(
                source(k),
                target(col if inward else row),
                sent.at[k],
                arrived.at[col if inward else row],
                row=to_row,
                col=to_col,
            )
            waiter = remote(source(k), target(k), sent.at[k], arrived.at[k], row=to_row, col=to_col)
            local = pltpu.make_async_copy(
                source(k), target(col if inward else row), sent.at[k]
            )
            self.copies.append((mine, copy, waiter, local))

    def start(self):
        for mine, copy, _, local in self.copies:
            pl.when(jnp.logical_not(mine))(copy.start)
            pl.when(mine)(local.start)

    def wait(self):
        for k, (mine, copy, waiter, local) in enumerate(self.copies):
            from_row, from_col = (self.col, k) if self.inward else (k, self.row)
            me = (from_row == self.row) & (from_col == self.col)
            pl.when(jnp.logical_not(me))(waiter.wait_recv)
            pl.when(jnp.logical_not(mine))(copy.wait_send)
            pl.when(mine)(local.wait)


def half_of(kind, ref, c, h):
    if kind == "tall":
        count = ref.shape[0] // 16
        return ref.at[pl.ds(pl.multiple_of((2 * c + h) * count, count), count)]
    count, width = ref.shape[0] // 2, ref.shape[1] // 8
    return ref.at[
        pl.ds(pl.multiple_of(h * count, count), count), pl.ds(pl.multiple_of(c * width, width), width)
    ]


def half_shard(ref, h):
    count = ref.shape[0] // 2
    return ref.at[pl.ds(pl.multiple_of(h * count, count), count)]


def mean_rate(values):
    return lax.rsqrt(jnp.mean(values * values, axis=-1, keepdims=True) + EPS)


def call(kernel, name, number, outs, ins, in_specs, out_specs, scratch):
    return pl.pallas_call(
        kernel,
        name=name,
        out_shape=outs,
        in_specs=in_specs,
        out_specs=out_specs,
        scratch_shapes=scratch,
        compiler_params=pltpu.CompilerParams(
            collective_id=number, has_side_effects=True, vmem_limit_bytes=62 * 2**20
        ),
    )(*ins)


def struct(shape, kind):
    return jax.ShapeDtypeStruct(shape, kind)


def dot(left, right):
    return jnp.dot(left, right, preferred_element_type=F32)


def dot_flipped(left, right):
    return lax.dot_general(left, right, (((1,), (1,)), ((), ())), preferred_element_type=F32)


def span(k, count):
    return pl.ds(pl.multiple_of(k * count, count), count)


def near_row(row, dx, dy):
    return (row // 4 + dy) % 2 * 4 + (row % 4 + dx) % 4


class Scatter:
    def __init__(self, part, total, from_y, from_x, last_y, last_x, stage, sent, arrived):
        dp, row, col = here()
        self.row, self.part, self.total = row, part, total
        self.from_y, self.from_x, self.last_y, self.last_x, self.stage = from_y, from_x, last_y, last_x, stage
        self.count, self.half = total.shape[0], total.shape[1] // 2
        number = iter(range(14))

        def copy(source, target, dx, dy):
            i = next(number)
            return remote(source, target, sent.at[i], arrived.at[i], row=near_row(row, dx, dy))

        self.y_first = {dx: copy(self.block(dx, 1, 1), from_y.at[dx], 0, 1) for dx in (1, 3, 2, 0)}
        self.x_first = {
            (dx, dy): copy(self.block(dx, dy, 0), from_x.at[dy, dx - 1], dx, 0)
            for dy in (1, 0)
            for dx in (1, 3, 2)
        }
        self.x_last = {dx: copy(stage.at[dx], last_x.at[dx - 1], dx, 0) for dx in (1, 3, 2)}
        self.y_last = copy(stage.at[0], last_y, 0, 1)

    def block(self, dx, dy, side):
        return self.part.at[
            span(near_row(self.row, dx, dy), self.count), pl.ds(side * self.half, self.half)
        ]

    def start_right(self):
        for copy in self.y_first.values():
            copy.start()

    def start_left(self):
        for copy in self.x_first.values():
            copy.start()

    def chunks(self, body):
        @pl.loop(0, self.count // 16)
        def _(i):
            body(span(i, 16))

    def middle(self):
        for dx in (1, 3, 2):
            self.y_first[dx].wait_recv()
            own = self.block(dx, 0, 1)

            def add(at):
                self.stage[dx, at] = (own[at].astype(F32) + self.from_y[dx, at].astype(F32)).astype(BF16)

            self.chunks(add)
            self.x_last[dx].start()
        for dx in (1, 3, 2):
            self.x_first[dx, 1].wait_recv()
        other = self.block(0, 1, 0)

        def add(at):
            total = other[at].astype(F32)
            for k in range(3):
                total = total + self.from_x[1, k, at].astype(F32)
            self.stage[0, at] = total.astype(BF16)

        self.chunks(add)
        self.y_last.start()

    def end(self):
        self.y_first[0].wait_recv()
        for dx in (1, 3, 2):
            self.x_first[dx, 0].wait_recv()
            self.x_last[dx].wait_recv()
        self.y_last.wait_recv()
        left, right = self.block(0, 0, 0), self.block(0, 0, 1)

        def add(at):
            total = left[at].astype(F32) + self.last_y[at].astype(F32)
            for k in range(3):
                total = total + self.from_x[0, k, at].astype(F32)
            self.total[at, : self.half] = total
            total = right[at].astype(F32) + self.from_y[0, at].astype(F32)
            for k in range(3):
                total = total + self.last_x[k, at].astype(F32)
            self.total[at, self.half :] = total

        self.chunks(add)

    def finish(self):
        for copies in (self.y_first, self.x_first, self.x_last):
            for copy in copies.values():
                copy.wait_send()
        self.y_last.wait_send()


def scatter_scratch(share, width):
    half = width // 2
    return [
        pltpu.VMEM((share, width), F32),
        pltpu.VMEM((4, share, half), BF16),
        pltpu.VMEM((2, 3, share, half), BF16),
        pltpu.VMEM((share, half), BF16),
        pltpu.VMEM((3, share, half), BF16),
        pltpu.VMEM((4, share, half), BF16),
        DMA((14,)),
        DMA((14,)),
    ]


class Gather:
    def __init__(self, whole, share, left, sent, arrived):
        dp, row, col = here()
        self.row = row
        number = iter(range(19))
        sides = (pl.ds(0, left), pl.ds(left, whole.shape[1] - left))
        right = left < whole.shape[1]

        def copy(fx, fy, side, dx, dy, start=0, count=share):
            i = next(number)
            k = near_row(row, fx, fy)
            ref = whole.at[pl.ds(pl.multiple_of(k * share + start, count), count), sides[side]]
            return remote(ref, ref, sent.at[i], arrived.at[i], row=near_row(row, dx, dy))

        part = share // 2
        self.y_left = copy(0, 0, 0, 0, 1)
        self.x_left = [copy(0, 0, 0, dx, 0) for dx in (1, 3)]
        self.x_other = [copy(0, 1, 0, dx, 0) for dx in (1, 3)]
        steps = list(enumerate((1, 3)))
        self.on_left = [copy(4 - dx, 0, 0, dx, 0, i * part, part) for i, dx in steps]
        self.on_other = [copy(4 - dx, 1, 0, dx, 0, i * part, part) for i, dx in steps]
        self.y_right, self.x_right, self.on_right, self.y_near, self.y_far = [], [], [], [], []
        if right:
            self.y_right = [copy(0, 0, 1, 0, 1)]
            self.x_right = [copy(0, 0, 1, dx, 0) for dx in (1, 3)]
            self.on_right = [copy(4 - dx, 0, 1, dx, 0, i * part, part) for i, dx in steps]
            self.y_near = [copy(4 - dx, 0, 1, 0, 1) for dx in (1, 3)]
            self.y_far = [copy(2, 0, 1, 0, 1, i * part, part) for i in range(2)]

    def start(self):
        for copy in (self.y_left, *self.x_right, *self.y_right, *self.x_left):
            copy.start()

    def relay(self):
        self.y_left.wait_recv()
        for copy in self.x_other:
            copy.start()
        for i, came in enumerate(self.x_right):
            came.wait_recv()
            self.on_right[i].start()
            self.y_near[i].start()

    def relay_again(self):
        for i in range(2):
            self.x_left[i].wait_recv()
            self.on_left[i].start()
        for i, came in enumerate(self.on_right):
            came.wait_recv()
            self.y_far[i].start()
        for i in range(2):
            self.x_other[i].wait_recv()
            self.on_other[i].start()

    def wait(self):
        for copy in (*self.y_right, *self.on_left, *self.on_other, *self.y_near, *self.y_far):
            copy.wait_recv()
        for copy in (self.y_left, *self.x_left, *self.x_other, *self.on_left, *self.on_other, *self.y_right,
                     *self.x_right, *self.on_right, *self.y_near, *self.y_far):
            copy.wait_send()


def gather_scratch():
    return [DMA((19,)), DMA((19,))]


def cols(ref, k, width):
    return ref.at[:, pl.ds(pl.multiple_of(k * width, width), width)]


def rows_of(ref, k, count):
    return ref.at[pl.ds(pl.multiple_of(k * count, count), count)]


def back_of(grad, values, gain):
    rate = mean_rate(values)
    hat = values * rate
    grad_hat = grad * gain
    dots = jnp.mean(grad_hat * hat, axis=-1, keepdims=True)
    return hat, rate * (grad_hat - hat * dots)


class GradSum:
    def __init__(self, kind, part, out, between, far, near, sent, arrived):
        dp, _, col = here()
        self.kind, self.part, self.col = kind, part, col
        self.between, self.far, self.near = between, far, near
        self.rows, self.width = near.shape[1], near.shape[2]
        number = iter(range(10))

        def copy(source, target, **where):
            i = next(number)
            return remote(source, target, sent.at[i], arrived.at[i], **where)

        self.steps = (1, 3)
        self.on = [
            [
                copy(self.piece(self.z_block(2, k), i), between.at[i, k], col=z_peer(col, d))
                for k in range(2)
            ]
            for i, d in enumerate(self.steps)
        ]
        self.zs = [
            [copy(self.block(self.z_block(d, k)), far.at[i, k], col=z_peer(col, d)) for k in range(2)]
            for i, d in enumerate(self.steps)
        ]
        self.ys = copy(near.at[0], near.at[1], col=y_peer(col))
        self.last = copy(near.at[0], half_shard(out, dp), dp=1 - dp)
        self.keep = pltpu.make_async_copy(near.at[0], half_shard(out, dp), sent.at[10])

    def z_block(self, d, k):
        return z_peer(self.col, d) // 2 * 2 + k

    def block(self, c):
        if self.kind == "tall":
            return self.part.at[span(c, self.rows)]
        return self.part.at[:, span(c, self.width)]

    def piece(self, c, i):
        return self.block(c).at[pl.ds(i * (self.rows // 2), self.rows // 2)]

    def each(self, rows, body):
        count = min(rows, 32768 // self.width // 16 * 16)

        @pl.loop(0, rows // count)
        def _(i):
            body(span(i, count))

    def start(self):
        for pair in self.on:
            for copy in pair:
                copy.start()

    def over_z(self):
        for i, d in enumerate(self.steps):
            for k in range(2):
                self.on[i][k].wait_recv()
                own = self.piece(self.z_block(d, k), i)

                def add(at):
                    own[at] = (own[at].astype(F32) + self.between[i, k, at].astype(F32)).astype(BF16)

                self.each(self.rows // 2, add)
                self.zs[i][k].start()

    def over_y(self):
        for pair in self.zs:
            for copy in pair:
                copy.wait_recv()
        yl = self.col % 2
        keep, give = self.block(self.col), self.block(y_peer(self.col))

        def total(at, ref, k):
            return (
                ref[at].astype(F32) + self.far[0, k, at].astype(F32) + self.far[1, k, at].astype(F32)
            ).astype(BF16)

        def add(at):
            self.near[0, at] = total(at, give, 1 - yl)

        self.each(self.rows, add)
        self.ys.start()

        def add(at):
            keep[at] = total(at, keep, yl)

        self.each(self.rows, add)
        for pair in (*self.zs, *self.on):
            for copy in pair:
                copy.wait_send()

    def end(self):
        self.ys.wait()
        keep = self.block(self.col)

        def add(at):
            self.near[0, at] = (keep[at].astype(F32) + self.near[1, at].astype(F32)).astype(BF16)

        self.each(self.rows, add)
        self.last.start()
        self.keep.start()

    def wait(self):
        self.last.wait()
        self.keep.wait()


def grad_sum_scratch(shape):
    rows, width = shape[0] // 2, shape[1]
    return [
        pltpu.VMEM((2, 2, rows // 2, width), BF16),
        pltpu.VMEM((2, 2, rows, width), BF16),
        pltpu.VMEM((2, rows, width), BF16),
        DMA((11,)),
        DMA((10,)),
    ]


class Bring:
    def __init__(self, kind, shard, whole, sent, arrived):
        dp, _, col = here()
        rows, width = shard.shape
        near = y_peer(col)
        number = iter(range(20))

        def block(c, s=None):
            count, at = (rows // 2, dp) if s is None else (rows // 4, 2 * dp + s)
            if kind == "tall":
                return whole.at[span((2 if s is None else 4) * c + at, count)]
            return whole.at[span(at, count), span(c, width)]

        def copy(source, target, **where):
            i = next(number)
            return remote(source, target, sent.at[i], arrived.at[i], **where)

        mine = half_shard(shard, dp)
        place = whole.at[span(col, rows)] if kind == "tall" else whole.at[:, span(col, width)]
        self.local = pltpu.make_async_copy(shard, place, sent.at[20])
        self.y_own = copy(mine, block(col), col=near)
        self.z_own = [copy(mine, block(col), col=z_peer(col, d)) for d in (1, 3)]
        self.z_near = [copy(block(near), block(near), col=z_peer(col, d)) for d in (1, 3)]
        self.on, self.on_near, self.a_own, self.a_near = [], [], [], []
        self.a_far, self.a_far_near = [], []
        for i, d in enumerate((1, 3)):
            came, two = z_source(col, d), z_peer(col, 2)
            self.on.append(copy(block(came, i), block(came, i), col=z_peer(col, d)))
            self.on_near.append(copy(block(y_peer(came), i), block(y_peer(came), i), col=z_peer(col, d)))
            self.a_own.append(copy(block(came), block(came), dp=1 - dp))
            self.a_near.append(copy(block(y_peer(came)), block(y_peer(came)), dp=1 - dp))
            self.a_far.append(copy(block(two, i), block(two, i), dp=1 - dp))
            self.a_far_near.append(copy(block(y_peer(two), i), block(y_peer(two), i), dp=1 - dp))
        self.a_y = copy(block(near), block(near), dp=1 - dp)

    def start_y(self):
        self.y_own.start()

    def start_z(self):
        for copy in (*self.z_own, self.local):
            copy.start()

    def relay(self):
        self.y_own.wait_recv()
        for copy in (*self.z_near, self.a_y):
            copy.start()

    def relay_own(self):
        for i in range(2):
            self.z_own[i].wait_recv()
            self.on[i].start()
            self.a_own[i].start()

    def relay_near(self):
        for i in range(2):
            self.z_near[i].wait_recv()
            self.on_near[i].start()
            self.a_near[i].start()

    def hand_over(self):
        for i in range(2):
            self.on[i].wait_recv()
            self.a_far[i].start()
        for i in range(2):
            self.on_near[i].wait_recv()
            self.a_far_near[i].start()

    def wait(self):
        for copy in (self.a_y, *self.a_own, *self.a_near, *self.a_far, *self.a_far_near):
            copy.wait()
        for copy in (self.y_own, *self.z_own, *self.z_near, *self.on, *self.on_near):
            copy.wait_send()
        self.local.wait()


def bring_scratch():
    return [DMA((21,)), DMA((20,))]


class SpreadIn:
    def __init__(self, source, target, sent, arrived):
        dp, row, col = here()
        self.row, self.col = row, col
        self.copies, self.waits = [], []
        for k in range(8):
            out = remote(source(k), target(k, col), sent.at[k], arrived.at[col], row=k, col=row)
            came = remote(source(k), target(row, k), sent.at[k], arrived.at[k], row=k, col=row)
            local = pltpu.make_async_copy(source(k), target(k, col), sent.at[k])
            self.copies.append(((row == k) & (row == col), out, local))
            self.waits.append(((row == col) & (col == k), came))

    def start(self):
        for mine, out, local in self.copies:
            pl.when(jnp.logical_not(mine))(out.start)
            pl.when(mine)(local.start)

    def wait(self):
        for mine, came in self.waits:
            pl.when(jnp.logical_not(mine))(came.wait_recv)
        for mine, out, local in self.copies:
            pl.when(jnp.logical_not(mine))(out.wait_send)
            pl.when(mine)(local.wait)


class TokenSums:
    def __init__(self, stats, mine, came, sent, arrived):
        dp, row, col = here()
        self.stats, self.mine, self.came = stats, mine, came
        self.copies = [
            remote(mine, came.at[d - 1], sent.at[d - 1], arrived.at[d - 1], row=row_peer(row, d))
            for d in range(1, 8)
        ]

    def put(self, at, one, two):
        lane = lax.broadcasted_iota(jnp.int32, (one.shape[0], 128), 1)
        self.stats[at] = jnp.where(lane == 0, one, jnp.where(lane == 1, two, 0.0))

    def start(self):
        self.mine[...] = self.stats[...].T[:8]
        for copy in self.copies:
            copy.start()

    def end(self):
        total = self.mine[...]
        for d, copy in enumerate(self.copies):
            copy.wait_recv()
            total = total + self.came[d]
        self.stats[...] = jnp.concatenate([total] * 16, axis=0).T
        for copy in self.copies:
            copy.wait_send()


def sums_scratch(tokens):
    return [pltpu.VMEM((8, tokens), F32), pltpu.VMEM((7, 8, tokens), F32), DMA((7,)), DMA((7,))]


def turn(values, cosine, sine):
    heads = [values[:, i : i + HD] for i in range(0, values.shape[1], HD)]
    return jnp.concatenate([h * cosine + pltpu.roll(h, HD // 2, 1) * sine for h in heads], axis=1)


QUERY_BLOCK = 128


def key_span(b):
    start = max(0, b * QUERY_BLOCK - WINDOW)
    return start, (b + 1) * QUERY_BLOCK - start


def attend_kernel(
    x, g, heads_in, merge_in, expand_in, reduce_in, cosine, sine, docs, doc_row, gain_query, gain_key, gain_merge,
    xs_out, share_out, heads_out, merge_out, expand_out, reduce_out, raw_out, qkv_out, probs_out, mix_out, rates_out,
    merged, residual, rows_out,
    xs, heads32, merge32, expand32, reduce32, heads16, merge16, expand16, reduce16, heads, merge, raw, qkv, probs, mix,
    rates, part, rows, load, put, xsent, xcame, gsent, gcame, asent, acame, bsent, bcame, *refs,
):
    dp, row, col = here()
    share, width = merged.shape
    tokens = xs.shape[0]
    head_width = mix.shape[1]
    own = span(row, share)
    loads = [
        pltpu.make_async_copy(source, target, load.at[i])
        for i, (source, target) in enumerate(
            ((heads_in, heads32), (merge_in, merge32), (reduce_in, reduce32), (expand_in, expand32))
        )
    ]
    for copy in loads:
        copy.start()
    spread_x = SpreadIn(
        lambda k: rows_of(x, k, share), lambda k, c: xs.at[span(k, share), span(c, 256)], xsent, xcame
    )
    spread_g = SpreadIn(
        lambda k: rows_of(g, k, share), lambda k, c: share_out.at[:, span(c, 256)], gsent, gcame
    )
    gather_x = Gather(xs, share, width, asent, acame)
    gather = Gather(rows, share, width // 2, bsent, bcame)
    scatter = Scatter(part, *refs[:8])
    sums = TokenSums(rates, *refs[8:12])
    bring_heads = Bring("tall", heads16, heads, *refs[12:14])
    bring_merge = Bring("wide", merge16, merge, *refs[14:16])
    bring_reduce = Bring("wide", reduce16, reduce_out, *refs[16:18])
    bring_expand = Bring("tall", expand16, expand_out, *refs[18:20])
    puts = [
        pltpu.make_async_copy(source, target, put.at[i])
        for i, (source, target) in enumerate(
            ((xs, xs_out), (heads, heads_out), (merge, merge_out), (raw, raw_out), (qkv, qkv_out),
             (probs, probs_out), (mix, mix_out), (rates, rates_out), (rows, rows_out))
        )
    ]

    def narrow(source, target):
        @pl.loop(0, source.shape[0] // 16)
        def _(i):
            at = span(i, 16)
            target[at] = source[at].astype(BF16)

    meet(rows=True, weights=True, core=True, spread_in=True)
    spread_x.start()
    loads[0].wait()
    narrow(heads32, heads16)
    bring_heads.start_y()
    bring_heads.start_z()
    loads[1].wait()
    narrow(merge32, merge16)
    bring_merge.start_y()
    bring_merge.start_z()
    loads[2].wait()
    narrow(reduce32, reduce16)
    loads[3].wait()
    narrow(expand32, expand16)
    spread_x.wait()
    gather_x.start()
    bring_heads.relay()
    bring_heads.relay_own()
    gather_x.relay()
    bring_expand.start_y()
    bring_reduce.start_y()
    bring_heads.relay_near()
    bring_merge.relay()
    gather_x.relay_again()
    bring_heads.hand_over()
    bring_expand.start_z()
    bring_reduce.start_z()
    gather_x.wait()
    bring_heads.wait()
    puts[0].start()
    puts[1].start()

    for i in range(2):
        raw[:, i * head_width : (i + 1) * head_width] = dot(
            xs[...], heads[:, i * head_width : (i + 1) * head_width]
        )

    @pl.loop(0, tokens // 64)
    def _(i):
        at = span(i, 64)
        squares = raw[at] * raw[at]
        sums.put(
            at,
            jnp.sum(squares[:, :head_width], axis=1, keepdims=True),
            jnp.sum(squares[:, head_width:], axis=1, keepdims=True),
        )

    sums.start()
    qkv[:, 2 * head_width :] = dot(xs[...], heads[:, 2 * head_width :]).astype(BF16)
    bring_merge.relay_own()
    bring_merge.relay_near()
    sums.end()
    spread_g.start()

    @pl.loop(0, tokens // 64)
    def _(i):
        at = span(i, 64)
        rate = lax.rsqrt(rates[at] * (1.0 / width) + EPS)
        rates[at] = rate
        for j, gain in enumerate((gain_query, gain_key)):
            some = slice(j * head_width, (j + 1) * head_width)
            hat = raw[at, some] * rate[:, j : j + 1]
            qkv[at, some] = turn(hat * gain[...], cosine[at], sine[at]).astype(BF16)

    puts[3].start()
    puts[4].start()
    puts[7].start()
    for b in range(tokens // QUERY_BLOCK):
        start, count = key_span(b)
        query_at = pl.ds(b * QUERY_BLOCK, QUERY_BLOCK)
        key_at = pl.ds(start, count)
        there = lax.broadcasted_iota(jnp.int32, (QUERY_BLOCK, count), 0) + (b * QUERY_BLOCK - start)
        distance = there - lax.broadcasted_iota(jnp.int32, (QUERY_BLOCK, count), 1)
        doc = docs[query_at, 0:1]
        allowed = (doc == doc_row[0:1, start : start + count]) & (distance >= 0) & (distance < WINDOW)
        live = (doc < 5.0).astype(F32)
        for h in range(head_width // HD):
            query, key, value = (
                slice(i * head_width + h * HD, i * head_width + (h + 1) * HD) for i in range(3)
            )
            scores = dot_flipped(qkv[query_at, query], qkv[key_at, key]) * HD**-0.5
            scores = jnp.where(allowed, scores, -1e30)
            weights = jnp.exp(scores - jnp.max(scores, axis=1, keepdims=True))
            shares = (weights / jnp.sum(weights, axis=1, keepdims=True)).astype(BF16)
            probs[h, b, :, :count] = shares
            if count < probs.shape[3]:
                probs[h, b, :, count:] = jnp.zeros((QUERY_BLOCK, probs.shape[3] - count), BF16)
            mix[query_at, h * HD : (h + 1) * HD] = (dot(shares, qkv[key_at, value]) * live).astype(BF16)

    puts[5].start()
    puts[6].start()
    bring_expand.relay()
    bring_reduce.relay()
    bring_merge.hand_over()
    bring_merge.wait()
    puts[2].start()

    def merge_part(j):
        at = span(j, 256)
        part[:, at] = dot(mix[...], merge[:, at]).astype(BF16)

    n = width // 512
    pl.loop(n, 2 * n)(merge_part)
    scatter.start_right()
    pl.loop(0, n)(merge_part)
    scatter.start_left()
    bring_expand.relay_own()
    bring_reduce.relay_own()
    scatter.middle()
    bring_expand.relay_near()
    bring_reduce.relay_near()
    scatter.end()

    @pl.loop(0, share // 16)
    def _(i):
        at = span(i, 16)
        total = scatter.total[at]
        merged[at] = total
        mine = pl.ds(pl.multiple_of(row * share + i * 16, 16), 16)
        result = xs[mine, :].astype(F32) + total * mean_rate(total) * gain_merge[...]
        residual[at] = result
        rows[mine, :] = result.astype(BF16)

    gather.start()
    gather.relay()
    bring_expand.hand_over()
    gather.relay_again()
    bring_reduce.hand_over()
    gather.wait()
    puts[8].start()
    scatter.finish()
    spread_g.wait()
    bring_expand.wait()
    bring_reduce.wait()
    for copy in puts:
        copy.wait()


def rest_kernel(
    rows_in, expand_in, reduce_in, heads_in, merge_in, xs_in, raw_in, qkv_in, probs_in, mix_in, rates_in,
    residual, g, merged, cosine, sine, docs, gain_query, gain_key, gain_merge, gain_reduce,
    out, input_grad, gains_grad, heads_grad, merge_grad, expand_grad, reduce_grad,
    rows, turned, expand, reduce, heads, merge, gate, up, act, act_turned, part, back, hidden, probs, mix, mix_turned,
    rates, stats, grad_mix, done, final, grad_resid, sums, grad_gate,
    gains, gain_row, gain_col, gain_core, gain_sum, act_other, turned_other, hidden_other, back_other, mix_other,
    joined_other, free, load, late, osent, ocame, isent, icame, nsent, ncame, xsent, xcame,
    g1sent, g1came, g2sent, g2came, *refs,
):
    dp, row, col = here()
    share, width = residual.shape
    tokens, units = act.shape
    head_width = mix.shape[1]
    tiles = units // 256
    n = width // 512
    scatter = [Scatter(part, *refs[:6], *refs[6 + 2 * i : 8 + 2 * i]) for i in range(3)]
    token_sums = TokenSums(stats, *refs[12:16])
    half_units, half_width, half_heads = units // 2, width // 2, head_width // 2
    reduce_part, merge_part = reduce.at[pl.ds(0, half_units)], merge.at[pl.ds(0, half_heads)]
    expand_part, heads_part = expand.at[pl.ds(0, half_width)], heads.at[pl.ds(0, half_width)]
    reduce_sum = GradSum("wide", reduce_part, reduce_grad, *refs[16:21])
    expand_sum = GradSum("tall", expand_part, expand_grad, *refs[21:26])
    merge_sum = GradSum("wide", merge_part, merge_grad, *refs[26:31])
    heads_sum = GradSum("tall", heads_part, heads_grad, *refs[31:36])
    gather = Gather(back, share, width // 2, g1sent, g1came)
    last_gather = Gather(back, share, width // 2, g2sent, g2came)
    spread = Spread(False, lambda k: cols(done, k, 256), lambda k: rows_of(out, k, 64), osent, ocame)
    spread_grad = Spread(False, lambda k: cols(final, k, 256), lambda k: rows_of(input_grad, k, 64), isent, icame)
    row_gains = [
        remote(gains, gain_row.at[row], nsent.at[d - 1], ncame.at[d - 1], row=row_peer(row, d))
        for d in range(1, 8)
    ]
    col_gains = [
        remote(gain_sum.at[0], gain_col.at[col], nsent.at[6 + d], ncame.at[6 + d], col=(col + d) % 8)
        for d in range(1, 8)
    ]
    core_gains = remote(gain_sum.at[1], gain_core, nsent.at[14], ncame.at[14], dp=1 - dp)

    raw, qkv, new_rows = up.at[:, : 2 * head_width], act.at[:, : 3 * head_width], back
    heads_change = gate.at[:, : 3 * head_width]
    joined = hidden.at[:, : 3 * head_width]
    get_rows = pltpu.make_async_copy(rows_in, rows, load.at[0])
    get_reduce = pltpu.make_async_copy(reduce_in, reduce, load.at[1])

    def get_expand(j):
        at = span(j, 256)
        return pltpu.make_async_copy(expand_in.at[:, at], expand.at[:, at], load.at[2 + j])

    early = [
        pltpu.make_async_copy(source, target, late.at[i])
        for i, (source, target) in enumerate(
            ((heads_in, heads), (merge_in, merge), (probs_in, probs), (mix_in, mix), (rates_in, rates))
        )
    ]
    get_raw = pltpu.make_async_copy(raw_in, raw, late.at[5])
    get_qkv = pltpu.make_async_copy(qkv_in, qkv, late.at[6])
    get_xs = pltpu.make_async_copy(xs_in, rows, late.at[7])

    def hand(i, source, target):
        return remote(source, target, xsent.at[i], xcame.at[i], dp=1 - dp)

    hand_act = hand(0, act_turned.at[span(1 - dp, half_units)], act_other)
    hand_rows = hand(1, turned.at[span(1 - dp, half_width)], turned_other)
    hand_back = hand(2, back, back_other)
    hand_hidden = hand(3, hidden, hidden_other)
    hand_mix = hand(4, mix_turned.at[span(1 - dp, half_heads)], mix_other)
    hand_new = hand(5, back, back_other)
    hand_xs = hand(6, turned.at[span(1 - dp, half_width)], turned_other)
    hand_joined = hand(7, joined, joined_other)

    def turn_rows(j):
        values = rows[:, span(j, 256)].T
        turned[span(j, 128), :] = values[:128]
        turned[span(2 * tiles + j, 128), :] = values[128:]

    def two(target, at, wide, own, own_at, right, other, right_other):
        target[at, wide] = (
            dot(own[own_at, :], right[:, wide]) + dot(other[at, :], right_other[:, wide])
        ).astype(BF16)

    get_rows.start()
    for j in range(tiles):
        get_expand(j).start()
        get_expand(tiles + j).start()
    get_reduce.start()
    meet(rows=True, cols=True, core=True, spread_out=True)
    get_rows.wait()

    @pl.loop(0, tiles)
    def _(j):
        get_expand(j).wait()
        get_expand(tiles + j).wait()
        at = span(j, 256)
        gate[:, at] = dot(rows[...], expand[:, at])
        up[:, at] = dot(rows[...], expand[:, span(tiles + j, 256)])

        @pl.loop(0, tokens // 64)
        def _(i):
            some = span(i, 64)
            x = gate[some, at]
            act[some, at] = (x * jax.nn.sigmoid(x) * up[some, at]).astype(BF16)

    get_reduce.wait()

    def reduced(j):
        at = span(j, 256)
        part[:, at] = dot(act[...], reduce[:, at]).astype(BF16)

    pl.loop(n, 2 * n)(reduced)
    scatter[0].start_right()
    pl.loop(0, n)(reduced)
    scatter[0].start_left()

    @pl.loop(0, tiles)
    def _(j):
        at = span(j, 256)
        act_turned[at, :] = act[:, at].T

    hand_act.start()
    for copy in early:
        copy.start()
    get_qkv.start()

    scatter[0].middle()
    scatter[0].end()
    sums[...] = jnp.zeros_like(sums)

    @pl.loop(0, share // 16)
    def _(i):
        at = span(i, 16)
        grad = g[at].astype(F32)
        hat, change = back_of(grad, scatter[0].total[at], gain_reduce[...])
        back[pl.ds(pl.multiple_of(row * share + i * 16, 16), 16), :] = change.astype(BF16)
        done[at] = (residual[at] + hat * gain_reduce[...]).astype(BF16)
        product = grad * hat
        sums[...] += product[:8] + product[8:]

    gather.start()
    gains[...] = jnp.zeros_like(gains)
    gains[3:4] = jnp.sum(sums[...], axis=0, keepdims=True)
    scatter[0].finish()
    gather.relay()

    pl.loop(0, 2 * tiles)(turn_rows)
    hand_rows.start()
    get_xs.start()
    gather.relay_again()
    gather.wait()
    hand_back.start()
    spread.start()

    @pl.loop(0, tiles)
    def _(j):
        at, up_at = span(j, 256), span(tiles + j, 256)
        grad_gate[...] = dot_flipped(back[...], reduce[at, :])

        @pl.loop(0, tokens // 64)
        def _(i):
            some = span(i, 64)
            x, change = gate[some, at], grad_gate[some]
            s = jax.nn.sigmoid(x)
            hidden[some, at] = (change * up[some, at] * s * (1.0 + x * (1.0 - s))).astype(BF16)
            hidden[some, up_at] = (change * (x * s)).astype(BF16)

    hand_hidden.start()
    get_raw.start()

    def branch(j):
        at = span(j, 256)
        part[:, at] = dot_flipped(hidden[...], expand[at, :]).astype(BF16)

    pl.loop(n, 2 * n)(branch)
    scatter[1].start_right()
    pl.loop(0, n)(branch)
    scatter[1].start_left()

    hand_act.wait()
    hand_back.wait()
    halves = [pl.ds(side * (width // 2), width // 2) for side in range(2)]

    @pl.loop(0, tiles // 2)
    def _(j):
        for wide in halves:
            two(reduce, span(j, 256), wide, act_turned, span(dp * (tiles // 2) + j, 256), back, act_other, back_other)

    pl.semaphore_signal(free.at[0], inc=1, device_id={"dp": 1 - dp}, device_id_type=MESH)
    reduce_sum.start()
    scatter[1].middle()
    hand_rows.wait()
    hand_hidden.wait()

    @pl.loop(0, tiles)
    def _(j):
        for wide in halves:
            two(expand, span(j, 256), wide, turned, span(dp * tiles + j, 256), hidden, turned_other, hidden_other)

    pl.semaphore_signal(free.at[1], inc=1, device_id={"dp": 1 - dp}, device_id_type=MESH)
    expand_sum.start()
    reduce_sum.over_z()
    scatter[1].end()
    sums[...] = jnp.zeros_like(sums)

    @pl.loop(0, share // 16)
    def _(i):
        at = span(i, 16)
        grad = g[at].astype(F32) + scatter[1].total[at]
        grad_resid[at] = grad
        hat, change = back_of(grad, merged[at], gain_merge[...])
        new_rows[pl.ds(pl.multiple_of(row * share + i * 16, 16), 16), :] = change.astype(BF16)
        product = grad * hat
        sums[...] += product[:8] + product[8:]

    last_gather.start()
    gains[2:3] = jnp.sum(sums[...], axis=0, keepdims=True)
    get_xs.wait()
    pl.loop(0, 2 * tiles)(turn_rows)
    pl.semaphore_wait(free.at[1], 1)
    hand_xs.start()
    last_gather.relay()
    last_gather.relay_again()
    for copy in early:
        copy.wait()
    get_raw.wait()
    get_qkv.wait()
    mix_turned[...] = mix[...].T
    hand_mix.start()
    expand_sum.over_z()
    scatter[1].finish()
    last_gather.wait()
    pl.semaphore_wait(free.at[0], 1)
    hand_new.start()

    live = (docs[:, 0:1] < 5.0).astype(F32)
    grad_mix[...] = (dot_flipped(new_rows[...], merge[...]) * live).astype(BF16)
    heads_change[:, head_width:] = jnp.zeros((tokens, 2 * head_width), F32)
    for b in range(tokens // QUERY_BLOCK):
        start, count = key_span(b)
        query_at = pl.ds(b * QUERY_BLOCK, QUERY_BLOCK)
        key_at = pl.ds(start, count)
        for h in range(head_width // HD):
            query, key, value = (
                slice(i * head_width + h * HD, i * head_width + (h + 1) * HD) for i in range(3)
            )
            shares = probs[h, b, :, :count]
            change = grad_mix[query_at, h * HD : (h + 1) * HD]
            grad_shares = dot_flipped(change, qkv[key_at, value])
            weighted = shares.astype(F32) * grad_shares
            center = jnp.sum(weighted, axis=1, keepdims=True)
            grad_scores = (weighted - shares.astype(F32) * center).astype(BF16)
            heads_change[query_at, query] = dot(grad_scores, qkv[key_at, key]) * HD**-0.5
            heads_change[key_at, key] += dot(grad_scores.T, qkv[query_at, query]) * HD**-0.5
            heads_change[key_at, value] += dot(shares.T, change)

    reduce_sum.over_y()
    sums[...] = jnp.zeros_like(sums)

    @pl.loop(0, tokens // 64)
    def _(i):
        at = span(i, 64)
        dots = []
        for j, gain in enumerate((gain_query, gain_key)):
            some = slice(j * head_width, (j + 1) * head_width)
            change = turn(heads_change[at, some], cosine[at], -sine[at])
            hat = raw[at, some] * rates[at, j : j + 1]
            product = change * hat
            sums[:, some] += jnp.sum(product.reshape(8, 8, head_width), axis=0)
            heads_change[at, some] = change * gain[...]
            dots.append(jnp.sum(product * gain[...], axis=1, keepdims=True))
        token_sums.put(at, *dots)

    token_sums.start()
    gains[0:1, span(row, head_width)] = jnp.sum(sums[:, :head_width], axis=0, keepdims=True)
    gains[1:2, span(row, head_width)] = jnp.sum(sums[:, head_width : 2 * head_width], axis=0, keepdims=True)
    for copy in row_gains:
        copy.start()
    hand_mix.wait()
    hand_new.wait()
    mine = span(dp, half_heads)
    for side in range(4):
        wide = pl.ds(side * (width // 4), width // 4)
        merge[:half_heads, wide] = (
            dot(mix_turned[mine, :], back[:, wide]) + dot(mix_other[...], back_other[:, wide])
        ).astype(BF16)
    merge_sum.start()
    joined[:, 2 * head_width :] = heads_change[:, 2 * head_width :].astype(BF16)
    token_sums.end()

    @pl.loop(0, tokens // 64)
    def _(i):
        at = span(i, 64)
        dots = stats[at] * (1.0 / width)
        for j in range(2):
            some = slice(j * head_width, (j + 1) * head_width)
            rate = rates[at, j : j + 1]
            hat = raw[at, some] * rate
            joined[at, some] = (rate * (heads_change[at, some] - hat * dots[:, j : j + 1])).astype(BF16)

    hand_joined.start()
    for copy in row_gains:
        copy.wait()
    gain_row[row] = gains[...]
    total = gain_row[0]
    for k in range(1, 8):
        total = total + gain_row[k]
    gain_sum[0] = total
    gain_col[col] = total
    for copy in col_gains:
        copy.start()

    def input_part(j):
        at = span(j, 256)
        part[:, at] = dot_flipped(joined[...], heads[at, :]).astype(BF16)

    pl.loop(n, 2 * n)(input_part)
    scatter[2].start_right()
    pl.loop(0, n)(input_part)
    scatter[2].start_left()

    hand_xs.wait()
    hand_joined.wait()
    everything = pl.ds(0, 3 * head_width)

    @pl.loop(0, tiles)
    def _(j):
        two(heads, span(j, 256), everything, turned, span(dp * tiles + j, 256), joined, turned_other, joined_other)

    heads_sum.start()
    expand_sum.over_y()
    merge_sum.over_z()
    reduce_sum.end()
    scatter[2].middle()
    heads_sum.over_z()
    scatter[2].end()
    final[...] = (grad_resid[...] + scatter[2].total[...]).astype(BF16)
    spread_grad.start()
    for copy in col_gains:
        copy.wait()
    total = gain_col[0]
    for k in range(1, 8):
        total = total + gain_col[k]
    gain_sum[1] = total
    core_gains.start()
    merge_sum.over_y()
    heads_sum.over_y()
    expand_sum.end()
    merge_sum.end()
    heads_sum.end()
    core_gains.wait()
    gains_grad[...] = gain_sum[1] + gain_core[...]
    scatter[2].finish()
    spread.wait()
    spread_grad.wait()
    for grad in (reduce_sum, expand_sum, merge_sum, heads_sum):
        grad.wait()


def on_device(
    block_input,
    cotangent,
    doc_lengths,
    heads_weight,
    heads_first,
    heads_second,
    merge_weight,
    merge_first,
    merge_second,
    expand_weight,
    expand_first,
    expand_second,
    reduce_weight,
    reduce_first,
    reduce_second,
    norm_gains,
    gains_first,
    gains_second,
):
    row_at = lax.axis_index("row")
    col_width = block_input.shape[1]
    model_width = col_width * lax.axis_size("col")
    head_width = merge_weight.shape[0]
    unit_width = reduce_weight.shape[0]
    seq_len = block_input.shape[0] * lax.axis_size("row") // lax.axis_size("col")
    share = seq_len // lax.axis_size("row")
    head_count = head_width // HD
    doc_ids, places, live_rows = positions(doc_lengths[0], seq_len)
    gain_query = lax.dynamic_slice_in_dim(norm_gains[0], row_at * head_width, head_width)
    gain_key = lax.dynamic_slice_in_dim(norm_gains[1], row_at * head_width, head_width)
    gain_merge, gain_reduce = norm_gains[2:3], norm_gains[3:4]
    rows_shape = struct((seq_len, model_width), BF16)
    mine_f32 = struct((share, model_width), F32)
    half_dim = HD // 2
    frequency = THETA ** (-2.0 * jnp.arange(half_dim, dtype=F32) / HD)
    angles = places.astype(F32)[:, None] * frequency[None, :]
    cosine, sine = jnp.cos(angles), jnp.sin(angles)
    cosine = jnp.concatenate([cosine, cosine], axis=1)
    sine = jnp.concatenate([-sine, sine], axis=1)
    docs = jnp.broadcast_to(doc_ids.astype(F32)[:, None], (seq_len, 128))
    doc_row = jnp.broadcast_to(doc_ids.astype(F32)[None, :], (8, seq_len))
    blocks = seq_len // QUERY_BLOCK

    (
        input_rows, cot_share, heads_low, merge_low, expand_low, reduce_low, raw, qkv, probs, mixture_low, rates,
        merged, residual, residual_rows,
    ) = call(
        attend_kernel, "attend", 1,
        [
            rows_shape,
            struct((share, model_width), BF16),
            struct((model_width, 3 * head_width), BF16),
            struct((head_width, model_width), BF16),
            struct((model_width, 2 * unit_width), BF16),
            struct((unit_width, model_width), BF16),
            struct((seq_len, 2 * head_width), F32),
            struct((seq_len, 3 * head_width), BF16),
            struct((head_count, blocks, QUERY_BLOCK, WINDOW + QUERY_BLOCK), BF16),
            struct((seq_len, head_width), BF16),
            struct((seq_len, 128), F32),
            mine_f32,
            mine_f32,
            rows_shape,
        ],
        [
            block_input, cotangent, heads_weight, merge_weight, expand_weight, reduce_weight, cosine, sine, docs,
            doc_row, gain_query[None], gain_key[None], gain_merge,
        ],
        [ANY] * 6 + [VMEM] * 7,
        [ANY] * 11 + [VMEM] * 2 + [ANY],
        [
            pltpu.VMEM((seq_len, model_width), BF16),
            pltpu.VMEM(heads_weight.shape, F32),
            pltpu.VMEM(merge_weight.shape, F32),
            pltpu.VMEM(expand_weight.shape, F32),
            pltpu.VMEM(reduce_weight.shape, F32),
            pltpu.VMEM(heads_weight.shape, BF16),
            pltpu.VMEM(merge_weight.shape, BF16),
            pltpu.VMEM(expand_weight.shape, BF16),
            pltpu.VMEM(reduce_weight.shape, BF16),
            pltpu.VMEM((model_width, 3 * head_width), BF16),
            pltpu.VMEM((head_width, model_width), BF16),
            pltpu.VMEM((seq_len, 2 * head_width), F32),
            pltpu.VMEM((seq_len, 3 * head_width), BF16),
            pltpu.VMEM((head_count, blocks, QUERY_BLOCK, WINDOW + QUERY_BLOCK), BF16),
            pltpu.VMEM((seq_len, head_width), BF16),
            pltpu.VMEM((seq_len, 128), F32),
            pltpu.VMEM((seq_len, model_width), BF16),
            pltpu.VMEM((seq_len, model_width), BF16),
            DMA((4,)), DMA((9,)), DMA((8,)), DMA((8,)), DMA((8,)), DMA((8,)),
        ]
        + gather_scratch() + gather_scratch()
        + scatter_scratch(share, model_width) + sums_scratch(seq_len)
        + bring_scratch() + bring_scratch() + bring_scratch() + bring_scratch(),
    )
    gain_shape = (4, model_width)
    block_output, input_grad, gains_grad, heads_grad, merge_grad, expand_grad, reduce_grad = call(
        rest_kernel, "rest", 2,
        [
            struct(block_input.shape, BF16),
            struct(block_input.shape, BF16),
            struct(gain_shape, F32),
            struct(heads_weight.shape, BF16),
            struct(merge_weight.shape, BF16),
            struct(expand_weight.shape, BF16),
            struct(reduce_weight.shape, BF16),
        ],
        [
            residual_rows, expand_low, reduce_low, heads_low, merge_low, input_rows, raw, qkv, probs, mixture_low, rates,
            residual, cot_share, merged, cosine, sine, docs, gain_query[None], gain_key[None], gain_merge, gain_reduce,
        ],
        [ANY] * 11 + [VMEM] * 10,
        [ANY] * 2 + [VMEM] + [ANY] * 4,
        [
            pltpu.VMEM((seq_len, model_width), BF16),
            pltpu.VMEM((model_width, seq_len), BF16),
            pltpu.VMEM((model_width, 2 * unit_width), BF16),
            pltpu.VMEM((unit_width, model_width), BF16),
            pltpu.VMEM((model_width, 3 * head_width), BF16),
            pltpu.VMEM((head_width, model_width), BF16),
            pltpu.VMEM((seq_len, unit_width), F32),
            pltpu.VMEM((seq_len, unit_width), F32),
            pltpu.VMEM((seq_len, unit_width), BF16),
            pltpu.VMEM((unit_width, seq_len), BF16),
            pltpu.VMEM((seq_len, model_width), BF16),
            pltpu.VMEM((seq_len, model_width), BF16),
            pltpu.VMEM((seq_len, 2 * unit_width), BF16),
            pltpu.VMEM((head_count, blocks, QUERY_BLOCK, WINDOW + QUERY_BLOCK), BF16),
            pltpu.VMEM((seq_len, head_width), BF16),
            pltpu.VMEM((head_width, seq_len), BF16),
            pltpu.VMEM((seq_len, 128), F32),
            pltpu.VMEM((seq_len, 128), F32),
            pltpu.VMEM((seq_len, head_width), BF16),
            pltpu.VMEM((share, model_width), BF16),
            pltpu.VMEM((share, model_width), BF16),
            pltpu.VMEM((share, model_width), F32),
            pltpu.VMEM((8, model_width), F32),
            pltpu.VMEM((seq_len, 256), F32),
            pltpu.VMEM(gain_shape, F32),
            pltpu.VMEM((8, *gain_shape), F32),
            pltpu.VMEM((8, *gain_shape), F32),
            pltpu.VMEM(gain_shape, F32),
            pltpu.VMEM((2, *gain_shape), F32),
            pltpu.VMEM((unit_width // 2, seq_len), BF16),
            pltpu.VMEM((model_width // 2, seq_len), BF16),
            pltpu.VMEM((seq_len, model_width), BF16),
            pltpu.VMEM((seq_len, model_width), BF16),
            pltpu.VMEM((head_width // 2, seq_len), BF16),
            pltpu.VMEM((seq_len, 3 * head_width), BF16),
            pltpu.SemaphoreType.REGULAR((2,)),
            DMA((10,)), DMA((8,)), DMA((8,)), DMA((8,)), DMA((8,)), DMA((8,)), DMA((15,)), DMA((15,)), DMA((8,)), DMA((8,)),
        ]
        + gather_scratch() + gather_scratch()
        + scatter_scratch(share, model_width) + [DMA((14,))] * 4
        + sums_scratch(seq_len)
        + grad_sum_scratch(reduce_weight.shape) + grad_sum_scratch(expand_weight.shape)
        + grad_sum_scratch(merge_weight.shape) + grad_sum_scratch(heads_weight.shape),
    )
    heads_grad, merge_grad, expand_grad, reduce_grad = (
        heads_grad.astype(F32), merge_grad.astype(F32), expand_grad.astype(F32), reduce_grad.astype(F32)
    )
    heads_mean, heads_square, heads_fresh = adamw(
        heads_weight, heads_grad, heads_first, heads_second, LR, DECAY
    )
    merge_mean, merge_square, merge_fresh = adamw(
        merge_weight, merge_grad, merge_first, merge_second, LR, DECAY
    )
    expand_mean, expand_square, expand_fresh = adamw(
        expand_weight, expand_grad, expand_first, expand_second, LR, DECAY
    )
    reduce_mean, reduce_square, reduce_fresh = adamw(
        reduce_weight, reduce_grad, reduce_first, reduce_second, LR, DECAY
    )
    gains_mean, gains_square, gains_fresh = adamw(
        norm_gains, gains_grad, gains_first, gains_second, LR_GAIN, 0.0
    )
    return (
        block_output,
        input_grad.astype(F32),
        heads_grad,
        heads_mean,
        heads_square,
        heads_fresh,
        heads_fresh.astype(jnp.bfloat16),
        merge_grad,
        merge_mean,
        merge_square,
        merge_fresh,
        merge_fresh.astype(jnp.bfloat16),
        expand_grad,
        expand_mean,
        expand_square,
        expand_fresh,
        expand_fresh.astype(jnp.bfloat16),
        reduce_grad,
        reduce_mean,
        reduce_square,
        reduce_fresh,
        reduce_fresh.astype(jnp.bfloat16),
        gains_grad,
        gains_mean,
        gains_square,
        gains_fresh,
    )


def solution(mesh):
    return jax.shard_map(
        on_device,
        mesh=mesh,
        in_specs=(
            P(("dp", "row"), "col"),
            P(("dp", "row"), "col"),
            P(("dp", "col"), None),
            P("col", "row"),
            P("col", "row"),
            P("col", "row"),
            P("row", "col"),
            P("row", "col"),
            P("row", "col"),
            P("col", "row"),
            P("col", "row"),
            P("col", "row"),
            P("row", "col"),
            P("row", "col"),
            P("row", "col"),
            P(),
            P(),
            P(),
        ),
        out_specs=(
            P(("dp", "row"), "col"),
            P(("dp", "row"), "col"),
            P("col", "row"),
            P("col", "row"),
            P("col", "row"),
            P("col", "row"),
            P("col", "row"),
            P("row", "col"),
            P("row", "col"),
            P("row", "col"),
            P("row", "col"),
            P("row", "col"),
            P("col", "row"),
            P("col", "row"),
            P("col", "row"),
            P("col", "row"),
            P("col", "row"),
            P("row", "col"),
            P("row", "col"),
            P("row", "col"),
            P("row", "col"),
            P("row", "col"),
            P(),
            P(),
            P(),
            P(),
        ),
        check_vma=False,
    )
```

```python
import math

import jax
import jax.numpy as jnp
from jax import lax
from jax.experimental import pallas as pl
from jax.experimental.pallas import tpu as pltpu
from jax.sharding import PartitionSpec as P

HD = 128
WINDOW = 256
STEP = 5


EPS = 1e-06
THETA = 500000.0
LR = 0.02
LR_GAIN = 0.2
BETA_ONE = 0.5
BETA_TWO = 0.5
DECAY = 0.1
ADAM_EPS = 1e-08

BF16 = jnp.bfloat16
F32 = jnp.float32
MESH = pl.DeviceIdType.MESH
ANY = pl.BlockSpec(memory_space=pl.ANY)
VMEM = pl.BlockSpec(memory_space=pltpu.VMEM)
DMA = pltpu.SemaphoreType.DMA


def documents(lengths, shape, axis):
    tokens = lax.broadcasted_iota(jnp.int32, shape, axis)
    docs, starts, end = jnp.zeros(shape, F32), jnp.zeros(shape, jnp.int32), jnp.int32(0)
    for j in range(lengths.shape[1]):
        end = end + lengths[0, j]
        passed = tokens >= end
        docs = docs + passed.astype(F32)
        starts = starts + jnp.where(passed, lengths[0, j], 0)
    return docs, starts


def adamw(weight, gradient, first_mom, second_mom, step_rate, decay_rate):
    mean_new = BETA_ONE * first_mom + (1.0 - BETA_ONE) * gradient
    square_new = BETA_TWO * second_mom + (1.0 - BETA_TWO) * gradient * gradient
    fix_one = 1.0 - BETA_ONE**STEP
    fix_two = 1.0 - BETA_TWO**STEP
    update = mean_new / fix_one / (jnp.sqrt(square_new / fix_two) + ADAM_EPS) + decay_rate * weight
    return (mean_new, square_new, weight - step_rate * update)


def here():
    return lax.axis_index("dp"), lax.axis_index("row"), lax.axis_index("col")


def row_peer(row, d):
    return (row // 4 + d // 4) % 2 * 4 + (row % 4 + d % 4) % 4


def z_peer(col, d):
    return (col // 2 + d) % 4 * 2 + col % 2


def z_source(col, d):
    return (col // 2 + 4 - d) % 4 * 2 + col % 2


def y_peer(col):
    return col // 2 * 2 + 1 - col % 2


def remote(source, target, sent, arrived, **where):
    return pltpu.make_async_remote_copy(
        src_ref=source,
        dst_ref=target,
        send_sem=sent,
        recv_sem=arrived,
        device_id=where,
        device_id_type=MESH,
    )


def meet(rows=False, cols=False, weights=False, core=False, spread_in=False, spread_out=False):
    dp, row, col = here()
    barrier = pltpu.get_barrier_semaphore()
    count = 0

    def greet(**where):
        pl.semaphore_signal(barrier, inc=1, device_id=where, device_id_type=MESH)

    if rows:
        for d in range(1, 8):
            greet(row=row_peer(row, d))
        count = count + 7
    if cols:
        for d in range(1, 8):
            greet(col=(col + d) % 8)
        count = count + 7
    if weights:
        greet(col=y_peer(col))
        for d in (1, 3):
            greet(col=z_peer(col, d))
        count = count + 3
    if core:
        greet(dp=1 - dp)
        count = count + 1
    for wanted, inward in ((spread_in, True), (spread_out, False)):
        if wanted:
            for k in range(8):
                at_row, at_col = (col, k) if inward else (k, row)

                @pl.when(jnp.logical_not((at_row == row) & (at_col == col)))
                def _():
                    greet(row=at_row, col=at_col)

            count = count + 8 - (row == col).astype(jnp.int32)
    pl.semaphore_wait(barrier, count)


class Spread:
    def __init__(self, inward, source, target, sent, arrived):
        dp, row, col = here()
        self.row, self.col, self.inward = row, col, inward
        self.copies = []
        for k in range(8):
            to_row, to_col = (k, row) if inward else (col, k)
            mine = (row == to_row) & (col == to_col)
            copy = remote(
                source(k),
                target(col if inward else row),
                sent.at[k],
                arrived.at[col if inward else row],
                row=to_row,
                col=to_col,
            )
            waiter = remote(source(k), target(k), sent.at[k], arrived.at[k], row=to_row, col=to_col)
            local = pltpu.make_async_copy(
                source(k), target(col if inward else row), sent.at[k]
            )
            self.copies.append((mine, copy, waiter, local))

    def start(self):
        for mine, copy, _, local in self.copies:
            pl.when(jnp.logical_not(mine))(copy.start)
            pl.when(mine)(local.start)

    def wait(self):
        for k, (mine, copy, waiter, local) in enumerate(self.copies):
            from_row, from_col = (self.col, k) if self.inward else (k, self.row)
            me = (from_row == self.row) & (from_col == self.col)
            pl.when(jnp.logical_not(me))(waiter.wait_recv)
            pl.when(jnp.logical_not(mine))(copy.wait_send)
            pl.when(mine)(local.wait)


def half_of(kind, ref, c, h):
    if kind == "tall":
        count = ref.shape[0] // 16
        return ref.at[pl.ds(pl.multiple_of((2 * c + h) * count, count), count)]
    count, width = ref.shape[0] // 2, ref.shape[1] // 8
    return ref.at[
        pl.ds(pl.multiple_of(h * count, count), count), pl.ds(pl.multiple_of(c * width, width), width)
    ]


def half_shard(ref, h):
    count = ref.shape[0] // 2
    return ref.at[pl.ds(pl.multiple_of(h * count, count), count)]


def mean_rate(values):
    return lax.rsqrt(jnp.mean(values * values, axis=-1, keepdims=True) + EPS)


def call(kernel, name, number, outs, ins, in_specs, out_specs, scratch):
    return pl.pallas_call(
        kernel,
        name=name,
        out_shape=outs,
        in_specs=in_specs,
        out_specs=out_specs,
        scratch_shapes=scratch,
        compiler_params=pltpu.CompilerParams(
            collective_id=number, has_side_effects=True, vmem_limit_bytes=62 * 2**20
        ),
    )(*ins)


def struct(shape, kind):
    return jax.ShapeDtypeStruct(shape, kind)


def dot(left, right):
    return jnp.dot(left, right, preferred_element_type=F32)


def dot_flipped(left, right):
    return lax.dot_general(left, right, (((1,), (1,)), ((), ())), preferred_element_type=F32)


def span(k, count):
    return pl.ds(pl.multiple_of(k * count, count), count)


def near_row(row, dx, dy):
    return (row // 4 + dy) % 2 * 4 + (row % 4 + dx) % 4


class Scatter:
    def __init__(self, part, total, from_y, from_x, last_y, last_x, stage, sent, arrived):
        dp, row, col = here()
        self.row, self.part, self.total = row, part, total
        self.from_y, self.from_x, self.last_y, self.last_x, self.stage = from_y, from_x, last_y, last_x, stage
        self.count, self.half = total.shape[0], total.shape[1] // 2
        number = iter(range(14))

        def copy(source, target, dx, dy):
            i = next(number)
            return remote(source, target, sent.at[i], arrived.at[i], row=near_row(row, dx, dy))

        self.y_first = {dx: copy(self.block(dx, 1, 1), from_y.at[dx], 0, 1) for dx in (1, 3, 2, 0)}
        self.x_first = {
            (dx, dy): copy(self.block(dx, dy, 0), from_x.at[dy, dx - 1], dx, 0)
            for dy in (1, 0)
            for dx in (1, 3, 2)
        }
        self.x_last = {dx: copy(stage.at[dx], last_x.at[dx - 1], dx, 0) for dx in (1, 3, 2)}
        self.y_last = copy(stage.at[0], last_y, 0, 1)

    def block(self, dx, dy, side):
        return self.part.at[
            span(near_row(self.row, dx, dy), self.count), pl.ds(side * self.half, self.half)
        ]

    def start_right(self):
        for copy in self.y_first.values():
            copy.start()

    def start_left(self):
        for copy in self.x_first.values():
            copy.start()

    def chunks(self, body):
        @pl.loop(0, self.count // 16)
        def _(i):
            body(span(i, 16))

    def middle(self):
        for dx in (1, 3, 2):
            self.y_first[dx].wait_recv()
            own = self.block(dx, 0, 1)

            def add(at):
                self.stage[dx, at] = (own[at].astype(F32) + self.from_y[dx, at].astype(F32)).astype(BF16)

            self.chunks(add)
            self.x_last[dx].start()
        for dx in (1, 3, 2):
            self.x_first[dx, 1].wait_recv()
        other = self.block(0, 1, 0)

        def add(at):
            total = other[at].astype(F32)
            for k in range(3):
                total = total + self.from_x[1, k, at].astype(F32)
            self.stage[0, at] = total.astype(BF16)

        self.chunks(add)
        self.y_last.start()

    def end(self):
        self.y_first[0].wait_recv()
        for dx in (1, 3, 2):
            self.x_first[dx, 0].wait_recv()
            self.x_last[dx].wait_recv()
        self.y_last.wait_recv()
        left, right = self.block(0, 0, 0), self.block(0, 0, 1)

        def add(at):
            total = left[at].astype(F32) + self.last_y[at].astype(F32)
            for k in range(3):
                total = total + self.from_x[0, k, at].astype(F32)
            self.total[at, : self.half] = total
            total = right[at].astype(F32) + self.from_y[0, at].astype(F32)
            for k in range(3):
                total = total + self.last_x[k, at].astype(F32)
            self.total[at, self.half :] = total

        self.chunks(add)

    def finish(self):
        for copies in (self.y_first, self.x_first, self.x_last):
            for copy in copies.values():
                copy.wait_send()
        self.y_last.wait_send()


def scatter_scratch(share, width):
    half = width // 2
    return [
        pltpu.VMEM((share, width), F32),
        pltpu.VMEM((4, share, half), BF16),
        pltpu.VMEM((2, 3, share, half), BF16),
        pltpu.VMEM((share, half), BF16),
        pltpu.VMEM((3, share, half), BF16),
        pltpu.VMEM((4, share, half), BF16),
        DMA((14,)),
        DMA((14,)),
    ]


class Gather:
    def __init__(self, whole, share, left, sent, arrived):
        dp, row, col = here()
        self.row = row
        number = iter(range(19))
        sides = (pl.ds(0, left), pl.ds(left, whole.shape[1] - left))
        right = left < whole.shape[1]

        def copy(fx, fy, side, dx, dy, start=0, count=share):
            i = next(number)
            k = near_row(row, fx, fy)
            ref = whole.at[pl.ds(pl.multiple_of(k * share + start, count), count), sides[side]]
            return remote(ref, ref, sent.at[i], arrived.at[i], row=near_row(row, dx, dy))

        part = share // 2
        self.y_left = copy(0, 0, 0, 0, 1)
        self.x_left = [copy(0, 0, 0, dx, 0) for dx in (1, 3)]
        self.x_other = [copy(0, 1, 0, dx, 0) for dx in (1, 3)]
        steps = list(enumerate((1, 3)))
        self.on_left = [copy(4 - dx, 0, 0, dx, 0, i * part, part) for i, dx in steps]
        self.on_other = [copy(4 - dx, 1, 0, dx, 0, i * part, part) for i, dx in steps]
        self.y_right, self.x_right, self.on_right, self.y_near, self.y_far = [], [], [], [], []
        if right:
            self.y_right = [copy(0, 0, 1, 0, 1)]
            self.x_right = [copy(0, 0, 1, dx, 0) for dx in (1, 3)]
            self.on_right = [copy(4 - dx, 0, 1, dx, 0, i * part, part) for i, dx in steps]
            self.y_near = [copy(4 - dx, 0, 1, 0, 1) for dx in (1, 3)]
            self.y_far = [copy(2, 0, 1, 0, 1, i * part, part) for i in range(2)]

    def start(self):
        for copy in (self.y_left, *self.x_right, *self.y_right, *self.x_left):
            copy.start()

    def relay(self):
        self.y_left.wait_recv()
        for copy in self.x_other:
            copy.start()
        for i, came in enumerate(self.x_right):
            came.wait_recv()
            self.on_right[i].start()
            self.y_near[i].start()

    def relay_again(self):
        for i in range(2):
            self.x_left[i].wait_recv()
            self.on_left[i].start()
        for i, came in enumerate(self.on_right):
            came.wait_recv()
            self.y_far[i].start()
        for i in range(2):
            self.x_other[i].wait_recv()
            self.on_other[i].start()

    def wait(self):
        for copy in (*self.y_right, *self.on_left, *self.on_other, *self.y_near, *self.y_far):
            copy.wait_recv()
        for copy in (self.y_left, *self.x_left, *self.x_other, *self.on_left, *self.on_other, *self.y_right,
                     *self.x_right, *self.on_right, *self.y_near, *self.y_far):
            copy.wait_send()


def gather_scratch():
    return [DMA((19,)), DMA((19,))]


def cols(ref, k, width):
    return ref.at[:, pl.ds(pl.multiple_of(k * width, width), width)]


def rows_of(ref, k, count):
    return ref.at[pl.ds(pl.multiple_of(k * count, count), count)]


def back_of(grad, values, gain):
    rate = mean_rate(values)
    hat = values * rate
    grad_hat = grad * gain
    dots = jnp.mean(grad_hat * hat, axis=-1, keepdims=True)
    return hat, rate * (grad_hat - hat * dots)


class GradSum:
    def __init__(self, kind, part, out, between, far, near, sent, arrived):
        dp, _, col = here()
        self.kind, self.part, self.col = kind, part, col
        self.between, self.far, self.near = between, far, near
        self.rows, self.width = near.shape[1], near.shape[2]
        number = iter(range(10))

        def copy(source, target, **where):
            i = next(number)
            return remote(source, target, sent.at[i], arrived.at[i], **where)

        self.steps = (1, 3)
        self.on = [
            [
                copy(self.piece(self.z_block(2, k), i), between.at[i, k], col=z_peer(col, d))
                for k in range(2)
            ]
            for i, d in enumerate(self.steps)
        ]
        self.zs = [
            [copy(self.block(self.z_block(d, k)), far.at[i, k], col=z_peer(col, d)) for k in range(2)]
            for i, d in enumerate(self.steps)
        ]
        self.ys = copy(near.at[0], near.at[1], col=y_peer(col))
        self.last = copy(near.at[0], half_shard(out, dp), dp=1 - dp)
        self.keep = pltpu.make_async_copy(near.at[0], half_shard(out, dp), sent.at[10])

    def z_block(self, d, k):
        return z_peer(self.col, d) // 2 * 2 + k

    def block(self, c):
        if self.kind == "tall":
            return self.part.at[span(c, self.rows)]
        return self.part.at[:, span(c, self.width)]

    def piece(self, c, i):
        return self.block(c).at[pl.ds(i * (self.rows // 2), self.rows // 2)]

    def each(self, rows, body):
        count = min(rows, 32768 // self.width // 16 * 16)

        @pl.loop(0, rows // count)
        def _(i):
            body(span(i, count))

    def start(self):
        for pair in self.on:
            for copy in pair:
                copy.start()

    def over_z(self):
        for i, d in enumerate(self.steps):
            for k in range(2):
                self.on[i][k].wait_recv()
                own = self.piece(self.z_block(d, k), i)

                def add(at):
                    own[at] = (own[at].astype(F32) + self.between[i, k, at].astype(F32)).astype(BF16)

                self.each(self.rows // 2, add)
                self.zs[i][k].start()

    def over_y(self):
        for pair in self.zs:
            for copy in pair:
                copy.wait_recv()
        yl = self.col % 2
        keep, give = self.block(self.col), self.block(y_peer(self.col))

        def total(at, ref, k):
            return (
                ref[at].astype(F32) + self.far[0, k, at].astype(F32) + self.far[1, k, at].astype(F32)
            ).astype(BF16)

        def add(at):
            self.near[0, at] = total(at, give, 1 - yl)

        self.each(self.rows, add)
        self.ys.start()

        def add(at):
            keep[at] = total(at, keep, yl)

        self.each(self.rows, add)
        for pair in (*self.zs, *self.on):
            for copy in pair:
                copy.wait_send()

    def end(self):
        self.ys.wait()
        keep = self.block(self.col)

        def add(at):
            self.near[0, at] = (keep[at].astype(F32) + self.near[1, at].astype(F32)).astype(BF16)

        self.each(self.rows, add)
        self.last.start()
        self.keep.start()

    def wait(self):
        self.last.wait()
        self.keep.wait()


def grad_sum_scratch(shape):
    rows, width = shape[0] // 2, shape[1]
    return [
        pltpu.VMEM((2, 2, rows // 2, width), BF16),
        pltpu.VMEM((2, 2, rows, width), BF16),
        pltpu.VMEM((2, rows, width), BF16),
        DMA((11,)),
        DMA((10,)),
    ]


class Bring:
    def __init__(self, kind, shape, whole, sent, arrived):
        dp, _, col = here()
        rows, width = shape
        near = y_peer(col)
        number = iter(range(20))

        def block(c, s=None):
            count, at = (rows // 2, dp) if s is None else (rows // 4, 2 * dp + s)
            if kind == "tall":
                return whole.at[span((2 if s is None else 4) * c + at, count)]
            return whole.at[span(at, count), span(c, width)]

        def copy(source, target, **where):
            i = next(number)
            return remote(source, target, sent.at[i], arrived.at[i], **where)

        self.place = whole.at[span(col, rows)] if kind == "tall" else whole.at[:, span(col, width)]
        self.y_own = copy(block(col), block(col), col=near)
        self.z_own = [copy(block(col), block(col), col=z_peer(col, d)) for d in (1, 3)]
        self.z_near = [copy(block(near), block(near), col=z_peer(col, d)) for d in (1, 3)]
        self.on, self.on_near, self.a_own, self.a_near = [], [], [], []
        self.a_far, self.a_far_near = [], []
        for i, d in enumerate((1, 3)):
            came, two = z_source(col, d), z_peer(col, 2)
            self.on.append(copy(block(came, i), block(came, i), col=z_peer(col, d)))
            self.on_near.append(copy(block(y_peer(came), i), block(y_peer(came), i), col=z_peer(col, d)))
            self.a_own.append(copy(block(came), block(came), dp=1 - dp))
            self.a_near.append(copy(block(y_peer(came)), block(y_peer(came)), dp=1 - dp))
            self.a_far.append(copy(block(two, i), block(two, i), dp=1 - dp))
            self.a_far_near.append(copy(block(y_peer(two), i), block(y_peer(two), i), dp=1 - dp))
        self.a_y = copy(block(near), block(near), dp=1 - dp)

    def start_y(self):
        self.y_own.start()

    def start_z(self):
        for copy in self.z_own:
            copy.start()

    def relay(self):
        self.y_own.wait_recv()
        for copy in (*self.z_near, self.a_y):
            copy.start()

    def relay_own(self):
        for i in range(2):
            self.z_own[i].wait_recv()
            self.on[i].start()
            self.a_own[i].start()

    def relay_near(self):
        for i in range(2):
            self.z_near[i].wait_recv()
            self.on_near[i].start()
            self.a_near[i].start()

    def hand_over(self):
        for i in range(2):
            self.on[i].wait_recv()
            self.a_far[i].start()
        for i in range(2):
            self.on_near[i].wait_recv()
            self.a_far_near[i].start()

    def wait(self):
        for copy in (self.a_y, *self.a_own, *self.a_near, *self.a_far, *self.a_far_near):
            copy.wait()
        for copy in (self.y_own, *self.z_own, *self.z_near, *self.on, *self.on_near):
            copy.wait_send()


def bring_scratch():
    return [DMA((20,)), DMA((20,))]


class SpreadIn:
    def __init__(self, source, target, sent, arrived):
        dp, row, col = here()
        self.row, self.col = row, col
        self.copies, self.waits = [], []
        for k in range(8):
            out = remote(source(k), target(k, col), sent.at[k], arrived.at[col], row=k, col=row)
            came = remote(source(k), target(row, k), sent.at[k], arrived.at[k], row=k, col=row)
            local = pltpu.make_async_copy(source(k), target(k, col), sent.at[k])
            self.copies.append(((row == k) & (row == col), out, local))
            self.waits.append(((row == col) & (col == k), came))

    def start(self):
        for mine, out, local in self.copies:
            pl.when(jnp.logical_not(mine))(out.start)
            pl.when(mine)(local.start)

    def wait(self):
        for mine, came in self.waits:
            pl.when(jnp.logical_not(mine))(came.wait_recv)
        for mine, out, local in self.copies:
            pl.when(jnp.logical_not(mine))(out.wait_send)
            pl.when(mine)(local.wait)


class TokenSums:
    def __init__(self, stats, mine, came, sent, arrived):
        dp, row, col = here()
        self.stats, self.mine, self.came = stats, mine, came
        self.copies = [
            remote(mine, came.at[d - 1], sent.at[d - 1], arrived.at[d - 1], row=row_peer(row, d))
            for d in range(1, 8)
        ]

    def put(self, at, one, two):
        lane = lax.broadcasted_iota(jnp.int32, (one.shape[0], 128), 1)
        self.stats[at] = jnp.where(lane == 0, one, jnp.where(lane == 1, two, 0.0))

    def start(self):
        self.mine[...] = self.stats[...].T[:8]
        for copy in self.copies:
            copy.start()

    def end(self):
        total = self.mine[...]
        for d, copy in enumerate(self.copies):
            copy.wait_recv()
            total = total + self.came[d]
        self.stats[...] = jnp.concatenate([total] * 16, axis=0).T
        for copy in self.copies:
            copy.wait_send()


def sums_scratch(tokens):
    return [pltpu.VMEM((8, tokens), F32), pltpu.VMEM((7, 8, tokens), F32), DMA((7,)), DMA((7,))]


def turn(values, cosine, sine):
    heads = [values[:, i : i + HD] for i in range(0, values.shape[1], HD)]
    return jnp.concatenate([h * cosine + pltpu.roll(h, HD // 2, 1) * sine for h in heads], axis=1)


QUERY_BLOCK = 128


def key_span(b):
    start = max(0, b * QUERY_BLOCK - WINDOW)
    return start, (b + 1) * QUERY_BLOCK - start


def layer_kernel(
    x, g_in, heads_in, merge_in, expand_in, reduce_in, lengths, gain_all,
    out, input_grad, gains_grad, heads_grad, merge_grad, expand_grad, reduce_grad, xs_keep, raw_keep, qkv_keep,
    rows, turned, expand, reduce, heads, merge, gate, up, act, act_turned, part, back, hidden, probs, mix, mix_turned,
    rates, stats, grad_mix, done, final, grad_resid, merged, residual, g, sums, grad_gate,
    gains, gain_row, gain_col, gain_core, gain_sum, act_other, turned_other, hidden_other, back_other, mix_other,
    joined_other, docs, doc_row, cosine, sine, free, load, keep, late, osent, ocame, isent, icame, nsent, ncame, xsent, xcame,
    asent, acame, bsent, bcame, g1sent, g1came, g2sent, g2came, g3sent, g3came, g4sent, g4came, *refs,
):
    dp, row, col = here()
    share, width = residual.shape
    tokens, units = act.shape
    head_width = mix.shape[1]
    tiles = units // 256
    n = width // 512
    gain_query, gain_key = (gain_all.at[i : i + 1, span(row, head_width)] for i in range(2))
    gain_merge, gain_reduce = (gain_all.at[i : i + 1] for i in range(2, 4))
    scatter = [Scatter(part, *refs[:6], *refs[6 + 2 * i : 8 + 2 * i]) for i in range(4)]
    first_sums = TokenSums(rates, *refs[14:18])
    token_sums = TokenSums(stats, *refs[18:22])
    half_units, half_width, half_heads = units // 2, width // 2, head_width // 2
    reduce_part, merge_part_ref = reduce.at[pl.ds(0, half_units)], merge.at[pl.ds(0, half_heads)]
    expand_part, heads_part = expand.at[pl.ds(0, half_width)], heads.at[pl.ds(0, half_width)]
    reduce_sum = GradSum("wide", reduce_part, reduce_grad, *refs[22:27])
    expand_sum = GradSum("tall", expand_part, expand_grad, *refs[27:32])
    merge_sum = GradSum("wide", merge_part_ref, merge_grad, *refs[32:37])
    heads_sum = GradSum("tall", heads_part, heads_grad, *refs[37:42])
    bring_heads = Bring("tall", heads_in.shape, heads, *refs[42:44])
    bring_merge = Bring("wide", merge_in.shape, merge, *refs[44:46])
    bring_reduce = Bring("wide", reduce_in.shape, reduce, *refs[46:48])
    bring_expand = Bring("tall", expand_in.shape, expand, *refs[48:50])
    gather_x = Gather(back, share, width, g1sent, g1came)
    row_gather = Gather(rows, share, width // 2, g2sent, g2came)
    gather = Gather(back, share, width // 2, g3sent, g3came)
    last_gather = Gather(back, share, width // 2, g4sent, g4came)
    spread_x = SpreadIn(
        lambda k: rows_of(x, k, share), lambda k, c: back.at[span(k, share), span(c, 256)], asent, acame
    )
    spread_g = SpreadIn(lambda k: rows_of(g_in, k, share), lambda k, c: g.at[:, span(c, 256)], bsent, bcame)
    spread = Spread(False, lambda k: cols(done, k, 256), lambda k: rows_of(out, k, 64), osent, ocame)
    spread_grad = Spread(False, lambda k: cols(final, k, 256), lambda k: rows_of(input_grad, k, 64), isent, icame)
    row_gains = [
        remote(gains, gain_row.at[row], nsent.at[d - 1], ncame.at[d - 1], row=row_peer(row, d))
        for d in range(1, 8)
    ]
    col_gains = [
        remote(gain_sum.at[0], gain_col.at[col], nsent.at[6 + d], ncame.at[6 + d], col=(col + d) % 8)
        for d in range(1, 8)
    ]
    core_gains = remote(gain_sum.at[1], gain_core, nsent.at[14], ncame.at[14], dp=1 - dp)

    raw, qkv, new_rows = up.at[:, : 2 * head_width], act.at[:, : 3 * head_width], back
    heads_change = gate.at[:, : 3 * head_width]
    joined = hidden.at[:, : 3 * head_width]
    puts = [
        pltpu.make_async_copy(source, target, keep.at[i])
        for i, (source, target) in enumerate(((back, xs_keep), (raw, raw_keep), (qkv, qkv_keep)))
    ]
    get_xs = pltpu.make_async_copy(xs_keep, rows, late.at[0])
    get_raw = pltpu.make_async_copy(raw_keep, raw, late.at[1])
    get_qkv = pltpu.make_async_copy(qkv_keep, qkv, late.at[2])

    shard_rows, quarter = heads_in.shape[0], reduce_in.shape[0] // 4
    heads32 = gate.at[:shard_rows, : heads_in.shape[1]]
    merge32 = gate.at[:shard_rows, heads_in.shape[1] :]
    reduce32 = [gate.at[shard_rows:, pl.ds(i * 256, 256)] for i in range(4)]
    expand32 = [up.at[pl.ds(i * shard_rows, shard_rows)] for i in range(2)]
    moves = (
        [(heads_in, heads32), (merge_in, merge32)]
        + [(reduce_in.at[pl.ds(i * quarter, quarter)], reduce32[i]) for i in range(4)]
        + [(expand_in.at[:, pl.ds(i * units, units)], expand32[i]) for i in range(2)]
    )
    loads = [pltpu.make_async_copy(source, target, load.at[i]) for i, (source, target) in enumerate(moves)]
    for copy in loads:
        copy.start()

    def narrow(i, target):
        loads[i].wait()
        source = moves[i][1]

        @pl.loop(0, source.shape[0] // 16)
        def _(k):
            at = span(k, 16)
            target[at] = source[at].astype(BF16)

    def hand(i, source, target):
        return remote(source, target, xsent.at[i], xcame.at[i], dp=1 - dp)

    hand_act = hand(0, act_turned.at[span(1 - dp, half_units)], act_other)
    hand_rows = hand(1, turned.at[span(1 - dp, half_width)], turned_other)
    hand_back = hand(2, back, back_other)
    hand_hidden = hand(3, hidden, hidden_other)
    hand_mix = hand(4, mix_turned.at[span(1 - dp, half_heads)], mix_other)
    hand_new = hand(5, back, back_other)
    hand_xs = hand(6, turned.at[span(1 - dp, half_width)], turned_other)
    hand_joined = hand(7, joined, joined_other)

    def turn_rows(j):
        values = rows[:, span(j, 256)].T
        turned[span(j, 128), :] = values[:128]
        turned[span(2 * tiles + j, 128), :] = values[128:]

    def two(target, at, wide, own, own_at, right, other, right_other):
        target[at, wide] = (
            dot(own[own_at, :], right[:, wide]) + dot(other[at, :], right_other[:, wide])
        ).astype(BF16)

    meet(rows=True, cols=True, core=True, spread_in=True, spread_out=True)
    spread_x.start()
    narrow(0, bring_heads.place)
    bring_heads.start_y()
    bring_heads.start_z()
    narrow(1, bring_merge.place)
    bring_merge.start_y()
    bring_merge.start_z()
    for i in range(4):
        narrow(2 + i, bring_reduce.place.at[pl.ds(i * quarter, quarter)])
    for i in range(2):
        narrow(6 + i, bring_expand.place.at[:, pl.ds(i * units, units)])
    spread_x.wait()
    gather_x.start()
    bring_heads.relay()
    bring_heads.relay_own()
    gather_x.relay()
    bring_expand.start_y()
    bring_reduce.start_y()
    bring_heads.relay_near()
    bring_merge.relay()
    gather_x.relay_again()
    bring_merge.relay_own()
    bring_heads.hand_over()
    bring_merge.relay_near()
    bring_expand.start_z()
    bring_reduce.start_z()
    docs[...], starts = documents(lengths, docs.shape, 0)
    doc_row[...], _ = documents(lengths, doc_row.shape, 1)
    lane = lax.broadcasted_iota(jnp.int32, docs.shape, 1)
    frequency = jnp.exp((lane % (HD // 2)).astype(F32) * (-2.0 / HD * math.log(THETA)))
    angles = (lax.broadcasted_iota(jnp.int32, docs.shape, 0) - starts).astype(F32) * frequency
    cosine[...] = jnp.cos(angles)
    sine[...] = jnp.where(lane < HD // 2, -1.0, 1.0) * jnp.sin(angles)
    gather_x.wait()
    bring_heads.wait()
    puts[0].start()

    for i in range(2):
        raw[:, i * head_width : (i + 1) * head_width] = dot(
            back[...], heads[:, i * head_width : (i + 1) * head_width]
        )

    @pl.loop(0, tokens // 64)
    def _(i):
        at = span(i, 64)
        squares = raw[at] * raw[at]
        first_sums.put(
            at,
            jnp.sum(squares[:, :head_width], axis=1, keepdims=True),
            jnp.sum(squares[:, head_width:], axis=1, keepdims=True),
        )

    first_sums.start()
    qkv[:, 2 * head_width :] = dot(back[...], heads[:, 2 * head_width :]).astype(BF16)
    bring_merge.hand_over()
    first_sums.end()
    spread_g.start()

    @pl.loop(0, tokens // 64)
    def _(i):
        at = span(i, 64)
        rate = lax.rsqrt(rates[at] * (1.0 / width) + EPS)
        rates[at] = rate
        for j, gain in enumerate((gain_query, gain_key)):
            some = slice(j * head_width, (j + 1) * head_width)
            hat = raw[at, some] * rate[:, j : j + 1]
            qkv[at, some] = turn(hat * gain[...], cosine[at], sine[at]).astype(BF16)

    puts[1].start()
    puts[2].start()
    for b in range(tokens // QUERY_BLOCK):
        start, count = key_span(b)
        query_at = pl.ds(b * QUERY_BLOCK, QUERY_BLOCK)
        key_at = pl.ds(start, count)
        there = lax.broadcasted_iota(jnp.int32, (QUERY_BLOCK, count), 0) + (b * QUERY_BLOCK - start)
        distance = there - lax.broadcasted_iota(jnp.int32, (QUERY_BLOCK, count), 1)
        doc = docs[query_at, 0:1]
        allowed = (doc == doc_row[0:1, start : start + count]) & (distance >= 0) & (distance < WINDOW)
        live = (doc < 5.0).astype(F32)
        for h in range(head_width // HD):
            query, key, value = (
                slice(i * head_width + h * HD, i * head_width + (h + 1) * HD) for i in range(3)
            )
            scores = dot_flipped(qkv[query_at, query], qkv[key_at, key]) * HD**-0.5
            scores = jnp.where(allowed, scores, -1e30)
            weights = jnp.exp(scores - jnp.max(scores, axis=1, keepdims=True))
            shares = (weights / jnp.sum(weights, axis=1, keepdims=True)).astype(BF16)
            probs[h, b, :, :count] = shares
            if count < probs.shape[3]:
                probs[h, b, :, count:] = jnp.zeros((QUERY_BLOCK, probs.shape[3] - count), BF16)
            mix[query_at, h * HD : (h + 1) * HD] = (dot(shares, qkv[key_at, value]) * live).astype(BF16)

    bring_expand.relay()
    bring_reduce.relay()
    bring_merge.wait()

    def merge_part(j):
        at = span(j, 256)
        part[:, at] = dot(mix[...], merge[:, at]).astype(BF16)

    pl.loop(n, 2 * n)(merge_part)
    scatter[0].start_right()
    pl.loop(0, n)(merge_part)
    scatter[0].start_left()
    bring_expand.relay_own()
    bring_reduce.relay_own()
    scatter[0].middle()
    bring_expand.relay_near()
    bring_reduce.relay_near()
    scatter[0].end()

    @pl.loop(0, share // 16)
    def _(i):
        at = span(i, 16)
        total = scatter[0].total[at]
        merged[at] = total
        mine = pl.ds(pl.multiple_of(row * share + i * 16, 16), 16)
        result = back[mine, :].astype(F32) + total * mean_rate(total) * gain_merge[...]
        residual[at] = result
        rows[mine, :] = result.astype(BF16)

    row_gather.start()
    row_gather.relay()
    bring_expand.hand_over()
    row_gather.relay_again()
    bring_reduce.hand_over()
    row_gather.wait()
    scatter[0].finish()
    bring_expand.wait()
    for copy in puts:
        copy.wait()
    @pl.loop(0, tiles)
    def _(j):
        at = span(j, 256)
        gate[:, at] = dot(rows[...], expand[:, at])
        up[:, at] = dot(rows[...], expand[:, span(tiles + j, 256)])

        @pl.loop(0, tokens // 64)
        def _(i):
            some = span(i, 64)
            x = gate[some, at]
            act[some, at] = (x * jax.nn.sigmoid(x) * up[some, at]).astype(BF16)

    bring_reduce.wait()

    def reduced(j):
        at = span(j, 256)
        part[:, at] = dot(act[...], reduce[:, at]).astype(BF16)

    pl.loop(n, 2 * n)(reduced)
    scatter[1].start_right()
    pl.loop(0, n)(reduced)
    scatter[1].start_left()

    @pl.loop(0, tiles)
    def _(j):
        at = span(j, 256)
        act_turned[at, :] = act[:, at].T

    hand_act.start()
    get_qkv.start()

    spread_g.wait()
    scatter[1].middle()
    scatter[1].end()
    sums[...] = jnp.zeros_like(sums)

    @pl.loop(0, share // 16)
    def _(i):
        at = span(i, 16)
        grad = g[at].astype(F32)
        hat, change = back_of(grad, scatter[1].total[at], gain_reduce[...])
        back[pl.ds(pl.multiple_of(row * share + i * 16, 16), 16), :] = change.astype(BF16)
        done[at] = (residual[at] + hat * gain_reduce[...]).astype(BF16)
        product = grad * hat
        sums[...] += product[:8] + product[8:]

    gather.start()
    gains[...] = jnp.zeros_like(gains)
    gains[3:4] = jnp.sum(sums[...], axis=0, keepdims=True)
    scatter[1].finish()
    gather.relay()

    pl.loop(0, 2 * tiles)(turn_rows)
    hand_rows.start()
    get_xs.start()
    gather.relay_again()
    gather.wait()
    hand_back.start()
    spread.start()

    @pl.loop(0, tiles)
    def _(j):
        at, up_at = span(j, 256), span(tiles + j, 256)
        grad_gate[...] = dot_flipped(back[...], reduce[at, :])

        @pl.loop(0, tokens // 64)
        def _(i):
            some = span(i, 64)
            x, change = gate[some, at], grad_gate[some]
            s = jax.nn.sigmoid(x)
            hidden[some, at] = (change * up[some, at] * s * (1.0 + x * (1.0 - s))).astype(BF16)
            hidden[some, up_at] = (change * (x * s)).astype(BF16)

    hand_hidden.start()
    get_raw.start()

    def branch(j):
        at = span(j, 256)
        part[:, at] = dot_flipped(hidden[...], expand[at, :]).astype(BF16)

    pl.loop(n, 2 * n)(branch)
    scatter[2].start_right()
    pl.loop(0, n)(branch)
    scatter[2].start_left()

    hand_act.wait()
    hand_back.wait()
    halves = [pl.ds(side * (width // 2), width // 2) for side in range(2)]

    @pl.loop(0, tiles // 2)
    def _(j):
        for wide in halves:
            two(reduce, span(j, 256), wide, act_turned, span(dp * (tiles // 2) + j, 256), back, act_other, back_other)

    pl.semaphore_signal(free.at[0], inc=1, device_id={"dp": 1 - dp}, device_id_type=MESH)
    reduce_sum.start()
    scatter[2].middle()
    hand_rows.wait()
    hand_hidden.wait()

    @pl.loop(0, tiles)
    def _(j):
        for wide in halves:
            two(expand, span(j, 256), wide, turned, span(dp * tiles + j, 256), hidden, turned_other, hidden_other)

    pl.semaphore_signal(free.at[1], inc=1, device_id={"dp": 1 - dp}, device_id_type=MESH)
    expand_sum.start()
    reduce_sum.over_z()
    scatter[2].end()
    sums[...] = jnp.zeros_like(sums)

    @pl.loop(0, share // 16)
    def _(i):
        at = span(i, 16)
        grad = g[at].astype(F32) + scatter[2].total[at]
        grad_resid[at] = grad
        hat, change = back_of(grad, merged[at], gain_merge[...])
        new_rows[pl.ds(pl.multiple_of(row * share + i * 16, 16), 16), :] = change.astype(BF16)
        product = grad * hat
        sums[...] += product[:8] + product[8:]

    last_gather.start()
    gains[2:3] = jnp.sum(sums[...], axis=0, keepdims=True)
    get_xs.wait()
    pl.loop(0, 2 * tiles)(turn_rows)
    pl.semaphore_wait(free.at[1], 1)
    hand_xs.start()
    last_gather.relay()
    last_gather.relay_again()
    get_raw.wait()
    get_qkv.wait()
    mix_turned[...] = mix[...].T
    hand_mix.start()
    expand_sum.over_z()
    scatter[2].finish()
    last_gather.wait()
    pl.semaphore_wait(free.at[0], 1)
    hand_new.start()

    live = (docs[:, 0:1] < 5.0).astype(F32)
    grad_mix[...] = (dot_flipped(new_rows[...], merge[...]) * live).astype(BF16)
    heads_change[:, head_width:] = jnp.zeros((tokens, 2 * head_width), F32)
    for b in range(tokens // QUERY_BLOCK):
        start, count = key_span(b)
        query_at = pl.ds(b * QUERY_BLOCK, QUERY_BLOCK)
        key_at = pl.ds(start, count)
        for h in range(head_width // HD):
            query, key, value = (
                slice(i * head_width + h * HD, i * head_width + (h + 1) * HD) for i in range(3)
            )
            shares = probs[h, b, :, :count]
            change = grad_mix[query_at, h * HD : (h + 1) * HD]
            grad_shares = dot_flipped(change, qkv[key_at, value])
            weighted = shares.astype(F32) * grad_shares
            center = jnp.sum(weighted, axis=1, keepdims=True)
            grad_scores = (weighted - shares.astype(F32) * center).astype(BF16)
            heads_change[query_at, query] = dot(grad_scores, qkv[key_at, key]) * HD**-0.5
            heads_change[key_at, key] += dot(grad_scores.T, qkv[query_at, query]) * HD**-0.5
            heads_change[key_at, value] += dot(shares.T, change)

    reduce_sum.over_y()
    sums[...] = jnp.zeros_like(sums)

    @pl.loop(0, tokens // 64)
    def _(i):
        at = span(i, 64)
        dots = []
        for j, gain in enumerate((gain_query, gain_key)):
            some = slice(j * head_width, (j + 1) * head_width)
            change = turn(heads_change[at, some], cosine[at], -sine[at])
            hat = raw[at, some] * rates[at, j : j + 1]
            product = change * hat
            sums[:, some] += jnp.sum(product.reshape(8, 8, head_width), axis=0)
            heads_change[at, some] = change * gain[...]
            dots.append(jnp.sum(product * gain[...], axis=1, keepdims=True))
        token_sums.put(at, *dots)

    token_sums.start()
    gains[0:1, span(row, head_width)] = jnp.sum(sums[:, :head_width], axis=0, keepdims=True)
    gains[1:2, span(row, head_width)] = jnp.sum(sums[:, head_width : 2 * head_width], axis=0, keepdims=True)
    for copy in row_gains:
        copy.start()
    hand_mix.wait()
    hand_new.wait()
    mine = span(dp, half_heads)
    for side in range(4):
        wide = pl.ds(side * (width // 4), width // 4)
        merge[:half_heads, wide] = (
            dot(mix_turned[mine, :], back[:, wide]) + dot(mix_other[...], back_other[:, wide])
        ).astype(BF16)
    merge_sum.start()
    joined[:, 2 * head_width :] = heads_change[:, 2 * head_width :].astype(BF16)
    token_sums.end()

    @pl.loop(0, tokens // 64)
    def _(i):
        at = span(i, 64)
        dots = stats[at] * (1.0 / width)
        for j in range(2):
            some = slice(j * head_width, (j + 1) * head_width)
            rate = rates[at, j : j + 1]
            hat = raw[at, some] * rate
            joined[at, some] = (rate * (heads_change[at, some] - hat * dots[:, j : j + 1])).astype(BF16)

    hand_joined.start()
    for copy in row_gains:
        copy.wait()
    gain_row[row] = gains[...]
    total = gain_row[0]
    for k in range(1, 8):
        total = total + gain_row[k]
    gain_sum[0] = total
    gain_col[col] = total
    for copy in col_gains:
        copy.start()

    def input_part(j):
        at = span(j, 256)
        part[:, at] = dot_flipped(joined[...], heads[at, :]).astype(BF16)

    pl.loop(n, 2 * n)(input_part)
    scatter[3].start_right()
    pl.loop(0, n)(input_part)
    scatter[3].start_left()

    hand_xs.wait()
    hand_joined.wait()
    everything = pl.ds(0, 3 * head_width)

    @pl.loop(0, tiles)
    def _(j):
        two(heads, span(j, 256), everything, turned, span(dp * tiles + j, 256), joined, turned_other, joined_other)

    heads_sum.start()
    expand_sum.over_y()
    merge_sum.over_z()
    reduce_sum.end()
    scatter[3].middle()
    heads_sum.over_z()
    scatter[3].end()
    final[...] = (grad_resid[...] + scatter[3].total[...]).astype(BF16)
    spread_grad.start()
    for copy in col_gains:
        copy.wait()
    total = gain_col[0]
    for k in range(1, 8):
        total = total + gain_col[k]
    gain_sum[1] = total
    core_gains.start()
    merge_sum.over_y()
    heads_sum.over_y()
    expand_sum.end()
    merge_sum.end()
    heads_sum.end()
    core_gains.wait()
    gains_grad[...] = gain_sum[1] + gain_core[...]
    scatter[3].finish()
    spread.wait()
    spread_grad.wait()
    for grad in (reduce_sum, expand_sum, merge_sum, heads_sum):
        grad.wait()


def on_device(
    block_input,
    cotangent,
    doc_lengths,
    heads_weight,
    heads_first,
    heads_second,
    merge_weight,
    merge_first,
    merge_second,
    expand_weight,
    expand_first,
    expand_second,
    reduce_weight,
    reduce_first,
    reduce_second,
    norm_gains,
    gains_first,
    gains_second,
):
    col_width = block_input.shape[1]
    model_width = col_width * lax.axis_size("col")
    head_width = merge_weight.shape[0]
    unit_width = reduce_weight.shape[0]
    seq_len = block_input.shape[0] * lax.axis_size("row") // lax.axis_size("col")
    share = seq_len // lax.axis_size("row")
    head_count = head_width // HD
    rows_shape = struct((seq_len, model_width), BF16)
    blocks = seq_len // QUERY_BLOCK

    gain_shape = (4, model_width)
    block_output, input_grad, gains_grad, heads_grad, merge_grad, expand_grad, reduce_grad = call(
        layer_kernel, "layer", 1,
        [
            struct(block_input.shape, BF16),
            struct(block_input.shape, BF16),
            struct(gain_shape, F32),
            struct(heads_weight.shape, BF16),
            struct(merge_weight.shape, BF16),
            struct(expand_weight.shape, BF16),
            struct(reduce_weight.shape, BF16),
            rows_shape,
            struct((seq_len, 2 * head_width), F32),
            struct((seq_len, 3 * head_width), BF16),
        ],
        [
            block_input, cotangent, heads_weight, merge_weight, expand_weight, reduce_weight, doc_lengths, norm_gains,
        ],
        [ANY] * 6 + [pl.BlockSpec(memory_space=pltpu.SMEM), VMEM],
        [ANY] * 2 + [VMEM] + [ANY] * 7,
        [
            pltpu.VMEM((seq_len, model_width), BF16),
            pltpu.VMEM((model_width, seq_len), BF16),
            pltpu.VMEM((model_width, 2 * unit_width), BF16),
            pltpu.VMEM((unit_width, model_width), BF16),
            pltpu.VMEM((model_width, 3 * head_width), BF16),
            pltpu.VMEM((head_width, model_width), BF16),
            pltpu.VMEM((seq_len, unit_width), F32),
            pltpu.VMEM((seq_len, unit_width), F32),
            pltpu.VMEM((seq_len, unit_width), BF16),
            pltpu.VMEM((unit_width, seq_len), BF16),
            pltpu.VMEM((seq_len, model_width), BF16),
            pltpu.VMEM((seq_len, model_width), BF16),
            pltpu.VMEM((seq_len, 2 * unit_width), BF16),
            pltpu.VMEM((head_count, blocks, QUERY_BLOCK, WINDOW + QUERY_BLOCK), BF16),
            pltpu.VMEM((seq_len, head_width), BF16),
            pltpu.VMEM((head_width, seq_len), BF16),
            pltpu.VMEM((seq_len, 128), F32),
            pltpu.VMEM((seq_len, 128), F32),
            pltpu.VMEM((seq_len, head_width), BF16),
            pltpu.VMEM((share, model_width), BF16),
            pltpu.VMEM((share, model_width), BF16),
            pltpu.VMEM((share, model_width), F32),
            pltpu.VMEM((share, model_width), F32),
            pltpu.VMEM((share, model_width), F32),
            pltpu.VMEM((share, model_width), BF16),
            pltpu.VMEM((8, model_width), F32),
            pltpu.VMEM((seq_len, 256), F32),
            pltpu.VMEM(gain_shape, F32),
            pltpu.VMEM((8, *gain_shape), F32),
            pltpu.VMEM((8, *gain_shape), F32),
            pltpu.VMEM(gain_shape, F32),
            pltpu.VMEM((2, *gain_shape), F32),
            pltpu.VMEM((unit_width // 2, seq_len), BF16),
            pltpu.VMEM((model_width // 2, seq_len), BF16),
            pltpu.VMEM((seq_len, model_width), BF16),
            pltpu.VMEM((seq_len, model_width), BF16),
            pltpu.VMEM((head_width // 2, seq_len), BF16),
            pltpu.VMEM((seq_len, 3 * head_width), BF16),
            pltpu.VMEM((seq_len, HD), F32),
            pltpu.VMEM((8, seq_len), F32),
            pltpu.VMEM((seq_len, HD), F32),
            pltpu.VMEM((seq_len, HD), F32),
            pltpu.SemaphoreType.REGULAR((2,)),
            DMA((8,)), DMA((3,)), DMA((3,)), DMA((8,)), DMA((8,)), DMA((8,)), DMA((8,)), DMA((15,)), DMA((15,)),
            DMA((8,)), DMA((8,)), DMA((8,)), DMA((8,)), DMA((8,)), DMA((8,)),
        ]
        + gather_scratch() * 4
        + scatter_scratch(share, model_width) + [DMA((14,))] * 6
        + sums_scratch(seq_len) * 2
        + grad_sum_scratch(reduce_weight.shape) + grad_sum_scratch(expand_weight.shape)
        + grad_sum_scratch(merge_weight.shape) + grad_sum_scratch(heads_weight.shape)
        + bring_scratch() * 4,
    )[:7]
    heads_grad, merge_grad, expand_grad, reduce_grad = (
        heads_grad.astype(F32), merge_grad.astype(F32), expand_grad.astype(F32), reduce_grad.astype(F32)
    )
    heads_mean, heads_square, heads_fresh = adamw(
        heads_weight, heads_grad, heads_first, heads_second, LR, DECAY
    )
    merge_mean, merge_square, merge_fresh = adamw(
        merge_weight, merge_grad, merge_first, merge_second, LR, DECAY
    )
    expand_mean, expand_square, expand_fresh = adamw(
        expand_weight, expand_grad, expand_first, expand_second, LR, DECAY
    )
    reduce_mean, reduce_square, reduce_fresh = adamw(
        reduce_weight, reduce_grad, reduce_first, reduce_second, LR, DECAY
    )
    gains_mean, gains_square, gains_fresh = adamw(
        norm_gains, gains_grad, gains_first, gains_second, LR_GAIN, 0.0
    )
    return (
        block_output,
        input_grad.astype(F32),
        heads_grad,
        heads_mean,
        heads_square,
        heads_fresh,
        heads_fresh.astype(jnp.bfloat16),
        merge_grad,
        merge_mean,
        merge_square,
        merge_fresh,
        merge_fresh.astype(jnp.bfloat16),
        expand_grad,
        expand_mean,
        expand_square,
        expand_fresh,
        expand_fresh.astype(jnp.bfloat16),
        reduce_grad,
        reduce_mean,
        reduce_square,
        reduce_fresh,
        reduce_fresh.astype(jnp.bfloat16),
        gains_grad,
        gains_mean,
        gains_square,
        gains_fresh,
    )


def solution(mesh):
    return jax.shard_map(
        on_device,
        mesh=mesh,
        in_specs=(
            P(("dp", "row"), "col"),
            P(("dp", "row"), "col"),
            P(("dp", "col"), None),
            P("col", "row"),
            P("col", "row"),
            P("col", "row"),
            P("row", "col"),
            P("row", "col"),
            P("row", "col"),
            P("col", "row"),
            P("col", "row"),
            P("col", "row"),
            P("row", "col"),
            P("row", "col"),
            P("row", "col"),
            P(),
            P(),
            P(),
        ),
        out_specs=(
            P(("dp", "row"), "col"),
            P(("dp", "row"), "col"),
            P("col", "row"),
            P("col", "row"),
            P("col", "row"),
            P("col", "row"),
            P("col", "row"),
            P("row", "col"),
            P("row", "col"),
            P("row", "col"),
            P("row", "col"),
            P("row", "col"),
            P("col", "row"),
            P("col", "row"),
            P("col", "row"),
            P("col", "row"),
            P("col", "row"),
            P("row", "col"),
            P("row", "col"),
            P("row", "col"),
            P("row", "col"),
            P("row", "col"),
            P(),
            P(),
            P(),
            P(),
        ),
        check_vma=False,
    )
```

```python
import math

import jax
import jax.numpy as jnp
from jax import lax
from jax.experimental import pallas as pl
from jax.experimental.pallas import tpu as pltpu
from jax.sharding import PartitionSpec as P

HD = 128
WINDOW = 256
STEP = 5


EPS = 1e-06
THETA = 500000.0
LR = 0.02
LR_GAIN = 0.2
BETA_ONE = 0.5
BETA_TWO = 0.5
DECAY = 0.1
ADAM_EPS = 1e-08

BF16 = jnp.bfloat16
SCATTER_LEFT, GATHER_LEFT, INPUT_LEFT = 8, 9, 16
F32 = jnp.float32
MESH = pl.DeviceIdType.MESH
ANY = pl.BlockSpec(memory_space=pl.ANY)
VMEM = pl.BlockSpec(memory_space=pltpu.VMEM)
DMA = pltpu.SemaphoreType.DMA


def documents(lengths, shape, axis):
    tokens = lax.broadcasted_iota(jnp.int32, shape, axis)
    docs, starts, end = jnp.zeros(shape, F32), jnp.zeros(shape, jnp.int32), jnp.int32(0)
    for j in range(lengths.shape[1]):
        end = end + lengths[0, j]
        passed = tokens >= end
        docs = docs + passed.astype(F32)
        starts = starts + jnp.where(passed, lengths[0, j], 0)
    return docs, starts


def adamw(weight, gradient, first_mom, second_mom, step_rate, decay_rate):
    mean_new = BETA_ONE * first_mom + (1.0 - BETA_ONE) * gradient
    square_new = BETA_TWO * second_mom + (1.0 - BETA_TWO) * gradient * gradient
    fix_one = 1.0 - BETA_ONE**STEP
    fix_two = 1.0 - BETA_TWO**STEP
    update = mean_new / fix_one / (jnp.sqrt(square_new / fix_two) + ADAM_EPS) + decay_rate * weight
    return (mean_new, square_new, weight - step_rate * update)


def here():
    return lax.axis_index("dp"), lax.axis_index("row"), lax.axis_index("col")


def row_peer(row, d):
    return (row // 4 + d // 4) % 2 * 4 + (row % 4 + d % 4) % 4


def z_peer(col, d):
    return (col // 2 + d) % 4 * 2 + col % 2


def z_source(col, d):
    return (col // 2 + 4 - d) % 4 * 2 + col % 2


def y_peer(col):
    return col // 2 * 2 + 1 - col % 2


def remote(source, target, sent, arrived, **where):
    return pltpu.make_async_remote_copy(
        src_ref=source,
        dst_ref=target,
        send_sem=sent,
        recv_sem=arrived,
        device_id=where,
        device_id_type=MESH,
    )


def meet(rows=False, cols=False, weights=False, core=False, spread_in=False, spread_out=False):
    dp, row, col = here()
    barrier = pltpu.get_barrier_semaphore()
    count = 0

    def greet(**where):
        pl.semaphore_signal(barrier, inc=1, device_id=where, device_id_type=MESH)

    if rows:
        for d in range(1, 8):
            greet(row=row_peer(row, d))
        count = count + 7
    if cols:
        for d in range(1, 8):
            greet(col=(col + d) % 8)
        count = count + 7
    if weights:
        greet(col=y_peer(col))
        for d in (1, 3):
            greet(col=z_peer(col, d))
        count = count + 3
    if core:
        greet(dp=1 - dp)
        count = count + 1
    for wanted, inward in ((spread_in, True), (spread_out, False)):
        if wanted:
            for k in range(8):
                at_row, at_col = (col, k) if inward else (k, row)

                @pl.when(jnp.logical_not((at_row == row) & (at_col == col)))
                def _():
                    greet(row=at_row, col=at_col)

            count = count + 8 - (row == col).astype(jnp.int32)
    pl.semaphore_wait(barrier, count)


class Spread:
    def __init__(self, inward, source, target, sent, arrived):
        dp, row, col = here()
        self.row, self.col, self.inward = row, col, inward
        self.copies = []
        for k in range(8):
            to_row, to_col = (k, row) if inward else (col, k)
            mine = (row == to_row) & (col == to_col)
            copy = remote(
                source(k),
                target(col if inward else row),
                sent.at[k],
                arrived.at[col if inward else row],
                row=to_row,
                col=to_col,
            )
            waiter = remote(source(k), target(k), sent.at[k], arrived.at[k], row=to_row, col=to_col)
            local = pltpu.make_async_copy(
                source(k), target(col if inward else row), sent.at[k]
            )
            self.copies.append((mine, copy, waiter, local))

    def start(self):
        for mine, copy, _, local in self.copies:
            pl.when(jnp.logical_not(mine))(copy.start)
            pl.when(mine)(local.start)

    def wait(self):
        for k, (mine, copy, waiter, local) in enumerate(self.copies):
            from_row, from_col = (self.col, k) if self.inward else (k, self.row)
            me = (from_row == self.row) & (from_col == self.col)
            pl.when(jnp.logical_not(me))(waiter.wait_recv)
            pl.when(jnp.logical_not(mine))(copy.wait_send)
            pl.when(mine)(local.wait)


def half_of(kind, ref, c, h):
    if kind == "tall":
        count = ref.shape[0] // 16
        return ref.at[pl.ds(pl.multiple_of((2 * c + h) * count, count), count)]
    count, width = ref.shape[0] // 2, ref.shape[1] // 8
    return ref.at[
        pl.ds(pl.multiple_of(h * count, count), count), pl.ds(pl.multiple_of(c * width, width), width)
    ]


def half_shard(ref, h):
    count = ref.shape[0] // 2
    return ref.at[pl.ds(pl.multiple_of(h * count, count), count)]


def mean_rate(values):
    return lax.rsqrt(jnp.mean(values * values, axis=-1, keepdims=True) + EPS)


def call(kernel, name, number, outs, ins, in_specs, out_specs, scratch):
    return pl.pallas_call(
        kernel,
        name=name,
        out_shape=outs,
        in_specs=in_specs,
        out_specs=out_specs,
        scratch_shapes=scratch,
        compiler_params=pltpu.CompilerParams(
            collective_id=number, has_side_effects=True, vmem_limit_bytes=62 * 2**20
        ),
    )(*ins)


def struct(shape, kind):
    return jax.ShapeDtypeStruct(shape, kind)


def dot(left, right):
    return jnp.dot(left, right, preferred_element_type=F32)


def dot_flipped(left, right):
    return lax.dot_general(left, right, (((1,), (1,)), ((), ())), preferred_element_type=F32)


def span(k, count):
    return pl.ds(pl.multiple_of(k * count, count), count)


def near_row(row, dx, dy):
    return (row // 4 + dy) % 2 * 4 + (row % 4 + dx) % 4


class Scatter:
    def __init__(self, part, total, from_y, from_x, last_y, last_x, stage_y, stage_x, sent, arrived):
        dp, row, col = here()
        self.row, self.part, self.total = row, part, total
        self.from_y, self.from_x, self.last_y, self.last_x = from_y, from_x, last_y, last_x
        self.stage_y, self.stage_x = stage_y, stage_x
        self.count, self.left = total.shape[0], from_x.shape[3]
        self.sides = (pl.ds(0, self.left), pl.ds(self.left, total.shape[1] - self.left))
        number = iter(range(14))

        def copy(source, target, dx, dy):
            i = next(number)
            return remote(source, target, sent.at[i], arrived.at[i], row=near_row(row, dx, dy))

        self.y_first = {dx: copy(self.block(dx, 1, 1), from_y.at[dx], 0, 1) for dx in (1, 3, 2, 0)}
        self.x_first = {
            (dx, dy): copy(self.block(dx, dy, 0), from_x.at[dy, dx - 1], dx, 0)
            for dy in (1, 0)
            for dx in (1, 3, 2)
        }
        self.x_last = {dx: copy(stage_x.at[dx - 1], last_x.at[dx - 1], dx, 0) for dx in (1, 3, 2)}
        self.y_last = copy(stage_y, last_y, 0, 1)

    def block(self, dx, dy, side):
        return self.part.at[span(near_row(self.row, dx, dy), self.count), self.sides[side]]

    def start_right(self):
        for copy in self.y_first.values():
            copy.start()

    def start_left(self):
        for copy in self.x_first.values():
            copy.start()

    def chunks(self, body):
        @pl.loop(0, self.count // 16)
        def _(i):
            body(span(i, 16))

    def middle(self):
        for dx in (1, 3, 2):
            self.y_first[dx].wait_recv()
            own = self.block(dx, 0, 1)

            def add(at):
                self.stage_x[dx - 1, at] = (own[at].astype(F32) + self.from_y[dx, at].astype(F32)).astype(BF16)

            self.chunks(add)
            self.x_last[dx].start()
        for dx in (1, 3, 2):
            self.x_first[dx, 1].wait_recv()
        other = self.block(0, 1, 0)

        def add(at):
            total = other[at].astype(F32)
            for k in range(3):
                total = total + self.from_x[1, k, at].astype(F32)
            self.stage_y[at] = total.astype(BF16)

        self.chunks(add)
        self.y_last.start()

    def end(self):
        self.y_first[0].wait_recv()
        for dx in (1, 3, 2):
            self.x_first[dx, 0].wait_recv()
            self.x_last[dx].wait_recv()
        self.y_last.wait_recv()
        left, right = self.block(0, 0, 0), self.block(0, 0, 1)

        def add(at):
            total = left[at].astype(F32) + self.last_y[at].astype(F32)
            for k in range(3):
                total = total + self.from_x[0, k, at].astype(F32)
            self.total[at, self.sides[0]] = total
            total = right[at].astype(F32) + self.from_y[0, at].astype(F32)
            for k in range(3):
                total = total + self.last_x[k, at].astype(F32)
            self.total[at, self.sides[1]] = total

        self.chunks(add)

    def finish(self):
        for copies in (self.y_first, self.x_first, self.x_last):
            for copy in copies.values():
                copy.wait_send()
        self.y_last.wait_send()


def scatter_scratch(share, width):
    left = SCATTER_LEFT * width // 16
    right = width - left
    return [
        pltpu.VMEM((share, width), F32),
        pltpu.VMEM((4, share, right), BF16),
        pltpu.VMEM((2, 3, share, left), BF16),
        pltpu.VMEM((share, left), BF16),
        pltpu.VMEM((3, share, right), BF16),
        pltpu.VMEM((share, left), BF16),
        pltpu.VMEM((3, share, right), BF16),
        DMA((14,)),
        DMA((14,)),
    ]


class Gather:
    def __init__(self, whole, share, left, sent, arrived):
        dp, row, col = here()
        self.row = row
        number = iter(range(19))
        sides = (pl.ds(0, left), pl.ds(left, whole.shape[1] - left))
        right = left < whole.shape[1]

        def copy(fx, fy, side, dx, dy, start=0, count=share):
            i = next(number)
            k = near_row(row, fx, fy)
            ref = whole.at[pl.ds(pl.multiple_of(k * share + start, count), count), sides[side]]
            return remote(ref, ref, sent.at[i], arrived.at[i], row=near_row(row, dx, dy))

        part = share // 2
        steps = (1, 3, 2)
        two = steps[:2]
        self.y_left = copy(0, 0, 0, 0, 1)
        self.x_left = [copy(0, 0, 0, dx, 0) for dx in two]
        self.on_left = [copy(4 - dx, 0, 0, dx, 0, i * part, part) for i, dx in enumerate(two)]
        self.y_right, self.x_right, self.y_near, self.on_other = [], [], [], []
        if right:
            self.x_other = [copy(0, 1, 0, dx, 0) for dx in steps]
            self.y_right = [copy(0, 0, 1, 0, 1)]
            self.x_right = [copy(0, 0, 1, dx, 0) for dx in steps]
            self.y_near = [copy(4 - dx, 0, 1, 0, 1) for dx in steps]
        else:
            self.x_other = [copy(0, 1, 0, dx, 0) for dx in two]
            self.on_other = [copy(4 - dx, 1, 0, dx, 0, i * part, part) for i, dx in enumerate(two)]

    def start(self):
        for copy in (self.y_left, *self.x_right, *self.y_right, *self.x_left):
            copy.start()

    def relay(self):
        self.y_left.wait_recv()
        for copy in self.x_other:
            copy.start()
        for i, came in enumerate(self.x_right):
            came.wait_recv()
            self.y_near[i].start()

    def relay_again(self):
        for i in range(2):
            self.x_left[i].wait_recv()
            self.on_left[i].start()
        for i, copy in enumerate(self.on_other):
            self.x_other[i].wait_recv()
            copy.start()

    def wait(self):
        for copy in (*self.y_right, *self.x_other[len(self.on_other) :], *self.on_left, *self.on_other, *self.y_near):
            copy.wait_recv()
        for copy in (self.y_left, *self.x_left, *self.x_other, *self.on_left, *self.on_other, *self.y_right,
                     *self.x_right, *self.y_near):
            copy.wait_send()


def gather_scratch():
    return [DMA((19,)), DMA((19,))]


def cols(ref, k, width):
    return ref.at[:, pl.ds(pl.multiple_of(k * width, width), width)]


def rows_of(ref, k, count):
    return ref.at[pl.ds(pl.multiple_of(k * count, count), count)]


def back_of(grad, values, gain):
    rate = mean_rate(values)
    hat = values * rate
    grad_hat = grad * gain
    dots = jnp.mean(grad_hat * hat, axis=-1, keepdims=True)
    return hat, rate * (grad_hat - hat * dots)


class GradSum:
    def __init__(self, kind, part, out, between, far, near, sent, arrived):
        dp, _, col = here()
        self.kind, self.part, self.col = kind, part, col
        self.between, self.far, self.near = between, far, near
        self.rows, self.width = near.shape[1], near.shape[2]
        number = iter(range(10))

        def copy(source, target, **where):
            i = next(number)
            return remote(source, target, sent.at[i], arrived.at[i], **where)

        self.steps = (1, 3)
        self.on = [
            [
                copy(self.piece(self.z_block(2, k), i), between.at[i, k], col=z_peer(col, d))
                for k in range(2)
            ]
            for i, d in enumerate(self.steps)
        ]
        self.zs = [
            [copy(self.block(self.z_block(d, k)), far.at[i, k], col=z_peer(col, d)) for k in range(2)]
            for i, d in enumerate(self.steps)
        ]
        self.ys = copy(near.at[0], near.at[1], col=y_peer(col))
        self.last = copy(near.at[0], half_shard(out, dp), dp=1 - dp)
        self.keep = pltpu.make_async_copy(near.at[0], half_shard(out, dp), sent.at[10])

    def z_block(self, d, k):
        return z_peer(self.col, d) // 2 * 2 + k

    def block(self, c):
        if self.kind == "tall":
            return self.part.at[span(c, self.rows)]
        return self.part.at[:, span(c, self.width)]

    def piece(self, c, i):
        return self.block(c).at[pl.ds(i * (self.rows // 2), self.rows // 2)]

    def each(self, rows, body):
        count = min(rows, 32768 // self.width // 16 * 16)

        @pl.loop(0, rows // count)
        def _(i):
            body(span(i, count))

    def start(self):
        for pair in self.on:
            for copy in pair:
                copy.start()

    def over_z(self):
        for i, d in enumerate(self.steps):
            for k in range(2):
                self.on[i][k].wait_recv()
                own = self.piece(self.z_block(d, k), i)

                def add(at):
                    own[at] = (own[at].astype(F32) + self.between[i, k, at].astype(F32)).astype(BF16)

                self.each(self.rows // 2, add)
                self.zs[i][k].start()

    def over_y(self):
        for pair in self.zs:
            for copy in pair:
                copy.wait_recv()
        yl = self.col % 2
        keep, give = self.block(self.col), self.block(y_peer(self.col))

        def total(at, ref, k):
            return (
                ref[at].astype(F32) + self.far[0, k, at].astype(F32) + self.far[1, k, at].astype(F32)
            ).astype(BF16)

        def add(at):
            self.near[0, at] = total(at, give, 1 - yl)

        self.each(self.rows, add)
        self.ys.start()

        def add(at):
            keep[at] = total(at, keep, yl)

        self.each(self.rows, add)
        for pair in (*self.zs, *self.on):
            for copy in pair:
                copy.wait_send()

    def end(self):
        self.ys.wait()
        keep = self.block(self.col)

        def add(at):
            self.near[0, at] = (keep[at].astype(F32) + self.near[1, at].astype(F32)).astype(BF16)

        self.each(self.rows, add)
        self.last.start()
        self.keep.start()

    def wait(self):
        self.last.wait()
        self.keep.wait()


def grad_sum_scratch(shape):
    rows, width = shape[0] // 2, shape[1]
    return [
        pltpu.VMEM((2, 2, rows // 2, width), BF16),
        pltpu.VMEM((2, 2, rows, width), BF16),
        pltpu.VMEM((2, rows, width), BF16),
        DMA((11,)),
        DMA((10,)),
    ]


class Bring:
    def __init__(self, kind, shape, whole, sent, arrived):
        dp, _, col = here()
        rows, width = shape
        near = y_peer(col)
        number = iter(range(20))

        def block(c, s=None):
            count, at = (rows // 2, dp) if s is None else (rows // 4, 2 * dp + s)
            if kind == "tall":
                return whole.at[span((2 if s is None else 4) * c + at, count)]
            return whole.at[span(at, count), span(c, width)]

        def copy(source, target, **where):
            i = next(number)
            return remote(source, target, sent.at[i], arrived.at[i], **where)

        self.place = whole.at[span(col, rows)] if kind == "tall" else whole.at[:, span(col, width)]
        self.y_own = copy(block(col), block(col), col=near)
        self.z_own = [copy(block(col), block(col), col=z_peer(col, d)) for d in (1, 3)]
        self.z_near = [copy(block(near), block(near), col=z_peer(col, d)) for d in (1, 3)]
        self.on, self.on_near, self.a_own, self.a_near = [], [], [], []
        self.a_far, self.a_far_near = [], []
        for i, d in enumerate((1, 3)):
            came, two = z_source(col, d), z_peer(col, 2)
            self.on.append(copy(block(came, i), block(came, i), col=z_peer(col, d)))
            self.on_near.append(copy(block(y_peer(came), i), block(y_peer(came), i), col=z_peer(col, d)))
            self.a_own.append(copy(block(came), block(came), dp=1 - dp))
            self.a_near.append(copy(block(y_peer(came)), block(y_peer(came)), dp=1 - dp))
            self.a_far.append(copy(block(two, i), block(two, i), dp=1 - dp))
            self.a_far_near.append(copy(block(y_peer(two), i), block(y_peer(two), i), dp=1 - dp))
        self.a_y = copy(block(near), block(near), dp=1 - dp)

    def start_y(self):
        self.y_own.start()

    def start_z(self):
        for copy in self.z_own:
            copy.start()

    def relay(self):
        self.y_own.wait_recv()
        for copy in (*self.z_near, self.a_y):
            copy.start()

    def relay_own(self):
        for i in range(2):
            self.z_own[i].wait_recv()
            self.on[i].start()
            self.a_own[i].start()

    def relay_near(self):
        for i in range(2):
            self.z_near[i].wait_recv()
            self.on_near[i].start()
            self.a_near[i].start()

    def hand_over(self):
        for i in range(2):
            self.on[i].wait_recv()
            self.a_far[i].start()
        for i in range(2):
            self.on_near[i].wait_recv()
            self.a_far_near[i].start()

    def wait(self):
        for copy in (self.a_y, *self.a_own, *self.a_near, *self.a_far, *self.a_far_near):
            copy.wait()
        for copy in (self.y_own, *self.z_own, *self.z_near, *self.on, *self.on_near):
            copy.wait_send()


def bring_scratch():
    return [DMA((20,)), DMA((20,))]


class SpreadIn:
    def __init__(self, source, target, sent, arrived):
        dp, row, col = here()
        self.row, self.col = row, col
        self.copies, self.waits = [], []
        for k in range(8):
            out = remote(source(k), target(k, col), sent.at[k], arrived.at[col], row=k, col=row)
            came = remote(source(k), target(row, k), sent.at[k], arrived.at[k], row=k, col=row)
            local = pltpu.make_async_copy(source(k), target(k, col), sent.at[k])
            self.copies.append(((row == k) & (row == col), out, local))
            self.waits.append(((row == col) & (col == k), came))

    def start(self):
        for mine, out, local in self.copies:
            pl.when(jnp.logical_not(mine))(out.start)
            pl.when(mine)(local.start)

    def wait(self):
        for mine, came in self.waits:
            pl.when(jnp.logical_not(mine))(came.wait_recv)
        for mine, out, local in self.copies:
            pl.when(jnp.logical_not(mine))(out.wait_send)
            pl.when(mine)(local.wait)


class TokenSums:
    def __init__(self, stats, mine, came, sent, arrived):
        dp, row, col = here()
        self.stats, self.mine, self.came = stats, mine, came
        self.copies = [
            remote(mine, came.at[d - 1], sent.at[d - 1], arrived.at[d - 1], row=row_peer(row, d))
            for d in range(1, 8)
        ]

    def put(self, at, one, two):
        lane = lax.broadcasted_iota(jnp.int32, (one.shape[0], 128), 1)
        self.stats[at] = jnp.where(lane == 0, one, jnp.where(lane == 1, two, 0.0))

    def start(self):
        self.mine[...] = self.stats[...].T[:8]
        for copy in self.copies:
            copy.start()

    def end(self):
        total = self.mine[...]
        for d, copy in enumerate(self.copies):
            copy.wait_recv()
            total = total + self.came[d]
        self.stats[...] = jnp.concatenate([total] * 16, axis=0).T
        for copy in self.copies:
            copy.wait_send()


def sums_scratch(tokens):
    return [pltpu.VMEM((8, tokens), F32), pltpu.VMEM((7, 8, tokens), F32), DMA((7,)), DMA((7,))]


def turn(values, cosine, sine):
    heads = [values[:, i : i + HD] for i in range(0, values.shape[1], HD)]
    return jnp.concatenate([h * cosine + pltpu.roll(h, HD // 2, 1) * sine for h in heads], axis=1)


QUERY_BLOCK = 128


def key_span(b):
    start = max(0, b * QUERY_BLOCK - WINDOW)
    return start, (b + 1) * QUERY_BLOCK - start


UPDATE_STEPS = 4


def update_kernel(*refs):
    ins, outs = refs[:22], refs[22:]
    outs[0][...] = ins[0][...]
    outs[1][...] = ins[1][...].astype(F32)
    for i in range(4):
        gradient, weight, first_mom, second_mom = (ref[...] for ref in ins[2 + 4 * i : 6 + 4 * i])
        gradient = gradient.astype(F32)
        mean, square, fresh = adamw(weight, gradient, first_mom, second_mom, LR, DECAY)
        for ref, value in zip(outs[2 + 5 * i : 7 + 5 * i], (gradient, mean, square, fresh, fresh), strict=True):
            ref[...] = value.astype(ref.dtype)

    @pl.when(pl.program_id(0) == 0)
    def _():
        gradient, weight, first_mom, second_mom = (ref[...] for ref in ins[18:])
        mean, square, fresh = adamw(weight, gradient, first_mom, second_mom, LR_GAIN, 0.0)
        for ref, value in zip(outs[22:], (gradient, mean, square, fresh), strict=True):
            ref[...] = value


def update(block_output, input_grad, *groups):
    def part(shape):
        return pl.BlockSpec((shape[0] // UPDATE_STEPS, shape[1]), lambda i: (i, 0))

    ins, outs, in_specs, out_specs = [block_output, input_grad], [], [], []
    outs += [struct(block_output.shape, BF16), struct(input_grad.shape, F32)]
    in_specs += [part(block_output.shape)] * 2
    out_specs += [part(block_output.shape)] * 2
    for group in groups[:4]:
        shape = group[0].shape
        ins += group
        in_specs += [part(shape)] * 4
        outs += [struct(shape, F32)] * 4 + [struct(shape, BF16)]
        out_specs += [part(shape)] * 5
    whole = pl.BlockSpec(groups[4][0].shape, lambda i: (0, 0))
    ins += groups[4]
    in_specs += [whole] * 4
    outs += [struct(groups[4][0].shape, F32)] * 4
    out_specs += [whole] * 4
    return tuple(
        pl.pallas_call(
            update_kernel,
            name="update",
            grid=(UPDATE_STEPS,),
            out_shape=outs,
            in_specs=in_specs,
            out_specs=out_specs,
            compiler_params=pltpu.CompilerParams(vmem_limit_bytes=62 * 2**20),
        )(*ins)
    )


def layer_kernel(
    x, g_in, heads_in, merge_in, expand_in, reduce_in, lengths, gain_all,
    out, input_grad, gains_grad, heads_grad, merge_grad, expand_grad, reduce_grad, xs_keep, raw_keep, qkv_keep,
    rows, turned, expand, reduce, heads, merge, gate, up, act, act_turned, part, back, hidden, probs, mix, mix_turned,
    rates, stats, grad_mix, done, final, grad_resid, merged, residual, g, sums, grad_gate,
    gains, gain_row, gain_col, gain_core, gain_sum, act_other, turned_other, hidden_other, back_other, mix_other,
    joined_other, values_part, docs, doc_row, cosine, sine, free, load, keep, late, osent, ocame, isent, icame, nsent, ncame, xsent, xcame,
    asent, acame, bsent, bcame, g1sent, g1came, g2sent, g2came, g3sent, g3came, g4sent, g4came, g5sent, g5came, g6sent, g6came, *refs,
):
    dp, row, col = here()
    share, width = residual.shape
    tokens, units = act.shape
    head_width = mix.shape[1]
    tiles = units // 256
    n, first_right = width // 512, SCATTER_LEFT * width // 16 // 256
    gain_query, gain_key = (gain_all.at[i : i + 1, span(row, head_width)] for i in range(2))
    gain_merge, gain_reduce = (gain_all.at[i : i + 1] for i in range(2, 4))
    batch, half_share = tokens // 2, share // 2

    def scatter_of(i, m=None):
        sems = refs[7 + 2 * i : 9 + 2 * i]
        if m is None:
            return Scatter(part, *refs[:7], *sems)
        at = pl.ds(m * half_share, half_share)
        total, from_y, from_x, last_y, last_x, stage_y, stage_x = refs[:7]
        return Scatter(
            part.at[pl.ds(m * batch, batch)], total.at[at], from_y.at[:, at], from_x.at[:, :, at], last_y.at[at],
            last_x.at[:, at], stage_y.at[at], stage_x.at[:, at], *sems,
        )

    merge_scatter, input_scatter = scatter_of(0), scatter_of(5)
    reduced_scatter = [scatter_of(1 + m, m) for m in range(2)]
    branch_scatter = [scatter_of(3 + m, m) for m in range(2)]
    first_sums = TokenSums(rates, *refs[19:23])
    token_sums = TokenSums(stats, *refs[23:27])
    half_units, half_width, half_heads = units // 2, width // 2, head_width // 2
    reduce_part, merge_part_ref = reduce.at[pl.ds(0, half_units)], merge.at[pl.ds(0, half_heads)]
    expand_part, heads_part = expand.at[pl.ds(0, half_width)], heads.at[pl.ds(0, half_width)]
    reduce_sum = GradSum("wide", reduce_part, reduce_grad, *refs[27:32])
    expand_sum = GradSum("tall", expand_part, expand_grad, *refs[32:37])
    merge_sum = GradSum("wide", merge_part_ref, merge_grad, *refs[37:42])
    values_at, others_at = pl.ds(2 * head_width, head_width), pl.ds(0, 2 * head_width)
    values_sum = GradSum("tall", values_part, heads_grad.at[:, values_at], *refs[42:47])
    heads_sum = GradSum("tall", heads_part.at[:, others_at], heads_grad.at[:, others_at], *refs[47:52])
    bring_heads = Bring("tall", heads_in.shape, heads, *refs[52:54])
    bring_merge = Bring("wide", merge_in.shape, merge, *refs[54:56])
    bring_reduce = Bring("wide", reduce_in.shape, reduce, *refs[56:58])
    bring_expand = Bring("tall", expand_in.shape, expand, *refs[58:60])
    gather_x = Gather(back, share, INPUT_LEFT * width // 16, g1sent, g1came)
    left = GATHER_LEFT * width // 16
    row_gather = [
        Gather(rows.at[pl.ds(m * batch, batch)], half_share, left, *sems)
        for m, sems in enumerate(((g2sent, g2came), (g3sent, g3came)))
    ]
    gather = [
        Gather(back.at[pl.ds(m * batch, batch)], half_share, left, *sems)
        for m, sems in enumerate(((g4sent, g4came), (g5sent, g5came)))
    ]
    last_gather = Gather(back, share, left, g6sent, g6came)
    spread_x = SpreadIn(
        lambda k: rows_of(x, k, share), lambda k, c: back.at[span(k, share), span(c, 256)], asent, acame
    )
    spread_g = SpreadIn(lambda k: rows_of(g_in, k, share), lambda k, c: g.at[:, span(c, 256)], bsent, bcame)
    spread = Spread(False, lambda k: cols(done, k, 256), lambda k: rows_of(out, k, 64), osent, ocame)
    spread_grad = Spread(False, lambda k: cols(final, k, 256), lambda k: rows_of(input_grad, k, 64), isent, icame)
    row_gains = [
        remote(gains, gain_row.at[row], nsent.at[d - 1], ncame.at[d - 1], row=row_peer(row, d))
        for d in range(1, 8)
    ]
    col_gains = [
        remote(gain_sum.at[0], gain_col.at[col], nsent.at[6 + d], ncame.at[6 + d], col=(col + d) % 8)
        for d in range(1, 8)
    ]
    core_gains = remote(gain_sum.at[1], gain_core, nsent.at[14], ncame.at[14], dp=1 - dp)

    raw, qkv, new_rows = up.at[:, : 2 * head_width], act.at[:, : 3 * head_width], back
    heads_change = gate.at[:, : 3 * head_width]
    joined = hidden.at[:, : 3 * head_width]
    puts = [
        pltpu.make_async_copy(source, target, keep.at[i])
        for i, (source, target) in enumerate(((back, xs_keep), (raw, raw_keep), (qkv, qkv_keep)))
    ]
    get_xs = pltpu.make_async_copy(xs_keep, rows, late.at[0])
    get_raw = pltpu.make_async_copy(raw_keep, raw, late.at[1])
    get_qkv = pltpu.make_async_copy(qkv_keep, qkv, late.at[2])

    shard_rows, quarter = heads_in.shape[0], reduce_in.shape[0] // 4
    heads32 = gate.at[:shard_rows, : heads_in.shape[1]]
    merge32 = gate.at[:shard_rows, heads_in.shape[1] :]
    reduce32 = [gate.at[shard_rows:, pl.ds(i * 256, 256)] for i in range(4)]
    expand32 = [up.at[pl.ds(i * shard_rows, shard_rows)] for i in range(2)]
    moves = (
        [(heads_in, heads32), (merge_in, merge32)]
        + [(reduce_in.at[pl.ds(i * quarter, quarter)], reduce32[i]) for i in range(4)]
        + [(expand_in.at[:, pl.ds(i * units, units)], expand32[i]) for i in range(2)]
    )
    loads = [pltpu.make_async_copy(source, target, load.at[i]) for i, (source, target) in enumerate(moves)]
    for copy in loads:
        copy.start()

    def narrow(i, target):
        loads[i].wait()
        source = moves[i][1]

        @pl.loop(0, source.shape[0] // 16)
        def _(k):
            at = span(k, 16)
            target[at] = source[at].astype(BF16)

    def hand(i, source, target):
        return remote(source, target, xsent.at[i], xcame.at[i], dp=1 - dp)

    hand_act = hand(0, act_turned.at[span(1 - dp, half_units)], act_other)
    hand_rows = hand(1, turned.at[span(1 - dp, half_width)], turned_other)
    hand_back = hand(2, back, back_other)
    hand_hidden = hand(3, hidden, hidden_other)
    hand_mix = hand(4, mix_turned.at[span(1 - dp, half_heads)], mix_other)
    hand_new = hand(5, back, back_other)
    hand_xs = hand(6, turned.at[span(1 - dp, half_width)], turned_other)
    hand_joined = hand(7, joined.at[:, others_at], joined_other.at[:, others_at])
    hand_values = hand(8, joined.at[:, values_at], joined_other.at[:, values_at])

    def turn_rows(j):
        values = rows[:, span(j, 256)].T
        turned[span(j, 128), :] = values[:128]
        turned[span(2 * tiles + j, 128), :] = values[128:]

    def two(target, at, wide, own, own_at, right, other, right_other):
        target[at, wide] = (
            dot(own[own_at, :], right[:, wide]) + dot(other[at, :], right_other[:, wide])
        ).astype(BF16)

    meet(rows=True, cols=True, core=True, spread_in=True, spread_out=True)
    spread_x.start()
    narrow(0, bring_heads.place)
    bring_heads.start_y()
    bring_heads.start_z()
    narrow(1, bring_merge.place)
    bring_merge.start_y()
    bring_merge.start_z()
    for i in range(4):
        narrow(2 + i, bring_reduce.place.at[pl.ds(i * quarter, quarter)])
    for i in range(2):
        narrow(6 + i, bring_expand.place.at[:, pl.ds(i * units, units)])
    spread_x.wait()
    gather_x.start()
    bring_heads.relay()
    bring_heads.relay_own()
    gather_x.relay()
    bring_expand.start_y()
    bring_reduce.start_y()
    bring_heads.relay_near()
    bring_merge.relay()
    gather_x.relay_again()
    bring_merge.relay_own()
    bring_heads.hand_over()
    bring_merge.relay_near()
    bring_expand.start_z()
    bring_reduce.start_z()
    docs[...], starts = documents(lengths, docs.shape, 0)
    doc_row[...], _ = documents(lengths, doc_row.shape, 1)
    lane = lax.broadcasted_iota(jnp.int32, docs.shape, 1)
    frequency = jnp.exp((lane % (HD // 2)).astype(F32) * (-2.0 / HD * math.log(THETA)))
    angles = (lax.broadcasted_iota(jnp.int32, docs.shape, 0) - starts).astype(F32) * frequency
    cosine[...] = jnp.cos(angles)
    sine[...] = jnp.where(lane < HD // 2, -1.0, 1.0) * jnp.sin(angles)
    gather_x.wait()
    bring_heads.wait()
    puts[0].start()

    for i in range(2):
        raw[:, i * head_width : (i + 1) * head_width] = dot(
            back[...], heads[:, i * head_width : (i + 1) * head_width]
        )

    @pl.loop(0, tokens // 64)
    def _(i):
        at = span(i, 64)
        squares = raw[at] * raw[at]
        first_sums.put(
            at,
            jnp.sum(squares[:, :head_width], axis=1, keepdims=True),
            jnp.sum(squares[:, head_width:], axis=1, keepdims=True),
        )

    first_sums.start()
    qkv[:, 2 * head_width :] = dot(back[...], heads[:, 2 * head_width :]).astype(BF16)
    bring_merge.hand_over()
    bring_expand.relay()
    bring_reduce.relay()
    first_sums.end()
    spread_g.start()

    @pl.loop(0, tokens // 64)
    def _(i):
        at = span(i, 64)
        rate = lax.rsqrt(rates[at] * (1.0 / width) + EPS)
        rates[at] = rate
        for j, gain in enumerate((gain_query, gain_key)):
            some = slice(j * head_width, (j + 1) * head_width)
            hat = raw[at, some] * rate[:, j : j + 1]
            qkv[at, some] = turn(hat * gain[...], cosine[at], sine[at]).astype(BF16)

    puts[1].start()
    puts[2].start()
    for b in range(tokens // QUERY_BLOCK):
        start, count = key_span(b)
        query_at = pl.ds(b * QUERY_BLOCK, QUERY_BLOCK)
        key_at = pl.ds(start, count)
        there = lax.broadcasted_iota(jnp.int32, (QUERY_BLOCK, count), 0) + (b * QUERY_BLOCK - start)
        distance = there - lax.broadcasted_iota(jnp.int32, (QUERY_BLOCK, count), 1)
        doc = docs[query_at, 0:1]
        allowed = (doc == doc_row[0:1, start : start + count]) & (distance >= 0) & (distance < WINDOW)
        live = (doc < 5.0).astype(F32)
        for h in range(head_width // HD):
            query, key, value = (
                slice(i * head_width + h * HD, i * head_width + (h + 1) * HD) for i in range(3)
            )
            scores = dot_flipped(qkv[query_at, query], qkv[key_at, key]) * HD**-0.5
            scores = jnp.where(allowed, scores, -1e30)
            weights = jnp.exp(scores - jnp.max(scores, axis=1, keepdims=True))
            shares = (weights / jnp.sum(weights, axis=1, keepdims=True)).astype(BF16)
            probs[h, b, :, :count] = shares
            if count < probs.shape[3]:
                probs[h, b, :, count:] = jnp.zeros((QUERY_BLOCK, probs.shape[3] - count), BF16)
            mix[query_at, h * HD : (h + 1) * HD] = (dot(shares, qkv[key_at, value]) * live).astype(BF16)

    bring_merge.wait()

    def merge_part(j):
        at = span(j, 256)
        part[:, at] = dot(mix[...], merge[:, at]).astype(BF16)

    pl.loop(first_right, 2 * n)(merge_part)
    merge_scatter.start_right()
    pl.loop(0, first_right)(merge_part)
    merge_scatter.start_left()
    bring_expand.relay_own()
    bring_reduce.relay_own()
    merge_scatter.middle()
    bring_expand.relay_near()
    bring_reduce.relay_near()
    merge_scatter.end()

    def place(i):
        per = half_share // 16
        return pl.ds(pl.multiple_of(i // per * batch + row * half_share + i % per * 16, 16), 16)

    @pl.loop(0, share // 16)
    def _(i):
        at = span(i, 16)
        total = merge_scatter.total[at]
        merged[at] = total
        mine = pl.ds(pl.multiple_of(row * share + i * 16, 16), 16)
        result = back[mine, :].astype(F32) + total * mean_rate(total) * gain_merge[...]
        residual[at] = result
        rows[place(i), :] = result.astype(BF16)

    row_gather[0].start()
    row_gather[0].relay()
    row_gather[1].start()
    bring_expand.hand_over()
    row_gather[0].relay_again()
    row_gather[1].relay()
    bring_reduce.hand_over()
    row_gather[0].wait()
    row_gather[1].relay_again()
    merge_scatter.finish()
    bring_expand.wait()
    for copy in puts:
        copy.wait()

    def rows_in(m):
        return pl.ds(m * batch, batch)

    def gated(m):
        mine = rows_in(m)

        @pl.loop(0, tiles)
        def _(j):
            at = span(j, 256)
            gate[mine, at] = dot(rows[mine, :], expand[:, at])
            up[mine, at] = dot(rows[mine, :], expand[:, span(tiles + j, 256)])

            @pl.loop(m * (batch // 64), (m + 1) * (batch // 64))
            def _(i):
                some = span(i, 64)
                x = gate[some, at]
                act[some, at] = (x * jax.nn.sigmoid(x) * up[some, at]).astype(BF16)

    def reduced(m):
        mine = rows_in(m)

        def product(j):
            at = span(j, 256)
            part[mine, at] = dot(act[mine, :], reduce[:, at]).astype(BF16)

        pl.loop(first_right, 2 * n)(product)
        reduced_scatter[m].start_right()
        pl.loop(0, first_right)(product)
        reduced_scatter[m].start_left()

    def output_norm(m):
        @pl.loop(m * (half_share // 16), (m + 1) * (half_share // 16))
        def _(i):
            at = span(i, 16)
            grad = g[at].astype(F32)
            hat, change = back_of(grad, merge_scatter.total[at], gain_reduce[...])
            back[place(i), :] = change.astype(BF16)
            done[at] = (residual[at] + hat * gain_reduce[...]).astype(BF16)
            product = grad * hat
            sums[...] += product[:8] + product[8:]

    def activity_gradient(m):
        mine = rows_in(m)

        @pl.loop(0, tiles)
        def _(j):
            at, up_at = span(j, 256), span(tiles + j, 256)
            grad_gate[mine, :] = dot_flipped(back[mine, :], reduce[at, :])

            @pl.loop(m * (batch // 64), (m + 1) * (batch // 64))
            def _(i):
                some = span(i, 64)
                x, change = gate[some, at], grad_gate[some]
                s = jax.nn.sigmoid(x)
                hidden[some, at] = (change * up[some, at] * s * (1.0 + x * (1.0 - s))).astype(BF16)
                hidden[some, up_at] = (change * (x * s)).astype(BF16)

    def branch(m):
        mine = rows_in(m)

        def product(j):
            at = span(j, 256)
            part[mine, at] = dot_flipped(hidden[mine, :], expand[at, :]).astype(BF16)

        pl.loop(first_right, 2 * n)(product)
        branch_scatter[m].start_right()
        pl.loop(0, first_right)(product)
        branch_scatter[m].start_left()

    gated(0)
    bring_reduce.wait()
    reduced(0)
    row_gather[1].wait()
    gated(1)
    reduced_scatter[0].middle()
    reduced(1)
    spread_g.wait()
    sums[...] = jnp.zeros_like(sums)
    reduced_scatter[0].end()
    output_norm(0)
    gather[0].start()

    @pl.loop(0, tiles)
    def _(j):
        at = span(j, 256)
        act_turned[at, :] = act[:, at].T

    hand_act.start()
    get_qkv.start()
    reduced_scatter[1].middle()
    gather[0].relay()
    reduced_scatter[1].end()
    output_norm(1)
    gather[1].start()
    gather[0].relay_again()
    gains[...] = jnp.zeros_like(gains)
    gains[3:4] = jnp.sum(sums[...], axis=0, keepdims=True)
    for m in range(2):
        reduced_scatter[m].finish()
    pl.loop(0, 2 * tiles)(turn_rows)
    hand_rows.start()
    get_xs.start()
    gather[0].wait()
    gather[1].relay()
    activity_gradient(0)
    gather[1].relay_again()
    branch(0)
    gather[1].wait()
    hand_back.start()
    activity_gradient(1)
    hand_hidden.start()
    get_raw.start()
    branch_scatter[0].middle()
    branch(1)
    spread.start()
    hand_act.wait()
    hand_back.wait()
    halves = [pl.ds(side * (width // 2), width // 2) for side in range(2)]

    @pl.loop(0, tiles // 2)
    def _(j):
        for wide in halves:
            two(reduce, span(j, 256), wide, act_turned, span(dp * (tiles // 2) + j, 256), back, act_other, back_other)

    pl.semaphore_signal(free.at[0], inc=1, device_id={"dp": 1 - dp}, device_id_type=MESH)
    reduce_sum.start()
    branch_scatter[0].end()
    branch_scatter[1].middle()
    hand_rows.wait()
    hand_hidden.wait()

    @pl.loop(0, tiles)
    def _(j):
        for wide in halves:
            two(expand, span(j, 256), wide, turned, span(dp * tiles + j, 256), hidden, turned_other, hidden_other)

    pl.semaphore_signal(free.at[1], inc=1, device_id={"dp": 1 - dp}, device_id_type=MESH)
    expand_sum.start()
    reduce_sum.over_z()
    branch_scatter[1].end()
    sums[...] = jnp.zeros_like(sums)

    @pl.loop(0, share // 16)
    def _(i):
        at = span(i, 16)
        grad = g[at].astype(F32) + merge_scatter.total[at]
        grad_resid[at] = grad
        hat, change = back_of(grad, merged[at], gain_merge[...])
        new_rows[pl.ds(pl.multiple_of(row * share + i * 16, 16), 16), :] = change.astype(BF16)
        product = grad * hat
        sums[...] += product[:8] + product[8:]

    last_gather.start()
    gains[2:3] = jnp.sum(sums[...], axis=0, keepdims=True)
    get_xs.wait()
    pl.loop(0, 2 * tiles)(turn_rows)
    last_gather.relay()
    last_gather.relay_again()
    get_raw.wait()
    get_qkv.wait()
    mix_turned[...] = mix[...].T
    hand_mix.start()
    expand_sum.over_z()
    pl.semaphore_wait(free.at[1], 1)
    hand_xs.start()
    for m in range(2):
        branch_scatter[m].finish()
    last_gather.wait()
    pl.semaphore_wait(free.at[0], 1)
    hand_new.start()

    live = (docs[:, 0:1] < 5.0).astype(F32)
    grad_mix[...] = (dot_flipped(new_rows[...], merge[...]) * live).astype(BF16)
    heads_change[:, head_width:] = jnp.zeros((tokens, 2 * head_width), F32)
    for b in range(tokens // QUERY_BLOCK):
        start, count = key_span(b)
        query_at = pl.ds(b * QUERY_BLOCK, QUERY_BLOCK)
        key_at = pl.ds(start, count)
        for h in range(head_width // HD):
            query, key, value = (
                slice(i * head_width + h * HD, i * head_width + (h + 1) * HD) for i in range(3)
            )
            shares = probs[h, b, :, :count]
            change = grad_mix[query_at, h * HD : (h + 1) * HD]
            grad_shares = dot_flipped(change, qkv[key_at, value])
            weighted = shares.astype(F32) * grad_shares
            center = jnp.sum(weighted, axis=1, keepdims=True)
            grad_scores = (weighted - shares.astype(F32) * center).astype(BF16)
            heads_change[query_at, query] = dot(grad_scores, qkv[key_at, key]) * HD**-0.5
            heads_change[key_at, key] += dot(grad_scores.T, qkv[query_at, query]) * HD**-0.5
            heads_change[key_at, value] += dot(shares.T, change)

    joined[:, 2 * head_width :] = heads_change[:, 2 * head_width :].astype(BF16)
    hand_values.start()
    reduce_sum.over_y()
    sums[...] = jnp.zeros_like(sums)

    @pl.loop(0, tokens // 64)
    def _(i):
        at = span(i, 64)
        dots = []
        for j, gain in enumerate((gain_query, gain_key)):
            some = slice(j * head_width, (j + 1) * head_width)
            change = turn(heads_change[at, some], cosine[at], -sine[at])
            hat = raw[at, some] * rates[at, j : j + 1]
            product = change * hat
            sums[:, some] += jnp.sum(product.reshape(8, 8, head_width), axis=0)
            heads_change[at, some] = change * gain[...]
            dots.append(jnp.sum(product * gain[...], axis=1, keepdims=True))
        token_sums.put(at, *dots)

    token_sums.start()
    gains[0:1, span(row, head_width)] = jnp.sum(sums[:, :head_width], axis=0, keepdims=True)
    gains[1:2, span(row, head_width)] = jnp.sum(sums[:, head_width : 2 * head_width], axis=0, keepdims=True)
    for copy in row_gains:
        copy.start()
    hand_mix.wait()
    hand_new.wait()
    mine = span(dp, half_heads)
    for side in range(4):
        wide = pl.ds(side * (width // 4), width // 4)
        merge[:half_heads, wide] = (
            dot(mix_turned[mine, :], back[:, wide]) + dot(mix_other[...], back_other[:, wide])
        ).astype(BF16)
    merge_sum.start()
    hand_values.wait()
    hand_xs.wait()

    @pl.loop(0, tiles)
    def _(j):
        two(
            values_part, span(j, 256), pl.ds(0, head_width), turned, span(dp * tiles + j, 256), joined.at[:, values_at],
            turned_other, joined_other.at[:, values_at],
        )

    values_sum.start()
    token_sums.end()

    @pl.loop(0, tokens // 64)
    def _(i):
        at = span(i, 64)
        dots = stats[at] * (1.0 / width)
        for j in range(2):
            some = slice(j * head_width, (j + 1) * head_width)
            rate = rates[at, j : j + 1]
            hat = raw[at, some] * rate
            joined[at, some] = (rate * (heads_change[at, some] - hat * dots[:, j : j + 1])).astype(BF16)

    hand_joined.start()
    def input_part(j):
        at = span(j, 256)
        part[:, at] = dot_flipped(joined[...], heads[at, :]).astype(BF16)

    pl.loop(first_right, 2 * n)(input_part)
    input_scatter.start_right()
    pl.loop(0, first_right)(input_part)
    input_scatter.start_left()
    hand_joined.wait()

    @pl.loop(0, tiles)
    def _(j):
        two(heads, span(j, 256), others_at, turned, span(dp * tiles + j, 256), joined, turned_other, joined_other)

    heads_sum.start()
    for copy in row_gains:
        copy.wait()
    gain_row[row] = gains[...]
    total = gain_row[0]
    for k in range(1, 8):
        total = total + gain_row[k]
    gain_sum[0] = total
    gain_col[col] = total
    for copy in col_gains:
        copy.start()
    values_sum.over_z()
    input_scatter.middle()
    merge_sum.over_z()
    heads_sum.over_z()
    reduce_sum.end()
    expand_sum.over_y()
    input_scatter.end()
    final[...] = (grad_resid[...] + input_scatter.total[...]).astype(BF16)
    spread_grad.start()
    values_sum.over_y()
    merge_sum.over_y()
    heads_sum.over_y()
    for copy in col_gains:
        copy.wait()
    total = gain_col[0]
    for k in range(1, 8):
        total = total + gain_col[k]
    gain_sum[1] = total
    core_gains.start()
    expand_sum.end()
    values_sum.end()
    merge_sum.end()
    heads_sum.end()
    core_gains.wait()
    gains_grad[...] = gain_sum[1] + gain_core[...]
    input_scatter.finish()
    spread.wait()
    spread_grad.wait()
    for grad in (reduce_sum, expand_sum, values_sum, merge_sum, heads_sum):
        grad.wait()


def on_device(
    block_input,
    cotangent,
    doc_lengths,
    heads_weight,
    heads_first,
    heads_second,
    merge_weight,
    merge_first,
    merge_second,
    expand_weight,
    expand_first,
    expand_second,
    reduce_weight,
    reduce_first,
    reduce_second,
    norm_gains,
    gains_first,
    gains_second,
):
    col_width = block_input.shape[1]
    model_width = col_width * lax.axis_size("col")
    head_width = merge_weight.shape[0]
    unit_width = reduce_weight.shape[0]
    seq_len = block_input.shape[0] * lax.axis_size("row") // lax.axis_size("col")
    share = seq_len // lax.axis_size("row")
    head_count = head_width // HD
    rows_shape = struct((seq_len, model_width), BF16)
    blocks = seq_len // QUERY_BLOCK

    gain_shape = (4, model_width)
    block_output, input_grad, gains_grad, heads_grad, merge_grad, expand_grad, reduce_grad = call(
        layer_kernel, "layer", 1,
        [
            struct(block_input.shape, BF16),
            struct(block_input.shape, BF16),
            struct(gain_shape, F32),
            struct(heads_weight.shape, BF16),
            struct(merge_weight.shape, BF16),
            struct(expand_weight.shape, BF16),
            struct(reduce_weight.shape, BF16),
            rows_shape,
            struct((seq_len, 2 * head_width), F32),
            struct((seq_len, 3 * head_width), BF16),
        ],
        [
            block_input, cotangent, heads_weight, merge_weight, expand_weight, reduce_weight, doc_lengths, norm_gains,
        ],
        [ANY] * 6 + [pl.BlockSpec(memory_space=pltpu.SMEM), VMEM],
        [ANY] * 2 + [VMEM] + [ANY] * 7,
        [
            pltpu.VMEM((seq_len, model_width), BF16),
            pltpu.VMEM((model_width, seq_len), BF16),
            pltpu.VMEM((model_width, 2 * unit_width), BF16),
            pltpu.VMEM((unit_width, model_width), BF16),
            pltpu.VMEM((model_width, 3 * head_width), BF16),
            pltpu.VMEM((head_width, model_width), BF16),
            pltpu.VMEM((seq_len, unit_width), F32),
            pltpu.VMEM((seq_len, unit_width), F32),
            pltpu.VMEM((seq_len, unit_width), BF16),
            pltpu.VMEM((unit_width, seq_len), BF16),
            pltpu.VMEM((seq_len, model_width), BF16),
            pltpu.VMEM((seq_len, model_width), BF16),
            pltpu.VMEM((seq_len, 2 * unit_width), BF16),
            pltpu.VMEM((head_count, blocks, QUERY_BLOCK, WINDOW + QUERY_BLOCK), BF16),
            pltpu.VMEM((seq_len, head_width), BF16),
            pltpu.VMEM((head_width, seq_len), BF16),
            pltpu.VMEM((seq_len, 128), F32),
            pltpu.VMEM((seq_len, 128), F32),
            pltpu.VMEM((seq_len, head_width), BF16),
            pltpu.VMEM((share, model_width), BF16),
            pltpu.VMEM((share, model_width), BF16),
            pltpu.VMEM((share, model_width), F32),
            pltpu.VMEM((share, model_width), F32),
            pltpu.VMEM((share, model_width), F32),
            pltpu.VMEM((share, model_width), BF16),
            pltpu.VMEM((8, model_width), F32),
            pltpu.VMEM((seq_len, 256), F32),
            pltpu.VMEM(gain_shape, F32),
            pltpu.VMEM((8, *gain_shape), F32),
            pltpu.VMEM((8, *gain_shape), F32),
            pltpu.VMEM(gain_shape, F32),
            pltpu.VMEM((2, *gain_shape), F32),
            pltpu.VMEM((unit_width // 2, seq_len), BF16),
            pltpu.VMEM((model_width // 2, seq_len), BF16),
            pltpu.VMEM((seq_len, model_width), BF16),
            pltpu.VMEM((seq_len, model_width), BF16),
            pltpu.VMEM((head_width // 2, seq_len), BF16),
            pltpu.VMEM((seq_len, 3 * head_width), BF16),
            pltpu.VMEM((model_width // 2, head_width), BF16),
            pltpu.VMEM((seq_len, HD), F32),
            pltpu.VMEM((8, seq_len), F32),
            pltpu.VMEM((seq_len, HD), F32),
            pltpu.VMEM((seq_len, HD), F32),
            pltpu.SemaphoreType.REGULAR((2,)),
            DMA((8,)), DMA((3,)), DMA((3,)), DMA((8,)), DMA((8,)), DMA((8,)), DMA((8,)), DMA((15,)), DMA((15,)),
            DMA((9,)), DMA((9,)), DMA((8,)), DMA((8,)), DMA((8,)), DMA((8,)),
        ]
        + gather_scratch() * 6
        + scatter_scratch(share, model_width) + [DMA((14,))] * 10
        + sums_scratch(seq_len) * 2
        + grad_sum_scratch(reduce_weight.shape) + grad_sum_scratch(expand_weight.shape)
        + grad_sum_scratch(merge_weight.shape)
        + grad_sum_scratch((heads_weight.shape[0], head_width))
        + grad_sum_scratch((heads_weight.shape[0], 2 * head_width))
        + bring_scratch() * 4,
    )[:7]
    return update(
        block_output,
        input_grad,
        (heads_grad, heads_weight, heads_first, heads_second),
        (merge_grad, merge_weight, merge_first, merge_second),
        (expand_grad, expand_weight, expand_first, expand_second),
        (reduce_grad, reduce_weight, reduce_first, reduce_second),
        (gains_grad, norm_gains, gains_first, gains_second),
    )


def solution(mesh):
    return jax.shard_map(
        on_device,
        mesh=mesh,
        in_specs=(
            P(("dp", "row"), "col"),
            P(("dp", "row"), "col"),
            P(("dp", "col"), None),
            P("col", "row"),
            P("col", "row"),
            P("col", "row"),
            P("row", "col"),
            P("row", "col"),
            P("row", "col"),
            P("col", "row"),
            P("col", "row"),
            P("col", "row"),
            P("row", "col"),
            P("row", "col"),
            P("row", "col"),
            P(),
            P(),
            P(),
        ),
        out_specs=(
            P(("dp", "row"), "col"),
            P(("dp", "row"), "col"),
            P("col", "row"),
            P("col", "row"),
            P("col", "row"),
            P("col", "row"),
            P("col", "row"),
            P("row", "col"),
            P("row", "col"),
            P("row", "col"),
            P("row", "col"),
            P("row", "col"),
            P("col", "row"),
            P("col", "row"),
            P("col", "row"),
            P("col", "row"),
            P("col", "row"),
            P("row", "col"),
            P("row", "col"),
            P("row", "col"),
            P("row", "col"),
            P("row", "col"),
            P(),
            P(),
            P(),
            P(),
        ),
        check_vma=False,
    )
```

```python
import math

import jax
import jax.numpy as jnp
from jax import lax
from jax.experimental import pallas as pl
from jax.experimental.pallas import tpu as pltpu
from jax.sharding import PartitionSpec as P

HD = 128
WINDOW = 256
STEP = 5


EPS = 1e-06
THETA = 500000.0
LR = 0.02
LR_GAIN = 0.2
BETA_ONE = 0.5
BETA_TWO = 0.5
DECAY = 0.1
ADAM_EPS = 1e-08

BF16 = jnp.bfloat16
SCATTER_LEFT, GATHER_LEFT, INPUT_LEFT = 8, 9, 16
F32 = jnp.float32
MESH = pl.DeviceIdType.MESH
ANY = pl.BlockSpec(memory_space=pl.ANY)
VMEM = pl.BlockSpec(memory_space=pltpu.VMEM)
DMA = pltpu.SemaphoreType.DMA


def documents(lengths, shape, axis):
    tokens = lax.broadcasted_iota(jnp.int32, shape, axis)
    docs, starts, end = jnp.zeros(shape, F32), jnp.zeros(shape, jnp.int32), jnp.int32(0)
    for j in range(lengths.shape[1]):
        end = end + lengths[0, j]
        passed = tokens >= end
        docs = docs + passed.astype(F32)
        starts = starts + jnp.where(passed, lengths[0, j], 0)
    return docs, starts


def adamw(weight, gradient, first_mom, second_mom, step_rate, decay_rate):
    mean_new = BETA_ONE * first_mom + (1.0 - BETA_ONE) * gradient
    square_new = BETA_TWO * second_mom + (1.0 - BETA_TWO) * gradient * gradient
    fix_one = 1.0 - BETA_ONE**STEP
    fix_two = 1.0 - BETA_TWO**STEP
    update = mean_new / fix_one / (jnp.sqrt(square_new / fix_two) + ADAM_EPS) + decay_rate * weight
    return (mean_new, square_new, weight - step_rate * update)


def here():
    return lax.axis_index("dp"), lax.axis_index("row"), lax.axis_index("col")


def row_peer(row, d):
    return (row // 4 + d // 4) % 2 * 4 + (row % 4 + d % 4) % 4


def z_peer(col, d):
    return (col // 2 + d) % 4 * 2 + col % 2


def z_source(col, d):
    return (col // 2 + 4 - d) % 4 * 2 + col % 2


def y_peer(col):
    return col // 2 * 2 + 1 - col % 2


def remote(source, target, sent, arrived, **where):
    return pltpu.make_async_remote_copy(
        src_ref=source,
        dst_ref=target,
        send_sem=sent,
        recv_sem=arrived,
        device_id=where,
        device_id_type=MESH,
    )


def meet(rows=False, cols=False, weights=False, core=False, spread_in=False, spread_out=False):
    dp, row, col = here()
    barrier = pltpu.get_barrier_semaphore()
    count = 0

    def greet(**where):
        pl.semaphore_signal(barrier, inc=1, device_id=where, device_id_type=MESH)

    if rows:
        for d in range(1, 8):
            greet(row=row_peer(row, d))
        count = count + 7
    if cols:
        for d in range(1, 8):
            greet(col=(col + d) % 8)
        count = count + 7
    if weights:
        greet(col=y_peer(col))
        for d in (1, 3):
            greet(col=z_peer(col, d))
        count = count + 3
    if core:
        greet(dp=1 - dp)
        count = count + 1
    for wanted, inward in ((spread_in, True), (spread_out, False)):
        if wanted:
            for k in range(8):
                at_row, at_col = (col, k) if inward else (k, row)

                @pl.when(jnp.logical_not((at_row == row) & (at_col == col)))
                def _():
                    greet(row=at_row, col=at_col)

            count = count + 8 - (row == col).astype(jnp.int32)
    pl.semaphore_wait(barrier, count)


class Exchange:
    def __init__(self, first, second, source, middle, target, sent, arrived):
        dp, row, col = here()
        a, b = (row, col) if first == "row" else (col, row)
        self.keep = pltpu.make_async_copy(source(a), middle.at[a], sent.at[7])
        self.copies = []
        for d in range(1, 8):
            k = (a + d) % 8
            self.copies.append(remote(source(k), middle.at[a], sent.at[d - 1], arrived.at[d - 1], **{first: k}))
        self.passed = []
        for j in range(8):
            self.passed.append(
                (
                    b == j,
                    remote(middle.at[j], target(b), sent.at[8 + j], arrived.at[7 + b], **{second: j}),
                    remote(middle.at[j], target(j), sent.at[8 + j], arrived.at[7 + j], **{second: j}),
                    pltpu.make_async_copy(middle.at[j], target(b), sent.at[8 + j]),
                )
            )

    def start(self):
        self.keep.start()
        for copy in self.copies:
            copy.start()

    def relay(self):
        self.keep.wait()
        for copy in self.copies:
            copy.wait_recv()
        for mine, copy, _, local in self.passed:
            pl.when(jnp.logical_not(mine))(copy.start)
            pl.when(mine)(local.start)

    def wait(self):
        for mine, copy, came, local in self.passed:
            pl.when(jnp.logical_not(mine))(came.wait_recv)
            pl.when(jnp.logical_not(mine))(copy.wait_send)
            pl.when(mine)(local.wait)
        for copy in self.copies:
            copy.wait_send()


def half_of(kind, ref, c, h):
    if kind == "tall":
        count = ref.shape[0] // 16
        return ref.at[pl.ds(pl.multiple_of((2 * c + h) * count, count), count)]
    count, width = ref.shape[0] // 2, ref.shape[1] // 8
    return ref.at[
        pl.ds(pl.multiple_of(h * count, count), count), pl.ds(pl.multiple_of(c * width, width), width)
    ]


def half_shard(ref, h):
    count = ref.shape[0] // 2
    return ref.at[pl.ds(pl.multiple_of(h * count, count), count)]


def mean_rate(values):
    return lax.rsqrt(jnp.mean(values * values, axis=-1, keepdims=True) + EPS)


def call(kernel, name, number, outs, ins, in_specs, out_specs, scratch):
    return pl.pallas_call(
        kernel,
        name=name,
        out_shape=outs,
        in_specs=in_specs,
        out_specs=out_specs,
        scratch_shapes=scratch,
        compiler_params=pltpu.CompilerParams(
            collective_id=number, has_side_effects=True, vmem_limit_bytes=62 * 2**20
        ),
    )(*ins)


def struct(shape, kind):
    return jax.ShapeDtypeStruct(shape, kind)


def dot(left, right):
    return jnp.dot(left, right, preferred_element_type=F32)


def dot_flipped(left, right):
    return lax.dot_general(left, right, (((1,), (1,)), ((), ())), preferred_element_type=F32)


def span(k, count):
    return pl.ds(pl.multiple_of(k * count, count), count)


def near_row(row, dx, dy):
    return (row // 4 + dy) % 2 * 4 + (row % 4 + dx) % 4


class Scatter:
    def __init__(self, part, total, from_y, from_x, last_y, last_x, stage_y, stage_x, sent, arrived):
        dp, row, col = here()
        self.row, self.part, self.total = row, part, total
        self.from_y, self.from_x, self.last_y, self.last_x = from_y, from_x, last_y, last_x
        self.stage_y, self.stage_x = stage_y, stage_x
        self.count, self.left = total.shape[0], from_x.shape[3]
        self.sides = (pl.ds(0, self.left), pl.ds(self.left, total.shape[1] - self.left))
        number = iter(range(14))

        def copy(source, target, dx, dy):
            i = next(number)
            return remote(source, target, sent.at[i], arrived.at[i], row=near_row(row, dx, dy))

        self.y_first = {dx: copy(self.block(dx, 1, 1), from_y.at[dx], 0, 1) for dx in (1, 3, 2, 0)}
        self.x_first = {
            (dx, dy): copy(self.block(dx, dy, 0), from_x.at[dy, dx - 1], dx, 0)
            for dy in (1, 0)
            for dx in (1, 3, 2)
        }
        self.x_last = {dx: copy(stage_x.at[dx - 1], last_x.at[dx - 1], dx, 0) for dx in (1, 3, 2)}
        self.y_last = copy(stage_y, last_y, 0, 1)

    def block(self, dx, dy, side):
        return self.part.at[span(near_row(self.row, dx, dy), self.count), self.sides[side]]

    def start_right(self):
        for copy in self.y_first.values():
            copy.start()

    def start_left(self):
        for copy in self.x_first.values():
            copy.start()

    def chunks(self, body):
        @pl.loop(0, self.count // 16)
        def _(i):
            body(span(i, 16))

    def middle(self):
        for dx in (1, 3, 2):
            self.y_first[dx].wait_recv()
            own = self.block(dx, 0, 1)

            def add(at):
                self.stage_x[dx - 1, at] = (own[at].astype(F32) + self.from_y[dx, at].astype(F32)).astype(BF16)

            self.chunks(add)
            self.x_last[dx].start()
        for dx in (1, 3, 2):
            self.x_first[dx, 1].wait_recv()
        other = self.block(0, 1, 0)

        def add(at):
            total = other[at].astype(F32)
            for k in range(3):
                total = total + self.from_x[1, k, at].astype(F32)
            self.stage_y[at] = total.astype(BF16)

        self.chunks(add)
        self.y_last.start()

    def end(self):
        self.y_first[0].wait_recv()
        for dx in (1, 3, 2):
            self.x_first[dx, 0].wait_recv()
            self.x_last[dx].wait_recv()
        self.y_last.wait_recv()
        left, right = self.block(0, 0, 0), self.block(0, 0, 1)

        def add(at):
            total = left[at].astype(F32) + self.last_y[at].astype(F32)
            for k in range(3):
                total = total + self.from_x[0, k, at].astype(F32)
            self.total[at, self.sides[0]] = total
            total = right[at].astype(F32) + self.from_y[0, at].astype(F32)
            for k in range(3):
                total = total + self.last_x[k, at].astype(F32)
            self.total[at, self.sides[1]] = total

        self.chunks(add)

    def finish(self):
        for copies in (self.y_first, self.x_first, self.x_last):
            for copy in copies.values():
                copy.wait_send()
        self.y_last.wait_send()


def scatter_scratch(share, width):
    left = SCATTER_LEFT * width // 16
    right = width - left
    return [
        pltpu.VMEM((share, width), F32),
        pltpu.VMEM((4, share, right), BF16),
        pltpu.VMEM((2, 3, share, left), BF16),
        pltpu.VMEM((share, left), BF16),
        pltpu.VMEM((3, share, right), BF16),
        pltpu.VMEM((share, left), BF16),
        pltpu.VMEM((3, share, right), BF16),
        DMA((14,)),
        DMA((14,)),
    ]


class Gather:
    def __init__(self, whole, share, left, sent, arrived):
        dp, row, col = here()
        self.row = row
        number = iter(range(19))
        sides = (pl.ds(0, left), pl.ds(left, whole.shape[1] - left))
        right = left < whole.shape[1]

        def copy(fx, fy, side, dx, dy, start=0, count=share):
            i = next(number)
            k = near_row(row, fx, fy)
            ref = whole.at[pl.ds(pl.multiple_of(k * share + start, count), count), sides[side]]
            return remote(ref, ref, sent.at[i], arrived.at[i], row=near_row(row, dx, dy))

        part = share // 2
        steps = (1, 3, 2)
        two = steps[:2]
        self.y_left = copy(0, 0, 0, 0, 1)
        self.x_left = [copy(0, 0, 0, dx, 0) for dx in two]
        self.on_left = [copy(4 - dx, 0, 0, dx, 0, i * part, part) for i, dx in enumerate(two)]
        self.y_right, self.x_right, self.y_near, self.on_other = [], [], [], []
        if right:
            self.x_other = [copy(0, 1, 0, dx, 0) for dx in steps]
            self.y_right = [copy(0, 0, 1, 0, 1)]
            self.x_right = [copy(0, 0, 1, dx, 0) for dx in steps]
            self.y_near = [copy(4 - dx, 0, 1, 0, 1) for dx in steps]
        else:
            self.x_other = [copy(0, 1, 0, dx, 0) for dx in two]
            self.on_other = [copy(4 - dx, 1, 0, dx, 0, i * part, part) for i, dx in enumerate(two)]

    def start(self):
        for copy in (self.y_left, *self.x_right, *self.y_right, *self.x_left):
            copy.start()

    def relay(self):
        self.y_left.wait_recv()
        for copy in self.x_other:
            copy.start()
        for i, came in enumerate(self.x_right):
            came.wait_recv()
            self.y_near[i].start()

    def relay_again(self):
        for i in range(2):
            self.x_left[i].wait_recv()
            self.on_left[i].start()
        for i, copy in enumerate(self.on_other):
            self.x_other[i].wait_recv()
            copy.start()

    def wait(self):
        for copy in (*self.y_right, *self.x_other[len(self.on_other) :], *self.on_left, *self.on_other, *self.y_near):
            copy.wait_recv()
        for copy in (self.y_left, *self.x_left, *self.x_other, *self.on_left, *self.on_other, *self.y_right,
                     *self.x_right, *self.y_near):
            copy.wait_send()


def gather_scratch():
    return [DMA((19,)), DMA((19,))]


def cols(ref, k, width):
    return ref.at[:, pl.ds(pl.multiple_of(k * width, width), width)]


def rows_of(ref, k, count):
    return ref.at[pl.ds(pl.multiple_of(k * count, count), count)]


def back_of(grad, values, gain):
    rate = mean_rate(values)
    hat = values * rate
    grad_hat = grad * gain
    dots = jnp.mean(grad_hat * hat, axis=-1, keepdims=True)
    return hat, rate * (grad_hat - hat * dots)


class GradSum:
    def __init__(self, kind, part, out, between, far, near, sent, arrived):
        dp, _, col = here()
        self.kind, self.part, self.col = kind, part, col
        self.between, self.far, self.near = between, far, near
        self.rows, self.width = near.shape[1], near.shape[2]
        number = iter(range(10))

        def copy(source, target, **where):
            i = next(number)
            return remote(source, target, sent.at[i], arrived.at[i], **where)

        self.steps = (1, 3)
        self.on = [
            [
                copy(self.piece(self.z_block(2, k), i), between.at[i, k], col=z_peer(col, d))
                for k in range(2)
            ]
            for i, d in enumerate(self.steps)
        ]
        self.zs = [
            [copy(self.block(self.z_block(d, k)), far.at[i, k], col=z_peer(col, d)) for k in range(2)]
            for i, d in enumerate(self.steps)
        ]
        self.ys = copy(near.at[0], near.at[1], col=y_peer(col))
        self.last = copy(near.at[0], half_shard(out, dp), dp=1 - dp)
        self.keep = pltpu.make_async_copy(near.at[0], half_shard(out, dp), sent.at[10])

    def z_block(self, d, k):
        return z_peer(self.col, d) // 2 * 2 + k

    def block(self, c):
        if self.kind == "tall":
            return self.part.at[span(c, self.rows)]
        return self.part.at[:, span(c, self.width)]

    def piece(self, c, i):
        return self.block(c).at[pl.ds(i * (self.rows // 2), self.rows // 2)]

    def each(self, rows, body):
        count = min(rows, 32768 // self.width // 16 * 16)

        @pl.loop(0, rows // count)
        def _(i):
            body(span(i, count))

    def start(self):
        for pair in self.on:
            for copy in pair:
                copy.start()

    def over_z(self):
        for i, d in enumerate(self.steps):
            for k in range(2):
                self.on[i][k].wait_recv()
                own = self.piece(self.z_block(d, k), i)

                def add(at):
                    own[at] = (own[at].astype(F32) + self.between[i, k, at].astype(F32)).astype(BF16)

                self.each(self.rows // 2, add)
                self.zs[i][k].start()

    def over_y(self):
        for pair in self.zs:
            for copy in pair:
                copy.wait_recv()
        yl = self.col % 2
        keep, give = self.block(self.col), self.block(y_peer(self.col))

        def total(at, ref, k):
            return (
                ref[at].astype(F32) + self.far[0, k, at].astype(F32) + self.far[1, k, at].astype(F32)
            ).astype(BF16)

        def add(at):
            self.near[0, at] = total(at, give, 1 - yl)

        self.each(self.rows, add)
        self.ys.start()

        def add(at):
            keep[at] = total(at, keep, yl)

        self.each(self.rows, add)
        for pair in (*self.zs, *self.on):
            for copy in pair:
                copy.wait_send()

    def end(self):
        self.ys.wait()
        keep = self.block(self.col)

        def add(at):
            self.near[0, at] = (keep[at].astype(F32) + self.near[1, at].astype(F32)).astype(BF16)

        self.each(self.rows, add)
        self.last.start()
        self.keep.start()

    def wait(self):
        self.last.wait()
        self.keep.wait()


def grad_sum_scratch(shape):
    rows, width = shape[0] // 2, shape[1]
    return [
        pltpu.VMEM((2, 2, rows // 2, width), BF16),
        pltpu.VMEM((2, 2, rows, width), BF16),
        pltpu.VMEM((2, rows, width), BF16),
        DMA((11,)),
        DMA((10,)),
    ]


class Bring:
    def __init__(self, kind, shape, whole, sent, arrived):
        dp, _, col = here()
        rows, width = shape
        near = y_peer(col)
        number = iter(range(20))

        def block(c, s=None):
            count, at = (rows // 2, dp) if s is None else (rows // 4, 2 * dp + s)
            if kind == "tall":
                return whole.at[span((2 if s is None else 4) * c + at, count)]
            return whole.at[span(at, count), span(c, width)]

        def copy(source, target, **where):
            i = next(number)
            return remote(source, target, sent.at[i], arrived.at[i], **where)

        self.place = whole.at[span(col, rows)] if kind == "tall" else whole.at[:, span(col, width)]
        self.y_own = copy(block(col), block(col), col=near)
        self.z_own = [copy(block(col), block(col), col=z_peer(col, d)) for d in (1, 3)]
        self.z_near = [copy(block(near), block(near), col=z_peer(col, d)) for d in (1, 3)]
        self.on, self.on_near, self.a_own, self.a_near = [], [], [], []
        self.a_far, self.a_far_near = [], []
        for i, d in enumerate((1, 3)):
            came, two = z_source(col, d), z_peer(col, 2)
            self.on.append(copy(block(came, i), block(came, i), col=z_peer(col, d)))
            self.on_near.append(copy(block(y_peer(came), i), block(y_peer(came), i), col=z_peer(col, d)))
            self.a_own.append(copy(block(came), block(came), dp=1 - dp))
            self.a_near.append(copy(block(y_peer(came)), block(y_peer(came)), dp=1 - dp))
            self.a_far.append(copy(block(two, i), block(two, i), dp=1 - dp))
            self.a_far_near.append(copy(block(y_peer(two), i), block(y_peer(two), i), dp=1 - dp))
        self.a_y = copy(block(near), block(near), dp=1 - dp)

    def start_y(self):
        self.y_own.start()

    def start_z(self):
        for copy in self.z_own:
            copy.start()

    def relay(self):
        self.y_own.wait_recv()
        for copy in (*self.z_near, self.a_y):
            copy.start()

    def relay_own(self):
        for i in range(2):
            self.z_own[i].wait_recv()
            self.on[i].start()
            self.a_own[i].start()

    def relay_near(self):
        for i in range(2):
            self.z_near[i].wait_recv()
            self.on_near[i].start()
            self.a_near[i].start()

    def hand_over(self):
        for i in range(2):
            self.on[i].wait_recv()
            self.a_far[i].start()
        for i in range(2):
            self.on_near[i].wait_recv()
            self.a_far_near[i].start()

    def wait(self):
        for copy in (self.a_y, *self.a_own, *self.a_near, *self.a_far, *self.a_far_near):
            copy.wait()
        for copy in (self.y_own, *self.z_own, *self.z_near, *self.on, *self.on_near):
            copy.wait_send()


def bring_scratch():
    return [DMA((20,)), DMA((20,))]


class SpreadIn:
    def __init__(self, source, target, sent, arrived):
        dp, row, col = here()
        self.row, self.col = row, col
        self.copies, self.waits = [], []
        for k in range(8):
            out = remote(source(k), target(k, col), sent.at[k], arrived.at[col], row=k, col=row)
            came = remote(source(k), target(row, k), sent.at[k], arrived.at[k], row=k, col=row)
            local = pltpu.make_async_copy(source(k), target(k, col), sent.at[k])
            self.copies.append(((row == k) & (row == col), out, local))
            self.waits.append(((row == col) & (col == k), came))

    def start(self):
        for mine, out, local in self.copies:
            pl.when(jnp.logical_not(mine))(out.start)
            pl.when(mine)(local.start)

    def wait(self):
        for mine, came in self.waits:
            pl.when(jnp.logical_not(mine))(came.wait_recv)
        for mine, out, local in self.copies:
            pl.when(jnp.logical_not(mine))(out.wait_send)
            pl.when(mine)(local.wait)


class TokenSums:
    def __init__(self, stats, mine, came, sent, arrived):
        dp, row, col = here()
        self.stats, self.mine, self.came = stats, mine, came
        self.copies = [
            remote(mine, came.at[d - 1], sent.at[d - 1], arrived.at[d - 1], row=row_peer(row, d))
            for d in range(1, 8)
        ]

    def put(self, at, one, two):
        lane = lax.broadcasted_iota(jnp.int32, (one.shape[0], 128), 1)
        self.stats[at] = jnp.where(lane == 0, one, jnp.where(lane == 1, two, 0.0))

    def start(self):
        self.mine[...] = self.stats[...].T[:8]
        for copy in self.copies:
            copy.start()

    def end(self):
        total = self.mine[...]
        for d, copy in enumerate(self.copies):
            copy.wait_recv()
            total = total + self.came[d]
        self.stats[...] = jnp.concatenate([total] * 16, axis=0).T
        for copy in self.copies:
            copy.wait_send()


def sums_scratch(tokens):
    return [pltpu.VMEM((8, tokens), F32), pltpu.VMEM((7, 8, tokens), F32), DMA((7,)), DMA((7,))]


def turn(values, cosine, sine):
    heads = [values[:, i : i + HD] for i in range(0, values.shape[1], HD)]
    return jnp.concatenate([h * cosine + pltpu.roll(h, HD // 2, 1) * sine for h in heads], axis=1)


QUERY_BLOCK = 128


def key_span(b):
    start = max(0, b * QUERY_BLOCK - WINDOW)
    return start, (b + 1) * QUERY_BLOCK - start


UPDATE_STEPS = 4


def update_kernel(*refs):
    ins, outs = refs[:22], refs[22:]
    outs[0][...] = ins[0][...]
    outs[1][...] = ins[1][...].astype(F32)
    for i in range(4):
        gradient, weight, first_mom, second_mom = (ref[...] for ref in ins[2 + 4 * i : 6 + 4 * i])
        gradient = gradient.astype(F32)
        mean, square, fresh = adamw(weight, gradient, first_mom, second_mom, LR, DECAY)
        for ref, value in zip(outs[2 + 5 * i : 7 + 5 * i], (gradient, mean, square, fresh, fresh), strict=True):
            ref[...] = value.astype(ref.dtype)

    @pl.when(pl.program_id(0) == 0)
    def _():
        gradient, weight, first_mom, second_mom = (ref[...] for ref in ins[18:])
        mean, square, fresh = adamw(weight, gradient, first_mom, second_mom, LR_GAIN, 0.0)
        for ref, value in zip(outs[22:], (gradient, mean, square, fresh), strict=True):
            ref[...] = value


def update(block_output, input_grad, *groups):
    def part(shape):
        return pl.BlockSpec((shape[0] // UPDATE_STEPS, shape[1]), lambda i: (i, 0))

    ins, outs, in_specs, out_specs = [block_output, input_grad], [], [], []
    outs += [struct(block_output.shape, BF16), struct(input_grad.shape, F32)]
    in_specs += [part(block_output.shape)] * 2
    out_specs += [part(block_output.shape)] * 2
    for group in groups[:4]:
        shape = group[0].shape
        ins += group
        in_specs += [part(shape)] * 4
        outs += [struct(shape, F32)] * 4 + [struct(shape, BF16)]
        out_specs += [part(shape)] * 5
    whole = pl.BlockSpec(groups[4][0].shape, lambda i: (0, 0))
    ins += groups[4]
    in_specs += [whole] * 4
    outs += [struct(groups[4][0].shape, F32)] * 4
    out_specs += [whole] * 4
    return tuple(
        pl.pallas_call(
            update_kernel,
            name="update",
            grid=(UPDATE_STEPS,),
            out_shape=outs,
            in_specs=in_specs,
            out_specs=out_specs,
            compiler_params=pltpu.CompilerParams(vmem_limit_bytes=62 * 2**20),
        )(*ins)
    )


def layer_kernel(
    x, g_in, heads_in, merge_in, expand_in, reduce_in, lengths, gain_all,
    out, input_grad, gains_grad, heads_grad, merge_grad, expand_grad, reduce_grad, xs_keep, raw_keep, qkv_keep,
    rows, turned, expand, reduce, heads, merge, gate, up, act, act_turned, part, back, hidden, probs, mix, mix_turned,
    rates, stats, grad_mix, done, final, grad_resid, merged, residual, g, sums, grad_gate,
    gains, gain_row, gain_col, gain_core, gain_sum, act_other, turned_other, hidden_other, back_other, mix_other,
    joined_other, values_part, exchanged, docs, doc_row, cosine, sine, free, load, keep, late, osent, ocame, isent, icame, nsent, ncame, xsent, xcame,
    asent, acame, bsent, bcame, g1sent, g1came, g2sent, g2came, g3sent, g3came, g4sent, g4came, g5sent, g5came, g6sent, g6came, *refs,
):
    dp, row, col = here()
    share, width = residual.shape
    tokens, units = act.shape
    head_width = mix.shape[1]
    tiles = units // 256
    n, first_right = width // 512, SCATTER_LEFT * width // 16 // 256
    gain_query, gain_key = (gain_all.at[i : i + 1, span(row, head_width)] for i in range(2))
    gain_merge, gain_reduce = (gain_all.at[i : i + 1] for i in range(2, 4))
    batch, half_share = tokens // 2, share // 2

    def scatter_of(i, m=None):
        sems = refs[7 + 2 * i : 9 + 2 * i]
        if m is None:
            return Scatter(part, *refs[:7], *sems)
        at = pl.ds(m * half_share, half_share)
        total, from_y, from_x, last_y, last_x, stage_y, stage_x = refs[:7]
        return Scatter(
            part.at[pl.ds(m * batch, batch)], total.at[at], from_y.at[:, at], from_x.at[:, :, at], last_y.at[at],
            last_x.at[:, at], stage_y.at[at], stage_x.at[:, at], *sems,
        )

    merge_scatter, input_scatter = scatter_of(0), scatter_of(5)
    reduced_scatter = [scatter_of(1 + m, m) for m in range(2)]
    branch_scatter = [scatter_of(3 + m, m) for m in range(2)]
    first_sums = TokenSums(rates, *refs[19:23])
    token_sums = TokenSums(stats, *refs[23:27])
    half_units, half_width, half_heads = units // 2, width // 2, head_width // 2
    reduce_part, merge_part_ref = reduce.at[pl.ds(0, half_units)], merge.at[pl.ds(0, half_heads)]
    expand_part, heads_part = expand.at[pl.ds(0, half_width)], heads.at[pl.ds(0, half_width)]
    reduce_sum = GradSum("wide", reduce_part, reduce_grad, *refs[27:32])
    expand_sum = GradSum("tall", expand_part, expand_grad, *refs[32:37])
    merge_sum = GradSum("wide", merge_part_ref, merge_grad, *refs[37:42])
    values_at, others_at = pl.ds(2 * head_width, head_width), pl.ds(0, 2 * head_width)
    values_sum = GradSum("tall", values_part, heads_grad.at[:, values_at], *refs[42:47])
    heads_sum = GradSum("tall", heads_part.at[:, others_at], heads_grad.at[:, others_at], *refs[47:52])
    bring_heads = Bring("tall", heads_in.shape, heads, *refs[52:54])
    bring_merge = Bring("wide", merge_in.shape, merge, *refs[54:56])
    bring_reduce = Bring("wide", reduce_in.shape, reduce, *refs[56:58])
    bring_expand = Bring("tall", expand_in.shape, expand, *refs[58:60])
    gather_x = Gather(back, share, INPUT_LEFT * width // 16, g1sent, g1came)
    left = GATHER_LEFT * width // 16
    row_gather = [
        Gather(rows.at[pl.ds(m * batch, batch)], half_share, left, *sems)
        for m, sems in enumerate(((g2sent, g2came), (g3sent, g3came)))
    ]
    gather = [
        Gather(back.at[pl.ds(m * batch, batch)], half_share, left, *sems)
        for m, sems in enumerate(((g4sent, g4came), (g5sent, g5came)))
    ]
    last_gather = Gather(back, share, left, g6sent, g6came)
    spread_x = SpreadIn(
        lambda k: rows_of(x, k, share), lambda k, c: back.at[span(k, share), span(c, 256)], asent, acame
    )
    spread_g = Exchange(
        "row", "col", lambda k: rows_of(g_in, k, share), exchanged.at[0], lambda k: g.at[:, span(k, 256)], bsent, bcame
    )
    spread = Exchange(
        "col", "row", lambda k: cols(done, k, 256), exchanged.at[1], lambda k: rows_of(out, k, 64), osent, ocame
    )
    spread_grad = Exchange(
        "col", "row", lambda k: cols(final, k, 256), exchanged.at[2], lambda k: rows_of(input_grad, k, 64), isent, icame
    )
    row_gains = [
        remote(gains, gain_row.at[row], nsent.at[d - 1], ncame.at[d - 1], row=row_peer(row, d))
        for d in range(1, 8)
    ]
    col_gains = [
        remote(gain_sum.at[0], gain_col.at[col], nsent.at[6 + d], ncame.at[6 + d], col=(col + d) % 8)
        for d in range(1, 8)
    ]
    core_gains = remote(gain_sum.at[1], gain_core, nsent.at[14], ncame.at[14], dp=1 - dp)

    raw, qkv, new_rows = up.at[:, : 2 * head_width], act.at[:, : 3 * head_width], back
    heads_change = gate.at[:, : 3 * head_width]
    joined = hidden.at[:, : 3 * head_width]
    puts = [
        pltpu.make_async_copy(source, target, keep.at[i])
        for i, (source, target) in enumerate(((back, xs_keep), (raw, raw_keep), (qkv, qkv_keep)))
    ]
    get_xs = pltpu.make_async_copy(xs_keep, rows, late.at[0])
    get_raw = pltpu.make_async_copy(raw_keep, raw, late.at[1])
    get_qkv = pltpu.make_async_copy(qkv_keep, qkv, late.at[2])

    shard_rows, quarter = heads_in.shape[0], reduce_in.shape[0] // 4
    heads32 = gate.at[:shard_rows, : heads_in.shape[1]]
    merge32 = gate.at[:shard_rows, heads_in.shape[1] :]
    reduce32 = [gate.at[shard_rows:, pl.ds(i * 256, 256)] for i in range(4)]
    expand32 = [up.at[pl.ds(i * shard_rows, shard_rows)] for i in range(2)]
    moves = (
        [(heads_in, heads32), (merge_in, merge32)]
        + [(reduce_in.at[pl.ds(i * quarter, quarter)], reduce32[i]) for i in range(4)]
        + [(expand_in.at[:, pl.ds(i * units, units)], expand32[i]) for i in range(2)]
    )
    loads = [pltpu.make_async_copy(source, target, load.at[i]) for i, (source, target) in enumerate(moves)]
    for copy in loads:
        copy.start()

    def narrow(i, target):
        loads[i].wait()
        source = moves[i][1]

        @pl.loop(0, source.shape[0] // 16)
        def _(k):
            at = span(k, 16)
            target[at] = source[at].astype(BF16)

    def hand(i, source, target):
        return remote(source, target, xsent.at[i], xcame.at[i], dp=1 - dp)

    hand_act = hand(0, act_turned.at[span(1 - dp, half_units)], act_other)
    hand_rows = hand(1, turned.at[span(1 - dp, half_width)], turned_other)
    hand_back = hand(2, back, back_other)
    hand_hidden = hand(3, hidden, hidden_other)
    hand_mix = hand(4, mix_turned.at[span(1 - dp, half_heads)], mix_other)
    hand_new = hand(5, back, back_other)
    hand_xs = hand(6, turned.at[span(1 - dp, half_width)], turned_other)
    hand_joined = hand(7, joined.at[:, others_at], joined_other.at[:, others_at])
    hand_values = hand(8, joined.at[:, values_at], joined_other.at[:, values_at])

    def turn_rows(j):
        values = rows[:, span(j, 256)].T
        turned[span(j, 128), :] = values[:128]
        turned[span(2 * tiles + j, 128), :] = values[128:]

    def two(target, at, wide, own, own_at, right, other, right_other):
        target[at, wide] = (
            dot(own[own_at, :], right[:, wide]) + dot(other[at, :], right_other[:, wide])
        ).astype(BF16)

    meet(rows=True, cols=True, core=True, spread_in=True)
    spread_x.start()
    narrow(0, bring_heads.place)
    bring_heads.start_y()
    bring_heads.start_z()
    narrow(1, bring_merge.place)
    bring_merge.start_y()
    bring_merge.start_z()
    for i in range(4):
        narrow(2 + i, bring_reduce.place.at[pl.ds(i * quarter, quarter)])
    for i in range(2):
        narrow(6 + i, bring_expand.place.at[:, pl.ds(i * units, units)])
    spread_x.wait()
    gather_x.start()
    bring_heads.relay()
    bring_heads.relay_own()
    gather_x.relay()
    bring_expand.start_y()
    bring_reduce.start_y()
    bring_heads.relay_near()
    bring_merge.relay()
    gather_x.relay_again()
    bring_merge.relay_own()
    bring_heads.hand_over()
    bring_merge.relay_near()
    bring_expand.start_z()
    bring_reduce.start_z()
    docs[...], starts = documents(lengths, docs.shape, 0)
    doc_row[...], _ = documents(lengths, doc_row.shape, 1)
    lane = lax.broadcasted_iota(jnp.int32, docs.shape, 1)
    frequency = jnp.exp((lane % (HD // 2)).astype(F32) * (-2.0 / HD * math.log(THETA)))
    angles = (lax.broadcasted_iota(jnp.int32, docs.shape, 0) - starts).astype(F32) * frequency
    cosine[...] = jnp.cos(angles)
    sine[...] = jnp.where(lane < HD // 2, -1.0, 1.0) * jnp.sin(angles)
    gather_x.wait()
    bring_heads.wait()
    puts[0].start()

    for i in range(2):
        raw[:, i * head_width : (i + 1) * head_width] = dot(
            back[...], heads[:, i * head_width : (i + 1) * head_width]
        )

    @pl.loop(0, tokens // 64)
    def _(i):
        at = span(i, 64)
        squares = raw[at] * raw[at]
        first_sums.put(
            at,
            jnp.sum(squares[:, :head_width], axis=1, keepdims=True),
            jnp.sum(squares[:, head_width:], axis=1, keepdims=True),
        )

    first_sums.start()
    qkv[:, 2 * head_width :] = dot(back[...], heads[:, 2 * head_width :]).astype(BF16)
    bring_merge.hand_over()
    bring_expand.relay()
    bring_reduce.relay()
    first_sums.end()

    @pl.loop(0, tokens // 64)
    def _(i):
        at = span(i, 64)
        rate = lax.rsqrt(rates[at] * (1.0 / width) + EPS)
        rates[at] = rate
        for j, gain in enumerate((gain_query, gain_key)):
            some = slice(j * head_width, (j + 1) * head_width)
            hat = raw[at, some] * rate[:, j : j + 1]
            qkv[at, some] = turn(hat * gain[...], cosine[at], sine[at]).astype(BF16)

    puts[1].start()
    puts[2].start()
    for b in range(tokens // QUERY_BLOCK):
        start, count = key_span(b)
        query_at = pl.ds(b * QUERY_BLOCK, QUERY_BLOCK)
        key_at = pl.ds(start, count)
        there = lax.broadcasted_iota(jnp.int32, (QUERY_BLOCK, count), 0) + (b * QUERY_BLOCK - start)
        distance = there - lax.broadcasted_iota(jnp.int32, (QUERY_BLOCK, count), 1)
        doc = docs[query_at, 0:1]
        allowed = (doc == doc_row[0:1, start : start + count]) & (distance >= 0) & (distance < WINDOW)
        live = (doc < 5.0).astype(F32)
        for h in range(head_width // HD):
            query, key, value = (
                slice(i * head_width + h * HD, i * head_width + (h + 1) * HD) for i in range(3)
            )
            scores = dot_flipped(qkv[query_at, query], qkv[key_at, key]) * HD**-0.5
            scores = jnp.where(allowed, scores, -1e30)
            weights = jnp.exp(scores - jnp.max(scores, axis=1, keepdims=True))
            shares = (weights / jnp.sum(weights, axis=1, keepdims=True)).astype(BF16)
            probs[h, b, :, :count] = shares
            if count < probs.shape[3]:
                probs[h, b, :, count:] = jnp.zeros((QUERY_BLOCK, probs.shape[3] - count), BF16)
            mix[query_at, h * HD : (h + 1) * HD] = (dot(shares, qkv[key_at, value]) * live).astype(BF16)

    bring_merge.wait()

    def merge_part(j):
        at = span(j, 256)
        part[:, at] = dot(mix[...], merge[:, at]).astype(BF16)

    pl.loop(first_right, 2 * n)(merge_part)
    merge_scatter.start_right()
    pl.loop(0, first_right)(merge_part)
    merge_scatter.start_left()
    bring_expand.relay_own()
    bring_reduce.relay_own()
    merge_scatter.middle()
    bring_expand.relay_near()
    bring_reduce.relay_near()
    merge_scatter.end()

    def place(i):
        per = half_share // 16
        return pl.ds(pl.multiple_of(i // per * batch + row * half_share + i % per * 16, 16), 16)

    @pl.loop(0, share // 16)
    def _(i):
        at = span(i, 16)
        total = merge_scatter.total[at]
        merged[at] = total
        mine = pl.ds(pl.multiple_of(row * share + i * 16, 16), 16)
        result = back[mine, :].astype(F32) + total * mean_rate(total) * gain_merge[...]
        residual[at] = result
        rows[place(i), :] = result.astype(BF16)

    row_gather[0].start()
    row_gather[0].relay()
    row_gather[1].start()
    bring_expand.hand_over()
    row_gather[0].relay_again()
    row_gather[1].relay()
    bring_reduce.hand_over()
    row_gather[0].wait()
    spread_g.start()
    row_gather[1].relay_again()
    merge_scatter.finish()
    bring_expand.wait()
    for copy in puts:
        copy.wait()

    def rows_in(m):
        return pl.ds(m * batch, batch)

    def gated(m):
        mine = rows_in(m)

        @pl.loop(0, tiles)
        def _(j):
            at = span(j, 256)
            gate[mine, at] = dot(rows[mine, :], expand[:, at])
            up[mine, at] = dot(rows[mine, :], expand[:, span(tiles + j, 256)])

            @pl.loop(m * (batch // 64), (m + 1) * (batch // 64))
            def _(i):
                some = span(i, 64)
                x = gate[some, at]
                act[some, at] = (x * jax.nn.sigmoid(x) * up[some, at]).astype(BF16)

    def reduced(m):
        mine = rows_in(m)

        def product(j):
            at = span(j, 256)
            part[mine, at] = dot(act[mine, :], reduce[:, at]).astype(BF16)

        pl.loop(first_right, 2 * n)(product)
        reduced_scatter[m].start_right()
        pl.loop(0, first_right)(product)
        reduced_scatter[m].start_left()

    def output_norm(m):
        @pl.loop(m * (half_share // 16), (m + 1) * (half_share // 16))
        def _(i):
            at = span(i, 16)
            grad = g[at].astype(F32)
            hat, change = back_of(grad, merge_scatter.total[at], gain_reduce[...])
            back[place(i), :] = change.astype(BF16)
            done[at] = (residual[at] + hat * gain_reduce[...]).astype(BF16)
            product = grad * hat
            sums[...] += product[:8] + product[8:]

    def activity_gradient(m):
        mine = rows_in(m)

        @pl.loop(0, tiles)
        def _(j):
            at, up_at = span(j, 256), span(tiles + j, 256)
            grad_gate[mine, :] = dot_flipped(back[mine, :], reduce[at, :])

            @pl.loop(m * (batch // 64), (m + 1) * (batch // 64))
            def _(i):
                some = span(i, 64)
                x, change = gate[some, at], grad_gate[some]
                s = jax.nn.sigmoid(x)
                hidden[some, at] = (change * up[some, at] * s * (1.0 + x * (1.0 - s))).astype(BF16)
                hidden[some, up_at] = (change * (x * s)).astype(BF16)

    def branch(m):
        mine = rows_in(m)

        def product(j):
            at = span(j, 256)
            part[mine, at] = dot_flipped(hidden[mine, :], expand[at, :]).astype(BF16)

        pl.loop(first_right, 2 * n)(product)
        branch_scatter[m].start_right()
        pl.loop(0, first_right)(product)
        branch_scatter[m].start_left()

    gated(0)
    bring_reduce.wait()
    spread_g.relay()
    reduced(0)
    row_gather[1].wait()
    gated(1)
    reduced_scatter[0].middle()
    reduced(1)
    spread_g.wait()
    sums[...] = jnp.zeros_like(sums)
    reduced_scatter[0].end()
    output_norm(0)
    gather[0].start()

    @pl.loop(0, tiles)
    def _(j):
        at = span(j, 256)
        act_turned[at, :] = act[:, at].T

    hand_act.start()
    get_qkv.start()
    reduced_scatter[1].middle()
    gather[0].relay()
    reduced_scatter[1].end()
    output_norm(1)
    gather[1].start()
    spread.start()
    gather[0].relay_again()
    gains[...] = jnp.zeros_like(gains)
    gains[3:4] = jnp.sum(sums[...], axis=0, keepdims=True)
    for m in range(2):
        reduced_scatter[m].finish()
    pl.loop(0, 2 * tiles)(turn_rows)
    hand_rows.start()
    get_xs.start()
    gather[0].wait()
    gather[1].relay()
    activity_gradient(0)
    gather[1].relay_again()
    branch(0)
    gather[1].wait()
    hand_back.start()
    activity_gradient(1)
    hand_hidden.start()
    get_raw.start()
    branch_scatter[0].middle()
    branch(1)
    hand_act.wait()
    hand_back.wait()
    quarter_width = width // 4
    z_far = (col // 2 + 2) % 4

    def reduce_tile(k):
        two(
            reduce, pl.ds(0, half_units), span(k, quarter_width), act_turned, span(dp, half_units), back, act_other,
            back_other,
        )

    reduce_tile(z_far)
    reduce_sum.start()

    @pl.loop(1, 4)
    def _(j):
        reduce_tile((z_far + j) % 4)

    pl.semaphore_signal(free.at[0], inc=1, device_id={"dp": 1 - dp}, device_id_type=MESH)
    branch_scatter[0].end()
    branch_scatter[1].middle()
    hand_rows.wait()
    hand_hidden.wait()
    halves = [pl.ds(side * (width // 2), width // 2) for side in range(2)]

    def expand_tile(k):
        for wide in halves:
            two(expand, span(k, 256), wide, turned, span(dp * tiles + k, 256), hidden, turned_other, hidden_other)

    expand_tile(z_far)
    expand_sum.start()

    @pl.loop(1, 4)
    def _(j):
        expand_tile((z_far + j) % 4)

    pl.semaphore_signal(free.at[1], inc=1, device_id={"dp": 1 - dp}, device_id_type=MESH)
    reduce_sum.over_z()
    branch_scatter[1].end()
    sums[...] = jnp.zeros_like(sums)

    @pl.loop(0, share // 16)
    def _(i):
        at = span(i, 16)
        grad = g[at].astype(F32) + merge_scatter.total[at]
        grad_resid[at] = grad
        hat, change = back_of(grad, merged[at], gain_merge[...])
        new_rows[pl.ds(pl.multiple_of(row * share + i * 16, 16), 16), :] = change.astype(BF16)
        product = grad * hat
        sums[...] += product[:8] + product[8:]

    last_gather.start()
    gains[2:3] = jnp.sum(sums[...], axis=0, keepdims=True)
    get_xs.wait()
    pl.loop(0, 2 * tiles)(turn_rows)
    last_gather.relay()
    last_gather.relay_again()
    get_raw.wait()
    get_qkv.wait()
    mix_turned[...] = mix[...].T
    hand_mix.start()
    expand_sum.over_z()
    pl.semaphore_wait(free.at[1], 1)
    hand_xs.start()
    for m in range(2):
        branch_scatter[m].finish()
    last_gather.wait()
    pl.semaphore_wait(free.at[0], 1)
    hand_new.start()

    spread.relay()
    live = (docs[:, 0:1] < 5.0).astype(F32)
    grad_mix[...] = (dot_flipped(new_rows[...], merge[...]) * live).astype(BF16)
    heads_change[:, head_width:] = jnp.zeros((tokens, 2 * head_width), F32)
    for b in range(tokens // QUERY_BLOCK):
        start, count = key_span(b)
        query_at = pl.ds(b * QUERY_BLOCK, QUERY_BLOCK)
        key_at = pl.ds(start, count)
        for h in range(head_width // HD):
            query, key, value = (
                slice(i * head_width + h * HD, i * head_width + (h + 1) * HD) for i in range(3)
            )
            shares = probs[h, b, :, :count]
            change = grad_mix[query_at, h * HD : (h + 1) * HD]
            grad_shares = dot_flipped(change, qkv[key_at, value])
            weighted = shares.astype(F32) * grad_shares
            center = jnp.sum(weighted, axis=1, keepdims=True)
            grad_scores = (weighted - shares.astype(F32) * center).astype(BF16)
            heads_change[query_at, query] = dot(grad_scores, qkv[key_at, key]) * HD**-0.5
            heads_change[key_at, key] += dot(grad_scores.T, qkv[query_at, query]) * HD**-0.5
            heads_change[key_at, value] += dot(shares.T, change)

    joined[:, 2 * head_width :] = heads_change[:, 2 * head_width :].astype(BF16)
    hand_values.start()
    reduce_sum.over_y()
    sums[...] = jnp.zeros_like(sums)

    @pl.loop(0, tokens // 64)
    def _(i):
        at = span(i, 64)
        dots = []
        for j, gain in enumerate((gain_query, gain_key)):
            some = slice(j * head_width, (j + 1) * head_width)
            change = turn(heads_change[at, some], cosine[at], -sine[at])
            hat = raw[at, some] * rates[at, j : j + 1]
            product = change * hat
            sums[:, some] += jnp.sum(product.reshape(8, 8, head_width), axis=0)
            heads_change[at, some] = change * gain[...]
            dots.append(jnp.sum(product * gain[...], axis=1, keepdims=True))
        token_sums.put(at, *dots)

    token_sums.start()
    gains[0:1, span(row, head_width)] = jnp.sum(sums[:, :head_width], axis=0, keepdims=True)
    gains[1:2, span(row, head_width)] = jnp.sum(sums[:, head_width : 2 * head_width], axis=0, keepdims=True)
    for copy in row_gains:
        copy.start()
    hand_mix.wait()
    hand_new.wait()
    mine = span(dp, half_heads)
    for side in range(4):
        wide = pl.ds(side * (width // 4), width // 4)
        merge[:half_heads, wide] = (
            dot(mix_turned[mine, :], back[:, wide]) + dot(mix_other[...], back_other[:, wide])
        ).astype(BF16)
    merge_sum.start()
    hand_values.wait()
    hand_xs.wait()

    @pl.loop(0, tiles)
    def _(j):
        two(
            values_part, span(j, 256), pl.ds(0, head_width), turned, span(dp * tiles + j, 256), joined.at[:, values_at],
            turned_other, joined_other.at[:, values_at],
        )

    values_sum.start()
    token_sums.end()

    @pl.loop(0, tokens // 64)
    def _(i):
        at = span(i, 64)
        dots = stats[at] * (1.0 / width)
        for j in range(2):
            some = slice(j * head_width, (j + 1) * head_width)
            rate = rates[at, j : j + 1]
            hat = raw[at, some] * rate
            joined[at, some] = (rate * (heads_change[at, some] - hat * dots[:, j : j + 1])).astype(BF16)

    hand_joined.start()
    def input_part(j):
        at = span(j, 256)
        part[:, at] = dot_flipped(joined[...], heads[at, :]).astype(BF16)

    pl.loop(first_right, 2 * n)(input_part)
    input_scatter.start_right()
    pl.loop(0, first_right)(input_part)
    input_scatter.start_left()
    hand_joined.wait()

    def heads_tile(k):
        two(heads, span(k, 256), others_at, turned, span(dp * tiles + k, 256), joined, turned_other, joined_other)

    heads_tile(z_far)
    heads_sum.start()

    @pl.loop(1, 4)
    def _(j):
        heads_tile((z_far + j) % 4)

    for copy in row_gains:
        copy.wait()
    gain_row[row] = gains[...]
    total = gain_row[0]
    for k in range(1, 8):
        total = total + gain_row[k]
    gain_sum[0] = total
    gain_col[col] = total
    for copy in col_gains:
        copy.start()
    input_scatter.middle()
    values_sum.over_z()
    merge_sum.over_z()
    heads_sum.over_z()
    reduce_sum.end()
    expand_sum.over_y()
    input_scatter.end()
    final[...] = (grad_resid[...] + input_scatter.total[...]).astype(BF16)
    spread_grad.start()
    values_sum.over_y()
    merge_sum.over_y()
    heads_sum.over_y()
    for copy in col_gains:
        copy.wait()
    total = gain_col[0]
    for k in range(1, 8):
        total = total + gain_col[k]
    gain_sum[1] = total
    core_gains.start()
    spread_grad.relay()
    expand_sum.end()
    values_sum.end()
    merge_sum.end()
    heads_sum.end()
    core_gains.wait()
    gains_grad[...] = gain_sum[1] + gain_core[...]
    input_scatter.finish()
    spread.wait()
    spread_grad.wait()
    for grad in (reduce_sum, expand_sum, values_sum, merge_sum, heads_sum):
        grad.wait()


def on_device(
    block_input,
    cotangent,
    doc_lengths,
    heads_weight,
    heads_first,
    heads_second,
    merge_weight,
    merge_first,
    merge_second,
    expand_weight,
    expand_first,
    expand_second,
    reduce_weight,
    reduce_first,
    reduce_second,
    norm_gains,
    gains_first,
    gains_second,
):
    col_width = block_input.shape[1]
    model_width = col_width * lax.axis_size("col")
    head_width = merge_weight.shape[0]
    unit_width = reduce_weight.shape[0]
    seq_len = block_input.shape[0] * lax.axis_size("row") // lax.axis_size("col")
    share = seq_len // lax.axis_size("row")
    head_count = head_width // HD
    rows_shape = struct((seq_len, model_width), BF16)
    blocks = seq_len // QUERY_BLOCK

    gain_shape = (4, model_width)
    block_output, input_grad, gains_grad, heads_grad, merge_grad, expand_grad, reduce_grad = call(
        layer_kernel, "layer", 1,
        [
            struct(block_input.shape, BF16),
            struct(block_input.shape, BF16),
            struct(gain_shape, F32),
            struct(heads_weight.shape, BF16),
            struct(merge_weight.shape, BF16),
            struct(expand_weight.shape, BF16),
            struct(reduce_weight.shape, BF16),
            rows_shape,
            struct((seq_len, 2 * head_width), F32),
            struct((seq_len, 3 * head_width), BF16),
        ],
        [
            block_input, cotangent, heads_weight, merge_weight, expand_weight, reduce_weight, doc_lengths, norm_gains,
        ],
        [ANY] * 6 + [pl.BlockSpec(memory_space=pltpu.SMEM), VMEM],
        [ANY] * 2 + [VMEM] + [ANY] * 7,
        [
            pltpu.VMEM((seq_len, model_width), BF16),
            pltpu.VMEM((model_width, seq_len), BF16),
            pltpu.VMEM((model_width, 2 * unit_width), BF16),
            pltpu.VMEM((unit_width, model_width), BF16),
            pltpu.VMEM((model_width, 3 * head_width), BF16),
            pltpu.VMEM((head_width, model_width), BF16),
            pltpu.VMEM((seq_len, unit_width), F32),
            pltpu.VMEM((seq_len, unit_width), F32),
            pltpu.VMEM((seq_len, unit_width), BF16),
            pltpu.VMEM((unit_width, seq_len), BF16),
            pltpu.VMEM((seq_len, model_width), BF16),
            pltpu.VMEM((seq_len, model_width), BF16),
            pltpu.VMEM((seq_len, 2 * unit_width), BF16),
            pltpu.VMEM((head_count, blocks, QUERY_BLOCK, WINDOW + QUERY_BLOCK), BF16),
            pltpu.VMEM((seq_len, head_width), BF16),
            pltpu.VMEM((head_width, seq_len), BF16),
            pltpu.VMEM((seq_len, 128), F32),
            pltpu.VMEM((seq_len, 128), F32),
            pltpu.VMEM((seq_len, head_width), BF16),
            pltpu.VMEM((share, model_width), BF16),
            pltpu.VMEM((share, model_width), BF16),
            pltpu.VMEM((share, model_width), F32),
            pltpu.VMEM((share, model_width), F32),
            pltpu.VMEM((share, model_width), F32),
            pltpu.VMEM((share, model_width), BF16),
            pltpu.VMEM((8, model_width), F32),
            pltpu.VMEM((seq_len, 256), F32),
            pltpu.VMEM(gain_shape, F32),
            pltpu.VMEM((8, *gain_shape), F32),
            pltpu.VMEM((8, *gain_shape), F32),
            pltpu.VMEM(gain_shape, F32),
            pltpu.VMEM((2, *gain_shape), F32),
            pltpu.VMEM((unit_width // 2, seq_len), BF16),
            pltpu.VMEM((model_width // 2, seq_len), BF16),
            pltpu.VMEM((seq_len, model_width), BF16),
            pltpu.VMEM((seq_len, model_width), BF16),
            pltpu.VMEM((head_width // 2, seq_len), BF16),
            pltpu.VMEM((seq_len, 3 * head_width), BF16),
            pltpu.VMEM((model_width // 2, head_width), BF16),
            pltpu.VMEM((3, 8, share, block_input.shape[1]), BF16),
            pltpu.VMEM((seq_len, HD), F32),
            pltpu.VMEM((8, seq_len), F32),
            pltpu.VMEM((seq_len, HD), F32),
            pltpu.VMEM((seq_len, HD), F32),
            pltpu.SemaphoreType.REGULAR((2,)),
            DMA((8,)), DMA((3,)), DMA((3,)), DMA((16,)), DMA((15,)), DMA((16,)), DMA((15,)), DMA((15,)), DMA((15,)),
            DMA((9,)), DMA((9,)), DMA((8,)), DMA((8,)), DMA((16,)), DMA((15,)),
        ]
        + gather_scratch() * 6
        + scatter_scratch(share, model_width) + [DMA((14,))] * 10
        + sums_scratch(seq_len) * 2
        + grad_sum_scratch(reduce_weight.shape) + grad_sum_scratch(expand_weight.shape)
        + grad_sum_scratch(merge_weight.shape)
        + grad_sum_scratch((heads_weight.shape[0], head_width))
        + grad_sum_scratch((heads_weight.shape[0], 2 * head_width))
        + bring_scratch() * 4,
    )[:7]
    return update(
        block_output,
        input_grad,
        (heads_grad, heads_weight, heads_first, heads_second),
        (merge_grad, merge_weight, merge_first, merge_second),
        (expand_grad, expand_weight, expand_first, expand_second),
        (reduce_grad, reduce_weight, reduce_first, reduce_second),
        (gains_grad, norm_gains, gains_first, gains_second),
    )


def solution(mesh):
    return jax.shard_map(
        on_device,
        mesh=mesh,
        in_specs=(
            P(("dp", "row"), "col"),
            P(("dp", "row"), "col"),
            P(("dp", "col"), None),
            P("col", "row"),
            P("col", "row"),
            P("col", "row"),
            P("row", "col"),
            P("row", "col"),
            P("row", "col"),
            P("col", "row"),
            P("col", "row"),
            P("col", "row"),
            P("row", "col"),
            P("row", "col"),
            P("row", "col"),
            P(),
            P(),
            P(),
        ),
        out_specs=(
            P(("dp", "row"), "col"),
            P(("dp", "row"), "col"),
            P("col", "row"),
            P("col", "row"),
            P("col", "row"),
            P("col", "row"),
            P("col", "row"),
            P("row", "col"),
            P("row", "col"),
            P("row", "col"),
            P("row", "col"),
            P("row", "col"),
            P("col", "row"),
            P("col", "row"),
            P("col", "row"),
            P("col", "row"),
            P("col", "row"),
            P("row", "col"),
            P("row", "col"),
            P("row", "col"),
            P("row", "col"),
            P("row", "col"),
            P(),
            P(),
            P(),
            P(),
        ),
        check_vma=False,
    )
```

```python
import math

import jax
import jax.numpy as jnp
from jax import lax
from jax.experimental import pallas as pl
from jax.experimental.pallas import tpu as pltpu
from jax.sharding import PartitionSpec as P

HD = 128
WINDOW = 256
STEP = 5


EPS = 1e-06
THETA = 500000.0
LR = 0.02
LR_GAIN = 0.2
BETA_ONE = 0.5
BETA_TWO = 0.5
DECAY = 0.1
ADAM_EPS = 1e-08

BF16 = jnp.bfloat16
SCATTER_LEFT, GATHER_LEFT, INPUT_LEFT = 8, 8, 16
F32 = jnp.float32
MESH = pl.DeviceIdType.MESH
ANY = pl.BlockSpec(memory_space=pl.ANY)
VMEM = pl.BlockSpec(memory_space=pltpu.VMEM)
DMA = pltpu.SemaphoreType.DMA


def documents(lengths, shape, axis):
    tokens = lax.broadcasted_iota(jnp.int32, shape, axis)
    docs, starts, end = jnp.zeros(shape, F32), jnp.zeros(shape, jnp.int32), jnp.int32(0)
    for j in range(lengths.shape[1]):
        end = end + lengths[0, j]
        passed = tokens >= end
        docs = docs + passed.astype(F32)
        starts = starts + jnp.where(passed, lengths[0, j], 0)
    return docs, starts


def adamw(weight, gradient, first_mom, second_mom, step_rate, decay_rate):
    mean_new = BETA_ONE * first_mom + (1.0 - BETA_ONE) * gradient
    square_new = BETA_TWO * second_mom + (1.0 - BETA_TWO) * gradient * gradient
    fix_one = 1.0 - BETA_ONE**STEP
    fix_two = 1.0 - BETA_TWO**STEP
    update = mean_new / fix_one / (jnp.sqrt(square_new / fix_two) + ADAM_EPS) + decay_rate * weight
    return (mean_new, square_new, weight - step_rate * update)


def here():
    return lax.axis_index("dp"), lax.axis_index("row"), lax.axis_index("col")


def row_peer(row, d):
    return (row // 4 + d // 4) % 2 * 4 + (row % 4 + d % 4) % 4


def z_peer(col, d):
    return (col // 2 + d) % 4 * 2 + col % 2


def z_source(col, d):
    return (col // 2 + 4 - d) % 4 * 2 + col % 2


def y_peer(col):
    return col // 2 * 2 + 1 - col % 2


def remote(source, target, sent, arrived, **where):
    return pltpu.make_async_remote_copy(
        src_ref=source,
        dst_ref=target,
        send_sem=sent,
        recv_sem=arrived,
        device_id=where,
        device_id_type=MESH,
    )


def meet(rows=False, cols=False, weights=False, core=False, spread_in=False, spread_out=False):
    dp, row, col = here()
    barrier = pltpu.get_barrier_semaphore()
    count = 0

    def greet(**where):
        pl.semaphore_signal(barrier, inc=1, device_id=where, device_id_type=MESH)

    if rows:
        for d in range(1, 8):
            greet(row=row_peer(row, d))
        count = count + 7
    if cols:
        for d in range(1, 8):
            greet(col=(col + d) % 8)
        count = count + 7
    if weights:
        greet(col=y_peer(col))
        for d in (1, 3):
            greet(col=z_peer(col, d))
        count = count + 3
    if core:
        greet(dp=1 - dp)
        count = count + 1
    for wanted, inward in ((spread_in, True), (spread_out, False)):
        if wanted:
            for k in range(8):
                at_row, at_col = (col, k) if inward else (k, row)

                @pl.when(jnp.logical_not((at_row == row) & (at_col == col)))
                def _():
                    greet(row=at_row, col=at_col)

            count = count + 8 - (row == col).astype(jnp.int32)
    pl.semaphore_wait(barrier, count)


class Exchange:
    def __init__(self, first, second, source, middle, target, sent, arrived):
        dp, row, col = here()
        a, b = (row, col) if first == "row" else (col, row)
        self.keep = pltpu.make_async_copy(source(a), middle.at[a], sent.at[7])
        self.copies = []
        for d in range(1, 8):
            k = (a + d) % 8
            self.copies.append(remote(source(k), middle.at[a], sent.at[d - 1], arrived.at[d - 1], **{first: k}))
        self.passed = []
        for j in range(8):
            self.passed.append(
                (
                    b == j,
                    remote(middle.at[j], target(b), sent.at[8 + j], arrived.at[7 + b], **{second: j}),
                    remote(middle.at[j], target(j), sent.at[8 + j], arrived.at[7 + j], **{second: j}),
                    pltpu.make_async_copy(middle.at[j], target(b), sent.at[8 + j]),
                )
            )

    def start(self):
        self.keep.start()
        for copy in self.copies:
            copy.start()

    def relay(self):
        self.keep.wait()
        for copy in self.copies:
            copy.wait_recv()
        for mine, copy, _, local in self.passed:
            pl.when(jnp.logical_not(mine))(copy.start)
            pl.when(mine)(local.start)

    def wait(self):
        for mine, copy, came, local in self.passed:
            pl.when(jnp.logical_not(mine))(came.wait_recv)
            pl.when(jnp.logical_not(mine))(copy.wait_send)
            pl.when(mine)(local.wait)
        for copy in self.copies:
            copy.wait_send()


def half_of(kind, ref, c, h):
    if kind == "tall":
        count = ref.shape[0] // 16
        return ref.at[pl.ds(pl.multiple_of((2 * c + h) * count, count), count)]
    count, width = ref.shape[0] // 2, ref.shape[1] // 8
    return ref.at[
        pl.ds(pl.multiple_of(h * count, count), count), pl.ds(pl.multiple_of(c * width, width), width)
    ]


def half_shard(ref, h):
    count = ref.shape[0] // 2
    return ref.at[pl.ds(pl.multiple_of(h * count, count), count)]


def mean_rate(values):
    return lax.rsqrt(jnp.mean(values * values, axis=-1, keepdims=True) + EPS)


def call(kernel, name, number, outs, ins, in_specs, out_specs, scratch):
    return pl.pallas_call(
        kernel,
        name=name,
        out_shape=outs,
        in_specs=in_specs,
        out_specs=out_specs,
        scratch_shapes=scratch,
        compiler_params=pltpu.CompilerParams(
            collective_id=number, has_side_effects=True, vmem_limit_bytes=62 * 2**20
        ),
    )(*ins)


def struct(shape, kind):
    return jax.ShapeDtypeStruct(shape, kind)


def dot(left, right):
    return jnp.dot(left, right, preferred_element_type=F32)


def dot_flipped(left, right):
    return lax.dot_general(left, right, (((1,), (1,)), ((), ())), preferred_element_type=F32)


def span(k, count):
    return pl.ds(pl.multiple_of(k * count, count), count)


def near_row(row, dx, dy):
    return (row // 4 + dy) % 2 * 4 + (row % 4 + dx) % 4


class Scatter:
    def __init__(self, part, total, from_y, from_x, last_y, last_x, stage_y, stage_x, sent, arrived):
        dp, row, col = here()
        self.row, self.part, self.total = row, part, total
        self.from_y, self.from_x, self.last_y, self.last_x = from_y, from_x, last_y, last_x
        self.stage_y, self.stage_x = stage_y, stage_x
        self.count, self.left = total.shape[0], from_x.shape[3]
        self.sides = (pl.ds(0, self.left), pl.ds(self.left, total.shape[1] - self.left))
        number = iter(range(14))

        def copy(source, target, dx, dy):
            i = next(number)
            return remote(source, target, sent.at[i], arrived.at[i], row=near_row(row, dx, dy))

        self.y_first = {dx: copy(self.block(dx, 1, 1), from_y.at[dx], 0, 1) for dx in (1, 3, 2, 0)}
        self.x_first = {
            (dx, dy): copy(self.block(dx, dy, 0), from_x.at[dy, dx - 1], dx, 0)
            for dy in (1, 0)
            for dx in (1, 3, 2)
        }
        self.x_last = {dx: copy(stage_x.at[dx - 1], last_x.at[dx - 1], dx, 0) for dx in (1, 3, 2)}
        self.y_last = copy(stage_y, last_y, 0, 1)

    def block(self, dx, dy, side):
        return self.part.at[span(near_row(self.row, dx, dy), self.count), self.sides[side]]

    def start_right(self):
        for copy in self.y_first.values():
            copy.start()

    def start_left(self):
        for copy in self.x_first.values():
            copy.start()

    def chunks(self, body):
        @pl.loop(0, self.count // 16)
        def _(i):
            body(span(i, 16))

    def middle(self):
        for dx in (1, 3, 2):
            self.y_first[dx].wait_recv()
            own = self.block(dx, 0, 1)

            def add(at):
                self.stage_x[dx - 1, at] = (own[at].astype(F32) + self.from_y[dx, at].astype(F32)).astype(BF16)

            self.chunks(add)
            self.x_last[dx].start()
        for dx in (1, 3, 2):
            self.x_first[dx, 1].wait_recv()
        other = self.block(0, 1, 0)

        def add(at):
            total = other[at].astype(F32)
            for k in range(3):
                total = total + self.from_x[1, k, at].astype(F32)
            self.stage_y[at] = total.astype(BF16)

        self.chunks(add)
        self.y_last.start()

    def end(self):
        self.y_first[0].wait_recv()
        for dx in (1, 3, 2):
            self.x_first[dx, 0].wait_recv()
            self.x_last[dx].wait_recv()
        self.y_last.wait_recv()
        left, right = self.block(0, 0, 0), self.block(0, 0, 1)

        def add(at):
            total = left[at].astype(F32) + self.last_y[at].astype(F32)
            for k in range(3):
                total = total + self.from_x[0, k, at].astype(F32)
            self.total[at, self.sides[0]] = total
            total = right[at].astype(F32) + self.from_y[0, at].astype(F32)
            for k in range(3):
                total = total + self.last_x[k, at].astype(F32)
            self.total[at, self.sides[1]] = total

        self.chunks(add)

    def finish(self):
        for copies in (self.y_first, self.x_first, self.x_last):
            for copy in copies.values():
                copy.wait_send()
        self.y_last.wait_send()


def scatter_scratch(share, width):
    left = SCATTER_LEFT * width // 16
    right = width - left
    return [
        pltpu.VMEM((share, width), F32),
        pltpu.VMEM((4, share, right), BF16),
        pltpu.VMEM((2, 3, share, left), BF16),
        pltpu.VMEM((share, left), BF16),
        pltpu.VMEM((3, share, right), BF16),
        pltpu.VMEM((share, left), BF16),
        pltpu.VMEM((3, share, right), BF16),
        DMA((14,)),
        DMA((14,)),
    ]


class Gather:
    def __init__(self, whole, share, left, sent, arrived):
        dp, row, col = here()
        self.row = row
        number = iter(range(19))
        sides = (pl.ds(0, left), pl.ds(left, whole.shape[1] - left))
        right = left < whole.shape[1]

        def copy(fx, fy, side, dx, dy, start=0, count=share):
            i = next(number)
            k = near_row(row, fx, fy)
            ref = whole.at[pl.ds(pl.multiple_of(k * share + start, count), count), sides[side]]
            return remote(ref, ref, sent.at[i], arrived.at[i], row=near_row(row, dx, dy))

        part = share // 2
        steps = (1, 3, 2)
        two = steps[:2]
        self.y_left = copy(0, 0, 0, 0, 1)
        self.x_left = [copy(0, 0, 0, dx, 0) for dx in two]
        self.on_left = [copy(4 - dx, 0, 0, dx, 0, i * part, part) for i, dx in enumerate(two)]
        self.y_right, self.x_right, self.y_near, self.on_other = [], [], [], []
        if right:
            self.x_other = [copy(0, 1, 0, dx, 0) for dx in steps]
            self.y_right = [copy(0, 0, 1, 0, 1)]
            self.x_right = [copy(0, 0, 1, dx, 0) for dx in steps]
            self.y_near = [copy(4 - dx, 0, 1, 0, 1) for dx in steps]
        else:
            self.x_other = [copy(0, 1, 0, dx, 0) for dx in two]
            self.on_other = [copy(4 - dx, 1, 0, dx, 0, i * part, part) for i, dx in enumerate(two)]

    def start(self):
        for copy in (self.y_left, *self.x_right, *self.y_right, *self.x_left):
            copy.start()

    def relay(self):
        self.y_left.wait_recv()
        for copy in self.x_other:
            copy.start()
        for i, came in enumerate(self.x_right):
            came.wait_recv()
            self.y_near[i].start()

    def relay_again(self):
        for i in range(2):
            self.x_left[i].wait_recv()
            self.on_left[i].start()
        for i, copy in enumerate(self.on_other):
            self.x_other[i].wait_recv()
            copy.start()

    def wait(self):
        for copy in (*self.y_right, *self.x_other[len(self.on_other) :], *self.on_left, *self.on_other, *self.y_near):
            copy.wait_recv()
        for copy in (self.y_left, *self.x_left, *self.x_other, *self.on_left, *self.on_other, *self.y_right,
                     *self.x_right, *self.y_near):
            copy.wait_send()


def gather_scratch():
    return [DMA((19,)), DMA((19,))]


def cols(ref, k, width):
    return ref.at[:, pl.ds(pl.multiple_of(k * width, width), width)]


def rows_of(ref, k, count):
    return ref.at[pl.ds(pl.multiple_of(k * count, count), count)]


def back_of(grad, values, gain):
    rate = mean_rate(values)
    hat = values * rate
    grad_hat = grad * gain
    dots = jnp.mean(grad_hat * hat, axis=-1, keepdims=True)
    return hat, rate * (grad_hat - hat * dots)


class GradSum:
    def __init__(self, kind, part, out, between, far, near, sent, arrived):
        dp, _, col = here()
        self.kind, self.part, self.col = kind, part, col
        self.between, self.far, self.near = between, far, near
        self.rows, self.width = near.shape[1], near.shape[2]
        number = iter(range(10))

        def copy(source, target, **where):
            i = next(number)
            return remote(source, target, sent.at[i], arrived.at[i], **where)

        self.steps = (1, 3)
        self.on = [
            [
                copy(self.piece(self.z_block(2, k), i), between.at[i, k], col=z_peer(col, d))
                for k in range(2)
            ]
            for i, d in enumerate(self.steps)
        ]
        self.zs = [
            [copy(self.block(self.z_block(d, k)), far.at[i, k], col=z_peer(col, d)) for k in range(2)]
            for i, d in enumerate(self.steps)
        ]
        self.ys = copy(near.at[0], near.at[1], col=y_peer(col))
        self.last = copy(near.at[0], half_shard(out, dp), dp=1 - dp)
        self.keep = pltpu.make_async_copy(near.at[0], half_shard(out, dp), sent.at[10])

    def z_block(self, d, k):
        return z_peer(self.col, d) // 2 * 2 + k

    def block(self, c):
        if self.kind == "tall":
            return self.part.at[span(c, self.rows)]
        return self.part.at[:, span(c, self.width)]

    def piece(self, c, i):
        return self.block(c).at[pl.ds(i * (self.rows // 2), self.rows // 2)]

    def each(self, rows, body):
        count = min(rows, 32768 // self.width // 16 * 16)

        @pl.loop(0, rows // count)
        def _(i):
            body(span(i, count))

    def start(self):
        for pair in self.on:
            for copy in pair:
                copy.start()

    def over_z(self):
        for i, d in enumerate(self.steps):
            for k in range(2):
                self.on[i][k].wait_recv()
                own = self.piece(self.z_block(d, k), i)

                def add(at):
                    own[at] = (own[at].astype(F32) + self.between[i, k, at].astype(F32)).astype(BF16)

                self.each(self.rows // 2, add)
                self.zs[i][k].start()

    def over_y(self):
        for pair in self.zs:
            for copy in pair:
                copy.wait_recv()
        yl = self.col % 2
        keep, give = self.block(self.col), self.block(y_peer(self.col))

        def total(at, ref, k):
            return (
                ref[at].astype(F32) + self.far[0, k, at].astype(F32) + self.far[1, k, at].astype(F32)
            ).astype(BF16)

        def add(at):
            self.near[0, at] = total(at, give, 1 - yl)

        self.each(self.rows, add)
        self.ys.start()

        def add(at):
            keep[at] = total(at, keep, yl)

        self.each(self.rows, add)
        for pair in (*self.zs, *self.on):
            for copy in pair:
                copy.wait_send()

    def end(self):
        self.ys.wait()
        keep = self.block(self.col)

        def add(at):
            self.near[0, at] = (keep[at].astype(F32) + self.near[1, at].astype(F32)).astype(BF16)

        self.each(self.rows, add)
        self.last.start()
        self.keep.start()

    def wait(self):
        self.last.wait()
        self.keep.wait()


def grad_sum_scratch(shape):
    rows, width = shape[0] // 2, shape[1]
    return [
        pltpu.VMEM((2, 2, rows // 2, width), BF16),
        pltpu.VMEM((2, 2, rows, width), BF16),
        pltpu.VMEM((2, rows, width), BF16),
        DMA((11,)),
        DMA((10,)),
    ]


class Bring:
    def __init__(self, kind, shape, whole, sent, arrived):
        dp, _, col = here()
        rows, width = shape
        near = y_peer(col)
        number = iter(range(20))

        def block(c, s=None):
            count, at = (rows // 2, dp) if s is None else (rows // 4, 2 * dp + s)
            if kind == "tall":
                return whole.at[span((2 if s is None else 4) * c + at, count)]
            return whole.at[span(at, count), span(c, width)]

        def copy(source, target, **where):
            i = next(number)
            return remote(source, target, sent.at[i], arrived.at[i], **where)

        self.place = whole.at[span(col, rows)] if kind == "tall" else whole.at[:, span(col, width)]
        self.y_own = copy(block(col), block(col), col=near)
        self.z_own = [copy(block(col), block(col), col=z_peer(col, d)) for d in (1, 3)]
        self.z_near = [copy(block(near), block(near), col=z_peer(col, d)) for d in (1, 3)]
        self.on, self.on_near, self.a_own, self.a_near = [], [], [], []
        self.a_far, self.a_far_near = [], []
        for i, d in enumerate((1, 3)):
            came, two = z_source(col, d), z_peer(col, 2)
            self.on.append(copy(block(came, i), block(came, i), col=z_peer(col, d)))
            self.on_near.append(copy(block(y_peer(came), i), block(y_peer(came), i), col=z_peer(col, d)))
            self.a_own.append(copy(block(came), block(came), dp=1 - dp))
            self.a_near.append(copy(block(y_peer(came)), block(y_peer(came)), dp=1 - dp))
            self.a_far.append(copy(block(two, i), block(two, i), dp=1 - dp))
            self.a_far_near.append(copy(block(y_peer(two), i), block(y_peer(two), i), dp=1 - dp))
        self.a_y = copy(block(near), block(near), dp=1 - dp)

    def start_y(self):
        self.y_own.start()

    def start_z(self):
        for copy in self.z_own:
            copy.start()

    def relay(self):
        self.y_own.wait_recv()
        for copy in (*self.z_near, self.a_y):
            copy.start()

    def relay_own(self):
        for i in range(2):
            self.z_own[i].wait_recv()
            self.on[i].start()
            self.a_own[i].start()

    def relay_near(self):
        for i in range(2):
            self.z_near[i].wait_recv()
            self.on_near[i].start()
            self.a_near[i].start()

    def hand_over(self):
        for i in range(2):
            self.on[i].wait_recv()
            self.a_far[i].start()
        for i in range(2):
            self.on_near[i].wait_recv()
            self.a_far_near[i].start()

    def wait(self):
        for copy in (self.a_y, *self.a_own, *self.a_near, *self.a_far, *self.a_far_near):
            copy.wait()
        for copy in (self.y_own, *self.z_own, *self.z_near, *self.on, *self.on_near):
            copy.wait_send()


def bring_scratch():
    return [DMA((20,)), DMA((20,))]


class SpreadIn:
    def __init__(self, source, target, sent, arrived):
        dp, row, col = here()
        self.row, self.col = row, col
        self.copies, self.waits = [], []
        for k in range(8):
            out = remote(source(k), target(k, col), sent.at[k], arrived.at[col], row=k, col=row)
            came = remote(source(k), target(row, k), sent.at[k], arrived.at[k], row=k, col=row)
            local = pltpu.make_async_copy(source(k), target(k, col), sent.at[k])
            self.copies.append(((row == k) & (row == col), out, local))
            self.waits.append(((row == col) & (col == k), came))

    def start(self):
        for mine, out, local in self.copies:
            pl.when(jnp.logical_not(mine))(out.start)
            pl.when(mine)(local.start)

    def wait(self):
        for mine, came in self.waits:
            pl.when(jnp.logical_not(mine))(came.wait_recv)
        for mine, out, local in self.copies:
            pl.when(jnp.logical_not(mine))(out.wait_send)
            pl.when(mine)(local.wait)


class TokenSums:
    def __init__(self, stats, mine, came, sent, arrived):
        dp, row, col = here()
        self.stats, self.mine, self.came = stats, mine, came
        self.copies = [
            remote(mine, came.at[d - 1], sent.at[d - 1], arrived.at[d - 1], row=row_peer(row, d))
            for d in range(1, 8)
        ]

    def put(self, at, one, two):
        lane = lax.broadcasted_iota(jnp.int32, (one.shape[0], 128), 1)
        self.stats[at] = jnp.where(lane == 0, one, jnp.where(lane == 1, two, 0.0))

    def start(self):
        self.mine[...] = self.stats[...].T[:8]
        for copy in self.copies:
            copy.start()

    def end(self):
        total = self.mine[...]
        for d, copy in enumerate(self.copies):
            copy.wait_recv()
            total = total + self.came[d]
        self.stats[...] = jnp.concatenate([total] * 16, axis=0).T
        for copy in self.copies:
            copy.wait_send()


def sums_scratch(tokens):
    return [pltpu.VMEM((8, tokens), F32), pltpu.VMEM((7, 8, tokens), F32), DMA((7,)), DMA((7,))]


def turn(values, cosine, sine):
    heads = [values[:, i : i + HD] for i in range(0, values.shape[1], HD)]
    return jnp.concatenate([h * cosine + pltpu.roll(h, HD // 2, 1) * sine for h in heads], axis=1)


QUERY_BLOCK = 128


def key_span(b):
    start = max(0, b * QUERY_BLOCK - WINDOW)
    return start, (b + 1) * QUERY_BLOCK - start


UPDATE_STEPS = 4


def update_kernel(*refs):
    ins, outs = refs[:22], refs[22:]
    outs[0][...] = ins[0][...]
    outs[1][...] = ins[1][...].astype(F32)
    for i in range(4):
        gradient, weight, first_mom, second_mom = (ref[...] for ref in ins[2 + 4 * i : 6 + 4 * i])
        gradient = gradient.astype(F32)
        mean, square, fresh = adamw(weight, gradient, first_mom, second_mom, LR, DECAY)
        for ref, value in zip(outs[2 + 5 * i : 7 + 5 * i], (gradient, mean, square, fresh, fresh), strict=True):
            ref[...] = value.astype(ref.dtype)

    @pl.when(pl.program_id(0) == 0)
    def _():
        gradient, weight, first_mom, second_mom = (ref[...] for ref in ins[18:])
        mean, square, fresh = adamw(weight, gradient, first_mom, second_mom, LR_GAIN, 0.0)
        for ref, value in zip(outs[22:], (gradient, mean, square, fresh), strict=True):
            ref[...] = value


def update(block_output, input_grad, *groups):
    def part(shape):
        return pl.BlockSpec((shape[0] // UPDATE_STEPS, shape[1]), lambda i: (i, 0))

    ins, outs, in_specs, out_specs = [block_output, input_grad], [], [], []
    outs += [struct(block_output.shape, BF16), struct(input_grad.shape, F32)]
    in_specs += [part(block_output.shape)] * 2
    out_specs += [part(block_output.shape)] * 2
    for group in groups[:4]:
        shape = group[0].shape
        ins += group
        in_specs += [part(shape)] * 4
        outs += [struct(shape, F32)] * 4 + [struct(shape, BF16)]
        out_specs += [part(shape)] * 5
    whole = pl.BlockSpec(groups[4][0].shape, lambda i: (0, 0))
    ins += groups[4]
    in_specs += [whole] * 4
    outs += [struct(groups[4][0].shape, F32)] * 4
    out_specs += [whole] * 4
    return tuple(
        pl.pallas_call(
            update_kernel,
            name="update",
            grid=(UPDATE_STEPS,),
            out_shape=outs,
            in_specs=in_specs,
            out_specs=out_specs,
            compiler_params=pltpu.CompilerParams(vmem_limit_bytes=62 * 2**20),
        )(*ins)
    )


def layer_kernel(
    x, g_in, heads_in, merge_in, expand_in, reduce_in, lengths, gain_all,
    out, input_grad, gains_grad, heads_grad, merge_grad, expand_grad, reduce_grad, xs_keep, raw_keep, qkv_keep,
    rows, turned, expand, reduce, heads, merge, gate, up, act, act_turned, part, back, hidden, probs, mix, mix_turned,
    rates, stats, grad_mix, done, final, grad_resid, merged, residual, g, sums, grad_gate,
    gains, gain_row, gain_col, gain_core, gain_sum, act_other, turned_other, hidden_other, back_other, mix_other,
    joined_other, values_part, exchanged, docs, doc_row, cosine, sine, free, load, keep, late, osent, ocame, isent, icame, nsent, ncame, xsent, xcame,
    asent, acame, bsent, bcame, g1sent, g1came, g2sent, g2came, g3sent, g3came, g4sent, g4came, g5sent, g5came, g6sent, g6came, *refs,
):
    dp, row, col = here()
    share, width = residual.shape
    tokens, units = act.shape
    head_width = mix.shape[1]
    tiles = units // 256
    n, first_right = width // 512, SCATTER_LEFT * width // 16 // 256
    gain_query, gain_key = (gain_all.at[i : i + 1, span(row, head_width)] for i in range(2))
    gain_merge, gain_reduce = (gain_all.at[i : i + 1] for i in range(2, 4))
    batch, half_share = tokens // 2, share // 2

    def scatter_of(i, m=None):
        sems = refs[7 + 2 * i : 9 + 2 * i]
        if m is None:
            return Scatter(part, *refs[:7], *sems)
        at = pl.ds(m * half_share, half_share)
        total, from_y, from_x, last_y, last_x, stage_y, stage_x = refs[:7]
        return Scatter(
            part.at[pl.ds(m * batch, batch)], total.at[at], from_y.at[:, at], from_x.at[:, :, at], last_y.at[at],
            last_x.at[:, at], stage_y.at[at], stage_x.at[:, at], *sems,
        )

    merge_scatter, input_scatter = scatter_of(0), scatter_of(5)
    reduced_scatter = [scatter_of(1 + m, m) for m in range(2)]
    branch_scatter = [scatter_of(3 + m, m) for m in range(2)]
    first_sums = TokenSums(rates, *refs[19:23])
    token_sums = TokenSums(stats, *refs[23:27])
    half_units, half_width, half_heads = units // 2, width // 2, head_width // 2
    reduce_part, merge_part_ref = reduce.at[pl.ds(0, half_units)], merge.at[pl.ds(0, half_heads)]
    expand_part, heads_part = expand.at[pl.ds(0, half_width)], heads.at[pl.ds(0, half_width)]
    reduce_sum = GradSum("wide", reduce_part, reduce_grad, *refs[27:32])
    expand_sum = GradSum("tall", expand_part, expand_grad, *refs[32:37])
    merge_sum = GradSum("wide", merge_part_ref, merge_grad, *refs[37:42])
    values_at, others_at = pl.ds(2 * head_width, head_width), pl.ds(0, 2 * head_width)
    values_sum = GradSum("tall", values_part, heads_grad.at[:, values_at], *refs[42:47])
    heads_sum = GradSum("tall", heads_part.at[:, others_at], heads_grad.at[:, others_at], *refs[47:52])
    bring_heads = Bring("tall", heads_in.shape, heads, *refs[52:54])
    bring_merge = Bring("wide", merge_in.shape, merge, *refs[54:56])
    bring_reduce = Bring("wide", reduce_in.shape, reduce, *refs[56:58])
    bring_expand = Bring("tall", expand_in.shape, expand, *refs[58:60])
    gather_x = Gather(back, share, INPUT_LEFT * width // 16, g1sent, g1came)
    left = GATHER_LEFT * width // 16
    row_gather = [
        Gather(rows.at[pl.ds(m * batch, batch)], half_share, left, *sems)
        for m, sems in enumerate(((g2sent, g2came), (g3sent, g3came)))
    ]
    gather = [
        Gather(back.at[pl.ds(m * batch, batch)], half_share, left, *sems)
        for m, sems in enumerate(((g4sent, g4came), (g5sent, g5came)))
    ]
    last_gather = Gather(back, share, left, g6sent, g6came)
    spread_x = SpreadIn(
        lambda k: rows_of(x, k, share), lambda k, c: back.at[span(k, share), span(c, 256)], asent, acame
    )
    spread_g = Exchange(
        "row", "col", lambda k: rows_of(g_in, k, share), exchanged.at[0], lambda k: g.at[:, span(k, 256)], bsent, bcame
    )
    spread = Exchange(
        "col", "row", lambda k: cols(done, k, 256), exchanged.at[1], lambda k: rows_of(out, k, 64), osent, ocame
    )
    spread_grad = Exchange(
        "col", "row", lambda k: cols(final, k, 256), exchanged.at[2], lambda k: rows_of(input_grad, k, 64), isent, icame
    )
    row_gains = [
        remote(gains, gain_row.at[row], nsent.at[d - 1], ncame.at[d - 1], row=row_peer(row, d))
        for d in range(1, 8)
    ]
    col_gains = [
        remote(gain_sum.at[0], gain_col.at[col], nsent.at[6 + d], ncame.at[6 + d], col=(col + d) % 8)
        for d in range(1, 8)
    ]
    core_gains = remote(gain_sum.at[1], gain_core, nsent.at[14], ncame.at[14], dp=1 - dp)

    raw, qkv, new_rows = up.at[:, : 2 * head_width], act.at[:, : 3 * head_width], back
    heads_change = gate.at[:, : 3 * head_width]
    joined = hidden.at[:, : 3 * head_width]
    puts = [
        pltpu.make_async_copy(source, target, keep.at[i])
        for i, (source, target) in enumerate(((back, xs_keep), (raw, raw_keep), (qkv, qkv_keep)))
    ]
    get_xs = pltpu.make_async_copy(xs_keep, rows, late.at[0])
    get_raw = pltpu.make_async_copy(raw_keep, raw, late.at[1])
    get_qkv = pltpu.make_async_copy(qkv_keep, qkv, late.at[2])

    shard_rows, quarter = heads_in.shape[0], reduce_in.shape[0] // 4
    heads32 = gate.at[:shard_rows, : heads_in.shape[1]]
    merge32 = gate.at[:shard_rows, heads_in.shape[1] :]
    reduce32 = [gate.at[shard_rows:, pl.ds(i * 256, 256)] for i in range(4)]
    expand32 = [up.at[pl.ds(i * shard_rows, shard_rows)] for i in range(2)]
    moves = (
        [(heads_in, heads32), (merge_in, merge32)]
        + [(reduce_in.at[pl.ds(i * quarter, quarter)], reduce32[i]) for i in range(4)]
        + [(expand_in.at[:, pl.ds(i * units, units)], expand32[i]) for i in range(2)]
    )
    loads = [pltpu.make_async_copy(source, target, load.at[i]) for i, (source, target) in enumerate(moves)]
    for copy in loads:
        copy.start()

    def narrow(i, target):
        loads[i].wait()
        source = moves[i][1]

        @pl.loop(0, source.shape[0] // 16)
        def _(k):
            at = span(k, 16)
            target[at] = source[at].astype(BF16)

    def hand(i, source, target):
        return remote(source, target, xsent.at[i], xcame.at[i], dp=1 - dp)

    hand_act = hand(0, act_turned.at[span(1 - dp, half_units)], act_other)
    hand_rows = hand(1, turned.at[span(1 - dp, half_width)], turned_other)
    hand_back = hand(2, back, back_other)
    hand_hidden = hand(3, hidden, hidden_other)
    hand_mix = hand(4, mix_turned.at[span(1 - dp, half_heads)], mix_other)
    hand_new = hand(5, back, back_other)
    hand_xs = hand(6, turned.at[span(1 - dp, half_width)], turned_other)
    hand_joined = hand(7, joined.at[:, others_at], joined_other.at[:, others_at])
    hand_values = hand(8, joined.at[:, values_at], joined_other.at[:, values_at])

    def turn_rows(j):
        values = rows[:, span(j, 256)].T
        turned[span(j, 128), :] = values[:128]
        turned[span(2 * tiles + j, 128), :] = values[128:]

    def two(target, at, wide, own, own_at, right, other, right_other):
        target[at, wide] = (
            dot(own[own_at, :], right[:, wide]) + dot(other[at, :], right_other[:, wide])
        ).astype(BF16)

    meet(rows=True, cols=True, core=True, spread_in=True)
    spread_x.start()
    narrow(0, bring_heads.place)
    bring_heads.start_y()
    bring_heads.start_z()
    narrow(1, bring_merge.place)
    bring_merge.start_y()
    bring_merge.start_z()
    for i in range(4):
        narrow(2 + i, bring_reduce.place.at[pl.ds(i * quarter, quarter)])
    for i in range(2):
        narrow(6 + i, bring_expand.place.at[:, pl.ds(i * units, units)])
    spread_x.wait()
    gather_x.start()
    bring_heads.relay()
    bring_heads.relay_own()
    gather_x.relay()
    bring_expand.start_y()
    bring_reduce.start_y()
    bring_heads.relay_near()
    bring_merge.relay()
    gather_x.relay_again()
    bring_merge.relay_own()
    bring_heads.hand_over()
    bring_merge.relay_near()
    bring_expand.start_z()
    bring_reduce.start_z()
    docs[...], starts = documents(lengths, docs.shape, 0)
    doc_row[...], _ = documents(lengths, doc_row.shape, 1)
    lane = lax.broadcasted_iota(jnp.int32, docs.shape, 1)
    frequency = jnp.exp((lane % (HD // 2)).astype(F32) * (-2.0 / HD * math.log(THETA)))
    angles = (lax.broadcasted_iota(jnp.int32, docs.shape, 0) - starts).astype(F32) * frequency
    cosine[...] = jnp.cos(angles)
    sine[...] = jnp.where(lane < HD // 2, -1.0, 1.0) * jnp.sin(angles)
    gather_x.wait()
    bring_heads.wait()
    puts[0].start()

    for i in range(2):
        raw[:, i * head_width : (i + 1) * head_width] = dot(
            back[...], heads[:, i * head_width : (i + 1) * head_width]
        )

    @pl.loop(0, tokens // 64)
    def _(i):
        at = span(i, 64)
        squares = raw[at] * raw[at]
        first_sums.put(
            at,
            jnp.sum(squares[:, :head_width], axis=1, keepdims=True),
            jnp.sum(squares[:, head_width:], axis=1, keepdims=True),
        )

    first_sums.start()
    qkv[:, 2 * head_width :] = dot(back[...], heads[:, 2 * head_width :]).astype(BF16)
    bring_merge.hand_over()
    bring_expand.relay()
    bring_reduce.relay()
    first_sums.end()

    @pl.loop(0, tokens // 64)
    def _(i):
        at = span(i, 64)
        rate = lax.rsqrt(rates[at] * (1.0 / width) + EPS)
        rates[at] = rate
        for j, gain in enumerate((gain_query, gain_key)):
            some = slice(j * head_width, (j + 1) * head_width)
            hat = raw[at, some] * rate[:, j : j + 1]
            qkv[at, some] = turn(hat * gain[...], cosine[at], sine[at]).astype(BF16)

    puts[1].start()
    puts[2].start()
    for b in range(tokens // QUERY_BLOCK):
        start, count = key_span(b)
        query_at = pl.ds(b * QUERY_BLOCK, QUERY_BLOCK)
        key_at = pl.ds(start, count)
        there = lax.broadcasted_iota(jnp.int32, (QUERY_BLOCK, count), 0) + (b * QUERY_BLOCK - start)
        distance = there - lax.broadcasted_iota(jnp.int32, (QUERY_BLOCK, count), 1)
        doc = docs[query_at, 0:1]
        allowed = (doc == doc_row[0:1, start : start + count]) & (distance >= 0) & (distance < WINDOW)
        live = (doc < 5.0).astype(F32)
        for h in range(head_width // HD):
            query, key, value = (
                slice(i * head_width + h * HD, i * head_width + (h + 1) * HD) for i in range(3)
            )
            scores = dot_flipped(qkv[query_at, query], qkv[key_at, key]) * HD**-0.5
            scores = jnp.where(allowed, scores, -1e30)
            weights = jnp.exp(scores - jnp.max(scores, axis=1, keepdims=True))
            shares = (weights / jnp.sum(weights, axis=1, keepdims=True)).astype(BF16)
            probs[h, b, :, :count] = shares
            if count < probs.shape[3]:
                probs[h, b, :, count:] = jnp.zeros((QUERY_BLOCK, probs.shape[3] - count), BF16)
            mix[query_at, h * HD : (h + 1) * HD] = (dot(shares, qkv[key_at, value]) * live).astype(BF16)

    bring_merge.wait()

    def merge_part(j):
        at = span(j, 256)
        part[:, at] = dot(mix[...], merge[:, at]).astype(BF16)

    pl.loop(first_right, 2 * n)(merge_part)
    merge_scatter.start_right()
    pl.loop(0, first_right)(merge_part)
    merge_scatter.start_left()
    bring_expand.relay_own()
    bring_reduce.relay_own()
    merge_scatter.middle()
    bring_expand.relay_near()
    bring_reduce.relay_near()
    merge_scatter.end()

    def place(i):
        per = half_share // 16
        return pl.ds(pl.multiple_of(i // per * batch + row * half_share + i % per * 16, 16), 16)

    @pl.loop(0, share // 16)
    def _(i):
        at = span(i, 16)
        total = merge_scatter.total[at]
        merged[at] = total
        mine = pl.ds(pl.multiple_of(row * share + i * 16, 16), 16)
        result = back[mine, :].astype(F32) + total * mean_rate(total) * gain_merge[...]
        residual[at] = result
        rows[place(i), :] = result.astype(BF16)

    row_gather[0].start()
    row_gather[0].relay()
    row_gather[1].start()
    bring_expand.hand_over()
    row_gather[0].relay_again()
    row_gather[1].relay()
    bring_reduce.hand_over()
    row_gather[0].wait()
    spread_g.start()
    row_gather[1].relay_again()
    merge_scatter.finish()
    bring_expand.wait()
    for copy in puts:
        copy.wait()

    def rows_in(m):
        return pl.ds(m * batch, batch)

    def gated(m):
        mine = rows_in(m)

        @pl.loop(0, tiles)
        def _(j):
            at = span(j, 256)
            gate[mine, at] = dot(rows[mine, :], expand[:, at])
            up[mine, at] = dot(rows[mine, :], expand[:, span(tiles + j, 256)])

            @pl.loop(m * (batch // 64), (m + 1) * (batch // 64))
            def _(i):
                some = span(i, 64)
                x = gate[some, at]
                act[some, at] = (x * jax.nn.sigmoid(x) * up[some, at]).astype(BF16)

    def reduced(m):
        mine = rows_in(m)

        def product(j):
            at = span(j, 256)
            part[mine, at] = dot(act[mine, :], reduce[:, at]).astype(BF16)

        pl.loop(first_right, 2 * n)(product)
        reduced_scatter[m].start_right()
        pl.loop(0, first_right)(product)
        reduced_scatter[m].start_left()

    def output_norm(m):
        @pl.loop(m * (half_share // 16), (m + 1) * (half_share // 16))
        def _(i):
            at = span(i, 16)
            grad = g[at].astype(F32)
            hat, change = back_of(grad, merge_scatter.total[at], gain_reduce[...])
            back[place(i), :] = change.astype(BF16)
            done[at] = (residual[at] + hat * gain_reduce[...]).astype(BF16)
            product = grad * hat
            sums[...] += product[:8] + product[8:]

    def activity_gradient(m):
        mine = rows_in(m)

        @pl.loop(0, tiles)
        def _(j):
            at, up_at = span(j, 256), span(tiles + j, 256)
            grad_gate[mine, :] = dot_flipped(back[mine, :], reduce[at, :])

            @pl.loop(m * (batch // 64), (m + 1) * (batch // 64))
            def _(i):
                some = span(i, 64)
                x, change = gate[some, at], grad_gate[some]
                s = jax.nn.sigmoid(x)
                hidden[some, at] = (change * up[some, at] * s * (1.0 + x * (1.0 - s))).astype(BF16)
                hidden[some, up_at] = (change * (x * s)).astype(BF16)

    def branch(m):
        mine = rows_in(m)

        def product(j):
            at = span(j, 256)
            part[mine, at] = dot_flipped(hidden[mine, :], expand[at, :]).astype(BF16)

        pl.loop(first_right, 2 * n)(product)
        branch_scatter[m].start_right()
        pl.loop(0, first_right)(product)
        branch_scatter[m].start_left()

    gated(0)
    bring_reduce.wait()
    spread_g.relay()
    reduced(0)
    row_gather[1].wait()
    gated(1)
    reduced_scatter[0].middle()
    reduced(1)
    spread_g.wait()
    sums[...] = jnp.zeros_like(sums)
    reduced_scatter[0].end()
    output_norm(0)
    gather[0].start()

    @pl.loop(0, tiles)
    def _(j):
        at = span(j, 256)
        act_turned[at, :] = act[:, at].T

    hand_act.start()
    get_qkv.start()
    reduced_scatter[1].middle()
    gather[0].relay()
    reduced_scatter[1].end()
    output_norm(1)
    gather[1].start()
    spread.start()
    gather[0].relay_again()
    gains[...] = jnp.zeros_like(gains)
    gains[3:4] = jnp.sum(sums[...], axis=0, keepdims=True)
    for m in range(2):
        reduced_scatter[m].finish()
    pl.loop(0, 2 * tiles)(turn_rows)
    hand_rows.start()
    get_xs.start()
    gather[0].wait()
    gather[1].relay()
    activity_gradient(0)
    gather[1].relay_again()
    branch(0)
    gather[1].wait()
    hand_back.start()
    activity_gradient(1)
    hand_hidden.start()
    get_raw.start()
    branch_scatter[0].middle()
    branch(1)
    hand_act.wait()
    hand_back.wait()
    quarter_width = width // 4
    z_far = (col // 2 + 2) % 4

    def reduce_tile(k):
        two(
            reduce, pl.ds(0, half_units), span(k, quarter_width), act_turned, span(dp, half_units), back, act_other,
            back_other,
        )

    reduce_tile(z_far)
    reduce_sum.start()

    @pl.loop(1, 4)
    def _(j):
        reduce_tile((z_far + j) % 4)

    pl.semaphore_signal(free.at[0], inc=1, device_id={"dp": 1 - dp}, device_id_type=MESH)
    branch_scatter[0].end()
    branch_scatter[1].middle()
    hand_rows.wait()
    hand_hidden.wait()
    halves = [pl.ds(side * (width // 2), width // 2) for side in range(2)]

    def expand_tile(k):
        for wide in halves:
            two(expand, span(k, 256), wide, turned, span(dp * tiles + k, 256), hidden, turned_other, hidden_other)

    expand_tile(z_far)
    expand_sum.start()

    @pl.loop(1, 4)
    def _(j):
        expand_tile((z_far + j) % 4)

    pl.semaphore_signal(free.at[1], inc=1, device_id={"dp": 1 - dp}, device_id_type=MESH)
    reduce_sum.over_z()
    branch_scatter[1].end()
    sums[...] = jnp.zeros_like(sums)

    @pl.loop(0, share // 16)
    def _(i):
        at = span(i, 16)
        grad = g[at].astype(F32) + merge_scatter.total[at]
        grad_resid[at] = grad
        hat, change = back_of(grad, merged[at], gain_merge[...])
        new_rows[pl.ds(pl.multiple_of(row * share + i * 16, 16), 16), :] = change.astype(BF16)
        product = grad * hat
        sums[...] += product[:8] + product[8:]

    last_gather.start()
    gains[2:3] = jnp.sum(sums[...], axis=0, keepdims=True)
    get_xs.wait()
    pl.loop(0, 2 * tiles)(turn_rows)
    last_gather.relay()
    last_gather.relay_again()
    get_raw.wait()
    get_qkv.wait()
    mix_turned[...] = mix[...].T
    hand_mix.start()
    expand_sum.over_z()
    pl.semaphore_wait(free.at[1], 1)
    hand_xs.start()
    for m in range(2):
        branch_scatter[m].finish()
    last_gather.wait()
    pl.semaphore_wait(free.at[0], 1)
    hand_new.start()

    spread.relay()
    live = (docs[:, 0:1] < 5.0).astype(F32)
    grad_mix[...] = (dot_flipped(new_rows[...], merge[...]) * live).astype(BF16)
    heads_change[:, head_width:] = jnp.zeros((tokens, 2 * head_width), F32)
    for b in range(tokens // QUERY_BLOCK):
        start, count = key_span(b)
        query_at = pl.ds(b * QUERY_BLOCK, QUERY_BLOCK)
        key_at = pl.ds(start, count)
        for h in range(head_width // HD):
            query, key, value = (
                slice(i * head_width + h * HD, i * head_width + (h + 1) * HD) for i in range(3)
            )
            shares = probs[h, b, :, :count]
            change = grad_mix[query_at, h * HD : (h + 1) * HD]
            grad_shares = dot_flipped(change, qkv[key_at, value])
            weighted = shares.astype(F32) * grad_shares
            center = jnp.sum(weighted, axis=1, keepdims=True)
            grad_scores = (weighted - shares.astype(F32) * center).astype(BF16)
            heads_change[query_at, query] = dot(grad_scores, qkv[key_at, key]) * HD**-0.5
            heads_change[key_at, key] += dot(grad_scores.T, qkv[query_at, query]) * HD**-0.5
            heads_change[key_at, value] += dot(shares.T, change)

    joined[:, 2 * head_width :] = heads_change[:, 2 * head_width :].astype(BF16)
    hand_values.start()
    reduce_sum.over_y()
    sums[...] = jnp.zeros_like(sums)

    @pl.loop(0, tokens // 64)
    def _(i):
        at = span(i, 64)
        dots = []
        for j, gain in enumerate((gain_query, gain_key)):
            some = slice(j * head_width, (j + 1) * head_width)
            change = turn(heads_change[at, some], cosine[at], -sine[at])
            hat = raw[at, some] * rates[at, j : j + 1]
            product = change * hat
            sums[:, some] += jnp.sum(product.reshape(8, 8, head_width), axis=0)
            heads_change[at, some] = change * gain[...]
            dots.append(jnp.sum(product * gain[...], axis=1, keepdims=True))
        token_sums.put(at, *dots)

    token_sums.start()
    gains[0:1, span(row, head_width)] = jnp.sum(sums[:, :head_width], axis=0, keepdims=True)
    gains[1:2, span(row, head_width)] = jnp.sum(sums[:, head_width : 2 * head_width], axis=0, keepdims=True)
    for copy in row_gains:
        copy.start()
    hand_mix.wait()
    hand_new.wait()
    mine = span(dp, half_heads)
    for side in range(4):
        wide = pl.ds(side * (width // 4), width // 4)
        merge[:half_heads, wide] = (
            dot(mix_turned[mine, :], back[:, wide]) + dot(mix_other[...], back_other[:, wide])
        ).astype(BF16)
    merge_sum.start()
    hand_values.wait()
    hand_xs.wait()

    @pl.loop(0, tiles)
    def _(j):
        two(
            values_part, span(j, 256), pl.ds(0, head_width), turned, span(dp * tiles + j, 256), joined.at[:, values_at],
            turned_other, joined_other.at[:, values_at],
        )

    values_sum.start()
    token_sums.end()

    @pl.loop(0, tokens // 64)
    def _(i):
        at = span(i, 64)
        dots = stats[at] * (1.0 / width)
        for j in range(2):
            some = slice(j * head_width, (j + 1) * head_width)
            rate = rates[at, j : j + 1]
            hat = raw[at, some] * rate
            joined[at, some] = (rate * (heads_change[at, some] - hat * dots[:, j : j + 1])).astype(BF16)

    hand_joined.start()
    def input_part(j):
        at = span(j, 256)
        part[:, at] = dot_flipped(joined[...], heads[at, :]).astype(BF16)

    pl.loop(first_right, 2 * n)(input_part)
    input_scatter.start_right()
    pl.loop(0, first_right)(input_part)
    input_scatter.start_left()
    hand_joined.wait()

    def heads_tile(k):
        two(heads, span(k, 256), others_at, turned, span(dp * tiles + k, 256), joined, turned_other, joined_other)

    heads_tile(z_far)
    heads_sum.start()

    @pl.loop(1, 4)
    def _(j):
        heads_tile((z_far + j) % 4)

    for copy in row_gains:
        copy.wait()
    gain_row[row] = gains[...]
    total = gain_row[0]
    for k in range(1, 8):
        total = total + gain_row[k]
    gain_sum[0] = total
    gain_col[col] = total
    for copy in col_gains:
        copy.start()
    input_scatter.middle()
    values_sum.over_z()
    merge_sum.over_z()
    heads_sum.over_z()
    reduce_sum.end()
    expand_sum.over_y()
    input_scatter.end()
    final[...] = (grad_resid[...] + input_scatter.total[...]).astype(BF16)
    spread_grad.start()
    values_sum.over_y()
    merge_sum.over_y()
    heads_sum.over_y()
    for copy in col_gains:
        copy.wait()
    total = gain_col[0]
    for k in range(1, 8):
        total = total + gain_col[k]
    gain_sum[1] = total
    core_gains.start()
    spread_grad.relay()
    expand_sum.end()
    values_sum.end()
    merge_sum.end()
    heads_sum.end()
    core_gains.wait()
    gains_grad[...] = gain_sum[1] + gain_core[...]
    input_scatter.finish()
    spread.wait()
    spread_grad.wait()
    for grad in (reduce_sum, expand_sum, values_sum, merge_sum, heads_sum):
        grad.wait()


def on_device(
    block_input,
    cotangent,
    doc_lengths,
    heads_weight,
    heads_first,
    heads_second,
    merge_weight,
    merge_first,
    merge_second,
    expand_weight,
    expand_first,
    expand_second,
    reduce_weight,
    reduce_first,
    reduce_second,
    norm_gains,
    gains_first,
    gains_second,
):
    col_width = block_input.shape[1]
    model_width = col_width * lax.axis_size("col")
    head_width = merge_weight.shape[0]
    unit_width = reduce_weight.shape[0]
    seq_len = block_input.shape[0] * lax.axis_size("row") // lax.axis_size("col")
    share = seq_len // lax.axis_size("row")
    head_count = head_width // HD
    rows_shape = struct((seq_len, model_width), BF16)
    blocks = seq_len // QUERY_BLOCK

    gain_shape = (4, model_width)
    block_output, input_grad, gains_grad, heads_grad, merge_grad, expand_grad, reduce_grad = call(
        layer_kernel, "layer", 1,
        [
            struct(block_input.shape, BF16),
            struct(block_input.shape, BF16),
            struct(gain_shape, F32),
            struct(heads_weight.shape, BF16),
            struct(merge_weight.shape, BF16),
            struct(expand_weight.shape, BF16),
            struct(reduce_weight.shape, BF16),
            rows_shape,
            struct((seq_len, 2 * head_width), F32),
            struct((seq_len, 3 * head_width), BF16),
        ],
        [
            block_input, cotangent, heads_weight, merge_weight, expand_weight, reduce_weight, doc_lengths, norm_gains,
        ],
        [ANY] * 6 + [pl.BlockSpec(memory_space=pltpu.SMEM), VMEM],
        [ANY] * 2 + [VMEM] + [ANY] * 7,
        [
            pltpu.VMEM((seq_len, model_width), BF16),
            pltpu.VMEM((model_width, seq_len), BF16),
            pltpu.VMEM((model_width, 2 * unit_width), BF16),
            pltpu.VMEM((unit_width, model_width), BF16),
            pltpu.VMEM((model_width, 3 * head_width), BF16),
            pltpu.VMEM((head_width, model_width), BF16),
            pltpu.VMEM((seq_len, unit_width), F32),
            pltpu.VMEM((seq_len, unit_width), F32),
            pltpu.VMEM((seq_len, unit_width), BF16),
            pltpu.VMEM((unit_width, seq_len), BF16),
            pltpu.VMEM((seq_len, model_width), BF16),
            pltpu.VMEM((seq_len, model_width), BF16),
            pltpu.VMEM((seq_len, 2 * unit_width), BF16),
            pltpu.VMEM((head_count, blocks, QUERY_BLOCK, WINDOW + QUERY_BLOCK), BF16),
            pltpu.VMEM((seq_len, head_width), BF16),
            pltpu.VMEM((head_width, seq_len), BF16),
            pltpu.VMEM((seq_len, 128), F32),
            pltpu.VMEM((seq_len, 128), F32),
            pltpu.VMEM((seq_len, head_width), BF16),
            pltpu.VMEM((share, model_width), BF16),
            pltpu.VMEM((share, model_width), BF16),
            pltpu.VMEM((share, model_width), F32),
            pltpu.VMEM((share, model_width), F32),
            pltpu.VMEM((share, model_width), F32),
            pltpu.VMEM((share, model_width), BF16),
            pltpu.VMEM((8, model_width), F32),
            pltpu.VMEM((seq_len, 256), F32),
            pltpu.VMEM(gain_shape, F32),
            pltpu.VMEM((8, *gain_shape), F32),
            pltpu.VMEM((8, *gain_shape), F32),
            pltpu.VMEM(gain_shape, F32),
            pltpu.VMEM((2, *gain_shape), F32),
            pltpu.VMEM((unit_width // 2, seq_len), BF16),
            pltpu.VMEM((model_width // 2, seq_len), BF16),
            pltpu.VMEM((seq_len, model_width), BF16),
            pltpu.VMEM((seq_len, model_width), BF16),
            pltpu.VMEM((head_width // 2, seq_len), BF16),
            pltpu.VMEM((seq_len, 3 * head_width), BF16),
            pltpu.VMEM((model_width // 2, head_width), BF16),
            pltpu.VMEM((3, 8, share, block_input.shape[1]), BF16),
            pltpu.VMEM((seq_len, HD), F32),
            pltpu.VMEM((8, seq_len), F32),
            pltpu.VMEM((seq_len, HD), F32),
            pltpu.VMEM((seq_len, HD), F32),
            pltpu.SemaphoreType.REGULAR((2,)),
            DMA((8,)), DMA((3,)), DMA((3,)), DMA((16,)), DMA((15,)), DMA((16,)), DMA((15,)), DMA((15,)), DMA((15,)),
            DMA((9,)), DMA((9,)), DMA((8,)), DMA((8,)), DMA((16,)), DMA((15,)),
        ]
        + gather_scratch() * 6
        + scatter_scratch(share, model_width) + [DMA((14,))] * 10
        + sums_scratch(seq_len) * 2
        + grad_sum_scratch(reduce_weight.shape) + grad_sum_scratch(expand_weight.shape)
        + grad_sum_scratch(merge_weight.shape)
        + grad_sum_scratch((heads_weight.shape[0], head_width))
        + grad_sum_scratch((heads_weight.shape[0], 2 * head_width))
        + bring_scratch() * 4,
    )[:7]
    return update(
        block_output,
        input_grad,
        (heads_grad, heads_weight, heads_first, heads_second),
        (merge_grad, merge_weight, merge_first, merge_second),
        (expand_grad, expand_weight, expand_first, expand_second),
        (reduce_grad, reduce_weight, reduce_first, reduce_second),
        (gains_grad, norm_gains, gains_first, gains_second),
    )


def solution(mesh):
    return jax.shard_map(
        on_device,
        mesh=mesh,
        in_specs=(
            P(("dp", "row"), "col"),
            P(("dp", "row"), "col"),
            P(("dp", "col"), None),
            P("col", "row"),
            P("col", "row"),
            P("col", "row"),
            P("row", "col"),
            P("row", "col"),
            P("row", "col"),
            P("col", "row"),
            P("col", "row"),
            P("col", "row"),
            P("row", "col"),
            P("row", "col"),
            P("row", "col"),
            P(),
            P(),
            P(),
        ),
        out_specs=(
            P(("dp", "row"), "col"),
            P(("dp", "row"), "col"),
            P("col", "row"),
            P("col", "row"),
            P("col", "row"),
            P("col", "row"),
            P("col", "row"),
            P("row", "col"),
            P("row", "col"),
            P("row", "col"),
            P("row", "col"),
            P("row", "col"),
            P("col", "row"),
            P("col", "row"),
            P("col", "row"),
            P("col", "row"),
            P("col", "row"),
            P("row", "col"),
            P("row", "col"),
            P("row", "col"),
            P("row", "col"),
            P("row", "col"),
            P(),
            P(),
            P(),
            P(),
        ),
        check_vma=False,
    )
```
